32 devices in a mesh: rows: 32 (over z, y, x, core).
Axes of the slice: x: 2, y: 2, z: 4, core: 2. Of those that a mesh axis runs over, the one named last changes fastest.
Arguments:
- trailing: float32 [16384, 1024], P('rows'), may hold values from -50 to 50
- leaf_vectors: float32 [16384, 256], P('rows'), may hold values from -2 to 2, as said below
- leaf_factors: float32 [8192, 256], P('rows'), may hold values from -2 to 2, as said below
- tree_vectors: float32 [8192, 256], P('rows'), may hold values from -2 to 2, as said below
- tree_factors: float32 [8192, 256], P('rows'), may hold values from -2 to 2, as said below
- inverse_factor: float32 [256, 256], replicated, may hold values from -2 to 2, as said below
Outputs:
- updated: float32 [16384, 1024], P('rows')
- panel_basis: float32 [16384, 256], P('rows')
- panel_gram: float32 [256, 256], replicated
The draws below stay inside these ranges and needn't reach their ends.
Inputs may be any that keep to these rules, and one draw needn't show every extreme that they name: Within each leaf, rows 0 to 255 of leaf_vectors form a unit lower triangular matrix (ones on the diagonal, zeros above); leaf_factors_p is the upper triangular factor for which I - leaf_vectors_p leaf_factors_p leaf_vectors_p^T is orthogonal. `leaf_factors`: each block is upper triangular and is the factor described for leaf_vectors. `tree_vectors`: each block is upper triangular, diagonal included; with Y = [I; tree_vectors_q], I - Y tree_factors_q Y^T is orthogonal. `tree_factors`: each block is upper triangular and is the factor described for tree_vectors. `inverse_factor`: upper triangular with a positive diagonal.
All inputs are finite; a program needn't handle non-finite values.
Results may differ from the reference program's by a relative error of at most 0.00018.
Values sent between devices are 32-bit elements; how exact they have to be, the bound alone decides.
No kernel may reach another device: no remote copies, remote signals or barrier semaphores. Data moves between devices by JAX's collectives and lax.ppermute only.
A program may use at most 64 MiB of HBM per device.

```python
import math
import jax
import jax.numpy as jnp
from jax import lax

PANEL = 256
NC = 1024
ROWS_DEV = 512
LEVELS = 5
ROWS_ALL = 16384
TREE_ROWS = 8192


def factor_from(gram_part):
    diagonal_part = jnp.diagonal(gram_part, axis1=1, axis2=2)
    upper_part = jnp.triu(gram_part, 1) + jax.vmap(jnp.diag)(diagonal_part * 0.5)
    identity = jnp.eye(PANEL, dtype=jnp.float32)
    return jax.vmap(lambda m: jax.scipy.linalg.solve_triangular(m, identity, lower=False))(upper_part)


def leaf_pair(key):
    draw_key = jax.random.fold_in(key, 11)
    block_count = ROWS_ALL // ROWS_DEV
    samples = jax.random.truncated_normal(draw_key, -6.0, 6.0, (block_count, ROWS_DEV, PANEL), jnp.float32) / math.sqrt(ROWS_DEV)
    row_index = lax.broadcasted_iota(jnp.int32, (ROWS_DEV, PANEL), 0)
    col_index = lax.broadcasted_iota(jnp.int32, (ROWS_DEV, PANEL), 1)
    vectors = jnp.where(row_index > col_index, samples, jnp.where(row_index == col_index, 1.0, 0.0))
    gram_part = jnp.einsum('brp,brq->bpq', vectors, vectors, precision=lax.Precision.HIGHEST)
    return (vectors, factor_from(gram_part))


def tree_pair(key):
    draw_key = jax.random.fold_in(key, 23)
    block_count = TREE_ROWS // PANEL
    samples = jax.random.truncated_normal(draw_key, -6.0, 6.0, (block_count, PANEL, PANEL), jnp.float32) / math.sqrt(PANEL)
    row_index = lax.broadcasted_iota(jnp.int32, (PANEL, PANEL), 0)
    col_index = lax.broadcasted_iota(jnp.int32, (PANEL, PANEL), 1)
    vectors = jnp.where(row_index <= col_index, samples, 0.0)
    gram_part = jnp.eye(PANEL, dtype=jnp.float32) + jnp.einsum('brp,brq->bpq', vectors, vectors, precision=lax.Precision.HIGHEST)
    return (vectors, factor_from(gram_part))


def draw_trailing(key, part):
    block_count = ROWS_ALL // ROWS_DEV
    leaf_index = jnp.arange(ROWS_ALL, dtype=jnp.int32) // ROWS_DEV
    row_ramp = 0.5 + leaf_index.astype(jnp.float32) / max(block_count - 1, 1)
    values = jax.random.truncated_normal(key, -6.0, 6.0, (ROWS_ALL, NC), jnp.float32)
    return values * row_ramp[:, None]


def draw_leaf_vectors(key, part):
    vectors, factors = leaf_pair(key)
    return vectors.reshape(ROWS_ALL, PANEL)


def draw_leaf_factors(key, part):
    vectors, factors = leaf_pair(key)
    return factors.reshape(TREE_ROWS, PANEL)


def draw_tree_vectors(key, part):
    vectors, factors = tree_pair(key)
    return vectors.reshape(TREE_ROWS, PANEL)


def draw_tree_factors(key, part):
    vectors, factors = tree_pair(key)
    return factors.reshape(TREE_ROWS, PANEL)


def draw_inverse_factor(key, part):
    key_a, key_b = jax.random.split(jax.random.fold_in(key, 37))
    diagonal_part = jnp.exp(jax.random.uniform(key_a, (PANEL,), jnp.float32, math.log(0.5), math.log(2.0)))
    samples = jax.random.truncated_normal(key_b, -6.0, 6.0, (PANEL, PANEL), jnp.float32) * (0.5 / math.sqrt(PANEL))
    return jnp.triu(samples, 1) + jnp.diag(diagonal_part)


def setup_inputs(seed: int = 0) -> dict:
    streams_of = jax.random.split(jax.random.key(seed), 7)
    trailing = draw_trailing(jax.random.fold_in(streams_of[6], 71), 0)
    leaf_vectors = draw_leaf_vectors(jax.random.fold_in(streams_of[6], 71), 0)
    leaf_factors = draw_leaf_factors(jax.random.fold_in(streams_of[6], 71), 0)
    tree_vectors = draw_tree_vectors(jax.random.fold_in(streams_of[6], 71), 0)
    tree_factors = draw_tree_factors(jax.random.fold_in(streams_of[6], 71), 0)
    inverse_factor = draw_inverse_factor(jax.random.fold_in(streams_of[6], 71), 0)
    return {"trailing": trailing, "leaf_vectors": leaf_vectors, "leaf_factors": leaf_factors, "tree_vectors": tree_vectors, "tree_factors": tree_factors, "inverse_factor": inverse_factor}


HIGHEST = lax.Precision.HIGHEST

def multiply(left_side, right_side):
    return jnp.dot(left_side.astype(jnp.float32), right_side.astype(jnp.float32), precision=HIGHEST, preferred_element_type=jnp.float32)

def leaf_apply(inputs):
    piece, vectors, factors = inputs
    coeffs = multiply(factors.T, multiply(vectors.T, piece))
    return piece - multiply(vectors, coeffs)

def reference(trailing, leaf_vectors, leaf_factors, tree_vectors, tree_factors, inverse_factor):
    block_count = ROWS_ALL // ROWS_DEV
    pieces = trailing.reshape(block_count, ROWS_DEV, NC)
    leaf_out = lax.map(leaf_apply, (pieces, leaf_vectors.reshape(block_count, ROWS_DEV, PANEL), leaf_factors.reshape(block_count, PANEL, PANEL)))
    head_rows = leaf_out[:, :PANEL, :]
    all_vectors = tree_vectors.reshape(block_count, PANEL, PANEL)
    all_factors = tree_factors.reshape(block_count, PANEL, PANEL)
    for tree_level in range(LEVELS):
        stride = 2 ** tree_level
        groups = block_count // (2 * stride)
        grouped = head_rows.reshape(groups, 2, stride, PANEL, NC)
        low_rows = grouped[:, 0, 0]
        high_rows = grouped[:, 1, 0]
        pair_vectors = all_vectors.reshape(groups, 2, stride, PANEL, PANEL)[:, 1, 0]
        pair_factors = all_factors.reshape(groups, 2, stride, PANEL, PANEL)[:, 1, 0]
        inner = low_rows + jnp.einsum('gqp,gqn->gpn', pair_vectors, high_rows, precision=HIGHEST)
        coeffs = jnp.einsum('gqp,gqn->gpn', pair_factors, inner, precision=HIGHEST)
        low_rows = low_rows - coeffs
        high_rows = high_rows - jnp.einsum('gpq,gqn->gpn', pair_vectors, coeffs, precision=HIGHEST)
        grouped = grouped.at[:, 0, 0].set(low_rows).at[:, 1, 0].set(high_rows)
        head_rows = grouped.reshape(block_count, PANEL, NC)
    result_rows = leaf_out.at[:, :PANEL, :].set(head_rows).reshape(ROWS_ALL, NC)
    panel_cols = result_rows[:, :PANEL]
    lower_cols = panel_cols[PANEL:]
    gram_sum = multiply(lower_cols.T, lower_cols) / ROWS_ALL
    row_index = lax.broadcasted_iota(jnp.int32, (ROWS_ALL, PANEL), 0)
    basis = jnp.where(row_index >= PANEL, multiply(panel_cols, inverse_factor), 0.0)
    return (result_rows, basis, gram_sum)
```

```python
import jax
import jax.numpy as jnp
from jax import lax
from jax.sharding import PartitionSpec as P

HIGH = lax.Precision.HIGH


def product(left_side, right_side):
    return jnp.dot(left_side, right_side, precision=HIGH, preferred_element_type=jnp.float32)


def across(left_side, right_side):
    return lax.dot_general(
        left_side,
        right_side,
        (((0,), (0,)), ((), ())),
        precision=HIGH,
        preferred_element_type=jnp.float32,
    )


def body(trailing, leaf_vectors, leaf_factors, tree_vectors, tree_factors, inverse_factor):
    width = leaf_vectors.shape[1]
    columns = trailing.shape[1]
    devices = lax.axis_size("rows")
    levels = devices.bit_length() - 1
    me = lax.axis_index("rows")
    upper = [(me >> level) % 2 == 1 for level in range(levels)]

    def exchange(value, level, member):
        stride = 1 << level
        return lax.ppermute(value, "rows", [(i, i ^ stride) for i in range(devices) if member(i)])

    panel = trailing[:, :width]
    gram_total = across(panel, panel)
    for level in range(levels):
        if level == 0:
            gram_total = gram_total + exchange(gram_total, 0, lambda i: True)
        else:
            gram_total = gram_total + exchange(gram_total, level, lambda i: i % 2 == 1)

    held_factors, held_vectors = tree_factors, tree_vectors
    node_factors, node_vectors = [], []
    for level in range(levels):
        stride = 1 << level
        lowest = level == 0
        highest = level == levels - 1
        if lowest or highest:
            there = exchange(held_factors, level, lambda i: (lowest or i % 2 == 0) and i & stride)
        else:
            there = exchange(held_factors, level, lambda i: i % 2 == 0)
        node_factors.append(jnp.where(upper[level], held_factors, there))
        node_vectors.append(held_vectors)
        if not (lowest or highest):
            there_vectors = exchange(held_vectors, level, lambda i: i % 2 == 0 and not i & stride)
            held_factors = jnp.where(upper[level], there, held_factors)
            held_vectors = jnp.where(upper[level], there_vectors, held_vectors)

    head_parts, rest_parts = [], []
    first_panel = None
    for start in range(0, columns, width):
        part = trailing[:, start : start + width]
        coeffs = across(leaf_factors, across(leaf_vectors, part))
        head = part[:width] - product(leaf_vectors[:width], coeffs)
        rest_parts.append(part[width:] - product(leaf_vectors[width:], coeffs))
        result = head
        for level in range(levels):
            stride = 1 << level
            mine = jnp.where(upper[level], across(node_vectors[level], head), head)
            if start == 0:
                there = exchange(mine, level, lambda i: level == 0 or i % 2 == 0)
            else:
                there = exchange(mine, level, lambda i: i % stride == 0)
            node = across(node_factors[level], mine + there)
            is_second = me % (2 * stride) == stride
            result = jnp.where(is_second, head - product(node_vectors[level], node), result)
            head = jnp.where(upper[level], there, head) - node
        result = jnp.where(me == 0, head, result)
        head_parts.append(result)
        if start == 0:
            first_panel = head

    first_gram = across(first_panel, first_panel)
    mine = jnp.where(upper[0], gram_total, first_gram)
    there = exchange(mine, 0, lambda i: True)
    gram = jnp.where(upper[0], mine - there, there - mine)
    panel_gram = gram / float(trailing.shape[0] * devices)
    head_basis = jnp.where(me == 0, 0.0, product(head_parts[0], inverse_factor))
    rest_basis = product(rest_parts[0], inverse_factor)
    panel_basis = jnp.concatenate([head_basis, rest_basis], axis=0)
    updated = jnp.concatenate(
        [jnp.concatenate(head_parts, axis=1), jnp.concatenate(rest_parts, axis=1)], axis=0
    )
    return (updated, panel_basis, panel_gram)


def solution(mesh):
    in_specs = (
        P("rows", None),
        P("rows", None),
        P("rows", None),
        P("rows", None),
        P("rows", None),
        P(),
    )
    out_specs = (P("rows", None), P("rows", None), P())
    return jax.shard_map(body, mesh=mesh, in_specs=in_specs, out_specs=out_specs, check_vma=False)
```

```python
import jax
import jax.numpy as jnp
from jax import lax
from jax.sharding import PartitionSpec as P

HIGH = lax.Precision.HIGH


def product(left_side, right_side):
    return jnp.dot(left_side, right_side, precision=HIGH, preferred_element_type=jnp.float32)


def across(left_side, right_side):
    return lax.dot_general(
        left_side,
        right_side,
        (((0,), (0,)), ((), ())),
        precision=HIGH,
        preferred_element_type=jnp.float32,
    )


def body(trailing, leaf_vectors, leaf_factors, tree_vectors, tree_factors, inverse_factor):
    width = leaf_vectors.shape[1]
    columns = trailing.shape[1]
    devices = lax.axis_size("rows")
    levels = devices.bit_length() - 1
    me = lax.axis_index("rows")
    upper = [(me >> level) % 2 == 1 for level in range(levels)]

    def exchange(value, level, member):
        stride = 1 << level
        return lax.ppermute(value, "rows", [(i, i ^ stride) for i in range(devices) if member(i)])

    panel = trailing[:, :width]
    slabs = across(panel, panel).reshape(devices, width // devices, width)
    slab = jnp.sum(lax.all_to_all(slabs, "rows", 0, 0), axis=0)
    slabs = jnp.broadcast_to(slab, slabs.shape)
    gram_total = lax.all_to_all(slabs, "rows", 0, 0).reshape(width, width)

    held = jnp.stack([tree_factors, tree_vectors])
    there = exchange(tree_factors, 0, lambda i: i % 2 == 1)
    node_factors = [jnp.where(upper[0], tree_factors, there)]
    node_vectors = [tree_vectors]
    for level in range(1, levels, 2):
        bits = min(2, levels - level)
        base = [i for i in range(devices) if (i >> level) % (1 << bits) == 0]
        groups = [[i + (j << level) for j in range(1 << bits)] for i in base]
        gathered = lax.all_gather(held, "rows", axis_index_groups=groups)
        if bits == 2:
            first = jnp.where(upper[level + 1], gathered[3], gathered[1])
            nodes = (first, gathered[2])
        else:
            nodes = (gathered[1],)
        for node in nodes:
            node_factors.append(node[0])
            node_vectors.append(node[1])
        held = gathered[0]

    head_parts, rest_parts = [], []
    first_panel = None
    for start in range(0, columns, width):
        part = trailing[:, start : start + width]
        coeffs = across(leaf_factors, across(leaf_vectors, part))
        head = part[:width] - product(leaf_vectors[:width], coeffs)
        rest_parts.append(part[width:] - product(leaf_vectors[width:], coeffs))
        result = head
        for level in range(levels):
            stride = 1 << level
            mine = jnp.where(upper[level], across(node_vectors[level], head), head)
            if start == 0:
                there = exchange(mine, level, lambda i: level == 0 or i % 2 == 0)
            else:
                there = exchange(mine, level, lambda i: i % stride == 0)
            node = across(node_factors[level], mine + there)
            is_second = me % (2 * stride) == stride
            result = jnp.where(is_second, head - product(node_vectors[level], node), result)
            head = jnp.where(upper[level], there, head) - node
        result = jnp.where(me == 0, head, result)
        head_parts.append(result)
        if start == 0:
            first_panel = head

    first_gram = across(first_panel, first_panel)
    mine = jnp.where(upper[0], gram_total, first_gram)
    there = exchange(mine, 0, lambda i: True)
    gram = jnp.where(upper[0], mine - there, there - mine)
    panel_gram = gram / float(trailing.shape[0] * devices)
    head_basis = jnp.where(me == 0, 0.0, product(head_parts[0], inverse_factor))
    rest_basis = product(rest_parts[0], inverse_factor)
    panel_basis = jnp.concatenate([head_basis, rest_basis], axis=0)
    updated = jnp.concatenate(
        [jnp.concatenate(head_parts, axis=1), jnp.concatenate(rest_parts, axis=1)], axis=0
    )
    return (updated, panel_basis, panel_gram)


def solution(mesh):
    in_specs = (
        P("rows", None),
        P("rows", None),
        P("rows", None),
        P("rows", None),
        P("rows", None),
        P(),
    )
    out_specs = (P("rows", None), P("rows", None), P())
    return jax.shard_map(body, mesh=mesh, in_specs=in_specs, out_specs=out_specs, check_vma=False)
```

```python
import functools
import jax
import jax.numpy as jnp
from jax import lax
from jax.experimental import pallas as pl
from jax.experimental.pallas import tpu as pltpu
from jax.sharding import PartitionSpec as P

F32 = jnp.float32
BF16 = jnp.bfloat16
EXTRA = 8
PARAMS = pltpu.CompilerParams(vmem_limit_bytes=40 * 1024 * 1024)
WHOLE = pl.BlockSpec(memory_space=pltpu.VMEM)
SCALAR = pl.BlockSpec(memory_space=pltpu.SMEM)


def halves(value):
    high = value.astype(BF16)
    return high, (value - high.astype(F32)).astype(BF16)


def times(left, right, sides):
    dims = ((sides[:1], sides[1:]), ((), ()))
    dot = functools.partial(lax.dot_general, dimension_numbers=dims, preferred_element_type=F32)
    return dot(left[0], right[0]) + (dot(left[0], right[1]) + dot(left[1], right[0]))


def plain(left, right):
    return times(left, right, (1, 0))


def by_transpose(left, right):
    return times(left, right, (1, 1))


def pack_kernel(vectors_ref, factors_ref, out_ref):
    width = vectors_ref.shape[0]
    row = lax.broadcasted_iota(jnp.int32, (width, width), 0)
    col = lax.broadcasted_iota(jnp.int32, (width, width), 1)
    factors = factors_ref[...]
    packed = jnp.where(row > col, factors.T, vectors_ref[...])
    diagonal = jnp.sum(jnp.where(row == col, factors, 0.0), axis=0, keepdims=True)
    half = width // 2
    for part in range(2):
        out_ref[part, :half] = packed[part * half : (part + 1) * half]
        out_ref[part, half:] = jnp.broadcast_to(diagonal, (EXTRA, width))


def unpack(first, second):
    half = first.shape[0] - EXTRA
    width = 2 * half
    packed = jnp.concatenate([first[:half], second[:half]], axis=0)
    row = lax.broadcasted_iota(jnp.int32, (width, width), 0)
    col = lax.broadcasted_iota(jnp.int32, (width, width), 1)
    diagonal = jnp.broadcast_to(first[half : half + 1], (width, width))
    vectors = jnp.where(row <= col, packed, 0.0)
    factors = jnp.where(row > col, packed, jnp.where(row == col, diagonal, 0.0))
    return halves(vectors), halves(factors)


def by_core(core, mine, there):
    odd = core == 1
    return jnp.where(odd, there, mine), jnp.where(odd, mine, there)


def tree_node(low, high, reflector):
    vectors, factors = reflector
    node = by_transpose(halves(low + plain(halves(high), vectors)), factors)
    return low - node, high - by_transpose(halves(node), vectors)


def leaf_kernel(
    me_ref, trailing_ref, vectors_ref, factors_ref, inverse_ref,
    own_ref, away_ref, updated_ref, basis_ref, head_ref, gram_ref, v_high, v_low, f_high, f_low,
):
    block = pl.program_id(0)
    width = factors_ref.shape[0]
    half = width // 2
    core = me_ref[0] % 2
    mine = pl.multiple_of(core * half, half)
    other = pl.multiple_of((1 - core) * half, half)

    @pl.when(block == 0)
    def _():
        v_high[...], v_low[...] = halves(vectors_ref[...])
        f_high[...], f_low[...] = halves(factors_ref[...])

    vectors = (v_high[...], v_low[...])
    part = trailing_ref[...].T
    split = halves(part)
    coeffs = plain(halves(plain(split, vectors)), (f_high[...], f_low[...]))
    out = part - by_transpose(halves(coeffs), vectors)
    head_ref[...] = out[:, :width]
    rows = pl.ds(pl.multiple_of(block * half, half), half)
    own_ref[rows] = head_ref[pl.ds(mine, half)]
    away_ref[rows] = head_ref[pl.ds(other, half)]
    rest = out[:, width:].T
    updated_ref[...] = rest

    @pl.when(block == 0)
    def _():
        gram_ref[...] = by_transpose(split, split)
        last = pl.ds(own_ref.shape[0] - half, half)
        own_ref[last] = gram_ref[pl.ds(mine, half)]
        away_ref[last] = gram_ref[pl.ds(other, half)]
        basis_ref[...] = plain(halves(rest), halves(inverse_ref[...]))


def core_kernel(me_ref, own_ref, there_ref, packed_ref, packed_there_ref, send_ref, done_ref):
    width = own_ref.shape[1]
    half = width // 2
    quarter = half // 4
    count = own_ref.shape[0] // half - 1
    core = me_ref[0] % 2
    odd = core == 1
    mine, there = own_ref[: count * half], there_ref[: count * half]
    first = jnp.where(odd, packed_ref[0], packed_there_ref[0])
    second = jnp.where(odd, packed_ref[1], packed_there_ref[1])
    low = jnp.where(odd, there, mine)
    high = jnp.where(odd, mine, there)
    low, high = tree_node(low, high, unpack(first, second))
    gram = own_ref[count * half :] + there_ref[count * half :]
    for j in range(4):
        for b in range(count):
            source = slice((b * 4 + j) * quarter, (b * 4 + j + 1) * quarter)
            target = slice(b * quarter, (b + 1) * quarter)
            send_ref[j, target] = low[source]
            done_ref[j, target] = high[source]
        send_ref[j, count * quarter :] = gram[j * quarter : (j + 1) * quarter]


def plane_kernel(
    me_ref, got_ref, packed_ref, packed_there_ref, head_ref, send_ref, done_ref, *, level
):
    me = me_ref[0]
    core = me % 2
    cols = done_ref.shape[1]
    reflectors = [
        unpack(*by_core(core, packed_ref[j], packed_there_ref[j])) for j in range(4)
    ]
    heads = [got_ref[j, :cols] for j in range(4)]
    gram = got_ref[0, cols:]
    for j in range(1, 4):
        gram = gram + got_ref[j, cols:]
    heads[0], heads[1] = tree_node(heads[0], heads[1], reflectors[1])
    heads[2], heads[3] = tree_node(heads[2], heads[3], reflectors[3])
    heads[0], heads[2] = tree_node(heads[0], heads[2], reflectors[2])
    for j in range(1, 4):
        done_ref[j - 1] = heads[j]
    head_ref[...] = heads[0]
    upper = (me >> level) % 2 == 1
    send_ref[:cols] = jnp.where(upper, plain(halves(heads[0]), reflectors[0][0]), heads[0])
    send_ref[cols:] = gram


def line_kernel(
    me_ref, head_ref, result_ref, mine_ref, there_ref, held_ref, held_there_ref,
    node_ref, node_there_ref, next_ref, next_there_ref,
    head_out, result_out, send_ref, *, level, last,
):
    me = me_ref[0]
    core = me % 2
    cols = head_ref.shape[0]
    upper = (me >> level) % 2 == 1
    held = unpack(*by_core(core, held_ref[...], held_there_ref[...]))
    node = unpack(*by_core(core, node_ref[...], node_there_ref[...]))
    head = head_ref[...]
    there = there_ref[:cols]
    coeffs = by_transpose(halves(mine_ref[:cols] + there), node[1])
    low = jnp.where(upper, there, head) - coeffs
    plane = me >> 3
    below = (1 << (level - 2)) - 1
    second = (plane & below) == (1 << (level - 3))
    result = jnp.where(second, head - by_transpose(halves(coeffs), held[0]), result_ref[...])
    gram = mine_ref[cols:] + there_ref[cols:]
    if last:
        result_out[...] = jnp.where(plane == 0, low, result)
    else:
        result_out[...] = result
        following = unpack(*by_core(core, next_ref[...], next_there_ref[...]))
        ahead = (me >> (level + 1)) % 2 == 1
        send_ref[:cols] = jnp.where(ahead, plain(halves(low), following[0]), low)
        send_ref[cols:] = gram
    head_out[...] = low
    if last:
        send_ref[:cols] = low
        send_ref[cols:] = gram


def final_kernel(
    me_ref, back_ref, there_ref, done_ref, inverse_ref, updated_in, basis_in,
    updated_ref, basis_ref, gram_ref, head_ref, *, total,
):
    block = pl.program_id(0)
    width = inverse_ref.shape[0]
    half = width // 2
    quarter = half // 4
    cols = back_ref.shape[1] - 2 * quarter
    me = me_ref[0]
    odd = me % 2 == 1
    rows = pl.ds(pl.multiple_of(block * quarter, quarter), quarter)
    for j in range(4):
        there = there_ref[j, rows]
        done = done_ref[j, rows]
        head_ref[j * quarter : (j + 1) * quarter] = jnp.where(odd, there, back_ref[j, rows])
        head_ref[half + j * quarter : half + (j + 1) * quarter] = jnp.where(odd, done, there)
    head = head_ref[...].T
    updated_ref[...] = head

    @pl.when(block == 0)
    def _():
        basis = plain(halves(head), halves(inverse_ref[...]))
        basis_ref[...] = jnp.where(me == 0, 0.0, basis)
        parts = []
        for start in (cols, cols + quarter):
            mine = jnp.concatenate([back_ref[j, start : start + quarter] for j in range(4)], axis=0)
            there = jnp.concatenate([there_ref[j, start : start + quarter] for j in range(4)], axis=0)
            parts.append(jnp.concatenate(by_core(me % 2, mine, there), axis=0))
        panel = halves(parts[0])
        gram_ref[...] = (parts[1] - by_transpose(panel, panel)) / total


def body(trailing, leaf_vectors, leaf_factors, tree_vectors, tree_factors, inverse_factor):
    rows, columns = trailing.shape
    width = leaf_vectors.shape[1]
    half = width // 2
    quarter = half // 4
    count = columns // width
    cols = count * quarter
    devices = lax.axis_size("rows")
    levels = devices.bit_length() - 1
    me = lax.axis_index("rows").astype(jnp.int32)
    me_array = me.reshape(1)
    odd = me % 2 == 1
    plane_groups = [[base + 2 * j + core for j in range(4)] for base in range(0, devices, 8) for core in range(2)]

    def exchange(value, level, member=lambda i: True):
        stride = 1 << level
        return lax.ppermute(value, "rows", [(i, i ^ stride) for i in range(devices) if member(i)])

    def around(value):
        return lax.all_to_all(value, "rows", 0, 0, axis_index_groups=plane_groups)

    def shape(*dims):
        return jax.ShapeDtypeStruct(dims, F32)

    def whole_call(kernel, scalars, operands, outs):
        return pl.pallas_call(
            kernel,
            out_shape=outs,
            in_specs=[SCALAR] * scalars + [WHOLE] * (len(operands) - scalars),
            out_specs=tuple([WHOLE] * len(outs)) if isinstance(outs, tuple) else WHOLE,
            compiler_params=PARAMS,
        )(*operands)

    packed = whole_call(pack_kernel, 0, (tree_vectors, tree_factors), shape(2, half + EXTRA, width))
    packed_there = exchange(packed, 0)
    chip_part = jnp.where(odd, packed_there[1], packed[0])
    plane_part = around(jnp.broadcast_to(chip_part, (4,) + chip_part.shape))
    plane_there = exchange(plane_part, 0)

    leaf_rows = count * half + half
    own, away, updated, basis = pl.pallas_call(
        leaf_kernel,
        grid=(count,),
        out_shape=(shape(leaf_rows, width), shape(leaf_rows, width), shape(rows, columns), shape(rows, width)),
        in_specs=[
            SCALAR,
            pl.BlockSpec((rows, width), lambda b: (0, b)),
            pl.BlockSpec((rows, width), lambda b: (0, 0)),
            pl.BlockSpec((width, width), lambda b: (0, 0)),
            pl.BlockSpec((width, width), lambda b: (0, 0)),
        ],
        out_specs=(
            pl.BlockSpec((leaf_rows, width), lambda b: (0, 0)),
            pl.BlockSpec((leaf_rows, width), lambda b: (0, 0)),
            pl.BlockSpec((width, width), lambda b: (1, b)),
            pl.BlockSpec((width, width), lambda b: (1, 0)),
        ),
        scratch_shapes=[
            pltpu.VMEM((width, width), F32),
            pltpu.VMEM((width, width), F32),
            pltpu.VMEM((rows, width), BF16),
            pltpu.VMEM((rows, width), BF16),
            pltpu.VMEM((width, width), BF16),
            pltpu.VMEM((width, width), BF16),
        ],
        compiler_params=PARAMS,
    )(me_array, trailing, leaf_vectors, leaf_factors, inverse_factor)
    away = exchange(away, 0)

    send, done = whole_call(
        core_kernel, 1, (me_array, own, away, packed, packed_there),
        (shape(4, cols + quarter, width), shape(4, cols + 2 * quarter, width)),
    )
    got = around(send)

    held_parts, node_parts = [], []
    held = plane_part[0]
    for level in range(3, levels):
        up = (me >> level) % 2 == 1
        if level == levels - 1:
            there = exchange(held, level, lambda i: (i >> level) % 2 == 1)
        else:
            there = exchange(held, level)
        held_parts.append(held)
        node_parts.append(jnp.where(up, held, there))
        held = jnp.where(up, there, held)
    line_parts = jnp.stack(held_parts + node_parts)
    line_there = exchange(line_parts, 0)

    head, send, plane_done = whole_call(
        functools.partial(plane_kernel, level=3), 1, (me_array, got, plane_part, plane_there),
        (shape(cols, width), shape(cols + quarter, width), shape(3, cols, width)),
    )
    result = head
    line_levels = levels - 3
    for step in range(line_levels):
        last = step == line_levels - 1
        there = exchange(send, step + 3)
        ahead = min(step + 1, line_levels - 1)
        head, result, send = whole_call(
            functools.partial(line_kernel, level=step + 3, last=last), 1,
            (
                me_array, head, result, send, there,
                line_parts[step], line_there[step],
                line_parts[line_levels + step], line_there[line_levels + step],
                line_parts[ahead], line_there[ahead],
            ),
            (shape(cols, width), shape(cols, width), shape(cols + quarter, width)),
        )

    finished = jnp.concatenate([result[None], plane_done], axis=0)
    common = jnp.concatenate([send[:quarter], send[cols:]], axis=0)
    common = jnp.broadcast_to(common, (4,) + common.shape)
    back = around(jnp.concatenate([finished, common], axis=1))
    row = lax.broadcasted_iota(jnp.int32, back.shape, 1)
    back_there = exchange(jnp.where(odd | (row >= cols), back, done), 0)

    return pl.pallas_call(
        functools.partial(final_kernel, total=float(rows * devices)),
        grid=(count,),
        out_shape=(shape(rows, columns), shape(rows, width), shape(width, width)),
        in_specs=[
            SCALAR,
            pl.BlockSpec(back.shape, lambda b: (0, 0, 0)),
            pl.BlockSpec(back.shape, lambda b: (0, 0, 0)),
            pl.BlockSpec(back.shape, lambda b: (0, 0, 0)),
            pl.BlockSpec((width, width), lambda b: (0, 0)),
            pl.BlockSpec(memory_space=pl.ANY),
            pl.BlockSpec(memory_space=pl.ANY),
        ],
        out_specs=(
            pl.BlockSpec((width, width), lambda b: (0, b)),
            pl.BlockSpec((width, width), lambda b: (0, 0)),
            pl.BlockSpec((width, width), lambda b: (0, 0)),
        ),
        scratch_shapes=[pltpu.VMEM((width, width), F32)],
        input_output_aliases={5: 0, 6: 1},
        compiler_params=PARAMS,
    )(me_array, back, back_there, done, inverse_factor, updated, basis)


def solution(mesh):
    in_specs = (
        P("rows", None),
        P("rows", None),
        P("rows", None),
        P("rows", None),
        P("rows", None),
        P(),
    )
    out_specs = (P("rows", None), P("rows", None), P())
    return jax.shard_map(body, mesh=mesh, in_specs=in_specs, out_specs=out_specs, check_vma=False)
```

```python
import functools
import jax
import jax.numpy as jnp
from jax import lax
from jax.experimental import pallas as pl
from jax.experimental.pallas import tpu as pltpu
from jax.sharding import PartitionSpec as P

F32 = jnp.float32
BF16 = jnp.bfloat16
EXTRA = 8
PARAMS = pltpu.CompilerParams(vmem_limit_bytes=40 * 1024 * 1024)
WHOLE = pl.BlockSpec(memory_space=pltpu.VMEM)
SCALAR = pl.BlockSpec(memory_space=pltpu.SMEM)


def halves(value):
    high = value.astype(BF16)
    return high, (value - high.astype(F32)).astype(BF16)


def times(left, right, sides):
    dims = ((sides[:1], sides[1:]), ((), ()))
    dot = functools.partial(lax.dot_general, dimension_numbers=dims, preferred_element_type=F32)
    return dot(left[0], right[0]) + (dot(left[0], right[1]) + dot(left[1], right[0]))


def plain(left, right):
    return times(left, right, (1, 0))


def by_transpose(left, right):
    return times(left, right, (1, 1))


def pack_kernel(vectors_ref, factors_ref, out_ref):
    width = vectors_ref.shape[0]
    row = lax.broadcasted_iota(jnp.int32, (width, width), 0)
    col = lax.broadcasted_iota(jnp.int32, (width, width), 1)
    factors = factors_ref[...]
    out_ref[:width] = jnp.where(row > col, factors.T, vectors_ref[...])
    diagonal = jnp.sum(jnp.where(row == col, factors, 0.0), axis=0, keepdims=True)
    out_ref[width:] = jnp.broadcast_to(diagonal, (EXTRA, width))


def unpack(value):
    width = value.shape[1]
    packed = value[:width]
    row = lax.broadcasted_iota(jnp.int32, (width, width), 0)
    col = lax.broadcasted_iota(jnp.int32, (width, width), 1)
    diagonal = jnp.broadcast_to(value[width : width + 1], (width, width))
    vectors = jnp.where(row <= col, packed, 0.0)
    factors = jnp.where(row > col, packed, jnp.where(row == col, diagonal, 0.0))
    return halves(vectors), halves(factors)


def place(me):
    return (me >> 1) & 3


def by_place(me, parts, wanted):
    source = place(me) ^ wanted
    out = parts[0]
    for r in range(1, 4):
        out = jnp.where(source == r, parts[r], out)
    return out


def tree_node(low, high, reflector):
    vectors, factors = reflector
    node = by_transpose(halves(low + plain(halves(high), vectors)), factors)
    return low - node, high - by_transpose(halves(node), vectors)


def leaf_kernel(
    me_ref, trailing_ref, vectors_ref, factors_ref, inverse_ref,
    own_ref, away_ref, updated_ref, basis_ref, head_ref, gram_ref, v_high, v_low, f_high, f_low,
):
    block = pl.program_id(0)
    width = factors_ref.shape[0]
    half = width // 2
    core = me_ref[0] % 2
    mine = pl.multiple_of(core * half, half)
    other = pl.multiple_of((1 - core) * half, half)

    @pl.when(block == 0)
    def _():
        v_high[...], v_low[...] = halves(vectors_ref[...])
        f_high[...], f_low[...] = halves(factors_ref[...])

    vectors = (v_high[...], v_low[...])
    part = trailing_ref[...].T
    split = halves(part)
    coeffs = plain(halves(plain(split, vectors)), (f_high[...], f_low[...]))
    out = part - by_transpose(halves(coeffs), vectors)
    head_ref[...] = out[:, :width]
    rows = pl.ds(pl.multiple_of(block * half, half), half)
    own_ref[rows] = head_ref[pl.ds(mine, half)]
    away_ref[rows] = head_ref[pl.ds(other, half)]
    rest = out[:, width:].T
    updated_ref[...] = rest

    @pl.when(block == 0)
    def _():
        gram_ref[...] = by_transpose(split, split)
        last = pl.ds(own_ref.shape[0] - half, half)
        own_ref[last] = gram_ref[pl.ds(mine, half)]
        away_ref[last] = gram_ref[pl.ds(other, half)]
        basis_ref[...] = plain(halves(rest), halves(inverse_ref[...]))


def core_kernel(
    me_ref, own_ref, there_ref, packed_ref, *refs
):
    sends, dones, (low_ref, high_ref) = refs[:4], refs[4:8], refs[8:]
    me = me_ref[0]
    width = own_ref.shape[1]
    half = width // 2
    quarter = half // 4
    count = own_ref.shape[0] // half - 1
    odd = me % 2 == 1
    mine, there = own_ref[: count * half], there_ref[: count * half]
    low = jnp.where(odd, there, mine)
    high = jnp.where(odd, mine, there)
    low, high = tree_node(low, high, unpack(packed_ref[...]))
    low_ref[: count * half] = low
    low_ref[count * half :] = own_ref[count * half :] + there_ref[count * half :]
    high_ref[...] = high
    for r in range(4):
        start = (place(me) ^ r) * quarter
        for b in range(count + 1):
            source = pl.ds(pl.multiple_of(b * half + start, quarter), quarter)
            target = slice(b * quarter, (b + 1) * quarter)
            sends[r][target] = low_ref[source]
            if b < count:
                dones[r][target] = high_ref[source]


def plane_kernel(me_ref, *refs, level):
    gots, packeds, (head_ref, send_ref, done_ref) = refs[:4], refs[4:8], refs[8:]
    me = me_ref[0]
    cols = done_ref.shape[1]
    parts = [ref[...] for ref in packeds]
    reflectors = [unpack(by_place(me, parts, j)) for j in range(4)]
    parts = [ref[:cols] for ref in gots]
    heads = [by_place(me, parts, j) for j in range(4)]
    gram = gots[0][cols:] + gots[1][cols:] + (gots[2][cols:] + gots[3][cols:])
    heads[0], heads[1] = tree_node(heads[0], heads[1], reflectors[1])
    heads[2], heads[3] = tree_node(heads[2], heads[3], reflectors[3])
    heads[0], heads[2] = tree_node(heads[0], heads[2], reflectors[2])
    for j in range(4):
        done_ref[j] = heads[j]
    head_ref[...] = heads[0]
    upper = (me >> level) % 2 == 1
    send_ref[:cols] = jnp.where(upper, plain(halves(heads[0]), reflectors[0][0]), heads[0])
    send_ref[cols:] = gram


def line_kernel(
    me_ref, head_ref, result_ref, mine_ref, there_ref, held_ref, node_ref, next_ref,
    head_out, result_out, send_ref, *, level,
):
    me = me_ref[0]
    cols = head_ref.shape[0]
    low, result, gram = line_node(
        me, head_ref, result_ref, mine_ref, there_ref, held_ref, node_ref, level
    )
    ahead = (me >> (level + 1)) % 2 == 1
    following = unpack(next_ref[...])
    head_out[...] = low
    result_out[...] = result
    send_ref[:cols] = jnp.where(ahead, plain(halves(low), following[0]), low)
    send_ref[cols:] = gram


def line_node(me, head_ref, result_ref, mine_ref, there_ref, held_ref, node_ref, level):
    cols = head_ref.shape[0]
    upper = (me >> level) % 2 == 1
    held = unpack(held_ref[...])
    node = unpack(node_ref[...])
    head = head_ref[...]
    there = there_ref[:cols]
    coeffs = by_transpose(halves(mine_ref[:cols] + there), node[1])
    low = jnp.where(upper, there, head) - coeffs
    plane = me >> 3
    below = (1 << (level - 2)) - 1
    second = (plane & below) == (1 << (level - 3))
    result = jnp.where(second, head - by_transpose(halves(coeffs), held[0]), result_ref[...])
    return low, result, mine_ref[cols:] + there_ref[cols:]


def last_kernel(
    me_ref, head_ref, result_ref, mine_ref, there_ref, held_ref, node_ref, done_ref, *refs, level
):
    sends, all_ref = refs[:4], refs[4]
    me = me_ref[0]
    cols = head_ref.shape[0]
    low, result, gram = line_node(
        me, head_ref, result_ref, mine_ref, there_ref, held_ref, node_ref, level
    )
    all_ref[0] = jnp.where((me >> 3) == 0, low, result)
    for j in range(1, 4):
        all_ref[j] = done_ref[j]
    quarter = gram.shape[0]
    for r in range(4):
        sends[r][:cols] = all_ref[place(me) ^ r]
        sends[r][cols : cols + quarter] = low[:quarter]
        sends[r][cols + quarter :] = gram


def pass_kernel(me_ref, *refs):
    backs, dones, out_ref = refs[:4], refs[4:8], refs[8]
    odd = me_ref[0] % 2 == 1
    cols = dones[0].shape[0]
    for r in range(4):
        out_ref[r, :cols] = jnp.where(odd, backs[r][:cols], dones[r][...])
        out_ref[r, cols:] = backs[r][cols:]


def final_kernel(me_ref, *refs, total):
    backs, dones = refs[:4], refs[4:8]
    there_ref, inverse_ref, _, _, updated_ref, basis_ref, gram_ref = refs[8:15]
    head_ref, panel_ref, sum_ref = refs[15:]
    block = pl.program_id(0)
    width = inverse_ref.shape[0]
    half = width // 2
    quarter = half // 4
    cols = dones[0].shape[0]
    me = me_ref[0]
    core = me % 2
    odd = core == 1
    rows = pl.ds(pl.multiple_of(block * quarter, quarter), quarter)

    def target(part, r):
        return pl.ds(pl.multiple_of(part * half + (place(me) ^ r) * quarter, quarter), quarter)

    for r in range(4):
        there = there_ref[r, rows]
        head_ref[target(0, r)] = jnp.where(odd, there, backs[r][rows])
        head_ref[target(1, r)] = jnp.where(odd, dones[r][rows], there)
    head = head_ref[...].T
    updated_ref[...] = head

    @pl.when(block == 0)
    def _():
        basis = plain(halves(head), halves(inverse_ref[...]))
        basis_ref[...] = jnp.where(me == 0, 0.0, basis)
        for r in range(4):
            panel_ref[target(core, r)] = backs[r][cols : cols + quarter]
            sum_ref[target(core, r)] = backs[r][cols + quarter :]
            panel_ref[target(1 - core, r)] = there_ref[r, cols : cols + quarter]
            sum_ref[target(1 - core, r)] = there_ref[r, cols + quarter :]
        panel = halves(panel_ref[...])
        gram_ref[...] = (sum_ref[...] - by_transpose(panel, panel)) / total


def body(trailing, leaf_vectors, leaf_factors, tree_vectors, tree_factors, inverse_factor):
    rows, columns = trailing.shape
    width = leaf_vectors.shape[1]
    half = width // 2
    quarter = half // 4
    count = columns // width
    cols = count * quarter
    devices = lax.axis_size("rows")
    levels = devices.bit_length() - 1
    me = lax.axis_index("rows").astype(jnp.int32)
    me_array = me.reshape(1)
    odd = me % 2 == 1

    def exchange(value, shift, member=lambda i: True):
        pairs = [(i, i ^ shift) for i in range(devices) if member(i)]
        return lax.ppermute(value, "rows", pairs)

    def even(i):
        return i % 2 == 0

    def both(value):
        return jnp.where(odd, exchange(value, 1, even), value)

    def shape(*dims):
        return jax.ShapeDtypeStruct(dims, F32)

    def whole_call(kernel, operands, outs, scratch=()):
        return pl.pallas_call(
            kernel,
            out_shape=outs,
            in_specs=[SCALAR] + [WHOLE] * len(operands),
            out_specs=tuple(WHOLE for _ in outs),
            scratch_shapes=[pltpu.VMEM(dims, F32) for dims in scratch],
            compiler_params=PARAMS,
        )(me_array, *operands)

    packed = pl.pallas_call(
        pack_kernel,
        out_shape=shape(width + EXTRA, width),
        in_specs=[WHOLE] * 2,
        out_specs=WHOLE,
        compiler_params=PARAMS,
    )(tree_vectors, tree_factors)
    plane_even = [exchange(packed, 2 * r, even) for r in range(1, 4)]
    packed_there = exchange(packed, 1)
    chip_low = jnp.where(odd, packed_there, packed)
    chip_high = jnp.where(odd, packed, packed_there)

    leaf_rows = count * half + half
    own, away, updated, basis = pl.pallas_call(
        leaf_kernel,
        grid=(count,),
        out_shape=(shape(leaf_rows, width), shape(leaf_rows, width), shape(rows, columns), shape(rows, width)),
        in_specs=[
            SCALAR,
            pl.BlockSpec((rows, width), lambda b: (0, b)),
            pl.BlockSpec((rows, width), lambda b: (0, 0)),
            pl.BlockSpec((width, width), lambda b: (0, 0)),
            pl.BlockSpec((width, width), lambda b: (0, 0)),
        ],
        out_specs=(
            pl.BlockSpec((leaf_rows, width), lambda b: (0, 0)),
            pl.BlockSpec((leaf_rows, width), lambda b: (0, 0)),
            pl.BlockSpec((width, width), lambda b: (1, b)),
            pl.BlockSpec((width, width), lambda b: (1, 0)),
        ),
        scratch_shapes=[
            pltpu.VMEM((width, width), F32),
            pltpu.VMEM((width, width), F32),
            pltpu.VMEM((rows, width), BF16),
            pltpu.VMEM((rows, width), BF16),
            pltpu.VMEM((width, width), BF16),
            pltpu.VMEM((width, width), BF16),
        ],
        compiler_params=PARAMS,
    )(me_array, trailing, leaf_vectors, leaf_factors, inverse_factor)
    away = exchange(away, 1)

    outs = whole_call(
        core_kernel, (own, away, chip_high),
        tuple([shape(cols + quarter, width)] * 4 + [shape(cols, width)] * 4),
        ((leaf_rows, width), (count * half, width)),
    )
    sends, dones = outs[:4], outs[4:]
    gots = [sends[0]] + [exchange(sends[r], 2 * r) for r in range(1, 4)]

    plane_parts = [chip_low] + [both(part) for part in plane_even]
    held = by_place(me, plane_parts, 0)
    head, send, plane_done = whole_call(
        functools.partial(plane_kernel, level=3), (*gots, *plane_parts),
        (shape(cols, width), shape(cols + quarter, width), shape(4, cols, width)),
    )

    result = head
    for level in range(3, levels):
        up = (me >> level) % 2 == 1
        last = level == levels - 1
        if last:
            other = both(exchange(held, 1 << level, lambda i: even(i) and (i >> level) % 2 == 1))
        else:
            other = both(exchange(held, 1 << level, even))
        node = jnp.where(up, held, other)
        there = exchange(send, 1 << level)
        operands = (head, result, send, there, held, node)
        if last:
            sends = whole_call(
                functools.partial(last_kernel, level=level), (*operands, plane_done),
                tuple([shape(cols + 2 * quarter, width)] * 4), ((4, cols, width),),
            )
        else:
            held = jnp.where(up, other, held)
            head, result, send = whole_call(
                functools.partial(line_kernel, level=level), (*operands, held),
                (shape(cols, width), shape(cols, width), shape(cols + quarter, width)),
            )

    backs = [sends[0]] + [exchange(sends[r], 2 * r) for r in range(1, 4)]
    (back,) = whole_call(pass_kernel, (*backs, *dones), (shape(4, cols + 2 * quarter, width),))
    there = exchange(back, 1)

    def fixed(*dims):
        return pl.BlockSpec(dims, lambda b: (0,) * len(dims))

    return pl.pallas_call(
        functools.partial(final_kernel, total=float(rows * devices)),
        grid=(count,),
        out_shape=(shape(rows, columns), shape(rows, width), shape(width, width)),
        in_specs=[SCALAR]
        + [fixed(cols + 2 * quarter, width)] * 4
        + [fixed(cols, width)] * 4
        + [fixed(*there.shape), fixed(width, width)]
        + [pl.BlockSpec(memory_space=pl.ANY)] * 2,
        out_specs=(pl.BlockSpec((width, width), lambda b: (0, b)), fixed(width, width), fixed(width, width)),
        scratch_shapes=[pltpu.VMEM((width, width), F32)] * 3,
        input_output_aliases={11: 0, 12: 1},
        compiler_params=PARAMS,
    )(me_array, *backs, *dones, there, inverse_factor, updated, basis)


def solution(mesh):
    in_specs = (
        P("rows", None),
        P("rows", None),
        P("rows", None),
        P("rows", None),
        P("rows", None),
        P(),
    )
    out_specs = (P("rows", None), P("rows", None), P())
    return jax.shard_map(body, mesh=mesh, in_specs=in_specs, out_specs=out_specs, check_vma=False)
```

```python
import functools
import jax
import jax.numpy as jnp
from jax import lax
from jax.experimental import pallas as pl
from jax.experimental.pallas import tpu as pltpu
from jax.sharding import PartitionSpec as P

F32 = jnp.float32
BF16 = jnp.bfloat16
EXTRA = 8
PARAMS = pltpu.CompilerParams(vmem_limit_bytes=40 * 1024 * 1024)
def room(megabytes):
    return pltpu.CompilerParams(vmem_limit_bytes=megabytes * 1024 * 1024)


WHOLE = pl.BlockSpec(memory_space=pltpu.VMEM)
SCALAR = pl.BlockSpec(memory_space=pltpu.SMEM)
AWAY = pl.BlockSpec(memory_space=pltpu.HBM)


def halves(value):
    high = value.astype(BF16)
    return high, (value - high.astype(F32)).astype(BF16)


def times(left, right, sides):
    dims = ((sides[:1], sides[1:]), ((), ()))
    dot = functools.partial(lax.dot_general, dimension_numbers=dims, preferred_element_type=F32)
    return dot(left[0], right[0]) + (dot(left[0], right[1]) + dot(left[1], right[0]))


def plain(left, right):
    return times(left, right, (1, 0))


def by_transpose(left, right):
    return times(left, right, (1, 1))


def pack_kernel(vectors_hbm, factors_hbm, out_ref, vectors_ref, factors_ref, sems):
    copies = [
        pltpu.make_async_copy(vectors_hbm, vectors_ref, sems.at[0]),
        pltpu.make_async_copy(factors_hbm, factors_ref, sems.at[1]),
    ]
    for copy in copies:
        copy.start()
    for copy in copies:
        copy.wait()
    width = vectors_ref.shape[0]
    half = width // 2
    row = lax.broadcasted_iota(jnp.int32, (width, width), 0)
    col = lax.broadcasted_iota(jnp.int32, (width, width), 1)
    factors = factors_ref[...]
    packed = jnp.where(row > col, factors.T, vectors_ref[...])
    diagonal = jnp.sum(jnp.where(row == col, factors, 0.0), axis=0, keepdims=True)
    for part in range(2):
        out_ref[part, :half] = packed[part * half : (part + 1) * half]
        out_ref[part, half:] = jnp.broadcast_to(diagonal, (EXTRA, width))


def unpack(first, second):
    half = first.shape[0] - EXTRA
    width = 2 * half
    packed = jnp.concatenate([first[:half], second[:half]], axis=0)
    row = lax.broadcasted_iota(jnp.int32, (width, width), 0)
    col = lax.broadcasted_iota(jnp.int32, (width, width), 1)
    diagonal = jnp.broadcast_to(first[half : half + 1], (width, width))
    vectors = jnp.where(row <= col, packed, 0.0)
    factors = jnp.where(row > col, packed, jnp.where(row == col, diagonal, 0.0))
    return halves(vectors), halves(factors)


def by_core(core, mine, there):
    odd = core == 1
    return jnp.where(odd, there, mine), jnp.where(odd, mine, there)


def place(me):
    return (me >> 1) & 3


def by_place(me, parts, wanted):
    source = place(me) ^ wanted
    out = parts[0]
    for r in range(1, 4):
        out = jnp.where(source == r, parts[r], out)
    return out


def tree_node(low, high, reflector):
    vectors, factors = reflector
    node = by_transpose(halves(low + plain(halves(high), vectors)), factors)
    return low - node, high - by_transpose(halves(node), vectors)


def leaf_kernel(
    me_ref, trailing_hbm, vectors_hbm, factors_hbm, inverse_hbm,
    own_hbm, away_hbm, updated_hbm, basis_hbm,
    own_ref, away_ref, part_ref, vectors_ref, factors_ref, inverse_ref, rest_ref, basis_ref, head_ref, gram_ref,
    in_sems, out_sems,
):
    count, rows, width = part_ref.shape
    half = width // 2
    core = me_ref[0] % 2
    mine = pl.ds(pl.multiple_of(core * half, half), half)
    other = pl.ds(pl.multiple_of((1 - core) * half, half), half)

    copies = []

    def fetch(source, target):
        copy = pltpu.make_async_copy(source, target, in_sems.at[len(copies)])
        copy.start()
        copies.append(copy)
        return copy

    def fetch_part(b):
        cuts = [slice(cut, cut + width) for cut in range(0, rows, width)]
        return [fetch(trailing_hbm.at[cut, pl.ds(b * width, width)], part_ref.at[b, cut]) for cut in cuts]

    parts = [fetch_part(0)]
    vectors_copy = fetch(vectors_hbm, vectors_ref)
    factors_copy = fetch(factors_hbm, factors_ref)
    inverse_copy = fetch(inverse_hbm, inverse_ref)
    parts += [fetch_part(b) for b in range(1, count)]

    out_copies = []

    def put(source, target):
        copy = pltpu.make_async_copy(source, target, out_sems.at[len(out_copies)])
        copy.start()
        out_copies.append(copy)

    for b in range(count):
        for copy in parts[b]:
            copy.wait()
        part = part_ref[b].T
        split = halves(part)
        if b == 0:
            gram_ref[...] = by_transpose(split, split)
            rows_b = slice(count * half, (count + 1) * half)
            own_ref[rows_b] = gram_ref[mine]
            away_ref[rows_b] = gram_ref[other]
            put(away_ref.at[rows_b], away_hbm.at[rows_b])
            put(own_ref.at[rows_b], own_hbm.at[rows_b])
            vectors_copy.wait()
            vectors = halves(vectors_ref[...])
            factors_copy.wait()
            factors = halves(factors_ref[...])
        coeffs = plain(halves(plain(split, vectors)), factors)
        out = part - by_transpose(halves(coeffs), vectors)
        head_ref[...] = out[:, :width]
        rows_b = slice(b * half, (b + 1) * half)
        own_ref[rows_b] = head_ref[mine]
        away_ref[rows_b] = head_ref[other]
        put(away_ref.at[rows_b], away_hbm.at[rows_b])
        put(own_ref.at[rows_b], own_hbm.at[rows_b])
        rest = out[:, width:].T
        rest_ref[b] = rest
        put(rest_ref.at[b], updated_hbm.at[pl.ds(width, width), pl.ds(b * width, width)])
        if b == 0:
            inverse_copy.wait()
            basis_ref[...] = plain(halves(rest), halves(inverse_ref[...]))
            put(basis_ref, basis_hbm.at[pl.ds(width, width)])
    for copy in out_copies:
        copy.wait()


def core_kernel(
    me_ref, own_ref, there_ref, packed_ref, packed_there_ref, *refs
):
    sends, dones, (low_ref, high_ref) = refs[:4], refs[4:8], refs[8:]
    me = me_ref[0]
    width = own_ref.shape[1]
    half = width // 2
    quarter = half // 4
    count = own_ref.shape[0] // half - 1
    odd = me % 2 == 1
    mine, there = own_ref[: count * half], there_ref[: count * half]
    low = jnp.where(odd, there, mine)
    high = jnp.where(odd, mine, there)
    first, second = [jnp.where(odd, packed_ref[part], packed_there_ref[part]) for part in range(2)]
    low, high = tree_node(low, high, unpack(first, second))
    low_ref[: count * half] = low
    low_ref[count * half :] = own_ref[count * half :] + there_ref[count * half :]
    high_ref[...] = high
    for r in range(4):
        start = (place(me) ^ r) * quarter
        for b in range(count + 1):
            source = pl.ds(pl.multiple_of(b * half + start, quarter), quarter)
            target = slice(b * quarter, (b + 1) * quarter)
            sends[r][target] = low_ref[source]
            if b < count:
                dones[r][target] = high_ref[source]


def gather_kernel(me_ref, *refs):
    parts, own_hbm, (stack_ref, held_ref, own_ref, sem) = refs[:4], refs[4], refs[5:]
    copy = pltpu.make_async_copy(own_hbm, own_ref, sem)
    copy.start()
    for r in range(1, 4):
        stack_ref[r - 1] = parts[r][...]
    held_ref[...] = by_place(me_ref[0], [ref[...] for ref in parts], 0)
    copy.wait()


def plane_kernel(
    me_ref, *refs, level
):
    gots, (packed_ref, packed_there_ref, stack_ref, stack_there_ref) = refs[:4], refs[4:8]
    head_ref, send_ref, done_ref, held_ref = refs[8:]
    me = me_ref[0]
    core = me % 2
    cols = done_ref.shape[1]
    odd = core == 1
    pairs = [[jnp.where(odd, packed_there_ref[part], packed_ref[part]) for part in range(2)]]
    pairs += [by_core(core, stack_ref[r], stack_there_ref[r]) for r in range(3)]
    firsts, seconds = [pair[0] for pair in pairs], [pair[1] for pair in pairs]
    pairs = [(by_place(me, firsts, j), by_place(me, seconds, j)) for j in range(4)]
    held_ref[0], held_ref[1] = pairs[0]
    reflectors = [unpack(*pair) for pair in pairs]
    parts = [ref[:cols] for ref in gots]
    heads = [by_place(me, parts, j) for j in range(4)]
    gram = gots[0][cols:] + gots[1][cols:] + (gots[2][cols:] + gots[3][cols:])
    heads[0], heads[1] = tree_node(heads[0], heads[1], reflectors[1])
    heads[2], heads[3] = tree_node(heads[2], heads[3], reflectors[3])
    heads[0], heads[2] = tree_node(heads[0], heads[2], reflectors[2])
    for j in range(4):
        done_ref[j] = heads[j]
    head_ref[...] = heads[0]
    upper = (me >> level) % 2 == 1
    send_ref[:cols] = jnp.where(upper, plain(halves(heads[0]), reflectors[0][0]), heads[0])
    send_ref[cols:] = gram


def line_node(
    me, head_ref, result_ref, mine_ref, there_ref, held_ref, part_ref, part_there_ref, level
):
    cols = head_ref.shape[0]
    upper = (me >> level) % 2 == 1
    held = held_ref[0], held_ref[1]
    others = by_core(me % 2, part_ref[...], part_there_ref[...])
    node = [jnp.where(upper, a, b) for a, b in zip(held, others)]
    following = [jnp.where(upper, b, a) for a, b in zip(held, others)]
    head = head_ref[...]
    there = there_ref[:cols]
    coeffs = by_transpose(halves(mine_ref[:cols] + there), unpack(*node)[1])
    low = jnp.where(upper, there, head) - coeffs
    plane = me >> 3
    below = (1 << (level - 2)) - 1
    second = (plane & below) == (1 << (level - 3))
    high = head - by_transpose(halves(coeffs), unpack(*held)[0])
    result = jnp.where(second, high, result_ref[...])
    return low, result, mine_ref[cols:] + there_ref[cols:], following


def line_kernel(me_ref, *refs, level):
    head_out, result_out, send_ref, held_out = refs[7:]
    me = me_ref[0]
    low, result, gram, following = line_node(me, *refs[:7], level)
    cols = low.shape[0]
    ahead = (me >> (level + 1)) % 2 == 1
    head_out[...] = low
    result_out[...] = result
    held_out[0], held_out[1] = following
    send_ref[:cols] = jnp.where(ahead, plain(halves(low), unpack(*following)[0]), low)
    send_ref[cols:] = gram


def last_kernel(me_ref, *refs, level):
    done_ref, sends, all_ref = refs[7], refs[8:12], refs[12]
    me = me_ref[0]
    low, result, gram, _ = line_node(me, *refs[:7], level)
    cols = low.shape[0]
    quarter = gram.shape[0]
    all_ref[0] = jnp.where((me >> 3) == 0, low, result)
    for j in range(1, 4):
        all_ref[j] = done_ref[j]
    for r in range(4):
        sends[r][:cols] = all_ref[place(me) ^ r]
        sends[r][cols : cols + quarter] = low[:quarter]
        sends[r][cols + quarter :] = gram


def pass_kernel(me_ref, *refs):
    backs, dones, out_ref = refs[:4], refs[4:8], refs[8]
    odd = me_ref[0] % 2 == 1
    cols = dones[0].shape[0]
    for r in range(4):
        out_ref[r, :cols] = jnp.where(odd, backs[r][:cols], dones[r][...])
        out_ref[r, cols:] = backs[r][cols:]


def final_kernel(me_ref, *refs, total):
    backs, dones = refs[:4], refs[4:8]
    there_ref, inverse_hbm, _, _, updated_hbm, basis_hbm, gram_ref = refs[8:15]
    head_ref, panel_ref, sum_ref, inverse_ref, out_ref, basis_ref, sems = refs[15:]
    count, width = out_ref.shape[:2]
    half = width // 2
    quarter = half // 4
    cols = count * quarter
    me = me_ref[0]
    core = me % 2
    odd = core == 1
    copy = pltpu.make_async_copy(inverse_hbm, inverse_ref, sems.at[0])
    copy.start()

    def target(part, r):
        return pl.ds(pl.multiple_of(part * half + (place(me) ^ r) * quarter, quarter), quarter)

    copies = []

    def put(source, place_there):
        copies.append(pltpu.make_async_copy(source, place_there, sems.at[len(copies) + 1]))
        copies[-1].start()

    for b in range(count):
        rows = slice(b * quarter, (b + 1) * quarter)
        for r in range(4):
            there = there_ref[r, rows]
            head_ref[b, target(0, r)] = jnp.where(odd, there, backs[r][rows])
            head_ref[b, target(1, r)] = jnp.where(odd, dones[r][rows], there)
        out_ref[b] = head_ref[b].T
        put(out_ref.at[b], updated_hbm.at[pl.ds(0, width), pl.ds(b * width, width)])
        if b == 0:
            copy.wait()
            basis = plain(halves(out_ref[0]), halves(inverse_ref[...]))
            basis_ref[...] = jnp.where(me == 0, 0.0, basis)
            put(basis_ref, basis_hbm.at[pl.ds(0, width)])
    for r in range(4):
        panel_ref[target(core, r)] = backs[r][cols : cols + quarter]
        sum_ref[target(core, r)] = backs[r][cols + quarter :]
        panel_ref[target(1 - core, r)] = there_ref[r, cols : cols + quarter]
        sum_ref[target(1 - core, r)] = there_ref[r, cols + quarter :]
    panel = halves(panel_ref[...])
    gram_ref[...] = (sum_ref[...] - by_transpose(panel, panel)) / total
    for copy in copies:
        copy.wait()


def after(value, *others):
    return lax.optimization_barrier((value, *others))[0]


def body(trailing, leaf_vectors, leaf_factors, tree_vectors, tree_factors, inverse_factor):
    rows, columns = trailing.shape
    width = leaf_vectors.shape[1]
    half = width // 2
    quarter = half // 4
    count = columns // width
    cols = count * quarter
    devices = lax.axis_size("rows")
    levels = devices.bit_length() - 1
    me = lax.axis_index("rows").astype(jnp.int32)
    me_array = me.reshape(1)
    odd = me % 2 == 1

    def exchange(value, shift):
        return lax.ppermute(value, "rows", [(i, i ^ shift) for i in range(devices)])

    def shape(*dims):
        return jax.ShapeDtypeStruct(dims, F32)

    def vmem(*dims):
        return pltpu.VMEM(dims, F32)

    def cost(flops, moved=0):
        return pl.CostEstimate(flops=flops, bytes_accessed=moved, transcendentals=0)

    def whole_call(kernel, operands, outs, scratch=(), flops=0):
        return pl.pallas_call(
            kernel,
            out_shape=outs,
            in_specs=[SCALAR] + [WHOLE] * len(operands),
            out_specs=tuple(WHOLE for _ in outs),
            scratch_shapes=list(scratch),
            compiler_params=PARAMS,
            cost_estimate=cost(flops),
        )(me_array, *operands)

    packed = pl.pallas_call(
        pack_kernel,
        out_shape=shape(2, half + EXTRA, width),
        in_specs=[AWAY] * 2,
        out_specs=WHOLE,
        scratch_shapes=[vmem(width, width), vmem(width, width), pltpu.SemaphoreType.DMA((2,))],
        compiler_params=room(62),
    )(tree_vectors, tree_factors)
    packed_there = exchange(packed, 1)
    chip_part = jnp.where(odd, packed_there[1], packed[0])
    plane_parts = [exchange(chip_part, 2 * r) for r in range(1, 4)]

    leaf_rows = count * half + half
    leaf_flops = 6 * width * columns * (2 * rows + width) + 6 * width * width * (rows + width)
    own, away, updated, basis = pl.pallas_call(
        leaf_kernel,
        out_shape=(shape(leaf_rows, width), shape(leaf_rows, width), shape(rows, columns), shape(rows, width)),
        in_specs=[SCALAR] + [AWAY] * 4,
        out_specs=(AWAY,) * 4,
        scratch_shapes=[
            vmem(leaf_rows, width),
            vmem(leaf_rows, width),
            vmem(count, rows, width),
            vmem(rows, width),
            vmem(width, width),
            vmem(width, width),
            vmem(count, width, width),
            vmem(width, width),
            vmem(width, width),
            vmem(width, width),
            pltpu.SemaphoreType.DMA((count * (rows // width) + 3,)),
            pltpu.SemaphoreType.DMA((3 * count + 3,)),
        ],
        compiler_params=room(61),
        cost_estimate=cost(leaf_flops, 4 * (2 * rows * columns + 3 * rows * width)),
    )(after(me_array, chip_part), trailing, leaf_vectors, leaf_factors, inverse_factor)
    plane_parts = [after(part, own) for part in plane_parts]
    away = exchange(after(away, *plane_parts), 1)
    stack, held_part, own = pl.pallas_call(
        gather_kernel,
        out_shape=(shape(3, half + EXTRA, width), shape(half + EXTRA, width), shape(leaf_rows, width)),
        in_specs=[SCALAR] + [WHOLE] * 4 + [AWAY],
        out_specs=(WHOLE,) * 3,
        scratch_shapes=[pltpu.SemaphoreType.DMA],
        compiler_params=PARAMS,
    )(me_array, chip_part, *plane_parts, own)
    stack_there = exchange(stack, 1)

    outs = whole_call(
        core_kernel, (own, away, packed, packed_there),
        tuple([shape(cols + quarter, width)] * 4 + [shape(cols, width)] * 4),
        (vmem(leaf_rows, width), vmem(count * half, width)),
        flops=18 * width * width * count * half,
    )
    sends, dones = outs[:4], outs[4:]
    gots = [sends[0]] + [exchange(sends[r], 2 * r) for r in range(1, 4)]

    part = after(exchange(held_part, 8), sends[1]) if levels > 3 else held_part
    head, send, plane_done, held = whole_call(
        functools.partial(plane_kernel, level=3), (*gots, packed, packed_there, stack, stack_there),
        (shape(cols, width), shape(cols + quarter, width), shape(4, cols, width), shape(2, half + EXTRA, width)),
        flops=18 * width * width * cols * 3,
    )

    result = head
    for level in range(3, levels):
        part_there = exchange(part, 1)
        operands = (head, result, send, exchange(send, 1 << level), held, part, part_there)
        if level == levels - 1:
            sends = whole_call(
                functools.partial(last_kernel, level=level), (*operands, plane_done),
                tuple([shape(cols + 2 * quarter, width)] * 4), (vmem(4, cols, width),),
                flops=18 * width * width * cols,
            )
        else:
            held_part = jnp.where((me >> level) % 2 == 1, part, held_part)
            part = after(exchange(held_part, 2 << level), head)
            head, result, send, held = whole_call(
                functools.partial(line_kernel, level=level), operands,
                (shape(cols, width), shape(cols, width), shape(cols + quarter, width), shape(*held.shape)),
                flops=18 * width * width * cols,
            )

    backs = [sends[0]] + [exchange(sends[r], 2 * r) for r in range(1, 4)]
    (back,) = whole_call(pass_kernel, (*backs, *dones), (shape(4, cols + 2 * quarter, width),))
    there = exchange(back, 1)

    return pl.pallas_call(
        functools.partial(final_kernel, total=float(rows * devices)),
        out_shape=(shape(rows, columns), shape(rows, width), shape(width, width)),
        in_specs=[SCALAR] + [WHOLE] * 9 + [AWAY] * 3,
        out_specs=(AWAY, AWAY, WHOLE),
        scratch_shapes=[
            vmem(count, width, width),
            vmem(width, width),
            vmem(width, width),
            vmem(width, width),
            vmem(count, width, width),
            vmem(width, width),
            pltpu.SemaphoreType.DMA((count + 2,)),
        ],
        input_output_aliases={11: 0, 12: 1},
        compiler_params=PARAMS,
    )(me_array, *backs, *dones, there, inverse_factor, updated, basis)


def solution(mesh):
    in_specs = (
        P("rows", None),
        P("rows", None),
        P("rows", None),
        P("rows", None),
        P("rows", None),
        P(),
    )
    out_specs = (P("rows", None), P("rows", None), P())
    return jax.shard_map(body, mesh=mesh, in_specs=in_specs, out_specs=out_specs, check_vma=False)
```

```python
import functools
import jax
import jax.numpy as jnp
from jax import lax
from jax.experimental import pallas as pl
from jax.experimental.pallas import tpu as pltpu
from jax.sharding import PartitionSpec as P

F32 = jnp.float32
BF16 = jnp.bfloat16
EXTRA = 8
PARAMS = pltpu.CompilerParams(vmem_limit_bytes=40 * 1024 * 1024)
def room(megabytes):
    return pltpu.CompilerParams(vmem_limit_bytes=megabytes * 1024 * 1024)


WHOLE = pl.BlockSpec(memory_space=pltpu.VMEM)
SCALAR = pl.BlockSpec(memory_space=pltpu.SMEM)
AWAY = pl.BlockSpec(memory_space=pltpu.HBM)


def halves(value):
    high = value.astype(BF16)
    return high, (value - high.astype(F32)).astype(BF16)


def times(left, right, sides):
    dims = ((sides[:1], sides[1:]), ((), ()))
    dot = functools.partial(lax.dot_general, dimension_numbers=dims, preferred_element_type=F32)
    return dot(left[0], right[0]) + (dot(left[0], right[1]) + dot(left[1], right[0]))


def plain(left, right):
    return times(left, right, (1, 0))


def by_transpose(left, right):
    return times(left, right, (1, 1))


def pack_kernel(me_ref, *refs):
    sources, (low_ref, high_ref, part_ref), (buffer_ref, sems) = refs[:4], refs[4:7], refs[7:]
    copies = [pltpu.make_async_copy(source, buffer_ref.at[i], sems.at[i]) for i, source in enumerate(sources)]
    for copy in copies:
        copy.start()
    for copy in copies:
        copy.wait()
    core = me_ref[0] % 2
    width = buffer_ref.shape[1]
    half = width // 2
    row = lax.broadcasted_iota(jnp.int32, (width, width), 0)
    col = lax.broadcasted_iota(jnp.int32, (width, width), 1)
    both_vectors = by_core(core, buffer_ref[0], buffer_ref[2])
    both_factors = by_core(core, buffer_ref[1], buffer_ref[3])
    for vectors, factors, out_ref in zip(both_vectors, both_factors, (low_ref, high_ref)):
        packed = jnp.where(row > col, factors.T, vectors)
        diagonal = jnp.sum(jnp.where(row == col, factors, 0.0), axis=0, keepdims=True)
        for part in range(2):
            out_ref[part, :half] = packed[part * half : (part + 1) * half]
            out_ref[part, half:] = jnp.broadcast_to(diagonal, (EXTRA, width))
    part_ref[...] = low_ref[core]


def unpack(first, second):
    half = first.shape[0] - EXTRA
    width = 2 * half
    packed = jnp.concatenate([first[:half], second[:half]], axis=0)
    row = lax.broadcasted_iota(jnp.int32, (width, width), 0)
    col = lax.broadcasted_iota(jnp.int32, (width, width), 1)
    diagonal = jnp.broadcast_to(first[half : half + 1], (width, width))
    vectors = jnp.where(row <= col, packed, 0.0)
    factors = jnp.where(row > col, packed, jnp.where(row == col, diagonal, 0.0))
    return halves(vectors), halves(factors)


def by_core(core, mine, there):
    odd = core == 1
    return jnp.where(odd, there, mine), jnp.where(odd, mine, there)


def place(me):
    return (me >> 1) & 3


def by_place(me, parts, wanted):
    source = place(me) ^ wanted
    out = parts[0]
    for r in range(1, 4):
        out = jnp.where(source == r, parts[r], out)
    return out


def tree_node(low, high, reflector):
    vectors, factors = reflector
    node = by_transpose(halves(low + plain(halves(high), vectors)), factors)
    return low - node, high - by_transpose(halves(node), vectors)


def leaf_kernel(
    me_ref, trailing_hbm, vectors_hbm, factors_hbm, inverse_hbm,
    own_hbm, away_hbm, updated_hbm, basis_hbm,
    own_ref, away_ref, part_ref, vectors_ref, factors_ref, inverse_ref, rest_ref, basis_ref, head_ref, gram_ref,
    in_sems, out_sems,
):
    count, rows, width = part_ref.shape
    half = width // 2
    core = me_ref[0] % 2
    mine = pl.ds(pl.multiple_of(core * half, half), half)
    other = pl.ds(pl.multiple_of((1 - core) * half, half), half)

    copies = []

    def fetch(source, target):
        copy = pltpu.make_async_copy(source, target, in_sems.at[len(copies)])
        copy.start()
        copies.append(copy)
        return copy

    def fetch_part(b):
        cuts = [slice(cut, cut + width) for cut in range(0, rows, width)]
        return [fetch(trailing_hbm.at[cut, pl.ds(b * width, width)], part_ref.at[b, cut]) for cut in cuts]

    vectors_copy = fetch(vectors_hbm, vectors_ref)
    parts = [fetch_part(0)]
    factors_copy = fetch(factors_hbm, factors_ref)
    inverse_copy = fetch(inverse_hbm, inverse_ref)
    parts += [fetch_part(b) for b in range(1, count)]

    out_copies = []

    def put(source, target):
        copy = pltpu.make_async_copy(source, target, out_sems.at[len(out_copies)])
        copy.start()
        out_copies.append(copy)

    vectors_copy.wait()
    vectors = halves(vectors_ref[...])
    vectors_across = halves(vectors_ref[...].T)
    for b in range(count):
        for copy in parts[b]:
            copy.wait()
        part = part_ref[b]
        split = halves(part)
        inner = halves(plain(vectors_across, split))
        if b == 0:
            factors_copy.wait()
            factors_across = halves(factors_ref[...].T)
        out = part - plain(vectors, halves(plain(factors_across, inner)))
        rest = out[width:]
        rest_ref[b] = rest
        put(rest_ref.at[b], updated_hbm.at[pl.ds(width, width), pl.ds(b * width, width)])
        head_ref[...] = out[:width].T
        rows_b = slice(b * half, (b + 1) * half)
        own_ref[rows_b] = head_ref[mine]
        away_ref[rows_b] = head_ref[other]
        put(away_ref.at[rows_b], away_hbm.at[rows_b])
        put(own_ref.at[rows_b], own_hbm.at[rows_b])
        if b == 0:
            gram_ref[...] = plain(halves(part.T), split)
            rows_b = slice(count * half, (count + 1) * half)
            own_ref[rows_b] = gram_ref[mine]
            away_ref[rows_b] = gram_ref[other]
            put(away_ref.at[rows_b], away_hbm.at[rows_b])
            put(own_ref.at[rows_b], own_hbm.at[rows_b])
            inverse_copy.wait()
            basis_ref[...] = plain(halves(rest), halves(inverse_ref[...]))
            put(basis_ref, basis_hbm.at[pl.ds(width, width)])
    for copy in out_copies:
        copy.wait()


def core_kernel(
    me_ref, own_ref, there_ref, packed_ref, *refs
):
    sends, dones, (low_ref, high_ref) = refs[:4], refs[4:8], refs[8:]
    me = me_ref[0]
    width = own_ref.shape[1]
    half = width // 2
    quarter = half // 4
    count = own_ref.shape[0] // half - 1
    odd = me % 2 == 1
    mine, there = own_ref[: count * half], there_ref[: count * half]
    low = jnp.where(odd, there, mine)
    high = jnp.where(odd, mine, there)
    low, high = tree_node(low, high, unpack(packed_ref[0], packed_ref[1]))
    low_ref[: count * half] = low
    low_ref[count * half :] = own_ref[count * half :] + there_ref[count * half :]
    high_ref[...] = high
    for r in range(4):
        start = (place(me) ^ r) * quarter
        for b in range(count + 1):
            source = pl.ds(pl.multiple_of(b * half + start, quarter), quarter)
            target = slice(b * quarter, (b + 1) * quarter)
            sends[r][target] = low_ref[source]
            if b < count:
                dones[r][target] = high_ref[source]


def gather_kernel(me_ref, *refs):
    parts, own_hbm, (stack_ref, held_ref, own_ref, sem) = refs[:4], refs[4], refs[5:]
    copy = pltpu.make_async_copy(own_hbm, own_ref, sem)
    copy.start()
    for r in range(1, 4):
        stack_ref[r - 1] = parts[r][...]
    held_ref[...] = by_place(me_ref[0], [ref[...] for ref in parts], 0)
    copy.wait()


def plane_kernel(
    me_ref, *refs, level
):
    gots, (packed_ref, stack_ref, stack_there_ref) = refs[:4], refs[4:7]
    head_ref, send_ref, done_ref, held_ref = refs[7:]
    me = me_ref[0]
    core = me % 2
    cols = done_ref.shape[1]
    pairs = [(packed_ref[0], packed_ref[1])]
    pairs += [by_core(core, stack_ref[r], stack_there_ref[r]) for r in range(3)]
    firsts, seconds = [pair[0] for pair in pairs], [pair[1] for pair in pairs]
    pairs = [(by_place(me, firsts, j), by_place(me, seconds, j)) for j in range(4)]
    held_ref[0], held_ref[1] = pairs[0]
    reflectors = [unpack(*pair) for pair in pairs]
    parts = [ref[:cols] for ref in gots]
    heads = [by_place(me, parts, j) for j in range(4)]
    gram = gots[0][cols:] + gots[1][cols:] + (gots[2][cols:] + gots[3][cols:])
    heads[0], heads[1] = tree_node(heads[0], heads[1], reflectors[1])
    heads[2], heads[3] = tree_node(heads[2], heads[3], reflectors[3])
    heads[0], heads[2] = tree_node(heads[0], heads[2], reflectors[2])
    for j in range(4):
        done_ref[j] = heads[j]
    head_ref[...] = heads[0]
    upper = (me >> level) % 2 == 1
    send_ref[:cols] = jnp.where(upper, plain(halves(heads[0]), reflectors[0][0]), heads[0])
    send_ref[cols:] = gram


def line_node(
    me, head_ref, result_ref, mine_ref, there_ref, held_ref, part_ref, part_there_ref, level
):
    cols = head_ref.shape[0]
    upper = (me >> level) % 2 == 1
    held = held_ref[0], held_ref[1]
    others = by_core(me % 2, part_ref[...], part_there_ref[...])
    node = [jnp.where(upper, a, b) for a, b in zip(held, others)]
    following = [jnp.where(upper, b, a) for a, b in zip(held, others)]
    head = head_ref[...]
    there = there_ref[:cols]
    coeffs = by_transpose(halves(mine_ref[:cols] + there), unpack(*node)[1])
    low = jnp.where(upper, there, head) - coeffs
    plane = me >> 3
    below = (1 << (level - 2)) - 1
    second = (plane & below) == (1 << (level - 3))
    high = head - by_transpose(halves(coeffs), unpack(*held)[0])
    result = jnp.where(second, high, result_ref[...])
    return low, result, mine_ref[cols:] + there_ref[cols:], following


def line_kernel(me_ref, *refs, level):
    head_out, result_out, send_ref, held_out = refs[7:]
    me = me_ref[0]
    low, result, gram, following = line_node(me, *refs[:7], level)
    cols = low.shape[0]
    ahead = (me >> (level + 1)) % 2 == 1
    head_out[...] = low
    result_out[...] = result
    held_out[0], held_out[1] = following
    send_ref[:cols] = jnp.where(ahead, plain(halves(low), unpack(*following)[0]), low)
    send_ref[cols:] = gram


def last_kernel(me_ref, *refs, level):
    done_ref, sends, all_ref = refs[7], refs[8:12], refs[12]
    me = me_ref[0]
    low, result, gram, _ = line_node(me, *refs[:7], level)
    cols = low.shape[0]
    quarter = gram.shape[0]
    all_ref[0] = jnp.where((me >> 3) == 0, low, result)
    for j in range(1, 4):
        all_ref[j] = done_ref[j]
    for r in range(4):
        sends[r][:cols] = all_ref[place(me) ^ r]
        sends[r][cols : cols + quarter] = low[:quarter]
        sends[r][cols + quarter :] = gram


def pass_kernel(me_ref, *refs):
    backs, dones, out_ref = refs[:4], refs[4:8], refs[8]
    odd = me_ref[0] % 2 == 1
    cols = dones[0].shape[0]
    for r in range(4):
        out_ref[r, :cols] = jnp.where(odd, backs[r][:cols], dones[r][...])
        out_ref[r, cols:] = backs[r][cols:]


def near_kernel(me_ref, *refs):
    backs, dones, (_, updated_hbm, out_ref, sems) = refs[:4], refs[4:8], refs[8:]
    count, width, half = out_ref.shape
    quarter = half // 4
    me = me_ref[0]
    core = me % 2
    odd = core == 1
    copies = []
    for b in range(count):
        rows = slice(b * quarter, (b + 1) * quarter)
        pieces = [jnp.where(odd, dones[r][rows], backs[r][rows]) for r in range(4)]
        out_ref[b] = jnp.concatenate([by_place(me, pieces, j) for j in range(4)], axis=0).T
        columns = pl.ds(pl.multiple_of(b * width + core * half, half), half)
        copies.append(pltpu.make_async_copy(out_ref.at[b], updated_hbm.at[pl.ds(0, width), columns], sems.at[b]))
        copies[-1].start()
    for copy in copies:
        copy.wait()


def far_kernel(me_ref, *refs, total):
    backs, dones = refs[:4], refs[4:8]
    there_ref, inverse_ref, _, _, updated_hbm, basis_hbm, gram_ref = refs[8:15]
    panel_ref, sum_ref, out_ref, basis_ref, sems = refs[15:]
    count, width, half = out_ref.shape
    quarter = half // 4
    cols = count * quarter
    me = me_ref[0]
    core = me % 2
    odd = core == 1
    copies = []

    def put(source, target):
        copies.append(pltpu.make_async_copy(source, target, sems.at[len(copies)]))
        copies[-1].start()

    for b in range(count):
        rows = slice(b * quarter, (b + 1) * quarter)
        pieces = [there_ref[r, rows] for r in range(4)]
        far = jnp.concatenate([by_place(me, pieces, j) for j in range(4)], axis=0).T
        out_ref[b] = far
        columns = pl.ds(pl.multiple_of(b * width + (1 - core) * half, half), half)
        put(out_ref.at[b], updated_hbm.at[pl.ds(0, width), columns])
        if b == 0:
            pieces = [jnp.where(odd, dones[r][rows], backs[r][rows]) for r in range(4)]
            near = jnp.concatenate([by_place(me, pieces, j) for j in range(4)], axis=0).T
            head = jnp.concatenate(by_core(core, near, far), axis=1)
            basis = plain(halves(head), halves(inverse_ref[...]))
            basis_ref[...] = jnp.where(me == 0, 0.0, basis)
            put(basis_ref, basis_hbm.at[pl.ds(0, width)])

    def target(part, r):
        return pl.ds(pl.multiple_of(part * half + (place(me) ^ r) * quarter, quarter), quarter)

    for r in range(4):
        panel_ref[target(core, r)] = backs[r][cols : cols + quarter]
        sum_ref[target(core, r)] = backs[r][cols + quarter :]
        panel_ref[target(1 - core, r)] = there_ref[r, cols : cols + quarter]
        sum_ref[target(1 - core, r)] = there_ref[r, cols + quarter :]
    panel = halves(panel_ref[...])
    gram_ref[...] = (sum_ref[...] - by_transpose(panel, panel)) / total
    for copy in copies:
        copy.wait()


def after(value, *others):
    return lax.optimization_barrier((value, *others))[0]


def body(trailing, leaf_vectors, leaf_factors, tree_vectors, tree_factors, inverse_factor):
    rows, columns = trailing.shape
    width = leaf_vectors.shape[1]
    half = width // 2
    quarter = half // 4
    count = columns // width
    cols = count * quarter
    devices = lax.axis_size("rows")
    levels = devices.bit_length() - 1
    me = lax.axis_index("rows").astype(jnp.int32)
    me_array = me.reshape(1)

    def exchange(value, shift):
        return lax.ppermute(value, "rows", [(i, i ^ shift) for i in range(devices)])

    def around(values):
        there = [exchange(values[r], 2 * r) for r in (3, 1, 2)]
        return [values[0], there[1], there[2], there[0]]

    def shape(*dims):
        return jax.ShapeDtypeStruct(dims, F32)

    def vmem(*dims):
        return pltpu.VMEM(dims, F32)

    def cost(flops, moved=0):
        return pl.CostEstimate(flops=flops, bytes_accessed=moved, transcendentals=0)

    def whole_call(kernel, operands, outs, scratch=(), flops=0):
        return pl.pallas_call(
            kernel,
            out_shape=outs,
            in_specs=[SCALAR] + [WHOLE] * len(operands),
            out_specs=tuple(WHOLE for _ in outs),
            scratch_shapes=list(scratch),
            compiler_params=PARAMS,
            cost_estimate=cost(flops),
        )(me_array, *operands)

    there = [exchange(tree_vectors, 1), exchange(tree_factors, 1)]
    chip_low, chip_high, chip_part = pl.pallas_call(
        pack_kernel,
        out_shape=(shape(2, half + EXTRA, width), shape(2, half + EXTRA, width), shape(half + EXTRA, width)),
        in_specs=[SCALAR] + [AWAY] * 4,
        out_specs=(WHOLE,) * 3,
        scratch_shapes=[vmem(4, width, width), pltpu.SemaphoreType.DMA((4,))],
        compiler_params=room(62),
    )(me_array, tree_vectors, tree_factors, *there)
    plane_parts = [exchange(chip_part, 2 * r) for r in (3, 1, 2)]
    plane_parts = [plane_parts[1], plane_parts[2], plane_parts[0]]

    leaf_rows = count * half + half
    leaf_flops = 6 * width * columns * (2 * rows + width) + 6 * width * width * (rows + width)
    own, away, updated, basis = pl.pallas_call(
        leaf_kernel,
        out_shape=(shape(leaf_rows, width), shape(leaf_rows, width), shape(rows, columns), shape(rows, width)),
        in_specs=[SCALAR] + [AWAY] * 4,
        out_specs=(AWAY,) * 4,
        scratch_shapes=[
            vmem(leaf_rows, width),
            vmem(leaf_rows, width),
            vmem(count, rows, width),
            vmem(rows, width),
            vmem(width, width),
            vmem(width, width),
            vmem(count, width, width),
            vmem(width, width),
            vmem(width, width),
            vmem(width, width),
            pltpu.SemaphoreType.DMA((count * (rows // width) + 3,)),
            pltpu.SemaphoreType.DMA((3 * count + 3,)),
        ],
        compiler_params=room(61),
        cost_estimate=cost(leaf_flops, 4 * (2 * rows * columns + 3 * rows * width)),
    )(after(me_array, chip_part), trailing, leaf_vectors, leaf_factors, inverse_factor)
    plane_parts = [after(part, own) for part in plane_parts]
    away = exchange(after(away, *plane_parts), 1)
    stack, held_part, own = pl.pallas_call(
        gather_kernel,
        out_shape=(shape(3, half + EXTRA, width), shape(half + EXTRA, width), shape(leaf_rows, width)),
        in_specs=[SCALAR] + [WHOLE] * 4 + [AWAY],
        out_specs=(WHOLE,) * 3,
        scratch_shapes=[pltpu.SemaphoreType.DMA],
        compiler_params=PARAMS,
    )(me_array, chip_part, *plane_parts, own)
    stack_there = exchange(stack, 1)

    outs = whole_call(
        core_kernel, (own, away, chip_high),
        tuple([shape(cols + quarter, width)] * 4 + [shape(cols, width)] * 4),
        (vmem(leaf_rows, width), vmem(count * half, width)),
        flops=18 * width * width * count * half,
    )
    sends, dones = outs[:4], outs[4:]
    gots = around(sends)

    part = after(exchange(held_part, 8), sends[1]) if levels > 3 else held_part
    head, send, plane_done, held = whole_call(
        functools.partial(plane_kernel, level=3), (*gots, chip_low, stack, stack_there),
        (shape(cols, width), shape(cols + quarter, width), shape(4, cols, width), shape(2, half + EXTRA, width)),
        flops=18 * width * width * cols * 3,
    )

    result = head
    for level in range(3, levels):
        part_there = exchange(part, 1)
        operands = (head, result, send, exchange(send, 1 << level), held, part, part_there)
        if level == levels - 1:
            sends = whole_call(
                functools.partial(last_kernel, level=level), (*operands, plane_done),
                tuple([shape(cols + 2 * quarter, width)] * 4), (vmem(4, cols, width),),
                flops=18 * width * width * cols,
            )
        else:
            held_part = jnp.where((me >> level) % 2 == 1, part, held_part)
            part = after(exchange(held_part, 2 << level), head)
            head, result, send, held = whole_call(
                functools.partial(line_kernel, level=level), operands,
                (shape(cols, width), shape(cols, width), shape(cols + quarter, width), shape(*held.shape)),
                flops=18 * width * width * cols,
            )

    backs = around(sends)
    (back,) = whole_call(pass_kernel, (*backs, *dones), (shape(4, cols + 2 * quarter, width),))
    there = exchange(back, 1)

    updated = pl.pallas_call(
        near_kernel,
        out_shape=shape(rows, columns),
        in_specs=[SCALAR] + [WHOLE] * 8 + [AWAY],
        out_specs=AWAY,
        scratch_shapes=[vmem(count, width, half), pltpu.SemaphoreType.DMA((count,))],
        input_output_aliases={9: 0},
        compiler_params=PARAMS,
        cost_estimate=cost(10**9, 8 * half * columns),
    )(me_array, *backs, *dones, updated)
    return pl.pallas_call(
        functools.partial(far_kernel, total=float(rows * devices)),
        out_shape=(shape(rows, columns), shape(rows, width), shape(width, width)),
        in_specs=[SCALAR] + [WHOLE] * 10 + [AWAY] * 2,
        out_specs=(AWAY, AWAY, WHOLE),
        scratch_shapes=[
            vmem(width, width),
            vmem(width, width),
            vmem(count, width, half),
            vmem(width, width),
            pltpu.SemaphoreType.DMA((count + 1,)),
        ],
        input_output_aliases={11: 0, 12: 1},
        compiler_params=PARAMS,
    )(me_array, *backs, *dones, there, inverse_factor, updated, basis)


def solution(mesh):
    in_specs = (
        P("rows", None),
        P("rows", None),
        P("rows", None),
        P("rows", None),
        P("rows", None),
        P(),
    )
    out_specs = (P("rows", None), P("rows", None), P())
    return jax.shard_map(body, mesh=mesh, in_specs=in_specs, out_specs=out_specs, check_vma=False)
```

```python
import functools
import jax
import jax.numpy as jnp
from jax import lax
from jax.experimental import pallas as pl
from jax.experimental.pallas import tpu as pltpu
from jax.sharding import PartitionSpec as P

F32 = jnp.float32
BF16 = jnp.bfloat16
EXTRA = 8
PARAMS = pltpu.CompilerParams(vmem_limit_bytes=40 * 1024 * 1024)
def room(megabytes):
    return pltpu.CompilerParams(vmem_limit_bytes=megabytes * 1024 * 1024)


WHOLE = pl.BlockSpec(memory_space=pltpu.VMEM)
SCALAR = pl.BlockSpec(memory_space=pltpu.SMEM)
AWAY = pl.BlockSpec(memory_space=pltpu.HBM)


def halves(value):
    high = value.astype(BF16)
    return high, (value - high.astype(F32)).astype(BF16)


def times(left, right, sides):
    dims = ((sides[:1], sides[1:]), ((), ()))
    dot = functools.partial(lax.dot_general, dimension_numbers=dims, preferred_element_type=F32)
    return dot(left[0], right[0]) + (dot(left[0], right[1]) + dot(left[1], right[0]))


def plain(left, right):
    return times(left, right, (1, 0))


def by_transpose(left, right):
    return times(left, right, (1, 1))


def pack_kernel(me_ref, *refs):
    sources, (low_ref, high_ref, part_ref), (buffer_ref, sems) = refs[:4], refs[4:7], refs[7:]
    copies = [pltpu.make_async_copy(source, buffer_ref.at[i], sems.at[i]) for i, source in enumerate(sources)]
    for copy in copies:
        copy.start()
    for copy in copies:
        copy.wait()
    core = me_ref[0] % 2
    width = buffer_ref.shape[1]
    half = width // 2
    row = lax.broadcasted_iota(jnp.int32, (width, width), 0)
    col = lax.broadcasted_iota(jnp.int32, (width, width), 1)
    both_vectors = by_core(core, buffer_ref[0], buffer_ref[2])
    both_factors = by_core(core, buffer_ref[1], buffer_ref[3])
    for vectors, factors, out_ref in zip(both_vectors, both_factors, (low_ref, high_ref)):
        packed = jnp.where(row > col, factors.T, vectors)
        diagonal = jnp.sum(jnp.where(row == col, factors, 0.0), axis=0, keepdims=True)
        for part in range(2):
            out_ref[part, :half] = packed[part * half : (part + 1) * half]
            out_ref[part, half:] = jnp.broadcast_to(diagonal, (EXTRA, width))
    part_ref[...] = low_ref[core]


def unpack(first, second):
    half = first.shape[0] - EXTRA
    width = 2 * half
    packed = jnp.concatenate([first[:half], second[:half]], axis=0)
    row = lax.broadcasted_iota(jnp.int32, (width, width), 0)
    col = lax.broadcasted_iota(jnp.int32, (width, width), 1)
    diagonal = jnp.broadcast_to(first[half : half + 1], (width, width))
    vectors = jnp.where(row <= col, packed, 0.0)
    factors = jnp.where(row > col, packed, jnp.where(row == col, diagonal, 0.0))
    return halves(vectors), halves(factors)


def by_core(core, mine, there):
    odd = core == 1
    return jnp.where(odd, there, mine), jnp.where(odd, mine, there)


def place(me):
    return (me >> 1) & 3


def by_place(me, parts, wanted):
    source = place(me) ^ wanted
    out = parts[0]
    for r in range(1, 4):
        out = jnp.where(source == r, parts[r], out)
    return out


def tree_node(low, high, reflector):
    vectors, factors = reflector
    node = by_transpose(halves(low + plain(halves(high), vectors)), factors)
    return low - node, high - by_transpose(halves(node), vectors)


def leaf_kernel(me_ref, *refs, first, start, stop):
    if first:
        trailing_hbm, vectors_hbm, factors_hbm, own_hbm, away_hbm, updated_hbm, combined_hbm = refs[:7]
    else:
        trailing_hbm, vectors_hbm, combined_hbm, inverse_hbm, _, own_hbm, away_hbm, updated_hbm, basis_hbm = refs[:9]
    scratch = refs[7 if first else 9 :]
    own_ref, away_ref, part_ref, vectors_ref, combined_ref, rest_ref, head_ref, spare_ref, in_sems, out_sems = scratch
    rows, width = vectors_ref.shape
    half = width // 2
    core = me_ref[0] % 2
    mine = pl.ds(pl.multiple_of(core * half, half), half)
    other = pl.ds(pl.multiple_of((1 - core) * half, half), half)
    copies, out_copies = [], []

    def fetch(source, target):
        copies.append(pltpu.make_async_copy(source, target, in_sems.at[len(copies)]))
        copies[-1].start()
        return copies[-1]

    def put(source, target):
        out_copies.append(pltpu.make_async_copy(source, target, out_sems.at[len(out_copies)]))
        out_copies[-1].start()

    def fetch_part(b, slot):
        cuts = [slice(c, c + width) for c in range(0, rows, width)]
        return [fetch(trailing_hbm.at[c, pl.ds(b * width, width)], part_ref.at[slot, c]) for c in cuts]

    def hand_over(value_ref, slot):
        rows_b = slice(slot * half, (slot + 1) * half)
        own_ref[rows_b] = value_ref[mine]
        away_ref[rows_b] = value_ref[other]
        put(away_ref.at[rows_b], away_hbm.at[rows_b])
        put(own_ref.at[rows_b], own_hbm.at[rows_b])

    vectors_copy = fetch(vectors_hbm, vectors_ref)
    if first:
        other_copy = fetch(factors_hbm, spare_ref.at[0])
    else:
        other_copy = fetch(combined_hbm, combined_ref)
    parts = [fetch_part(b, b - start) for b in range(start, stop)]
    if not first:
        panel_copy = fetch_part(0, stop - start)
        basis_copies = [
            fetch(inverse_hbm, spare_ref.at[0]),
            fetch(updated_hbm.at[pl.ds(width, width), pl.ds(0, width)], spare_ref.at[1]),
        ]
    vectors_copy.wait()
    across = halves(vectors_ref[...].T)
    other_copy.wait()
    if first:
        combined_ref[...] = by_transpose(halves(vectors_ref[...]), halves(spare_ref[0]))
        put(combined_ref, combined_hbm)
    combined = halves(combined_ref[...])
    for slot in range(stop - start):
        for copy in parts[slot]:
            copy.wait()
        part = part_ref[slot]
        out = part - plain(combined, halves(plain(across, halves(part))))
        rest_ref[slot] = out[width:]
        head_ref[slot] = out[:width].T
        hand_over(head_ref.at[slot], slot)
        columns = pl.ds((start + slot) * width, width)
        put(rest_ref.at[slot], updated_hbm.at[pl.ds(width, width), columns])
    if not first:
        for copy in panel_copy:
            copy.wait()
        panel = part_ref[stop - start]
        head_ref[stop - start] = plain(halves(panel.T), halves(panel))
        hand_over(head_ref.at[stop - start], stop - start)
        for copy in basis_copies:
            copy.wait()
        spare_ref[2] = plain(halves(spare_ref[1]), halves(spare_ref[0]))
        put(spare_ref.at[2], basis_hbm.at[pl.ds(width, width)])
    for copy in out_copies:
        copy.wait()


def core_kernel(me_ref, own_ref, there_ref, packed_ref, *refs):
    sends, dones, (low_ref, high_ref) = refs[:4], refs[4:8], refs[8:]
    me = me_ref[0]
    half = own_ref.shape[1] // 2
    quarter = half // 4
    count = dones[0].shape[0] // quarter
    more = own_ref.shape[0] // half
    odd = me % 2 == 1
    mine, there = own_ref[: count * half], there_ref[: count * half]
    low = jnp.where(odd, there, mine)
    high = jnp.where(odd, mine, there)
    low, high = tree_node(low, high, unpack(packed_ref[0], packed_ref[1]))
    low_ref[: count * half] = low
    if more > count:
        low_ref[count * half :] = own_ref[count * half :] + there_ref[count * half :]
    high_ref[...] = high
    for r in range(4):
        start = (place(me) ^ r) * quarter
        for b in range(more):
            source = pl.ds(pl.multiple_of(b * half + start, quarter), quarter)
            target = slice(b * quarter, (b + 1) * quarter)
            sends[r][target] = low_ref[source]
            if b < count:
                dones[r][target] = high_ref[source]


def gather_kernel(me_ref, *refs):
    parts, own_hbm, (stack_ref, held_ref, own_ref, sem) = refs[:4], refs[4], refs[5:]
    copy = pltpu.make_async_copy(own_hbm, own_ref, sem)
    copy.start()
    for r in range(1, 4):
        stack_ref[r - 1] = parts[r][...]
    held_ref[...] = by_place(me_ref[0], [ref[...] for ref in parts], 0)
    copy.wait()


def plane_kernel(
    me_ref, *refs, level
):
    gots, (packed_ref, stack_ref, stack_there_ref) = refs[:4], refs[4:7]
    head_ref, send_ref, done_ref, held_ref = refs[7:]
    me = me_ref[0]
    core = me % 2
    cols = done_ref.shape[1]
    pairs = [(packed_ref[0], packed_ref[1])]
    pairs += [by_core(core, stack_ref[r], stack_there_ref[r]) for r in range(3)]
    firsts, seconds = [pair[0] for pair in pairs], [pair[1] for pair in pairs]
    pairs = [(by_place(me, firsts, j), by_place(me, seconds, j)) for j in range(4)]
    held_ref[0], held_ref[1] = pairs[0]
    reflectors = [unpack(*pair) for pair in pairs]
    parts = [ref[:cols] for ref in gots]
    heads = [by_place(me, parts, j) for j in range(4)]
    if gots[0].shape[0] > cols:
        send_ref[cols:] = gots[0][cols:] + gots[1][cols:] + (gots[2][cols:] + gots[3][cols:])
    heads[0], heads[1] = tree_node(heads[0], heads[1], reflectors[1])
    heads[2], heads[3] = tree_node(heads[2], heads[3], reflectors[3])
    heads[0], heads[2] = tree_node(heads[0], heads[2], reflectors[2])
    for j in range(4):
        done_ref[j] = heads[j]
    head_ref[...] = heads[0]
    upper = (me >> level) % 2 == 1
    send_ref[:cols] = jnp.where(upper, plain(halves(heads[0]), reflectors[0][0]), heads[0])


def line_node(
    me, head_ref, result_ref, mine_ref, there_ref, held_ref, part_ref, part_there_ref, level
):
    cols = head_ref.shape[0]
    upper = (me >> level) % 2 == 1
    held = held_ref[0], held_ref[1]
    others = by_core(me % 2, part_ref[...], part_there_ref[...])
    node = [jnp.where(upper, a, b) for a, b in zip(held, others)]
    following = [jnp.where(upper, b, a) for a, b in zip(held, others)]
    head = head_ref[...]
    there = there_ref[:cols]
    coeffs = by_transpose(halves(mine_ref[:cols] + there), unpack(*node)[1])
    low = jnp.where(upper, there, head) - coeffs
    plane = me >> 3
    below = (1 << (level - 2)) - 1
    second = (plane & below) == (1 << (level - 3))
    high = head - by_transpose(halves(coeffs), unpack(*held)[0])
    result = jnp.where(second, high, result_ref[...])
    gram = None
    if mine_ref.shape[0] > cols:
        gram = mine_ref[cols:] + there_ref[cols:]
    return low, result, gram, following


def line_kernel(me_ref, *refs, level):
    head_out, result_out, send_ref, held_out = refs[7:]
    me = me_ref[0]
    low, result, gram, following = line_node(me, *refs[:7], level)
    cols = low.shape[0]
    ahead = (me >> (level + 1)) % 2 == 1
    head_out[...] = low
    result_out[...] = result
    held_out[0], held_out[1] = following
    send_ref[:cols] = jnp.where(ahead, plain(halves(low), unpack(*following)[0]), low)
    if gram is not None:
        send_ref[cols:] = gram


def last_kernel(me_ref, *refs, level):
    done_ref, sends, all_ref = refs[7], refs[8:12], refs[12]
    me = me_ref[0]
    low, result, gram, _ = line_node(me, *refs[:7], level)
    cols = low.shape[0]
    all_ref[0] = jnp.where((me >> 3) == 0, low, result)
    for j in range(1, 4):
        all_ref[j] = done_ref[j]
    for r in range(4):
        sends[r][:cols] = all_ref[place(me) ^ r]
        sends[r][cols:] = low[: sends[r].shape[0] - cols] if gram is None else gram


def pass_kernel(me_ref, *refs):
    backs, dones, out_ref = refs[:4], refs[4:8], refs[8]
    odd = me_ref[0] % 2 == 1
    cols = dones[0].shape[0]
    for r in range(4):
        out_ref[r, :cols] = jnp.where(odd, backs[r][:cols], dones[r][...])
        out_ref[r, cols:] = backs[r][cols:]


def final_kernel(me_ref, *refs, start, first, total):
    backs, dones, there_ref, refs = refs[:4], refs[4:8], refs[8], refs[9:]
    if first:
        inverse_ref, _, _, updated_hbm, basis_hbm, panel_out, head_ref, out_ref, sems = refs
    else:
        panel_in, _, updated_hbm, gram_ref, head_ref, out_ref, sems = refs
    count, width = out_ref.shape[:2]
    half = width // 2
    quarter = half // 4
    me = me_ref[0]
    core = me % 2
    odd = core == 1
    copies = []

    def put(source, target):
        copies.append(pltpu.make_async_copy(source, target, sems.at[len(copies)]))
        copies[-1].start()

    def target(part, r):
        return pl.ds(pl.multiple_of(part * half + (place(me) ^ r) * quarter, quarter), quarter)

    blocks = count - 1 if first else count
    for b in range(blocks):
        rows = slice(b * quarter, (b + 1) * quarter)
        for r in range(4):
            head_ref[b, target(core, r)] = jnp.where(odd, dones[r][rows], backs[r][rows])
            head_ref[b, target(1 - core, r)] = there_ref[r, rows]
        out_ref[b] = head_ref[b].T
        put(out_ref.at[b], updated_hbm.at[pl.ds(0, width), pl.ds((start + b) * width, width)])
    rows = slice(blocks * quarter, (blocks + 1) * quarter)
    if first:
        basis = plain(halves(out_ref[0]), halves(inverse_ref[...]))
        out_ref[blocks] = jnp.where(me == 0, 0.0, basis)
        put(out_ref.at[blocks], basis_hbm.at[pl.ds(0, width)])
        for r in range(4):
            panel_out[target(core, r)] = backs[r][rows]
            panel_out[target(1 - core, r)] = there_ref[r, rows]
    else:
        for r in range(4):
            head_ref[blocks, target(core, r)] = backs[r][rows]
            head_ref[blocks, target(1 - core, r)] = there_ref[r, rows]
        panel = halves(panel_in[...])
        gram_ref[...] = (head_ref[blocks] - by_transpose(panel, panel)) / total
    for copy in copies:
        copy.wait()


def after(value, *others):
    return lax.optimization_barrier((value, *others))[0]


def body(trailing, leaf_vectors, leaf_factors, tree_vectors, tree_factors, inverse_factor):
    rows, columns = trailing.shape
    width = leaf_vectors.shape[1]
    half = width // 2
    quarter = half // 4
    count = columns // width
    devices = lax.axis_size("rows")
    levels = devices.bit_length() - 1
    me = lax.axis_index("rows").astype(jnp.int32)
    me_array = me.reshape(1)
    chunks = ((0, count // 2), (count // 2, count))
    part_shape = (half + EXTRA, width)
    latest = [me_array]

    def exchange(value, shift):
        return lax.ppermute(value, "rows", [(i, i ^ shift) for i in range(devices)])

    def around(values):
        there = [exchange(values[r], 2 * r) for r in (3, 1, 2)]
        return [values[0], there[1], there[2], there[0]]

    def shape(*dims):
        return jax.ShapeDtypeStruct(dims, F32)

    def vmem(*dims):
        return pltpu.VMEM(dims, F32)

    def sems(number):
        return pltpu.SemaphoreType.DMA((number,))

    def call(kernel, operands, outs, scratch=(), away_in=(), away_out=(), params=PARAMS, aliases=()):
        values = pl.pallas_call(
            kernel,
            out_shape=tuple(outs),
            in_specs=[SCALAR] + [AWAY if i in away_in else WHOLE for i in range(len(operands))],
            out_specs=tuple(AWAY if i in away_out else WHOLE for i in range(len(outs))),
            scratch_shapes=list(scratch),
            input_output_aliases=dict(aliases),
            compiler_params=params,
            cost_estimate=pl.CostEstimate(flops=1, bytes_accessed=1, transcendentals=0),
        )(after(me_array, latest[0]), *operands)
        latest[0] = values[0]
        return values

    def leaf(first, start, stop, operands, outs, aliases):
        blocks = stop - start
        more = 0 if first else 1
        outs = [shape((blocks + more) * half, width)] * 2 + outs
        scratch = [
            vmem((blocks + more) * half, width),
            vmem((blocks + more) * half, width),
            vmem(blocks + more, rows, width),
            vmem(rows, width),
            vmem(rows, width),
            vmem(blocks, width, width),
            vmem(blocks + more, width, width),
            vmem(3, width, width),
            sems((blocks + more) * (rows // width) + 4),
            sems(3 * blocks + 3),
        ]
        return call(
            functools.partial(leaf_kernel, first=first, start=start, stop=stop),
            operands, outs, scratch, range(len(operands)), range(len(outs)), room(61), aliases,
        )

    raw = [exchange(tree_vectors, 1), exchange(tree_factors, 1)]
    own_a, away_a, updated, combined = leaf(
        True, *chunks[0], (trailing, leaf_vectors, leaf_factors),
        [shape(rows, columns), shape(rows, width)], (),
    )
    there_a = exchange(away_a, 1)

    chip_low, chip_high, chip_part = call(
        pack_kernel, (tree_vectors, tree_factors, *raw),
        (shape(2, *part_shape), shape(2, *part_shape), shape(*part_shape)),
        [vmem(4, width, width), sems(4)], range(4), (), PARAMS,
    )
    plane_parts = [exchange(chip_part, 2 * r) for r in (3, 1, 2)]
    plane_parts = [plane_parts[1], plane_parts[2], plane_parts[0]]

    def core_call(own, there, start, stop):
        blocks = stop - start
        more = own.shape[0] // half
        outs = call(
            core_kernel, (own, there, chip_high),
            [shape(more * quarter, width)] * 4 + [shape(blocks * quarter, width)] * 4,
            [vmem(more * half, width), vmem(blocks * half, width)],
        )
        return outs[:4], outs[4:]

    sends_a, dones_a = core_call(own_a, there_a, *chunks[0])
    gots_a = around(sends_a)

    own_b, away_b, updated, basis = leaf(
        False, *chunks[1], (trailing, leaf_vectors, combined, inverse_factor, updated),
        [shape(rows, columns), shape(rows, width)], {5: 2},
    )
    plane_parts = [after(part, own_b) for part in plane_parts]
    there_b = exchange(after(away_b, *plane_parts), 1)
    stack, held_part, own_b = call(
        gather_kernel, (chip_part, *plane_parts, own_b),
        (shape(3, *part_shape), shape(*part_shape), shape(*own_b.shape)),
        [pltpu.SemaphoreType.DMA], (4,),
    )
    stack_there = exchange(stack, 1)
    line_part = exchange(held_part, 8)
    sends_b, dones_b = core_call(own_b, there_b, *chunks[1])
    gots_b = around(sends_b)
    parts = [after(line_part, sends_b[0])]
    held_parts = [held_part]

    def plane_call(gots, start, stop):
        cols = (stop - start) * quarter
        return call(
            functools.partial(plane_kernel, level=3), (*gots, chip_low, stack, stack_there),
            (shape(cols, width), shape(*gots[0].shape), shape(4, cols, width), shape(2, *part_shape)),
        )

    state = []
    for gots, chunk in ((gots_a, chunks[0]), (gots_b, chunks[1])):
        low, send, done, held = plane_call(gots, *chunk)
        state.append([low, low, send, exchange(send, 8), held, done])

    sends = [None, None]
    for level in range(3, levels):
        part = parts[-1]
        part_there = exchange(part, 1)
        if level < levels - 1:
            held_parts.append(jnp.where((me >> level) % 2 == 1, part, held_parts[-1]))
            next_part = exchange(held_parts[-1], 2 << level)
        for i, (start, stop) in enumerate(chunks):
            low, result, send, there, held, done = state[i]
            operands = (low, result, send, there, held, part, part_there)
            cols = (stop - start) * quarter
            if level == levels - 1:
                sends[i] = call(
                    functools.partial(last_kernel, level=level), (*operands, done),
                    [shape(cols + quarter, width)] * 4, [vmem(4, cols, width)],
                )
            else:
                low, result, send, held = call(
                    functools.partial(line_kernel, level=level), operands,
                    (shape(cols, width), shape(cols, width), shape(*send.shape), shape(*held.shape)),
                )
                state[i] = [low, result, send, exchange(send, 2 << level), held, done]
        if level < levels - 1:
            parts.append(after(next_part, latest[0]))

    backs = [around(values) for values in sends]
    there = []
    for i, dones in enumerate((dones_a, dones_b)):
        (back,) = call(pass_kernel, (*backs[i], *dones), (shape(4, *backs[i][0].shape),))
        there.append(exchange(back, 1))

    def final(first, operands, outs, away_in, away_out, aliases):
        start, stop = chunks[0 if first else 1]
        blocks = stop - start
        return call(
            functools.partial(final_kernel, start=start, first=first, total=float(rows * devices)),
            operands, outs,
            [vmem(blocks + 1, width, width), vmem(blocks + (1 if first else 0), width, width), sems(blocks + 1)],
            away_in, away_out, PARAMS, aliases,
        )

    updated, basis, panel = final(
        True, (*backs[0], *dones_a, there[0], inverse_factor, updated, basis),
        (shape(rows, columns), shape(rows, width), shape(width, width)), (10, 11), (0, 1), {11: 0, 12: 1},
    )
    updated, gram = final(
        False, (*backs[1], *dones_b, there[1], panel, updated),
        (shape(rows, columns), shape(width, width)), (10,), (0,), {11: 0},
    )
    return (updated, basis, gram)


def solution(mesh):
    in_specs = (
        P("rows", None),
        P("rows", None),
        P("rows", None),
        P("rows", None),
        P("rows", None),
        P(),
    )
    out_specs = (P("rows", None), P("rows", None), P())
    return jax.shard_map(body, mesh=mesh, in_specs=in_specs, out_specs=out_specs, check_vma=False)
```

```python
import functools
import jax
import jax.numpy as jnp
from jax import lax
from jax.experimental import pallas as pl
from jax.experimental.pallas import tpu as pltpu
from jax.sharding import PartitionSpec as P

F32 = jnp.float32
BF16 = jnp.bfloat16
EXTRA = 8
PARAMS = pltpu.CompilerParams(vmem_limit_bytes=40 * 1024 * 1024)
def room(megabytes):
    return pltpu.CompilerParams(vmem_limit_bytes=megabytes * 1024 * 1024)


WHOLE = pl.BlockSpec(memory_space=pltpu.VMEM)
SCALAR = pl.BlockSpec(memory_space=pltpu.SMEM)
AWAY = pl.BlockSpec(memory_space=pltpu.HBM)


def halves(value):
    high = value.astype(BF16)
    return high, (value - high.astype(F32)).astype(BF16)


def times(left, right, sides):
    first = jnp.concatenate([left[0], left[0], left[1]], axis=sides[0])
    second = jnp.concatenate([right[0], right[1], right[0]], axis=sides[1])
    dims = ((sides[:1], sides[1:]), ((), ()))
    return lax.dot_general(first, second, dims, preferred_element_type=F32)


def plain(left, right):
    return times(left, right, (1, 0))


def by_transpose(left, right):
    return times(left, right, (1, 1))


def pack_kernel(me_ref, *refs):
    sources, (low_ref, high_ref, part_ref), (buffer_ref, sems) = refs[:4], refs[4:7], refs[7:]
    copies = [pltpu.make_async_copy(source, buffer_ref.at[i], sems.at[i]) for i, source in enumerate(sources)]
    for copy in copies:
        copy.start()
    for copy in copies:
        copy.wait()
    core = me_ref[0] % 2
    width = buffer_ref.shape[1]
    half = width // 2
    row = lax.broadcasted_iota(jnp.int32, (width, width), 0)
    col = lax.broadcasted_iota(jnp.int32, (width, width), 1)
    both_vectors = by_core(core, buffer_ref[0], buffer_ref[2])
    both_factors = by_core(core, buffer_ref[1], buffer_ref[3])
    for vectors, factors, out_ref in zip(both_vectors, both_factors, (low_ref, high_ref)):
        packed = jnp.where(row > col, factors.T, vectors)
        diagonal = jnp.sum(jnp.where(row == col, factors, 0.0), axis=0, keepdims=True)
        for part in range(2):
            out_ref[part, :half] = packed[part * half : (part + 1) * half]
            out_ref[part, half:] = jnp.broadcast_to(diagonal, (EXTRA, width))
    part_ref[...] = low_ref[core]


def unpack(first, second):
    half = first.shape[0] - EXTRA
    width = 2 * half
    packed = jnp.concatenate([first[:half], second[:half]], axis=0)
    row = lax.broadcasted_iota(jnp.int32, (width, width), 0)
    col = lax.broadcasted_iota(jnp.int32, (width, width), 1)
    diagonal = jnp.broadcast_to(first[half : half + 1], (width, width))
    vectors = jnp.where(row <= col, packed, 0.0)
    factors = jnp.where(row > col, packed, jnp.where(row == col, diagonal, 0.0))
    return halves(vectors), halves(factors)


def by_core(core, mine, there):
    odd = core == 1
    return jnp.where(odd, there, mine), jnp.where(odd, mine, there)


def place(me):
    return (me >> 1) & 3


def by_place(me, parts, wanted):
    source = place(me) ^ wanted
    out = parts[0]
    for r in range(1, 4):
        out = jnp.where(source == r, parts[r], out)
    return out


def tree_node(low, high, reflector):
    vectors, factors = reflector
    node = by_transpose(halves(low + plain(halves(high), vectors)), factors)
    return low - node, high - by_transpose(halves(node), vectors)


def leaf_kernel(me_ref, *refs, first, start, stop):
    if first:
        trailing_hbm, vectors_hbm, factors_hbm, own_hbm, away_hbm, updated_hbm, combined_hbm = refs[:7]
    else:
        trailing_hbm, vectors_hbm, combined_hbm, inverse_hbm, _, own_hbm, away_hbm, updated_hbm, basis_hbm = refs[:9]
    scratch = refs[7 if first else 9 :]
    own_ref, away_ref, part_ref, vectors_ref, combined_ref, rest_ref, head_ref, spare_ref, in_sems, out_sems = scratch
    rows, width = vectors_ref.shape
    half = width // 2
    core = me_ref[0] % 2
    mine = pl.ds(pl.multiple_of(core * half, half), half)
    other = pl.ds(pl.multiple_of((1 - core) * half, half), half)
    copies, out_copies = [], []

    def fetch(source, target):
        copies.append(pltpu.make_async_copy(source, target, in_sems.at[len(copies)]))
        copies[-1].start()
        return copies[-1]

    def put(source, target):
        out_copies.append(pltpu.make_async_copy(source, target, out_sems.at[len(out_copies)]))
        out_copies[-1].start()

    def fetch_part(b, slot):
        cuts = [slice(c, c + width) for c in range(0, rows, width)]
        return [fetch(trailing_hbm.at[c, pl.ds(b * width, width)], part_ref.at[slot, c]) for c in cuts]

    def hand_over(value_ref, slot):
        rows_b = slice(slot * half, (slot + 1) * half)
        own_ref[rows_b] = value_ref[mine]
        away_ref[rows_b] = value_ref[other]
        put(away_ref.at[rows_b], away_hbm.at[rows_b])
        put(own_ref.at[rows_b], own_hbm.at[rows_b])

    vectors_copy = fetch(vectors_hbm, vectors_ref)
    if first:
        other_copy = fetch(factors_hbm, spare_ref.at[0])
    else:
        other_copy = fetch(combined_hbm, combined_ref)
    parts = [fetch_part(b, b - start) for b in range(start, stop)]
    if not first:
        panel_copy = fetch_part(0, stop - start)
        basis_copies = [
            fetch(inverse_hbm, spare_ref.at[0]),
            fetch(updated_hbm.at[pl.ds(width, width), pl.ds(0, width)], spare_ref.at[1]),
        ]
    vectors_copy.wait()
    across = halves(vectors_ref[...].T)
    other_copy.wait()
    if first:
        combined_ref[...] = by_transpose(halves(vectors_ref[...]), halves(spare_ref[0]))
        put(combined_ref, combined_hbm)
    combined = halves(combined_ref[...])
    for slot in range(stop - start):
        for copy in parts[slot]:
            copy.wait()
        part = part_ref[slot]
        out = part - plain(combined, halves(plain(across, halves(part))))
        rest_ref[slot] = out[width:]
        head_ref[slot] = out[:width].T
        hand_over(head_ref.at[slot], slot)
        columns = pl.ds((start + slot) * width, width)
        put(rest_ref.at[slot], updated_hbm.at[pl.ds(width, width), columns])
    if not first:
        for copy in panel_copy:
            copy.wait()
        panel = part_ref[stop - start]
        head_ref[stop - start] = plain(halves(panel.T), halves(panel))
        hand_over(head_ref.at[stop - start], stop - start)
        for copy in basis_copies:
            copy.wait()
        spare_ref[2] = plain(halves(spare_ref[1]), halves(spare_ref[0]))
        put(spare_ref.at[2], basis_hbm.at[pl.ds(width, width)])
    for copy in out_copies:
        copy.wait()


def core_kernel(
    me_ref, own_ref, first_ref, second_ref, packed_ref, *refs
):
    sends, dones, (low_ref, high_ref) = refs[:4], refs[4:8], refs[8:]
    me = me_ref[0]
    width = own_ref.shape[1]
    half = width // 2
    quarter = half // 4
    count = own_ref.shape[0] // half - 1
    odd = me % 2 == 1
    there = jnp.concatenate([first_ref[...], second_ref[...]], axis=0)
    gram = own_ref[count * half :] + there[count * half :]
    mine, there = own_ref[: count * half], there[: count * half]
    low = jnp.where(odd, there, mine)
    high = jnp.where(odd, mine, there)
    low, high = tree_node(low, high, unpack(packed_ref[0], packed_ref[1]))
    low_ref[: count * half] = low
    low_ref[count * half :] = gram
    high_ref[...] = high
    for r in range(4):
        start = (place(me) ^ r) * quarter
        for b in range(count + 1):
            source = pl.ds(pl.multiple_of(b * half + start, quarter), quarter)
            target = slice(b * quarter, (b + 1) * quarter)
            sends[r][target] = low_ref[source]
            if b < count:
                dones[r][target] = high_ref[source]


def gather_kernel(me_ref, *refs):
    parts, owns, (stack_ref, held_ref, own_ref, sems) = refs[:4], refs[4:6], refs[6:]
    cut = owns[0].shape[0]
    copies = [
        pltpu.make_async_copy(owns[0], own_ref.at[:cut], sems.at[0]),
        pltpu.make_async_copy(owns[1], own_ref.at[cut:], sems.at[1]),
    ]
    for copy in copies:
        copy.start()
    for r in range(1, 4):
        stack_ref[r - 1] = parts[r][...]
    held_ref[...] = by_place(me_ref[0], [ref[...] for ref in parts], 0)
    for copy in copies:
        copy.wait()


def plane_kernel(
    me_ref, *refs, level
):
    gots, (packed_ref, stack_ref, stack_there_ref) = refs[:4], refs[4:7]
    head_ref, send_ref, done_ref, held_ref = refs[7:]
    me = me_ref[0]
    core = me % 2
    cols = done_ref.shape[1]
    pairs = [(packed_ref[0], packed_ref[1])]
    pairs += [by_core(core, stack_ref[r], stack_there_ref[r]) for r in range(3)]
    firsts, seconds = [pair[0] for pair in pairs], [pair[1] for pair in pairs]
    pairs = [(by_place(me, firsts, j), by_place(me, seconds, j)) for j in range(4)]
    held_ref[0], held_ref[1] = pairs[0]
    reflectors = [unpack(*pair) for pair in pairs]
    parts = [ref[:cols] for ref in gots]
    heads = [by_place(me, parts, j) for j in range(4)]
    gram = gots[0][cols:] + gots[1][cols:] + (gots[2][cols:] + gots[3][cols:])
    heads[0], heads[1] = tree_node(heads[0], heads[1], reflectors[1])
    heads[2], heads[3] = tree_node(heads[2], heads[3], reflectors[3])
    heads[0], heads[2] = tree_node(heads[0], heads[2], reflectors[2])
    for j in range(4):
        done_ref[j] = heads[j]
    head_ref[...] = heads[0]
    upper = (me >> level) % 2 == 1
    send_ref[:cols] = jnp.where(upper, plain(halves(heads[0]), reflectors[0][0]), heads[0])
    send_ref[cols:] = gram


def line_node(me, head, result, mine, there, held, part_ref, part_there_ref, level):
    cols = head.shape[0]
    upper = (me >> level) % 2 == 1
    others = by_core(me % 2, part_ref[...], part_there_ref[...])
    node = [jnp.where(upper, a, b) for a, b in zip(held, others)]
    following = [jnp.where(upper, b, a) for a, b in zip(held, others)]
    coeffs = by_transpose(halves(mine[:cols] + there[:cols]), unpack(*node)[1])
    low = jnp.where(upper, there[:cols], head) - coeffs
    plane = me >> 3
    below = (1 << (level - 2)) - 1
    second = (plane & below) == (1 << (level - 3))
    high = head - by_transpose(halves(coeffs), unpack(*held)[0])
    result = jnp.where(second, high, result)
    return low, result, mine[cols:] + there[cols:], following


def line_kernel(me_ref, *refs, level, cut):
    head_ref, result_ref, mine_ref, there_ref, held_ref, part_ref, part_there_ref, head_out, result_out, held_out = refs[:10]
    sends = refs[10:]
    me = me_ref[0]
    held = held_ref[0], held_ref[1]
    low, result, gram, following = line_node(
        me, head_ref[...], result_ref[...], mine_ref[...], there_ref[...], held, part_ref, part_there_ref, level
    )
    cols, quarter = low.shape[0], gram.shape[0]
    ahead = (me >> (level + 1)) % 2 == 1
    head_out[...] = low
    result_out[...] = result
    held_out[0], held_out[1] = following
    value = jnp.where(ahead, plain(halves(low), unpack(*following)[0]), low)
    if cut:
        sends[0][:quarter] = value[:quarter]
        sends[0][quarter:] = gram
        sends[1][...] = value[quarter:]
    else:
        sends[0][:cols] = value
        sends[0][cols:] = gram


def last_kernel(me_ref, *refs, level, cut):
    head_ref, result_ref, held_ref, part_ref, part_there_ref, done_ref = refs[:6]
    number = 2 if cut else 1
    mines, theres = refs[6 : 6 + number], refs[6 + number : 6 + 2 * number]
    sends, all_ref = refs[6 + 2 * number : 10 + 2 * number], refs[10 + 2 * number]
    me = me_ref[0]
    cols = head_ref.shape[0]
    quarter = sends[0].shape[0] - cols
    quarter = quarter // 2
    values = []
    for parts in (mines, theres):
        if cut:
            values.append(jnp.concatenate([parts[0][:quarter], parts[1][...], parts[0][quarter:]], axis=0))
        else:
            values.append(parts[0][...])
    held = held_ref[0], held_ref[1]
    low, result, gram, _ = line_node(
        me, head_ref[...], result_ref[...], values[0], values[1], held, part_ref, part_there_ref, level
    )
    all_ref[0] = jnp.where((me >> 3) == 0, low, result)
    for j in range(1, 4):
        all_ref[j] = done_ref[j]
    for r in range(4):
        sends[r][:cols] = all_ref[place(me) ^ r]
        sends[r][cols : cols + quarter] = low[:quarter]
        sends[r][cols + quarter :] = gram


def pass_kernel(me_ref, *refs):
    backs, dones, out_ref = refs[:4], refs[4:8], refs[8]
    odd = me_ref[0] % 2 == 1
    cols = dones[0].shape[0]
    for r in range(4):
        out_ref[r, :cols] = jnp.where(odd, backs[r][:cols], dones[r][...])
        out_ref[r, cols:] = backs[r][cols:]


def near_kernel(me_ref, *refs):
    backs, dones, (_, updated_hbm, out_ref, sems) = refs[:4], refs[4:8], refs[8:]
    count, width, half = out_ref.shape
    quarter = half // 4
    me = me_ref[0]
    core = me % 2
    odd = core == 1
    copies = []
    for b in range(count):
        rows = slice(b * quarter, (b + 1) * quarter)
        pieces = [jnp.where(odd, dones[r][rows], backs[r][rows]) for r in range(4)]
        out_ref[b] = jnp.concatenate([by_place(me, pieces, j) for j in range(4)], axis=0).T
        columns = pl.ds(pl.multiple_of(b * width + core * half, half), half)
        copies.append(pltpu.make_async_copy(out_ref.at[b], updated_hbm.at[pl.ds(0, width), columns], sems.at[b]))
        copies[-1].start()
    for copy in copies:
        copy.wait()


def far_kernel(me_ref, *refs, total):
    backs, dones = refs[:4], refs[4:8]
    there_ref, inverse_ref, _, _, updated_hbm, basis_hbm, gram_ref = refs[8:15]
    panel_ref, sum_ref, out_ref, basis_ref, sems = refs[15:]
    count, width, half = out_ref.shape
    quarter = half // 4
    cols = count * quarter
    me = me_ref[0]
    core = me % 2
    odd = core == 1
    copies = []

    def put(source, target):
        copies.append(pltpu.make_async_copy(source, target, sems.at[len(copies)]))
        copies[-1].start()

    for b in range(count):
        rows = slice(b * quarter, (b + 1) * quarter)
        pieces = [there_ref[r, rows] for r in range(4)]
        far = jnp.concatenate([by_place(me, pieces, j) for j in range(4)], axis=0).T
        out_ref[b] = far
        columns = pl.ds(pl.multiple_of(b * width + (1 - core) * half, half), half)
        put(out_ref.at[b], updated_hbm.at[pl.ds(0, width), columns])
        if b == 0:
            pieces = [jnp.where(odd, dones[r][rows], backs[r][rows]) for r in range(4)]
            near = jnp.concatenate([by_place(me, pieces, j) for j in range(4)], axis=0).T
            head = jnp.concatenate(by_core(core, near, far), axis=1)
            basis = plain(halves(head), halves(inverse_ref[...]))
            basis_ref[...] = jnp.where(me == 0, 0.0, basis)
            put(basis_ref, basis_hbm.at[pl.ds(0, width)])

    def target(part, r):
        return pl.ds(pl.multiple_of(part * half + (place(me) ^ r) * quarter, quarter), quarter)

    for r in range(4):
        panel_ref[target(core, r)] = backs[r][cols : cols + quarter]
        sum_ref[target(core, r)] = backs[r][cols + quarter :]
        panel_ref[target(1 - core, r)] = there_ref[r, cols : cols + quarter]
        sum_ref[target(1 - core, r)] = there_ref[r, cols + quarter :]
    panel = halves(panel_ref[...])
    gram_ref[...] = (sum_ref[...] - by_transpose(panel, panel)) / total
    for copy in copies:
        copy.wait()


def after(value, *others):
    return lax.optimization_barrier((value, *others))[0]


def body(trailing, leaf_vectors, leaf_factors, tree_vectors, tree_factors, inverse_factor):
    rows, columns = trailing.shape
    width = leaf_vectors.shape[1]
    half = width // 2
    quarter = half // 4
    count = columns // width
    devices = lax.axis_size("rows")
    levels = devices.bit_length() - 1
    me = lax.axis_index("rows").astype(jnp.int32)
    me_array = me.reshape(1)
    chunks = ((0, count // 2), (count // 2, count))
    part_shape = (half + EXTRA, width)
    latest = [me_array]

    def exchange(value, shift):
        return lax.ppermute(value, "rows", [(i, i ^ shift) for i in range(devices)])

    def around(values):
        there = [exchange(values[r], 2 * r) for r in (3, 1, 2)]
        return [values[0], there[1], there[2], there[0]]

    def shape(*dims):
        return jax.ShapeDtypeStruct(dims, F32)

    def vmem(*dims):
        return pltpu.VMEM(dims, F32)

    def sems(number):
        return pltpu.SemaphoreType.DMA((number,))

    def call(kernel, operands, outs, scratch=(), away_in=(), away_out=(), params=PARAMS, aliases=()):
        values = pl.pallas_call(
            kernel,
            out_shape=tuple(outs),
            in_specs=[SCALAR] + [AWAY if i in away_in else WHOLE for i in range(len(operands))],
            out_specs=tuple(AWAY if i in away_out else WHOLE for i in range(len(outs))),
            scratch_shapes=list(scratch),
            input_output_aliases=dict(aliases),
            compiler_params=params,
            cost_estimate=pl.CostEstimate(flops=1, bytes_accessed=1, transcendentals=0),
        )(after(me_array, latest[0]), *operands)
        latest[0] = values[0]
        return values

    def leaf(first, start, stop, operands, outs, aliases):
        blocks = stop - start
        more = 0 if first else 1
        outs = [shape((blocks + more) * half, width)] * 2 + outs
        scratch = [
            vmem((blocks + more) * half, width),
            vmem((blocks + more) * half, width),
            vmem(blocks + more, rows, width),
            vmem(rows, width),
            vmem(rows, width),
            vmem(blocks, width, width),
            vmem(blocks + more, width, width),
            vmem(3, width, width),
            sems((blocks + more) * (rows // width) + 4),
            sems(3 * blocks + 3),
        ]
        return call(
            functools.partial(leaf_kernel, first=first, start=start, stop=stop),
            operands, outs, scratch, range(len(operands)), range(len(outs)), room(61), aliases,
        )

    raw = [exchange(tree_vectors, 1), exchange(tree_factors, 1)]
    own_a, away_a, updated, combined = leaf(
        True, *chunks[0], (trailing, leaf_vectors, leaf_factors),
        [shape(rows, columns), shape(rows, width)], (),
    )
    there_a = exchange(away_a, 1)

    chip_low, chip_high, chip_part = call(
        pack_kernel, (tree_vectors, tree_factors, *raw),
        (shape(2, *part_shape), shape(2, *part_shape), shape(*part_shape)),
        [vmem(4, width, width), sems(4)], range(4), (), PARAMS,
    )
    plane_parts = [exchange(chip_part, 2 * r) for r in (3, 1, 2)]
    plane_parts = [plane_parts[1], plane_parts[2], plane_parts[0]]

    own_b, away_b, updated, basis = leaf(
        False, *chunks[1], (trailing, leaf_vectors, combined, inverse_factor, updated),
        [shape(rows, columns), shape(rows, width)], {5: 2},
    )
    plane_parts = [after(part, own_b) for part in plane_parts]
    there_b = exchange(after(away_b, *plane_parts), 1)
    stack, held_part, own = call(
        gather_kernel, (chip_part, *plane_parts, own_a, own_b),
        (shape(3, *part_shape), shape(*part_shape), shape(count * half + half, width)),
        [sems(2)], (4, 5),
    )
    stack_there = exchange(stack, 1)
    cols = count * quarter
    outs = call(
        core_kernel, (own, there_a, there_b, chip_high),
        [shape(cols + quarter, width)] * 4 + [shape(cols, width)] * 4,
        [vmem(count * half + half, width), vmem(count * half, width)],
    )
    sends, dones = outs[:4], outs[4:]
    gots = around(sends)

    def upper(level):
        return (me >> level) % 2 == 1

    def direct(shift):
        return lax.ppermute(held_part, "rows", [(i, i ^ shift) for i in range(devices) if (i >> 3) % 4 == 2])

    parts = [exchange(held_part, 8)]
    if levels == 5:
        parts += [direct(16), direct(24)]
    else:
        held = held_part
        for level in range(4, levels):
            held = jnp.where(upper(level - 1), parts[-1], held)
            parts.append(exchange(held, 1 << level))

    head, send, plane_done, held = call(
        functools.partial(plane_kernel, level=3), (*gots, chip_low, stack, stack_there),
        (shape(cols, width), shape(cols + quarter, width), shape(4, cols, width), shape(2, *part_shape)),
    )
    result = head
    mines, theres = [send], [exchange(send, 8)]
    for level in range(3, levels):
        part = after(parts[level - 3], head)
        if level == 4 and levels == 5:
            part = jnp.where(upper(3), after(parts[2], head), part)
        part_there = exchange(part, 1)
        if level == levels - 1:
            sends = call(
                functools.partial(last_kernel, level=level, cut=len(mines) == 2),
                (head, result, held, part, part_there, plane_done, *mines, *theres),
                [shape(cols + 2 * quarter, width)] * 4, [vmem(4, cols, width)],
            )
        else:
            cut = level + 1 == levels - 1
            outs = [shape(2 * quarter, width), shape(cols - quarter, width)] if cut else [shape(cols + quarter, width)]
            head, result, held, *outs = call(
                functools.partial(line_kernel, level=level, cut=cut),
                (head, result, mines[0], theres[0], held, part, part_there),
                [shape(cols, width), shape(cols, width), shape(*held.shape)] + outs,
            )
            mines, theres = outs, [exchange(outs[0], 2 << level)]
            if cut:
                ends = [i for i in range(devices) if (i >> 3) % (1 << (level - 2)) == 0]
                theres.append(lax.ppermute(outs[1], "rows", [(i, i ^ (2 << level)) for i in ends]))

    backs = around(sends)
    (back,) = call(pass_kernel, (*backs, *dones), (shape(4, cols + 2 * quarter, width),))
    there = exchange(back, 1)
    (updated,) = call(
        near_kernel, (*backs, *dones, updated), (shape(rows, columns),),
        [vmem(count, width, half), sems(count)], (8,), (0,), PARAMS, {9: 0},
    )
    return call(
        functools.partial(far_kernel, total=float(rows * devices)),
        (*backs, *dones, there, inverse_factor, updated, basis),
        (shape(rows, columns), shape(rows, width), shape(width, width)),
        [vmem(width, width), vmem(width, width), vmem(count, width, half), vmem(width, width), sems(count + 1)],
        (10, 11), (0, 1), PARAMS, {11: 0, 12: 1},
    )


def solution(mesh):
    in_specs = (
        P("rows", None),
        P("rows", None),
        P("rows", None),
        P("rows", None),
        P("rows", None),
        P(),
    )
    out_specs = (P("rows", None), P("rows", None), P())
    return jax.shard_map(body, mesh=mesh, in_specs=in_specs, out_specs=out_specs, check_vma=False)
```

```python
import functools
import jax
import jax.numpy as jnp
from jax import lax
from jax.experimental import pallas as pl
from jax.experimental.pallas import tpu as pltpu
from jax.sharding import PartitionSpec as P

F32 = jnp.float32
BF16 = jnp.bfloat16
EXTRA = 8
PARAMS = pltpu.CompilerParams(vmem_limit_bytes=40 * 1024 * 1024)
WHOLE = pl.BlockSpec(memory_space=pltpu.VMEM)
SCALAR = pl.BlockSpec(memory_space=pltpu.SMEM)
AWAY = pl.BlockSpec(memory_space=pltpu.HBM)


def halves(value):
    high = value.astype(BF16)
    return high, (value - high.astype(F32)).astype(BF16)


def times(left, right, sides):
    first = jnp.concatenate([left[0], left[0], left[1]], axis=sides[0])
    second = jnp.concatenate([right[0], right[1], right[0]], axis=sides[1])
    dims = ((sides[:1], sides[1:]), ((), ()))
    return lax.dot_general(first, second, dims, preferred_element_type=F32)


def plain(left, right):
    return times(left, right, (1, 0))


def by_transpose(left, right):
    return times(left, right, (1, 1))


def pack_kernel(me_ref, *refs):
    sources, (low_ref, high_ref, part_ref), (buffer_ref, sems) = refs[:4], refs[4:7], refs[7:]
    copies = [pltpu.make_async_copy(source, buffer_ref.at[i], sems.at[i]) for i, source in enumerate(sources)]
    for copy in copies:
        copy.start()
    for copy in copies:
        copy.wait()
    core = me_ref[0] % 2
    width = buffer_ref.shape[1]
    half = width // 2
    row = lax.broadcasted_iota(jnp.int32, (width, width), 0)
    col = lax.broadcasted_iota(jnp.int32, (width, width), 1)
    both_vectors = by_core(core, buffer_ref[0], buffer_ref[2])
    both_factors = by_core(core, buffer_ref[1], buffer_ref[3])
    for vectors, factors, out_ref in zip(both_vectors, both_factors, (low_ref, high_ref)):
        packed = jnp.where(row > col, factors.T, vectors)
        diagonal = jnp.sum(jnp.where(row == col, factors, 0.0), axis=0, keepdims=True)
        for part in range(2):
            out_ref[part, :half] = packed[part * half : (part + 1) * half]
            out_ref[part, half:] = jnp.broadcast_to(diagonal, (EXTRA, width))
    part_ref[...] = low_ref[core]


def unpack(first, second):
    half = first.shape[0] - EXTRA
    width = 2 * half
    packed = jnp.concatenate([first[:half], second[:half]], axis=0)
    row = lax.broadcasted_iota(jnp.int32, (width, width), 0)
    col = lax.broadcasted_iota(jnp.int32, (width, width), 1)
    diagonal = jnp.broadcast_to(first[half : half + 1], (width, width))
    vectors = jnp.where(row <= col, packed, 0.0)
    factors = jnp.where(row > col, packed, jnp.where(row == col, diagonal, 0.0))
    return halves(vectors), halves(factors)


def by_core(core, mine, there):
    odd = core == 1
    return jnp.where(odd, there, mine), jnp.where(odd, mine, there)


def place(me):
    return (me >> 1) & 3


def by_place(me, parts, wanted):
    source = place(me) ^ wanted
    out = parts[0]
    for r in range(1, 4):
        out = jnp.where(source == r, parts[r], out)
    return out


def tree_node(low, high, reflector):
    vectors, factors = reflector
    node = by_transpose(halves(low + plain(halves(high), vectors)), factors)
    return low - node, high - by_transpose(halves(node), vectors)


def leaf_first_kernel(
    me_ref, trailing_hbm, vectors_hbm, factors_hbm, inverse_hbm,
    own_ref, away_one, away_two, rest_ref, later_ref, inverse_ref, across_ref, combined_ref,
    part_ref, vectors_ref, factors_ref, value_ref, away_ref, sems,
):
    count, rows, width = part_ref.shape
    copies = []

    def fetch(source, target):
        copies.append(pltpu.make_async_copy(source, target, sems.at[len(copies)]))
        copies[-1].start()
        return copies[-1]

    def fetch_part(b, target):
        cuts = [slice(c, c + width) for c in range(0, rows, width)]
        return [fetch(trailing_hbm.at[c, pl.ds(b * width, width)], target.at[c]) for c in cuts]

    first = [fetch(vectors_hbm, vectors_ref), fetch(factors_hbm, factors_ref)]
    parts = [fetch_part(b, part_ref.at[b]) for b in range(count)]
    last = [fetch_part(count + b, later_ref.at[b]) for b in range(later_ref.shape[0])]
    last.append([fetch(inverse_hbm, inverse_ref)])
    for copy in first:
        copy.wait()
    vectors = vectors_ref[...]
    across = halves(vectors.T)
    across_ref[0], across_ref[1] = across
    combined = halves(by_transpose(halves(vectors), halves(factors_ref[...])))
    combined_ref[0], combined_ref[1] = combined
    for b in range(count):
        for copy in parts[b]:
            copy.wait()
        leaf_block(me_ref, part_ref[b], across, combined, value_ref, rest_ref.at[b], own_ref, away_ref, b)
    panel = part_ref[0]
    value_ref[...] = plain(halves(panel.T), halves(panel))
    hand_over(me_ref, value_ref, own_ref, away_ref, count)
    cut = away_one.shape[0]
    away_one[...] = away_ref[:cut]
    away_two[...] = away_ref[cut:]
    for group in last:
        for copy in group:
            copy.wait()


def hand_over(me_ref, value_ref, own_ref, away_ref, slot):
    half = value_ref.shape[0] // 2
    core = me_ref[0] % 2
    target = slice(slot * half, (slot + 1) * half)
    own_ref[target] = value_ref[pl.ds(pl.multiple_of(core * half, half), half)]
    away_ref[target] = value_ref[pl.ds(pl.multiple_of((1 - core) * half, half), half)]


def leaf_block(me_ref, part, across, combined, value_ref, rest_ref, own_ref, away_ref, slot):
    width = value_ref.shape[0]
    out = part - plain(combined, halves(plain(across, halves(part))))
    rest_ref[...] = out[width:]
    value_ref[...] = out[:width].T
    hand_over(me_ref, value_ref, own_ref, away_ref, slot)


def leaf_second_kernel(me_ref, later_ref, across_ref, combined_ref, own_ref, rest_ref, *refs):
    aways, value_ref = refs[:-1], refs[-1]
    half = value_ref.shape[0] // 2
    across = across_ref[0], across_ref[1]
    combined = combined_ref[0], combined_ref[1]
    for b in range(later_ref.shape[0]):
        own_b = own_ref.at[pl.ds(b * half, half)]
        leaf_block(me_ref, later_ref[b], across, combined, value_ref, rest_ref.at[b], own_b, aways[b], 0)


def store_kernel(me_ref, first_ref, second_ref, inverse_ref, mark_ref, updated_hbm, basis_hbm, basis_ref, sems):
    count, width = first_ref.shape[:2]
    copies = []
    for b in range(count + second_ref.shape[0]):
        source = first_ref.at[b] if b < count else second_ref.at[b - count]
        target = updated_hbm.at[pl.ds(width, width), pl.ds(b * width, width)]
        copies.append(pltpu.make_async_copy(source, target, sems.at[b]))
        copies[-1].start()
    basis_ref[...] = plain(halves(first_ref[0]), halves(inverse_ref[...]))
    copies.append(pltpu.make_async_copy(basis_ref, basis_hbm.at[pl.ds(width, width)], sems.at[len(copies)]))
    mark_ref[...] = jnp.zeros_like(mark_ref)
    copies[-1].start()
    for copy in copies:
        copy.wait()


def core_kernel(
    me_ref, own_a_ref, own_b_ref, one_ref, two_ref, *refs
):
    more = len(refs) - 17
    there_bs, packed_ref, parts = refs[:more], refs[more], refs[more + 1 : more + 5]
    sends, dones, (stack_ref, held_ref, low_ref, high_ref) = refs[more + 5 : more + 9], refs[more + 9 : more + 13], refs[more + 13 :]
    for r in range(1, 4):
        stack_ref[r - 1] = parts[r][...]
    held_ref[...] = by_place(me_ref[0], [ref[...] for ref in parts], 0)
    me = me_ref[0]
    width = own_a_ref.shape[1]
    half = width // 2
    quarter = half // 4
    cut = own_a_ref.shape[0] - half
    count = cut // half + len(there_bs)
    odd = me % 2 == 1
    there_a = jnp.concatenate([one_ref[...], two_ref[...]], axis=0)
    gram = own_a_ref[cut:] + there_a[cut:]
    mine = jnp.concatenate([own_a_ref[:cut], own_b_ref[...]], axis=0)
    there = jnp.concatenate([there_a[:cut]] + [ref[...] for ref in there_bs], axis=0)
    low = jnp.where(odd, there, mine)
    high = jnp.where(odd, mine, there)
    low, high = tree_node(low, high, unpack(packed_ref[0], packed_ref[1]))
    low_ref[: count * half] = low
    low_ref[count * half :] = gram
    high_ref[...] = high
    for r in range(4):
        start = (place(me) ^ r) * quarter
        for b in range(count + 1):
            source = pl.ds(pl.multiple_of(b * half + start, quarter), quarter)
            target = slice(b * quarter, (b + 1) * quarter)
            sends[r][target] = low_ref[source]
            if b < count:
                dones[r][target] = high_ref[source]


def plane_kernel(
    me_ref, *refs, level
):
    gots, (packed_ref, stack_ref, stack_there_ref) = refs[:4], refs[4:7]
    head_ref, send_ref, done_ref, held_ref = refs[7:]
    me = me_ref[0]
    core = me % 2
    cols = done_ref.shape[1]
    pairs = [(packed_ref[0], packed_ref[1])]
    pairs += [by_core(core, stack_ref[r], stack_there_ref[r]) for r in range(3)]
    firsts, seconds = [pair[0] for pair in pairs], [pair[1] for pair in pairs]
    pairs = [(by_place(me, firsts, j), by_place(me, seconds, j)) for j in range(4)]
    held_ref[0], held_ref[1] = pairs[0]
    reflectors = [unpack(*pair) for pair in pairs]
    parts = [ref[:cols] for ref in gots]
    heads = [by_place(me, parts, j) for j in range(4)]
    gram = gots[0][cols:] + gots[1][cols:] + (gots[2][cols:] + gots[3][cols:])
    heads[0], heads[1] = tree_node(heads[0], heads[1], reflectors[1])
    heads[2], heads[3] = tree_node(heads[2], heads[3], reflectors[3])
    heads[0], heads[2] = tree_node(heads[0], heads[2], reflectors[2])
    for j in range(4):
        done_ref[j] = heads[j]
    head_ref[...] = heads[0]
    upper = (me >> level) % 2 == 1
    send_ref[:cols] = jnp.where(upper, plain(halves(heads[0]), reflectors[0][0]), heads[0])
    send_ref[cols:] = gram


def line_node(me, head, result, mine, there, held, part_ref, part_there_ref, level):
    cols = head.shape[0]
    upper = (me >> level) % 2 == 1
    others = by_core(me % 2, part_ref[...], part_there_ref[...])
    node = [jnp.where(upper, a, b) for a, b in zip(held, others)]
    following = [jnp.where(upper, b, a) for a, b in zip(held, others)]
    coeffs = by_transpose(halves(mine[:cols] + there[:cols]), unpack(*node)[1])
    low = jnp.where(upper, there[:cols], head) - coeffs
    plane = me >> 3
    below = (1 << (level - 2)) - 1
    second = (plane & below) == (1 << (level - 3))
    high = head - by_transpose(halves(coeffs), unpack(*held)[0])
    result = jnp.where(second, high, result)
    return low, result, mine[cols:] + there[cols:], following


def line_kernel(me_ref, *refs, level, cut):
    head_ref, result_ref, mine_ref, there_ref, held_ref, part_ref, part_there_ref, head_out, result_out, held_out = refs[:10]
    sends = refs[10:]
    me = me_ref[0]
    held = held_ref[0], held_ref[1]
    low, result, gram, following = line_node(
        me, head_ref[...], result_ref[...], mine_ref[...], there_ref[...], held, part_ref, part_there_ref, level
    )
    cols, quarter = low.shape[0], gram.shape[0]
    ahead = (me >> (level + 1)) % 2 == 1
    head_out[...] = low
    result_out[...] = result
    held_out[0], held_out[1] = following
    value = jnp.where(ahead, plain(halves(low), unpack(*following)[0]), low)
    if cut:
        sends[0][:quarter] = value[:quarter]
        sends[0][quarter:] = gram
        sends[1][...] = value[quarter:]
    else:
        sends[0][:cols] = value
        sends[0][cols:] = gram


def last_kernel(me_ref, *refs, level, cut):
    head_ref, result_ref, held_ref, part_ref, part_there_ref, done_ref = refs[:6]
    number = 2 if cut else 1
    mines, theres = refs[6 : 6 + number], refs[6 + number : 6 + 2 * number]
    sends, all_ref = refs[6 + 2 * number : 10 + 2 * number], refs[10 + 2 * number]
    me = me_ref[0]
    cols = head_ref.shape[0]
    quarter = sends[0].shape[0] - cols
    quarter = quarter // 2
    values = []
    for parts in (mines, theres):
        if cut:
            values.append(jnp.concatenate([parts[0][:quarter], parts[1][...], parts[0][quarter:]], axis=0))
        else:
            values.append(parts[0][...])
    held = held_ref[0], held_ref[1]
    low, result, gram, _ = line_node(
        me, head_ref[...], result_ref[...], values[0], values[1], held, part_ref, part_there_ref, level
    )
    all_ref[0] = jnp.where((me >> 3) == 0, low, result)
    for j in range(1, 4):
        all_ref[j] = done_ref[j]
    for r in range(4):
        sends[r][:cols] = all_ref[place(me) ^ r]
        sends[r][cols : cols + quarter] = low[:quarter]
        sends[r][cols + quarter :] = gram


def pass_kernel(me_ref, *refs):
    backs, dones, out_ref = refs[:4], refs[4:8], refs[8]
    odd = me_ref[0] % 2 == 1
    cols = dones[0].shape[0]
    for r in range(4):
        out_ref[r, :cols] = jnp.where(odd, backs[r][:cols], dones[r][...])
        out_ref[r, cols:] = backs[r][cols:]


def near_kernel(me_ref, *refs):
    backs, dones, (_, updated_hbm, out_ref, sems) = refs[:4], refs[4:8], refs[8:]
    count, width, half = out_ref.shape
    quarter = half // 4
    me = me_ref[0]
    core = me % 2
    odd = core == 1
    copies = []
    for b in range(count):
        rows = slice(b * quarter, (b + 1) * quarter)
        pieces = [jnp.where(odd, dones[r][rows], backs[r][rows]) for r in range(4)]
        out_ref[b] = jnp.concatenate([by_place(me, pieces, j) for j in range(4)], axis=0).T
        columns = pl.ds(pl.multiple_of(b * width + core * half, half), half)
        copies.append(pltpu.make_async_copy(out_ref.at[b], updated_hbm.at[pl.ds(0, width), columns], sems.at[b]))
        copies[-1].start()
    for copy in copies:
        copy.wait()


def far_kernel(me_ref, *refs, total):
    backs, dones = refs[:4], refs[4:8]
    there_ref, inverse_ref, _, _, updated_hbm, basis_hbm, gram_hbm = refs[8:15]
    panel_ref, sum_ref, out_ref, basis_ref, gram_ref, sems = refs[15:]
    count, width, half = out_ref.shape
    quarter = half // 4
    cols = count * quarter
    me = me_ref[0]
    core = me % 2
    odd = core == 1
    copies = []

    def put(source, target):
        copies.append(pltpu.make_async_copy(source, target, sems.at[len(copies)]))
        copies[-1].start()

    for b in range(count):
        rows = slice(b * quarter, (b + 1) * quarter)
        pieces = [there_ref[r, rows] for r in range(4)]
        far = jnp.concatenate([by_place(me, pieces, j) for j in range(4)], axis=0).T
        out_ref[b] = far
        columns = pl.ds(pl.multiple_of(b * width + (1 - core) * half, half), half)
        put(out_ref.at[b], updated_hbm.at[pl.ds(0, width), columns])
        if b == 0:
            pieces = [jnp.where(odd, dones[r][rows], backs[r][rows]) for r in range(4)]
            near = jnp.concatenate([by_place(me, pieces, j) for j in range(4)], axis=0).T
            head = jnp.concatenate(by_core(core, near, far), axis=1)
            basis = plain(halves(head), halves(inverse_ref[...]))
            basis_ref[...] = jnp.where(me == 0, 0.0, basis)
            put(basis_ref, basis_hbm.at[pl.ds(0, width)])

    def target(part, r):
        return pl.ds(pl.multiple_of(part * half + (place(me) ^ r) * quarter, quarter), quarter)

    for r in range(4):
        panel_ref[target(core, r)] = backs[r][cols : cols + quarter]
        sum_ref[target(core, r)] = backs[r][cols + quarter :]
        panel_ref[target(1 - core, r)] = there_ref[r, cols : cols + quarter]
        sum_ref[target(1 - core, r)] = there_ref[r, cols + quarter :]
    panel = halves(panel_ref[...])
    gram_ref[...] = (sum_ref[...] - by_transpose(panel, panel)) / total
    put(gram_ref, gram_hbm)
    for copy in copies:
        copy.wait()


def body(trailing, leaf_vectors, leaf_factors, tree_vectors, tree_factors, inverse_factor):
    rows, columns = trailing.shape
    width = leaf_vectors.shape[1]
    half = width // 2
    quarter = half // 4
    count = columns // width
    devices = lax.axis_size("rows")
    levels = devices.bit_length() - 1
    me = lax.axis_index("rows").astype(jnp.int32)
    me_array = me.reshape(1)
    part_shape = (half + EXTRA, width)
    latest = []

    def exchange(value, shift):
        return lax.ppermute(value, "rows", [(i, i ^ shift) for i in range(devices)])

    def around(values):
        there = [exchange(values[r], 2 * r) for r in (3, 1, 2)]
        return [values[0], there[1], there[2], there[0]]

    def shape(*dims):
        return jax.ShapeDtypeStruct(dims, F32)

    def vmem(*dims):
        return pltpu.VMEM(dims, F32)

    def sems(number):
        return pltpu.SemaphoreType.DMA((number,))

    def call(kernel, operands, outs, scratch=(), away_in=(), away_out=(), aliases=(), before=()):
        number = len(operands)
        operands = [pltpu.with_memory_space_constraint(x, pltpu.HBM) if i in away_in else x for i, x in enumerate(operands)]
        outs = [(pltpu.HBM if i in away_out else pltpu.VMEM)(x.shape, x.dtype) for i, x in enumerate(outs)]
        unused = [*latest, *before]

        def kernel_on(*refs):
            kernel(*refs[: number + 1], *refs[number + 1 + len(unused) :])

        values = pl.pallas_call(
            kernel_on,
            out_shape=tuple(outs),
            in_specs=[SCALAR]
            + [AWAY if i in away_in else WHOLE for i in range(number)]
            + [pl.BlockSpec(memory_space=pl.ANY)] * len(unused),
            out_specs=tuple(AWAY if i in away_out else WHOLE for i in range(len(outs))),
            scratch_shapes=list(scratch),
            input_output_aliases=dict(aliases),
            compiler_params=PARAMS,
            cost_estimate=pl.CostEstimate(flops=1, bytes_accessed=1, transcendentals=0),
        )(me_array, *operands, *unused)
        if 0 not in away_out:
            latest[:] = values[:1]
        return values

    raw = [exchange(tree_vectors, 1), exchange(tree_factors, 1)]
    blocks = count // 2
    more = count - blocks
    split = jax.ShapeDtypeStruct((2, width, rows), BF16), jax.ShapeDtypeStruct((2, rows, width), BF16)
    rows_a = blocks * half + half
    own_a, away_one, away_two, rest_a, later, inverse_factor, across, combined = call(
        leaf_first_kernel, (trailing, leaf_vectors, leaf_factors, inverse_factor),
        [shape(rows_a, width), shape(rows_a // 2, width), shape(rows_a // 2, width)]
        + [shape(blocks, width, width), shape(more, rows, width), shape(width, width), *split],
        [
            vmem(blocks, rows, width), vmem(rows, width), vmem(width, width), vmem(width, width), vmem(rows_a, width),
            sems(count * (rows // width) + 3),
        ],
        range(4),
    )
    there_a = [exchange(away_one, 1), exchange(away_two, 1)]

    chip_low, chip_high, chip_part = call(
        pack_kernel, (tree_vectors, tree_factors, *raw),
        (shape(2, *part_shape), shape(2, *part_shape), shape(*part_shape)),
        [vmem(4, width, width), sems(4)], (),
    )
    plane_parts = [exchange(chip_part, 2 * r) for r in (3, 1, 2)]
    plane_parts = [plane_parts[1], plane_parts[2], plane_parts[0]]

    own_b, rest_b, *aways = call(
        leaf_second_kernel, (later, across, combined),
        [shape(more * half, width), shape(more, width, width)] + [shape(half, width)] * more,
        [vmem(width, width)], before=there_a,
    )
    theres = [exchange(away, 1) for away in aways]
    cols = count * quarter
    outs = call(
        core_kernel, (own_a, own_b, *there_a, *theres, chip_high, chip_part, *plane_parts),
        [shape(cols + quarter, width)] * 4 + [shape(cols, width)] * 4 + [shape(3, *part_shape), shape(*part_shape)],
        [vmem(count * half + half, width), vmem(count * half, width)],
    )
    sends, dones, (stack, held_part) = outs[:4], outs[4:8], outs[8:]
    gots = around(sends)
    stack_there = exchange(stack, 1)
    _, updated, basis = call(
        store_kernel, (rest_a, rest_b, inverse_factor), (shape(8, width), shape(rows, columns), shape(rows, width)),
        [vmem(width, width), sems(count + 1)], (), (1, 2),
    )

    def upper(level):
        return (me >> level) % 2 == 1

    def direct(shift):
        return lax.ppermute(held_part, "rows", [(i, i ^ shift) for i in range(devices) if (i >> 3) % 4 == 2])

    parts = [exchange(held_part, 8)]
    if levels == 5:
        parts += [direct(16), direct(24)]
    else:
        held = held_part
        for level in range(4, levels):
            held = jnp.where(upper(level - 1), parts[-1], held)
            parts.append(exchange(held, 1 << level))

    head, send, plane_done, held = call(
        functools.partial(plane_kernel, level=3), (*gots, chip_low, stack, stack_there),
        (shape(cols, width), shape(cols + quarter, width), shape(4, cols, width), shape(2, *part_shape)),
    )
    result = head
    mines, theres = [send], [exchange(send, 8)]
    for level in range(3, levels):
        part = parts[level - 3]
        if level == 4 and levels == 5:
            part = jnp.where(upper(3), parts[2], part)
        part_there = exchange(part, 1)
        if level == levels - 1:
            sends = call(
                functools.partial(last_kernel, level=level, cut=len(mines) == 2),
                (head, result, held, part, part_there, plane_done, *mines, *theres),
                [shape(cols + 2 * quarter, width)] * 4, [vmem(4, cols, width)],
            )
        else:
            cut = level + 1 == levels - 1
            outs = [shape(2 * quarter, width), shape(cols - quarter, width)] if cut else [shape(cols + quarter, width)]
            head, result, held, *outs = call(
                functools.partial(line_kernel, level=level, cut=cut),
                (head, result, mines[0], theres[0], held, part, part_there),
                [shape(cols, width), shape(cols, width), shape(*held.shape)] + outs,
            )
            mines, theres = outs, [exchange(outs[0], 2 << level)]
            if cut:
                ends = [i for i in range(devices) if (i >> 3) % (1 << (level - 2)) == 0]
                theres.append(lax.ppermute(outs[1], "rows", [(i, i ^ (2 << level)) for i in ends]))

    backs = around(sends)
    (back,) = call(pass_kernel, (*backs, *dones), (shape(4, cols + 2 * quarter, width),))
    there = exchange(back, 1)
    (updated,) = call(
        near_kernel, (*backs, *dones, updated), (shape(rows, columns),),
        [vmem(count, width, half), sems(count)], (8,), (0,), {9: 0},
    )
    return call(
        functools.partial(far_kernel, total=float(rows * devices)),
        (*backs, *dones, there, inverse_factor, updated, basis),
        (shape(rows, columns), shape(rows, width), shape(width, width)),
        [vmem(width, width), vmem(width, width), vmem(count, width, half), vmem(width, width), vmem(width, width), sems(count + 2)],
        (10, 11), (0, 1, 2), {11: 0, 12: 1},
    )


def solution(mesh):
    in_specs = (
        P("rows", None),
        P("rows", None),
        P("rows", None),
        P("rows", None),
        P("rows", None),
        P(),
    )
    out_specs = (P("rows", None), P("rows", None), P())
    return jax.shard_map(body, mesh=mesh, in_specs=in_specs, out_specs=out_specs, check_vma=False)
```

```python
import functools
import jax
import jax.numpy as jnp
from jax import lax
from jax.experimental import pallas as pl
from jax.experimental.pallas import tpu as pltpu
from jax.sharding import PartitionSpec as P

F32 = jnp.float32
BF16 = jnp.bfloat16
EXTRA = 8
PARAMS = pltpu.CompilerParams(vmem_limit_bytes=20 * 1024 * 1024)
WHOLE = pl.BlockSpec(memory_space=pltpu.VMEM)
SCALAR = pl.BlockSpec(memory_space=pltpu.SMEM)
AWAY = pl.BlockSpec(memory_space=pltpu.HBM)


def halves(value):
    high = value.astype(BF16)
    return high, (value - high.astype(F32)).astype(BF16)


def times(left, right, sides):
    first = jnp.concatenate([left[0], left[0], left[1]], axis=sides[0])
    second = jnp.concatenate([right[0], right[1], right[0]], axis=sides[1])
    dims = ((sides[:1], sides[1:]), ((), ()))
    return lax.dot_general(first, second, dims, preferred_element_type=F32)


def plain(left, right):
    return times(left, right, (1, 0))


def by_transpose(left, right):
    return times(left, right, (1, 1))


def pack_kernel(me_ref, *refs):
    sources, (low_ref, high_ref, part_ref), (buffer_ref, sems) = refs[:4], refs[4:7], refs[7:]
    copies = [pltpu.make_async_copy(source, buffer_ref.at[i], sems.at[i]) for i, source in enumerate(sources)]
    for copy in copies:
        copy.start()
    for copy in copies:
        copy.wait()
    core = me_ref[0] % 2
    width = buffer_ref.shape[1]
    half = width // 2
    row = lax.broadcasted_iota(jnp.int32, (width, width), 0)
    col = lax.broadcasted_iota(jnp.int32, (width, width), 1)
    both_vectors = by_core(core, buffer_ref[0], buffer_ref[2])
    both_factors = by_core(core, buffer_ref[1], buffer_ref[3])
    for vectors, factors, out_ref in zip(both_vectors, both_factors, (low_ref, high_ref)):
        packed = jnp.where(row > col, factors.T, vectors)
        diagonal = jnp.sum(jnp.where(row == col, factors, 0.0), axis=0, keepdims=True)
        for part in range(2):
            out_ref[part, :half] = packed[part * half : (part + 1) * half]
            out_ref[part, half:] = jnp.broadcast_to(diagonal, (EXTRA, width))
    part_ref[...] = low_ref[core]


def unpack(first, second):
    half = first.shape[0] - EXTRA
    width = 2 * half
    packed = jnp.concatenate([first[:half], second[:half]], axis=0)
    row = lax.broadcasted_iota(jnp.int32, (width, width), 0)
    col = lax.broadcasted_iota(jnp.int32, (width, width), 1)
    diagonal = jnp.broadcast_to(first[half : half + 1], (width, width))
    vectors = jnp.where(row <= col, packed, 0.0)
    factors = jnp.where(row > col, packed, jnp.where(row == col, diagonal, 0.0))
    return halves(vectors), halves(factors)


def by_core(core, mine, there):
    odd = core == 1
    return jnp.where(odd, there, mine), jnp.where(odd, mine, there)


def place(me):
    return (me >> 1) & 3


def by_place(me, parts, wanted):
    source = place(me) ^ wanted
    out = parts[0]
    for r in range(1, 4):
        out = jnp.where(source == r, parts[r], out)
    return out


def tree_node(low, high, reflector):
    vectors, factors = reflector
    node = by_transpose(halves(low + plain(halves(high), vectors)), factors)
    return low - node, high - by_transpose(halves(node), vectors)


def leaf_first_kernel(
    me_ref, trailing_hbm, vectors_hbm, factors_hbm, inverse_hbm,
    own_ref, away_one, away_two, rest_ref, later_ref, inverse_ref, across_ref, combined_ref,
    part_ref, vectors_ref, factors_ref, value_ref, away_ref, sems,
):
    count, rows, width = part_ref.shape
    copies = []

    def fetch(source, target):
        copies.append(pltpu.make_async_copy(source, target, sems.at[len(copies)]))
        copies[-1].start()
        return copies[-1]

    def fetch_part(b, target):
        cuts = [slice(c, c + width) for c in range(0, rows, width)]
        return [fetch(trailing_hbm.at[c, pl.ds(b * width, width)], target.at[c]) for c in cuts]

    first = [fetch(vectors_hbm, vectors_ref), fetch(factors_hbm, factors_ref)]
    parts = [fetch_part(b, part_ref.at[b]) for b in range(count)]
    last = [fetch_part(count + b, later_ref.at[b]) for b in range(later_ref.shape[0])]
    last.append([fetch(inverse_hbm, inverse_ref)])
    for copy in first:
        copy.wait()
    vectors = vectors_ref[...]
    across = halves(vectors.T)
    across_ref[0], across_ref[1] = across
    combined = halves(by_transpose(halves(vectors), halves(factors_ref[...])))
    combined_ref[0], combined_ref[1] = combined
    for b in range(count):
        for copy in parts[b]:
            copy.wait()
        leaf_block(me_ref, part_ref[b], across, combined, value_ref, rest_ref.at[b], own_ref, away_ref, b)
    panel = part_ref[0]
    value_ref[...] = plain(halves(panel.T), halves(panel))
    hand_over(me_ref, value_ref, own_ref, away_ref, count)
    cut = away_one.shape[0]
    away_one[...] = away_ref[:cut]
    away_two[...] = away_ref[cut:]
    for group in last:
        for copy in group:
            copy.wait()


def hand_over(me_ref, value_ref, own_ref, away_ref, slot):
    half = value_ref.shape[0] // 2
    core = me_ref[0] % 2
    target = slice(slot * half, (slot + 1) * half)
    own_ref[target] = value_ref[pl.ds(pl.multiple_of(core * half, half), half)]
    away_ref[target] = value_ref[pl.ds(pl.multiple_of((1 - core) * half, half), half)]


def leaf_block(me_ref, part, across, combined, value_ref, rest_ref, own_ref, away_ref, slot):
    width = value_ref.shape[0]
    out = part - plain(combined, halves(plain(across, halves(part))))
    rest_ref[...] = out[width:]
    value_ref[...] = out[:width].T
    hand_over(me_ref, value_ref, own_ref, away_ref, slot)


def leaf_second_kernel(me_ref, later_ref, across_ref, combined_ref, own_ref, rest_ref, *refs):
    aways, value_ref = refs[:-1], refs[-1]
    half = value_ref.shape[0] // 2
    across = across_ref[0], across_ref[1]
    combined = combined_ref[0], combined_ref[1]
    for b in range(later_ref.shape[0]):
        own_b = own_ref.at[pl.ds(b * half, half)]
        leaf_block(me_ref, later_ref[b], across, combined, value_ref, rest_ref.at[b], own_b, aways[b], 0)


def store_kernel(me_ref, first_ref, second_ref, inverse_ref, mark_ref, updated_hbm, basis_hbm, basis_ref, sems):
    count, width = first_ref.shape[:2]
    copies = []
    for b in range(count + second_ref.shape[0]):
        source = first_ref.at[b] if b < count else second_ref.at[b - count]
        target = updated_hbm.at[pl.ds(width, width), pl.ds(b * width, width)]
        copies.append(pltpu.make_async_copy(source, target, sems.at[b]))
        copies[-1].start()
    basis_ref[...] = plain(halves(first_ref[0]), halves(inverse_ref[...]))
    copies.append(pltpu.make_async_copy(basis_ref, basis_hbm.at[pl.ds(width, width)], sems.at[len(copies)]))
    mark_ref[...] = jnp.zeros_like(mark_ref)
    copies[-1].start()
    for copy in copies:
        copy.wait()


def core_kernel(
    me_ref, own_a_ref, own_b_ref, one_ref, two_ref, *refs
):
    more = len(refs) - 11
    there_bs, packed_ref = refs[:more], refs[more]
    sends, dones, (low_ref, high_ref) = refs[more + 1 : more + 5], refs[more + 5 : more + 9], refs[more + 9 :]
    me = me_ref[0]
    width = own_a_ref.shape[1]
    half = width // 2
    quarter = half // 4
    cut = own_a_ref.shape[0] - half
    count = cut // half + len(there_bs)
    odd = me % 2 == 1
    there_a = jnp.concatenate([one_ref[...], two_ref[...]], axis=0)
    gram = own_a_ref[cut:] + there_a[cut:]
    mine = jnp.concatenate([own_a_ref[:cut], own_b_ref[...]], axis=0)
    there = jnp.concatenate([there_a[:cut]] + [ref[...] for ref in there_bs], axis=0)
    low = jnp.where(odd, there, mine)
    high = jnp.where(odd, mine, there)
    low, high = tree_node(low, high, unpack(packed_ref[0], packed_ref[1]))
    low_ref[: count * half] = low
    low_ref[count * half :] = gram
    high_ref[...] = high
    for r in range(4):
        start = (place(me) ^ r) * quarter
        for b in range(count + 1):
            source = pl.ds(pl.multiple_of(b * half + start, quarter), quarter)
            target = slice(b * quarter, (b + 1) * quarter)
            sends[r][target] = low_ref[source]
            if b < count:
                dones[r][target] = high_ref[source]


def gather_kernel(me_ref, *refs):
    parts, (stack_ref, held_ref) = refs[:4], refs[4:]
    for r in range(1, 4):
        stack_ref[r - 1] = parts[r][...]
    held_ref[...] = by_place(me_ref[0], [ref[...] for ref in parts], 0)


def relay_kernel(me_ref, *refs):
    count = len(refs) // 2 if len(refs) % 2 == 0 else (len(refs) + 1) // 2
    parts, outs = refs[:count], refs[count:]
    if len(outs) < len(parts):
        outs[0][...] = parts[0][...]
        outs[1][...] = jnp.where((me_ref[0] >> 3) % 2 == 1, parts[2][...], parts[1][...])
    else:
        for part, out in zip(parts, outs):
            out[...] = part[...]


def plane_kernel(
    me_ref, *refs, level
):
    gots, (packed_ref, stack_ref, stack_there_ref) = refs[:4], refs[4:7]
    head_ref, send_ref, done_ref, held_ref = refs[7:]
    me = me_ref[0]
    core = me % 2
    cols = done_ref.shape[1]
    pairs = [(packed_ref[0], packed_ref[1])]
    pairs += [by_core(core, stack_ref[r], stack_there_ref[r]) for r in range(3)]
    firsts, seconds = [pair[0] for pair in pairs], [pair[1] for pair in pairs]
    pairs = [(by_place(me, firsts, j), by_place(me, seconds, j)) for j in range(4)]
    held_ref[0], held_ref[1] = pairs[0]
    reflectors = [unpack(*pair) for pair in pairs]
    parts = [ref[:cols] for ref in gots]
    heads = [by_place(me, parts, j) for j in range(4)]
    gram = gots[0][cols:] + gots[1][cols:] + (gots[2][cols:] + gots[3][cols:])
    heads[0], heads[1] = tree_node(heads[0], heads[1], reflectors[1])
    heads[2], heads[3] = tree_node(heads[2], heads[3], reflectors[3])
    heads[0], heads[2] = tree_node(heads[0], heads[2], reflectors[2])
    for j in range(4):
        done_ref[j] = heads[j]
    head_ref[...] = heads[0]
    upper = (me >> level) % 2 == 1
    send_ref[:cols] = jnp.where(upper, plain(halves(heads[0]), reflectors[0][0]), heads[0])
    send_ref[cols:] = gram


def line_node(me, head, result, mine, there, held, part_ref, part_there_ref, level):
    cols = head.shape[0]
    upper = (me >> level) % 2 == 1
    others = by_core(me % 2, part_ref[...], part_there_ref[...])
    node = [jnp.where(upper, a, b) for a, b in zip(held, others)]
    following = [jnp.where(upper, b, a) for a, b in zip(held, others)]
    coeffs = by_transpose(halves(mine[:cols] + there[:cols]), unpack(*node)[1])
    low = jnp.where(upper, there[:cols], head) - coeffs
    plane = me >> 3
    below = (1 << (level - 2)) - 1
    second = (plane & below) == (1 << (level - 3))
    high = head - by_transpose(halves(coeffs), unpack(*held)[0])
    result = jnp.where(second, high, result)
    return low, result, mine[cols:] + there[cols:], following


def line_kernel(me_ref, *refs, level, cut):
    head_ref, result_ref, mine_ref, there_ref, held_ref, part_ref, part_there_ref, head_out, result_out, held_out = refs[:10]
    sends = refs[10:]
    me = me_ref[0]
    held = held_ref[0], held_ref[1]
    low, result, gram, following = line_node(
        me, head_ref[...], result_ref[...], mine_ref[...], there_ref[...], held, part_ref, part_there_ref, level
    )
    cols, quarter = low.shape[0], gram.shape[0]
    ahead = (me >> (level + 1)) % 2 == 1
    head_out[...] = low
    result_out[...] = result
    held_out[0], held_out[1] = following
    value = jnp.where(ahead, plain(halves(low), unpack(*following)[0]), low)
    if cut:
        sends[0][:quarter] = value[:quarter]
        sends[0][quarter:] = gram
        sends[1][...] = value[quarter:]
    else:
        sends[0][:cols] = value
        sends[0][cols:] = gram


def last_kernel(me_ref, *refs, level, cut):
    head_ref, result_ref, held_ref, part_ref, part_there_ref, done_ref = refs[:6]
    number = 2 if cut else 1
    mines, theres = refs[6 : 6 + number], refs[6 + number : 6 + 2 * number]
    sends, all_ref = refs[6 + 2 * number : 10 + 2 * number], refs[10 + 2 * number]
    me = me_ref[0]
    cols = head_ref.shape[0]
    quarter = sends[0].shape[0] - cols
    quarter = quarter // 2
    values = []
    for parts in (mines, theres):
        if cut:
            values.append(jnp.concatenate([parts[0][:quarter], parts[1][...], parts[0][quarter:]], axis=0))
        else:
            values.append(parts[0][...])
    held = held_ref[0], held_ref[1]
    low, result, gram, _ = line_node(
        me, head_ref[...], result_ref[...], values[0], values[1], held, part_ref, part_there_ref, level
    )
    all_ref[0] = jnp.where((me >> 3) == 0, low, result)
    for j in range(1, 4):
        all_ref[j] = done_ref[j]
    for r in range(4):
        sends[r][:cols] = all_ref[place(me) ^ r]
        sends[r][cols : cols + quarter] = low[:quarter]
        sends[r][cols + quarter :] = gram


def pass_kernel(me_ref, *refs):
    backs, dones, out_ref = refs[:4], refs[4:8], refs[8]
    odd = me_ref[0] % 2 == 1
    cols = dones[0].shape[0]
    for r in range(4):
        out_ref[r, :cols] = jnp.where(odd, backs[r][:cols], dones[r][...])
        out_ref[r, cols:] = backs[r][cols:]


def near_kernel(me_ref, *refs):
    backs, dones, (_, updated_hbm, out_ref, sems) = refs[:4], refs[4:8], refs[8:]
    count, width, half = out_ref.shape
    quarter = half // 4
    me = me_ref[0]
    core = me % 2
    odd = core == 1
    copies = []
    for b in range(count):
        rows = slice(b * quarter, (b + 1) * quarter)
        pieces = [jnp.where(odd, dones[r][rows], backs[r][rows]) for r in range(4)]
        out_ref[b] = jnp.concatenate([by_place(me, pieces, j) for j in range(4)], axis=0).T
        columns = pl.ds(pl.multiple_of(b * width + core * half, half), half)
        copies.append(pltpu.make_async_copy(out_ref.at[b], updated_hbm.at[pl.ds(0, width), columns], sems.at[b]))
        copies[-1].start()
    for copy in copies:
        copy.wait()


def far_kernel(me_ref, *refs, total):
    backs, dones = refs[:4], refs[4:8]
    there_ref, inverse_ref, _, _, updated_hbm, basis_hbm, gram_hbm = refs[8:15]
    panel_ref, sum_ref, out_ref, basis_ref, gram_ref, sems = refs[15:]
    count, width, half = out_ref.shape
    quarter = half // 4
    cols = count * quarter
    me = me_ref[0]
    core = me % 2
    odd = core == 1
    copies = []

    def put(source, target):
        copies.append(pltpu.make_async_copy(source, target, sems.at[len(copies)]))
        copies[-1].start()

    for b in range(count):
        rows = slice(b * quarter, (b + 1) * quarter)
        pieces = [there_ref[r, rows] for r in range(4)]
        far = jnp.concatenate([by_place(me, pieces, j) for j in range(4)], axis=0).T
        out_ref[b] = far
        columns = pl.ds(pl.multiple_of(b * width + (1 - core) * half, half), half)
        put(out_ref.at[b], updated_hbm.at[pl.ds(0, width), columns])
        if b == 0:
            pieces = [jnp.where(odd, dones[r][rows], backs[r][rows]) for r in range(4)]
            near = jnp.concatenate([by_place(me, pieces, j) for j in range(4)], axis=0).T
            head = jnp.concatenate(by_core(core, near, far), axis=1)
            basis = plain(halves(head), halves(inverse_ref[...]))
            basis_ref[...] = jnp.where(me == 0, 0.0, basis)
            put(basis_ref, basis_hbm.at[pl.ds(0, width)])

    def target(part, r):
        return pl.ds(pl.multiple_of(part * half + (place(me) ^ r) * quarter, quarter), quarter)

    for r in range(4):
        panel_ref[target(core, r)] = backs[r][cols : cols + quarter]
        sum_ref[target(core, r)] = backs[r][cols + quarter :]
        panel_ref[target(1 - core, r)] = there_ref[r, cols : cols + quarter]
        sum_ref[target(1 - core, r)] = there_ref[r, cols + quarter :]
    panel = halves(panel_ref[...])
    gram_ref[...] = (sum_ref[...] - by_transpose(panel, panel)) / total
    put(gram_ref, gram_hbm)
    for copy in copies:
        copy.wait()


def body(trailing, leaf_vectors, leaf_factors, tree_vectors, tree_factors, inverse_factor):
    rows, columns = trailing.shape
    width = leaf_vectors.shape[1]
    half = width // 2
    quarter = half // 4
    count = columns // width
    devices = lax.axis_size("rows")
    levels = devices.bit_length() - 1
    me = lax.axis_index("rows").astype(jnp.int32)
    me_array = me.reshape(1)
    part_shape = (half + EXTRA, width)
    latest = []

    def exchange(value, shift):
        return lax.ppermute(value, "rows", [(i, i ^ shift) for i in range(devices)])

    def among(value, shift, member):
        return lax.ppermute(value, "rows", [(i, i ^ shift if member(i) else i) for i in range(devices)])

    def around(values):
        there = [exchange(values[r], 2 * r) for r in (3, 1, 2)]
        return [values[0], there[1], there[2], there[0]]

    def shape(*dims):
        return jax.ShapeDtypeStruct(dims, F32)

    def vmem(*dims):
        return pltpu.VMEM(dims, F32)

    def sems(number):
        return pltpu.SemaphoreType.DMA((number,))

    def call(kernel, operands, outs, scratch=(), away_in=(), away_out=(), aliases=(), before=()):
        number = len(operands)
        operands = [pltpu.with_memory_space_constraint(x, pltpu.HBM) if i in away_in else x for i, x in enumerate(operands)]
        outs = [(pltpu.HBM if i in away_out else pltpu.VMEM)(x.shape, x.dtype) for i, x in enumerate(outs)]
        unused = [*latest, *before]

        def kernel_on(*refs):
            kernel(*refs[: number + 1], *refs[number + 1 + len(unused) :])

        values = pl.pallas_call(
            kernel_on,
            out_shape=tuple(outs),
            in_specs=[SCALAR]
            + [AWAY if i in away_in else WHOLE for i in range(number)]
            + [pl.BlockSpec(memory_space=pl.ANY)] * len(unused),
            out_specs=tuple(AWAY if i in away_out else WHOLE for i in range(len(outs))),
            scratch_shapes=list(scratch),
            input_output_aliases=dict(aliases),
            compiler_params=PARAMS,
            cost_estimate=pl.CostEstimate(flops=1, bytes_accessed=1, transcendentals=0),
        )(me_array, *operands, *unused)
        if 0 not in away_out:
            latest[:] = values[:1]
        return values

    raw = [exchange(tree_vectors, 1), exchange(tree_factors, 1)]
    blocks = count // 2
    more = count - blocks
    split = jax.ShapeDtypeStruct((2, width, rows), BF16), jax.ShapeDtypeStruct((2, rows, width), BF16)
    rows_a = blocks * half + half
    own_a, away_one, away_two, rest_a, later, inverse_factor, across, combined = call(
        leaf_first_kernel, (trailing, leaf_vectors, leaf_factors, inverse_factor),
        [shape(rows_a, width), shape(rows_a // 2, width), shape(rows_a // 2, width)]
        + [shape(blocks, width, width), shape(more, rows, width), shape(width, width), *split],
        [
            vmem(blocks, rows, width), vmem(rows, width), vmem(width, width), vmem(width, width), vmem(rows_a, width),
            sems(count * (rows // width) + 3),
        ],
        range(4),
    )
    there_a = [exchange(away_one, 1), exchange(away_two, 1)]

    chip_low, chip_high, chip_part = call(
        pack_kernel, (tree_vectors, tree_factors, *raw),
        (shape(2, *part_shape), shape(2, *part_shape), shape(*part_shape)),
        [vmem(4, width, width), sems(4)], (),
    )
    plane_parts = [exchange(chip_part, 2 * r) for r in (3, 1, 2)]
    plane_parts = [plane_parts[1], plane_parts[2], plane_parts[0]]

    own_b, rest_b, *aways = call(
        leaf_second_kernel, (later, across, combined),
        [shape(more * half, width), shape(more, width, width)] + [shape(half, width)] * more,
        [vmem(width, width)], before=there_a,
    )
    theres = [exchange(away, 1) for away in aways]
    cols = count * quarter
    outs = call(
        core_kernel, (own_a, own_b, *there_a, *theres, chip_high),
        [shape(cols + quarter, width)] * 4 + [shape(cols, width)] * 4,
        [vmem(count * half + half, width), vmem(count * half, width)],
    )
    sends, dones = outs[:4], outs[4:]
    stack, held_part = call(
        gather_kernel, (chip_part, *plane_parts), (shape(3, *part_shape), shape(*part_shape)),
    )
    gots = around(sends)
    stack_there = exchange(stack, 1)
    _, updated, basis = call(
        store_kernel, (rest_a, rest_b, inverse_factor), (shape(8, width), shape(rows, columns), shape(rows, width)),
        [vmem(width, width), sems(count + 1)], (), (1, 2),
    )

    def upper(level):
        return (me >> level) % 2 == 1

    def direct(shift):
        return among(held_part, shift, lambda i: 2 in ((i >> 3) % 4, ((i ^ shift) >> 3) % 4))

    parts = [exchange(held_part, 8)]
    if levels == 5:
        parts += [direct(16), direct(24)]
    else:
        held = held_part
        for level in range(4, levels):
            held = jnp.where(upper(level - 1), parts[-1], held)
            parts.append(exchange(held, 1 << level))

    head, send, plane_done, held = call(
        functools.partial(plane_kernel, level=3), (*gots, chip_low, stack, stack_there),
        (shape(cols, width), shape(cols + quarter, width), shape(4, cols, width), shape(2, *part_shape)),
    )
    result = head
    mines, theres = [send], [exchange(send, 8)]
    parts = call(relay_kernel, parts, [shape(*part_shape)] * (levels - 3))
    for level in range(3, levels):
        part = parts[level - 3]
        part_there = exchange(part, 1)
        if level == levels - 1:
            sends = call(
                functools.partial(last_kernel, level=level, cut=len(mines) == 2),
                (head, result, held, part, part_there, plane_done, *mines, *theres),
                [shape(cols + 2 * quarter, width)] * 4, [vmem(4, cols, width)],
            )
        else:
            cut = level + 1 == levels - 1
            outs = [shape(2 * quarter, width), shape(cols - quarter, width)] if cut else [shape(cols + quarter, width)]
            head, result, held, *outs = call(
                functools.partial(line_kernel, level=level, cut=cut),
                (head, result, mines[0], theres[0], held, part, part_there),
                [shape(cols, width), shape(cols, width), shape(*held.shape)] + outs,
            )
            mines, theres = outs, [exchange(outs[0], 2 << level)]
            if cut:
                theres.append(among(outs[1], 2 << level, lambda i: (i >> 3) % (1 << (level - 2)) == 0))

    backs = around(sends)
    (back,) = call(pass_kernel, (*backs, *dones), (shape(4, cols + 2 * quarter, width),))
    there = exchange(back, 1)
    (updated,) = call(
        near_kernel, (*backs, *dones, updated), (shape(rows, columns),),
        [vmem(count, width, half), sems(count)], (8,), (0,), {9: 0},
    )
    return call(
        functools.partial(far_kernel, total=float(rows * devices)),
        (*backs, *dones, there, inverse_factor, updated, basis),
        (shape(rows, columns), shape(rows, width), shape(width, width)),
        [vmem(width, width), vmem(width, width), vmem(count, width, half), vmem(width, width), vmem(width, width), sems(count + 2)],
        (10, 11), (0, 1, 2), {11: 0, 12: 1},
    )


def solution(mesh):
    in_specs = (
        P("rows", None),
        P("rows", None),
        P("rows", None),
        P("rows", None),
        P("rows", None),
        P(),
    )
    out_specs = (P("rows", None), P("rows", None), P())
    return jax.shard_map(body, mesh=mesh, in_specs=in_specs, out_specs=out_specs, check_vma=False)
```

```python
import functools
import jax
import jax.numpy as jnp
from jax import lax
from jax.experimental import pallas as pl
from jax.experimental.pallas import tpu as pltpu
from jax.sharding import PartitionSpec as P

F32 = jnp.float32
BF16 = jnp.bfloat16
EXTRA = 8
PARAMS = pltpu.CompilerParams(vmem_limit_bytes=20 * 1024 * 1024)
WHOLE = pl.BlockSpec(memory_space=pltpu.VMEM)
SCALAR = pl.BlockSpec(memory_space=pltpu.SMEM)
AWAY = pl.BlockSpec(memory_space=pltpu.HBM)


def halves(value):
    high = value.astype(BF16)
    return high, (value - high.astype(F32)).astype(BF16)


def times(left, right, sides):
    first = jnp.concatenate([left[0], left[0], left[1]], axis=sides[0])
    second = jnp.concatenate([right[0], right[1], right[0]], axis=sides[1])
    dims = ((sides[:1], sides[1:]), ((), ()))
    return lax.dot_general(first, second, dims, preferred_element_type=F32)


def plain(left, right):
    return times(left, right, (1, 0))


def by_transpose(left, right):
    return times(left, right, (1, 1))


def pack_kernel(me_ref, *refs):
    sources, (low_ref, high_ref, part_ref), (buffer_ref, sems) = refs[:4], refs[4:7], refs[7:]
    copies = [pltpu.make_async_copy(source, buffer_ref.at[i], sems.at[i]) for i, source in enumerate(sources)]
    for copy in copies:
        copy.start()
    for copy in copies:
        copy.wait()
    core = me_ref[0] % 2
    width = buffer_ref.shape[1]
    half = width // 2
    row = lax.broadcasted_iota(jnp.int32, (width, width), 0)
    col = lax.broadcasted_iota(jnp.int32, (width, width), 1)
    both_vectors = by_core(core, buffer_ref[0], buffer_ref[2])
    both_factors = by_core(core, buffer_ref[1], buffer_ref[3])
    for vectors, factors, out_ref in zip(both_vectors, both_factors, (low_ref, high_ref)):
        packed = jnp.where(row > col, factors.T, vectors)
        diagonal = jnp.sum(jnp.where(row == col, factors, 0.0), axis=0, keepdims=True)
        for part in range(2):
            out_ref[part, :half] = packed[part * half : (part + 1) * half]
            out_ref[part, half:] = jnp.broadcast_to(diagonal, (EXTRA, width))
    part_ref[...] = low_ref[core]


def unpack(first, second):
    half = first.shape[0] - EXTRA
    width = 2 * half
    packed = jnp.concatenate([first[:half], second[:half]], axis=0)
    row = lax.broadcasted_iota(jnp.int32, (width, width), 0)
    col = lax.broadcasted_iota(jnp.int32, (width, width), 1)
    diagonal = jnp.broadcast_to(first[half : half + 1], (width, width))
    vectors = jnp.where(row <= col, packed, 0.0)
    factors = jnp.where(row > col, packed, jnp.where(row == col, diagonal, 0.0))
    return halves(vectors), halves(factors)


def by_core(core, mine, there):
    odd = core == 1
    return jnp.where(odd, there, mine), jnp.where(odd, mine, there)


def place(me):
    return (me >> 1) & 3


def by_place(me, parts, wanted):
    source = place(me) ^ wanted
    out = parts[0]
    for r in range(1, 4):
        out = jnp.where(source == r, parts[r], out)
    return out


def tree_node(low, high, reflector):
    vectors, factors = reflector
    node = by_transpose(halves(low + plain(halves(high), vectors)), factors)
    return low - node, high - by_transpose(halves(node), vectors)


def leaf_first_kernel(
    me_ref, trailing_hbm, vectors_hbm, factors_hbm, inverse_hbm,
    own_ref, away_one, away_two, rest_ref, later_ref, inverse_ref, across_ref, combined_ref,
    part_ref, vectors_ref, factors_ref, value_ref, away_ref, sems,
):
    count, rows, width = part_ref.shape
    copies = []

    def fetch(source, target):
        copies.append(pltpu.make_async_copy(source, target, sems.at[len(copies)]))
        copies[-1].start()
        return copies[-1]

    def fetch_part(b, target):
        cuts = [slice(c, c + width) for c in range(0, rows, width)]
        return [fetch(trailing_hbm.at[c, pl.ds(b * width, width)], target.at[c]) for c in cuts]

    first = [fetch(vectors_hbm, vectors_ref), fetch(factors_hbm, factors_ref)]
    parts = [fetch_part(b, part_ref.at[b]) for b in range(count)]
    last = [fetch_part(count + b, later_ref.at[b]) for b in range(later_ref.shape[0])]
    last.append([fetch(inverse_hbm, inverse_ref)])
    for copy in first:
        copy.wait()
    vectors = vectors_ref[...]
    across = halves(vectors.T)
    across_ref[0], across_ref[1] = across
    combined = halves(by_transpose(halves(vectors), halves(factors_ref[...])))
    combined_ref[0], combined_ref[1] = combined
    for b in range(count):
        for copy in parts[b]:
            copy.wait()
        leaf_block(me_ref, part_ref[b], across, combined, value_ref, rest_ref.at[b], own_ref, away_ref, b)
    panel = part_ref[0]
    value_ref[...] = plain(halves(panel.T), halves(panel))
    hand_over(me_ref, value_ref, own_ref, away_ref, count)
    cut = away_one.shape[0]
    away_one[...] = away_ref[:cut]
    away_two[...] = away_ref[cut:]
    for group in last:
        for copy in group:
            copy.wait()


def hand_over(me_ref, value_ref, own_ref, away_ref, slot):
    half = value_ref.shape[0] // 2
    core = me_ref[0] % 2
    target = slice(slot * half, (slot + 1) * half)
    own_ref[target] = value_ref[pl.ds(pl.multiple_of(core * half, half), half)]
    away_ref[target] = value_ref[pl.ds(pl.multiple_of((1 - core) * half, half), half)]


def leaf_block(me_ref, part, across, combined, value_ref, rest_ref, own_ref, away_ref, slot):
    width = value_ref.shape[0]
    out = part - plain(combined, halves(plain(across, halves(part))))
    rest_ref[...] = out[width:]
    value_ref[...] = out[:width].T
    hand_over(me_ref, value_ref, own_ref, away_ref, slot)


def leaf_second_kernel(me_ref, later_ref, across_ref, combined_ref, own_ref, rest_ref, *refs):
    aways, value_ref = refs[:-1], refs[-1]
    half = value_ref.shape[0] // 2
    across = across_ref[0], across_ref[1]
    combined = combined_ref[0], combined_ref[1]
    for b in range(later_ref.shape[0]):
        own_b = own_ref.at[pl.ds(b * half, half)]
        leaf_block(me_ref, later_ref[b], across, combined, value_ref, rest_ref.at[b], own_b, aways[b], 0)


def store_kernel(me_ref, first_ref, second_ref, inverse_ref, mark_ref, updated_hbm, basis_hbm, basis_ref, sems):
    count, width = first_ref.shape[:2]
    copies = []
    for b in range(count + second_ref.shape[0]):
        source = first_ref.at[b] if b < count else second_ref.at[b - count]
        target = updated_hbm.at[pl.ds(width, width), pl.ds(b * width, width)]
        copies.append(pltpu.make_async_copy(source, target, sems.at[b]))
        copies[-1].start()
    basis_ref[...] = plain(halves(first_ref[0]), halves(inverse_ref[...]))
    copies.append(pltpu.make_async_copy(basis_ref, basis_hbm.at[pl.ds(width, width)], sems.at[len(copies)]))
    mark_ref[...] = jnp.zeros_like(mark_ref)
    copies[-1].start()
    for copy in copies:
        copy.wait()


def core_kernel(
    me_ref, own_a_ref, own_b_ref, one_ref, two_ref, *refs
):
    more = len(refs) - 11
    there_bs, packed_ref = refs[:more], refs[more]
    sends, dones, (low_ref, high_ref) = refs[more + 1 : more + 5], refs[more + 5 : more + 9], refs[more + 9 :]
    me = me_ref[0]
    width = own_a_ref.shape[1]
    half = width // 2
    quarter = half // 4
    cut = own_a_ref.shape[0] - half
    count = cut // half + len(there_bs)
    odd = me % 2 == 1
    there_a = jnp.concatenate([one_ref[...], two_ref[...]], axis=0)
    gram = own_a_ref[cut:] + there_a[cut:]
    mine = jnp.concatenate([own_a_ref[:cut], own_b_ref[...]], axis=0)
    there = jnp.concatenate([there_a[:cut]] + [ref[...] for ref in there_bs], axis=0)
    low = jnp.where(odd, there, mine)
    high = jnp.where(odd, mine, there)
    low, high = tree_node(low, high, unpack(packed_ref[0], packed_ref[1]))
    low_ref[: count * half] = low
    low_ref[count * half :] = gram
    high_ref[...] = high
    for r in range(4):
        start = (place(me) ^ r) * quarter
        for b in range(count + 1):
            source = pl.ds(pl.multiple_of(b * half + start, quarter), quarter)
            target = slice(b * quarter, (b + 1) * quarter)
            sends[r][target] = low_ref[source]
            if b < count:
                dones[r][target] = high_ref[source]


def gather_kernel(me_ref, *refs):
    parts, (stack_ref, held_ref) = refs[:4], refs[4:]
    for r in range(1, 4):
        stack_ref[r - 1] = parts[r][...]
    held_ref[...] = by_place(me_ref[0], [ref[...] for ref in parts], 0)


def hold_kernel(me_ref, held_ref, part_ref, out_ref, *, level):
    rows = slice(0, held_ref.shape[0])
    mine = part_ref.shape[0]
    out_ref[rows] = jnp.where((me_ref[0] >> level) % 2 == 1, part_ref[rows], held_ref[...])
    if out_ref.shape[0] > mine:
        out_ref[mine:] = jnp.zeros_like(out_ref[mine:])


def relay_kernel(me_ref, part_ref, out_ref):
    out_ref[...] = part_ref[: out_ref.shape[0]]


def sort_kernel(me_ref, *refs):
    gots, (heads_ref, gram_ref) = refs[:4], refs[4:]
    cols = heads_ref.shape[1]
    parts = [ref[:cols] for ref in gots]
    for j in range(4):
        heads_ref[j] = by_place(me_ref[0], parts, j)
    gram_ref[...] = gots[0][cols:] + gots[1][cols:] + (gots[2][cols:] + gots[3][cols:])


def plane_kernel(
    me_ref, heads_ref, gram_ref, packed_ref, stack_ref, stack_there_ref, head_ref, send_ref, done_ref, held_ref, *, level
):
    me = me_ref[0]
    core = me % 2
    cols = done_ref.shape[1]
    pairs = [(packed_ref[0], packed_ref[1])]
    pairs += [by_core(core, stack_ref[r], stack_there_ref[r]) for r in range(3)]
    firsts, seconds = [pair[0] for pair in pairs], [pair[1] for pair in pairs]
    pairs = [(by_place(me, firsts, j), by_place(me, seconds, j)) for j in range(4)]
    held_ref[0], held_ref[1] = pairs[0]
    reflectors = [unpack(*pair) for pair in pairs]
    heads = [heads_ref[j] for j in range(4)]
    heads[0], heads[1] = tree_node(heads[0], heads[1], reflectors[1])
    heads[2], heads[3] = tree_node(heads[2], heads[3], reflectors[3])
    heads[0], heads[2] = tree_node(heads[0], heads[2], reflectors[2])
    for j in range(4):
        done_ref[j] = heads[j]
    head_ref[...] = heads[0]
    upper = (me >> level) % 2 == 1
    send_ref[:cols] = jnp.where(upper, plain(halves(heads[0]), reflectors[0][0]), heads[0])
    send_ref[cols:] = gram_ref[...]


def line_node(me, head, result, mine, there, held, part_ref, part_there_ref, level):
    cols = head.shape[0]
    upper = (me >> level) % 2 == 1
    others = by_core(me % 2, part_ref[...], part_there_ref[...])
    node = [jnp.where(upper, a, b) for a, b in zip(held, others)]
    following = [jnp.where(upper, b, a) for a, b in zip(held, others)]
    coeffs = by_transpose(halves(mine[:cols] + there[:cols]), unpack(*node)[1])
    low = jnp.where(upper, there[:cols], head) - coeffs
    plane = me >> 3
    below = (1 << (level - 2)) - 1
    second = (plane & below) == (1 << (level - 3))
    high = head - by_transpose(halves(coeffs), unpack(*held)[0])
    result = jnp.where(second, high, result)
    return low, result, mine[cols:] + there[cols:], following


def line_kernel(me_ref, *refs, level, cut):
    head_ref, result_ref, mine_ref, there_ref, held_ref, part_ref, part_there_ref, head_out, result_out, held_out = refs[:10]
    sends = refs[10:]
    me = me_ref[0]
    held = held_ref[0], held_ref[1]
    low, result, gram, following = line_node(
        me, head_ref[...], result_ref[...], mine_ref[...], there_ref[...], held, part_ref, part_there_ref, level
    )
    cols, quarter = low.shape[0], gram.shape[0]
    ahead = (me >> (level + 1)) % 2 == 1
    head_out[...] = low
    result_out[...] = result
    held_out[0], held_out[1] = following
    value = jnp.where(ahead, plain(halves(low), unpack(*following)[0]), low)
    if cut:
        sends[0][:quarter] = value[:quarter]
        sends[0][quarter:] = gram
        sends[1][...] = value[quarter:]
    else:
        sends[0][:cols] = value
        sends[0][cols:] = gram


def last_kernel(me_ref, *refs, level, cut):
    head_ref, result_ref, held_ref, part_ref, part_there_ref, done_ref = refs[:6]
    number = 2 if cut else 1
    mines, theres = refs[6 : 6 + number], refs[6 + number : 6 + 2 * number]
    sends, all_ref = refs[6 + 2 * number : 10 + 2 * number], refs[10 + 2 * number]
    me = me_ref[0]
    cols = head_ref.shape[0]
    quarter = sends[0].shape[0] - cols
    quarter = quarter // 2
    values = []
    for parts in (mines, theres):
        if cut:
            values.append(jnp.concatenate([parts[0][:quarter], parts[1][...], parts[0][quarter:]], axis=0))
        else:
            values.append(parts[0][...])
    held = held_ref[0], held_ref[1]
    low, result, gram, _ = line_node(
        me, head_ref[...], result_ref[...], values[0], values[1], held, part_ref, part_there_ref, level
    )
    all_ref[0] = jnp.where((me >> 3) == 0, low, result)
    for j in range(1, 4):
        all_ref[j] = done_ref[j]
    for r in range(4):
        sends[r][:cols] = all_ref[place(me) ^ r]
        sends[r][cols : cols + quarter] = low[:quarter]
        sends[r][cols + quarter :] = gram


def pass_kernel(me_ref, *refs):
    backs, dones, out_ref = refs[:4], refs[4:8], refs[8]
    odd = me_ref[0] % 2 == 1
    cols = dones[0].shape[0]
    for r in range(4):
        out_ref[r, :cols] = jnp.where(odd, backs[r][:cols], dones[r][...])
        out_ref[r, cols:] = backs[r][cols:]


def near_kernel(me_ref, *refs):
    backs, dones, (_, updated_hbm, out_ref, sems) = refs[:4], refs[4:8], refs[8:]
    count, width, half = out_ref.shape
    quarter = half // 4
    me = me_ref[0]
    core = me % 2
    odd = core == 1
    copies = []
    for b in range(count):
        rows = slice(b * quarter, (b + 1) * quarter)
        pieces = [jnp.where(odd, dones[r][rows], backs[r][rows]) for r in range(4)]
        out_ref[b] = jnp.concatenate([by_place(me, pieces, j) for j in range(4)], axis=0).T
        columns = pl.ds(pl.multiple_of(b * width + core * half, half), half)
        copies.append(pltpu.make_async_copy(out_ref.at[b], updated_hbm.at[pl.ds(0, width), columns], sems.at[b]))
        copies[-1].start()
    for copy in copies:
        copy.wait()


def far_kernel(me_ref, *refs, total):
    backs, dones = refs[:4], refs[4:8]
    there_ref, inverse_ref, _, _, updated_hbm, basis_hbm, gram_hbm = refs[8:15]
    panel_ref, sum_ref, out_ref, basis_ref, gram_ref, sems = refs[15:]
    count, width, half = out_ref.shape
    quarter = half // 4
    cols = count * quarter
    me = me_ref[0]
    core = me % 2
    odd = core == 1
    copies = []

    def put(source, target):
        copies.append(pltpu.make_async_copy(source, target, sems.at[len(copies)]))
        copies[-1].start()

    for b in range(count):
        rows = slice(b * quarter, (b + 1) * quarter)
        pieces = [there_ref[r, rows] for r in range(4)]
        far = jnp.concatenate([by_place(me, pieces, j) for j in range(4)], axis=0).T
        out_ref[b] = far
        columns = pl.ds(pl.multiple_of(b * width + (1 - core) * half, half), half)
        put(out_ref.at[b], updated_hbm.at[pl.ds(0, width), columns])
        if b == 0:
            pieces = [jnp.where(odd, dones[r][rows], backs[r][rows]) for r in range(4)]
            near = jnp.concatenate([by_place(me, pieces, j) for j in range(4)], axis=0).T
            head = jnp.concatenate(by_core(core, near, far), axis=1)
            basis = plain(halves(head), halves(inverse_ref[...]))
            basis_ref[...] = jnp.where(me == 0, 0.0, basis)
            put(basis_ref, basis_hbm.at[pl.ds(0, width)])

    def target(part, r):
        return pl.ds(pl.multiple_of(part * half + (place(me) ^ r) * quarter, quarter), quarter)

    for r in range(4):
        panel_ref[target(core, r)] = backs[r][cols : cols + quarter]
        sum_ref[target(core, r)] = backs[r][cols + quarter :]
        panel_ref[target(1 - core, r)] = there_ref[r, cols : cols + quarter]
        sum_ref[target(1 - core, r)] = there_ref[r, cols + quarter :]
    panel = halves(panel_ref[...])
    gram_ref[...] = (sum_ref[...] - by_transpose(panel, panel)) / total
    put(gram_ref, gram_hbm)
    for copy in copies:
        copy.wait()


def body(trailing, leaf_vectors, leaf_factors, tree_vectors, tree_factors, inverse_factor):
    rows, columns = trailing.shape
    width = leaf_vectors.shape[1]
    half = width // 2
    quarter = half // 4
    count = columns // width
    devices = lax.axis_size("rows")
    levels = devices.bit_length() - 1
    me = lax.axis_index("rows").astype(jnp.int32)
    me_array = me.reshape(1)
    part_shape = (half + EXTRA, width)
    latest = []

    def exchange(value, shift):
        return lax.ppermute(value, "rows", [(i, i ^ shift) for i in range(devices)])

    def among(value, shift, member):
        return lax.ppermute(value, "rows", [(i, i ^ shift if member(i) else i) for i in range(devices)])

    def around(values):
        there = [exchange(values[r], 2 * r) for r in (3, 1, 2)]
        return [values[0], there[1], there[2], there[0]]

    def shape(*dims):
        return jax.ShapeDtypeStruct(dims, F32)

    def vmem(*dims):
        return pltpu.VMEM(dims, F32)

    def sems(number):
        return pltpu.SemaphoreType.DMA((number,))

    def call(kernel, operands, outs, scratch=(), away_in=(), away_out=(), aliases=(), before=(), work=1, chained=True):
        number = len(operands)
        operands = [pltpu.with_memory_space_constraint(x, pltpu.HBM) if i in away_in else x for i, x in enumerate(operands)]
        outs = [(pltpu.HBM if i in away_out else pltpu.VMEM)(x.shape, x.dtype) for i, x in enumerate(outs)]
        unused = [*latest, *before] if chained else []

        def kernel_on(*refs):
            kernel(*refs[: number + 1], *refs[number + 1 + len(unused) :])

        values = pl.pallas_call(
            kernel_on,
            out_shape=tuple(outs),
            in_specs=[SCALAR]
            + [AWAY if i in away_in else WHOLE for i in range(number)]
            + [pl.BlockSpec(memory_space=pl.ANY)] * len(unused),
            out_specs=tuple(AWAY if i in away_out else WHOLE for i in range(len(outs))),
            scratch_shapes=list(scratch),
            input_output_aliases=dict(aliases),
            compiler_params=PARAMS,
            cost_estimate=pl.CostEstimate(flops=work, bytes_accessed=1, transcendentals=0),
        )(me_array, *operands, *unused)
        if chained and 0 not in away_out:
            latest[:] = values[:1]
        return values

    raw = [exchange(tree_vectors, 1), exchange(tree_factors, 1)]
    blocks = count // 2
    more = count - blocks
    split = jax.ShapeDtypeStruct((2, width, rows), BF16), jax.ShapeDtypeStruct((2, rows, width), BF16)
    rows_a = blocks * half + half
    own_a, away_one, away_two, rest_a, later, inverse_factor, across, combined = call(
        leaf_first_kernel, (trailing, leaf_vectors, leaf_factors, inverse_factor),
        [shape(rows_a, width), shape(rows_a // 2, width), shape(rows_a // 2, width)]
        + [shape(blocks, width, width), shape(more, rows, width), shape(width, width), *split],
        [
            vmem(blocks, rows, width), vmem(rows, width), vmem(width, width), vmem(width, width), vmem(rows_a, width),
            sems(count * (rows // width) + 3),
        ],
        range(4),
    )
    there_a = [exchange(away_one, 1), exchange(away_two, 1)]

    chip_low, chip_high, chip_part = call(
        pack_kernel, (tree_vectors, tree_factors, *raw),
        (shape(2, *part_shape), shape(2, *part_shape), shape(*part_shape)),
        [vmem(4, width, width), sems(4)], (),
    )
    plane_parts = [exchange(chip_part, 2 * r) for r in (3, 1, 2)]
    plane_parts = [plane_parts[1], plane_parts[2], plane_parts[0]]

    own_b, rest_b, *aways = call(
        leaf_second_kernel, (later, across, combined),
        [shape(more * half, width), shape(more, width, width)] + [shape(half, width)] * more,
        [vmem(width, width)], before=there_a,
    )
    theres = [exchange(away, 1) for away in aways]
    cols = count * quarter
    outs = call(
        core_kernel, (own_a, own_b, *there_a, *theres, chip_high),
        [shape(cols + quarter, width)] * 4 + [shape(cols, width)] * 4,
        [vmem(count * half + half, width), vmem(count * half, width)],
    )
    sends, dones = outs[:4], outs[4:]
    stack, held_part = call(
        gather_kernel, (chip_part, *plane_parts), (shape(3, *part_shape), shape(*part_shape)), work=1,
    )
    gots = around(sends)
    stack_there = exchange(stack, 1)
    parts = [exchange(held_part, 8)]
    long_shape = shape(cols + quarter + 8, width)
    for level in range(4, levels):
        (longer,) = call(functools.partial(hold_kernel, level=level - 1), (held_part, parts[-1]), (long_shape,))
        held_part = longer[: half + EXTRA]
        parts.append(exchange(longer, 1 << level))

    heads, gram_part = call(
        sort_kernel, gots, (shape(4, cols, width), shape(quarter, width)), work=1,
    )
    head, send, plane_done, held = call(
        functools.partial(plane_kernel, level=3), (heads, gram_part, chip_low, stack, stack_there),
        (shape(cols, width), shape(cols + quarter, width), shape(4, cols, width), shape(2, *part_shape)),
    )
    result = head
    mines, theres = [send], [exchange(send, 8)]
    parts = parts[:1] + [call(relay_kernel, (part,), (shape(*part_shape),))[0] for part in parts[1:]]
    for level in range(3, levels):
        part = parts[level - 3]
        part_there = exchange(part, 1)
        if level == levels - 1:
            sends = call(
                functools.partial(last_kernel, level=level, cut=len(mines) == 2),
                (head, result, held, part, part_there, plane_done, *mines, *theres),
                [shape(cols + 2 * quarter, width)] * 4, [vmem(4, cols, width)],
            )
        else:
            cut = False
            outs = [shape(2 * quarter, width), shape(cols - quarter, width)] if cut else [shape(cols + quarter, width)]
            head, result, held, *outs = call(
                functools.partial(line_kernel, level=level, cut=cut),
                (head, result, mines[0], theres[0], held, part, part_there),
                [shape(cols, width), shape(cols, width), shape(*held.shape)] + outs,
            )
            mines, theres = outs, [exchange(outs[0], 2 << level)]
            if cut:
                theres.append(among(outs[1], 2 << level, lambda i: (i >> 3) % (1 << (level - 2)) == 0))

    backs = around(sends)
    _, updated, basis = call(
        store_kernel, (rest_a, rest_b, inverse_factor), (shape(8, width), shape(rows, columns), shape(rows, width)),
        [vmem(width, width), sems(count + 1)], (), (1, 2),
    )
    (back,) = call(pass_kernel, (*backs, *dones), (shape(4, cols + 2 * quarter, width),))
    there = exchange(back, 1)
    (updated,) = call(
        near_kernel, (*backs, *dones, updated), (shape(rows, columns),),
        [vmem(count, width, half), sems(count)], (8,), (0,), {9: 0},
    )
    return call(
        functools.partial(far_kernel, total=float(rows * devices)),
        (*backs, *dones, there, inverse_factor, updated, basis),
        (shape(rows, columns), shape(rows, width), shape(width, width)),
        [vmem(width, width), vmem(width, width), vmem(count, width, half), vmem(width, width), vmem(width, width), sems(count + 2)],
        (10, 11), (0, 1, 2), {11: 0, 12: 1},
    )


def solution(mesh):
    in_specs = (
        P("rows", None),
        P("rows", None),
        P("rows", None),
        P("rows", None),
        P("rows", None),
        P(),
    )
    out_specs = (P("rows", None), P("rows", None), P())
    return jax.shard_map(body, mesh=mesh, in_specs=in_specs, out_specs=out_specs, check_vma=False)
```

```python
import functools
import jax
import jax.numpy as jnp
from jax import lax
from jax.experimental import pallas as pl
from jax.experimental.pallas import tpu as pltpu
from jax.sharding import PartitionSpec as P

F32 = jnp.float32
BF16 = jnp.bfloat16
EXTRA = 8
PARAMS = pltpu.CompilerParams(vmem_limit_bytes=20 * 1024 * 1024)
WHOLE = pl.BlockSpec(memory_space=pltpu.VMEM)
SCALAR = pl.BlockSpec(memory_space=pltpu.SMEM)
AWAY = pl.BlockSpec(memory_space=pltpu.HBM)


def halves(value):
    high = value.astype(BF16)
    return high, (value - high.astype(F32)).astype(BF16)


def times(left, right, sides):
    first = jnp.concatenate([left[0], left[0], left[1]], axis=sides[0])
    second = jnp.concatenate([right[0], right[1], right[0]], axis=sides[1])
    dims = ((sides[:1], sides[1:]), ((), ()))
    return lax.dot_general(first, second, dims, preferred_element_type=F32)


def plain(left, right):
    return times(left, right, (1, 0))


def by_transpose(left, right):
    return times(left, right, (1, 1))


def masks(size):
    row = lax.broadcasted_iota(jnp.int32, (size, size), 0)
    col = lax.broadcasted_iota(jnp.int32, (size, size), 1)
    return row, col


def diagonal_of(square):
    row, col = masks(square.shape[0])
    return jnp.sum(jnp.where(row == col, square, 0.0), axis=0, keepdims=True)


def pack_kernel(me_ref, *refs):
    sources, (low_ref, high_ref, part_ref), (buffer_ref, sems) = refs[:4], refs[4:7], refs[7:]
    copies = [pltpu.make_async_copy(source, buffer_ref.at[i], sems.at[i]) for i, source in enumerate(sources)]
    for copy in copies:
        copy.start()
    for copy in copies:
        copy.wait()
    core = me_ref[0] % 2
    half = buffer_ref.shape[1] // 2
    row, col = masks(half)
    both_vectors = by_core(core, buffer_ref[0], buffer_ref[2])
    both_factors = by_core(core, buffer_ref[1], buffer_ref[3])
    for vectors, factors, out_ref in zip(both_vectors, both_factors, (low_ref, high_ref)):
        first, second = factors[:half, :half], factors[half:, half:]
        square = jnp.where(row > col, first.T, jnp.where(row < col, second, 0.0))
        t_rows = jnp.concatenate([square, factors[:half, half:].T], axis=1)
        t_diagonal = jnp.concatenate([diagonal_of(first), diagonal_of(second)], axis=1)
        first, second = vectors[:half, :half], vectors[half:, half:]
        square = jnp.where(row <= col, first, second.T)
        v_rows = jnp.concatenate([square, vectors[:half, half:]], axis=1)
        v_diagonal = jnp.concatenate([diagonal_of(second)] * 2, axis=1)
        line = lax.broadcasted_iota(jnp.int32, (EXTRA, 2 * half), 0)
        diagonals = jnp.where(line == 0, t_diagonal, v_diagonal)
        for part in range(2):
            rows = slice(part * half // 2, (part + 1) * half // 2)
            out_ref[part, : half // 2] = t_rows[rows]
            out_ref[part, half // 2 : half // 2 + EXTRA] = diagonals
            out_ref[part, half // 2 + EXTRA :] = v_rows[rows]
    part_ref[...] = low_ref[core]


def unpack_factors(first, second):
    half = first.shape[1] // 2
    rows = jnp.concatenate([first[: half // 2], second[: half // 2]], axis=0)
    row, col = masks(half)
    square, corner = rows[:, :half], rows[:, half:]
    diagonal = first[half // 2 : half // 2 + 1]
    upper_left = jnp.where(row > col, square, jnp.where(row == col, diagonal[:, :half], 0.0))
    lower_right = jnp.where(row > col, square.T, jnp.where(row == col, diagonal[:, half:], 0.0))
    above = jnp.concatenate([upper_left, jnp.zeros_like(upper_left)], axis=1)
    return halves(jnp.concatenate([above, jnp.concatenate([corner, lower_right], axis=1)], axis=0))


def unpack_vectors(first, second):
    half = first.shape[1] // 2
    start = half // 2 + EXTRA
    rows = jnp.concatenate([first[start:], second[start:]], axis=0)
    row, col = masks(half)
    square, corner = rows[:, :half], rows[:, half:]
    diagonal = first[half // 2 + 1 : half // 2 + 2, :half]
    upper_left = jnp.where(row <= col, square, 0.0)
    lower_right = jnp.where(row < col, square.T, jnp.where(row == col, diagonal, 0.0))
    above = jnp.concatenate([upper_left, corner], axis=1)
    return halves(jnp.concatenate([above, jnp.concatenate([jnp.zeros_like(corner), lower_right], axis=1)], axis=0))


def unpack(first, second):
    return unpack_vectors(first, second), unpack_factors(first, second)


def by_core(core, mine, there):
    odd = core == 1
    return jnp.where(odd, there, mine), jnp.where(odd, mine, there)


def place(me):
    return (me >> 1) & 3


def by_place(me, parts, wanted):
    source = place(me) ^ wanted
    out = parts[0]
    for r in range(1, 4):
        out = jnp.where(source == r, parts[r], out)
    return out


def tree_node(low, high, reflector):
    vectors, factors = reflector
    node = by_transpose(halves(low + plain(halves(high), vectors)), factors)
    return low - node, high - by_transpose(halves(node), vectors)


def leaf_first_kernel(
    me_ref, trailing_hbm, vectors_hbm, factors_hbm, inverse_hbm,
    own_ref, away_one, away_two, rest_ref, later_ref, inverse_ref, across_ref, combined_ref,
    part_ref, vectors_ref, factors_ref, value_ref, away_ref, sems,
):
    count, rows, width = part_ref.shape
    copies = []

    def fetch(source, target):
        copies.append(pltpu.make_async_copy(source, target, sems.at[len(copies)]))
        copies[-1].start()
        return copies[-1]

    def fetch_part(b, target):
        cuts = [slice(c, c + width) for c in range(0, rows, width)]
        return [fetch(trailing_hbm.at[c, pl.ds(b * width, width)], target.at[c]) for c in cuts]

    first = [fetch(vectors_hbm, vectors_ref), fetch(factors_hbm, factors_ref)]
    parts = [fetch_part(b, part_ref.at[b]) for b in range(count)]
    last = [fetch_part(count + b, later_ref.at[b]) for b in range(later_ref.shape[0])]
    last.append([fetch(inverse_hbm, inverse_ref)])
    for copy in first:
        copy.wait()
    vectors = vectors_ref[...]
    across = halves(vectors.T)
    across_ref[0], across_ref[1] = across
    combined = halves(by_transpose(halves(vectors), halves(factors_ref[...])))
    combined_ref[0], combined_ref[1] = combined
    for b in range(count):
        for copy in parts[b]:
            copy.wait()
        leaf_block(me_ref, part_ref[b], across, combined, value_ref, rest_ref.at[b], own_ref, away_ref, b)
    panel = part_ref[0]
    value_ref[...] = plain(halves(panel.T), halves(panel))
    hand_over(me_ref, value_ref, own_ref, away_ref, count)
    cut = away_one.shape[0]
    away_one[...] = away_ref[:cut]
    away_two[...] = away_ref[cut:]
    for group in last:
        for copy in group:
            copy.wait()


def hand_over(me_ref, value_ref, own_ref, away_ref, slot):
    half = value_ref.shape[0] // 2
    core = me_ref[0] % 2
    target = slice(slot * half, (slot + 1) * half)
    own_ref[target] = value_ref[pl.ds(pl.multiple_of(core * half, half), half)]
    away_ref[target] = value_ref[pl.ds(pl.multiple_of((1 - core) * half, half), half)]


def leaf_block(me_ref, part, across, combined, value_ref, rest_ref, own_ref, away_ref, slot):
    width = value_ref.shape[0]
    out = part - plain(combined, halves(plain(across, halves(part))))
    rest_ref[...] = out[width:]
    value_ref[...] = out[:width].T
    hand_over(me_ref, value_ref, own_ref, away_ref, slot)


def leaf_second_kernel(me_ref, later_ref, across_ref, combined_ref, own_ref, rest_ref, *refs):
    aways, value_ref = refs[:-1], refs[-1]
    half = value_ref.shape[0] // 2
    across = across_ref[0], across_ref[1]
    combined = combined_ref[0], combined_ref[1]
    for b in range(later_ref.shape[0]):
        own_b = own_ref.at[pl.ds(b * half, half)]
        leaf_block(me_ref, later_ref[b], across, combined, value_ref, rest_ref.at[b], own_b, aways[b], 0)


def store_kernel(me_ref, first_ref, second_ref, inverse_ref, mark_ref, updated_hbm, basis_hbm, basis_ref, sems):
    count, width = first_ref.shape[:2]
    copies = []
    for b in range(count + second_ref.shape[0]):
        source = first_ref.at[b] if b < count else second_ref.at[b - count]
        target = updated_hbm.at[pl.ds(width, width), pl.ds(b * width, width)]
        copies.append(pltpu.make_async_copy(source, target, sems.at[b]))
        copies[-1].start()
    basis_ref[...] = plain(halves(first_ref[0]), halves(inverse_ref[...]))
    copies.append(pltpu.make_async_copy(basis_ref, basis_hbm.at[pl.ds(width, width)], sems.at[len(copies)]))
    mark_ref[...] = jnp.zeros_like(mark_ref)
    copies[-1].start()
    for copy in copies:
        copy.wait()


def core_kernel(
    me_ref, own_a_ref, own_b_ref, one_ref, two_ref, *refs
):
    more = len(refs) - 11
    there_bs, packed_ref = refs[:more], refs[more]
    sends, dones, (low_ref, high_ref) = refs[more + 1 : more + 5], refs[more + 5 : more + 9], refs[more + 9 :]
    me = me_ref[0]
    width = own_a_ref.shape[1]
    half = width // 2
    quarter = half // 4
    cut = own_a_ref.shape[0] - half
    count = cut // half + len(there_bs)
    odd = me % 2 == 1
    there_a = jnp.concatenate([one_ref[...], two_ref[...]], axis=0)
    gram = own_a_ref[cut:] + there_a[cut:]
    mine = jnp.concatenate([own_a_ref[:cut], own_b_ref[...]], axis=0)
    there = jnp.concatenate([there_a[:cut]] + [ref[...] for ref in there_bs], axis=0)
    low = jnp.where(odd, there, mine)
    high = jnp.where(odd, mine, there)
    low, high = tree_node(low, high, unpack(packed_ref[0], packed_ref[1]))
    low_ref[: count * half] = low
    low_ref[count * half :] = gram
    high_ref[...] = high
    for r in range(4):
        start = (place(me) ^ r) * quarter
        for b in range(count + 1):
            source = pl.ds(pl.multiple_of(b * half + start, quarter), quarter)
            target = slice(b * quarter, (b + 1) * quarter)
            sends[r][target] = low_ref[source]
            if b < count:
                dones[r][target] = high_ref[source]


def gather_kernel(me_ref, *refs):
    parts, (stack_ref, held_ref) = refs[:4], refs[4:]
    for r in range(1, 4):
        stack_ref[r - 1] = parts[r][...]
    held_ref[...] = by_place(me_ref[0], [ref[...] for ref in parts], 0)


def hold_kernel(me_ref, held_ref, part_ref, out_ref, *, level):
    rows = slice(0, out_ref.shape[0])
    out_ref[...] = jnp.where((me_ref[0] >> level) % 2 == 1, part_ref[rows], held_ref[rows])


def sort_kernel(me_ref, *refs):
    gots, (heads_ref, gram_ref) = refs[:4], refs[4:]
    cols = heads_ref.shape[1]
    parts = [ref[:cols] for ref in gots]
    for j in range(4):
        heads_ref[j] = by_place(me_ref[0], parts, j)
    gram_ref[...] = gots[0][cols:] + gots[1][cols:] + (gots[2][cols:] + gots[3][cols:])


def prepare_kernel(me_ref, packed_ref, stack_ref, stack_there_ref, ready_ref, held_ref):
    me = me_ref[0]
    pairs = [(packed_ref[0], packed_ref[1])]
    pairs += [by_core(me % 2, stack_ref[r], stack_there_ref[r]) for r in range(3)]
    firsts, seconds = [pair[0] for pair in pairs], [pair[1] for pair in pairs]
    pairs = [(by_place(me, firsts, j), by_place(me, seconds, j)) for j in range(4)]
    held_ref[0], held_ref[1] = pairs[0]
    for j in range(4):
        (ready_ref[j, 0], ready_ref[j, 1]), (ready_ref[j, 2], ready_ref[j, 3]) = unpack(*pairs[j])


def plane_kernel(me_ref, heads_ref, gram_ref, ready_ref, head_ref, send_ref, done_ref, *, level):
    cols = done_ref.shape[1]
    reflectors = [((ready_ref[j, 0], ready_ref[j, 1]), (ready_ref[j, 2], ready_ref[j, 3])) for j in range(4)]
    heads = [heads_ref[j] for j in range(4)]
    heads[0], heads[1] = tree_node(heads[0], heads[1], reflectors[1])
    heads[2], heads[3] = tree_node(heads[2], heads[3], reflectors[3])
    heads[0], heads[2] = tree_node(heads[0], heads[2], reflectors[2])
    for j in range(4):
        done_ref[j] = heads[j]
    head_ref[...] = heads[0]
    upper = (me_ref[0] >> level) % 2 == 1
    send_ref[:cols] = jnp.where(upper, plain(halves(heads[0]), reflectors[0][0]), heads[0])
    send_ref[cols:] = gram_ref[...]


def line_node(me, head, result, mine, there, held, part_ref, part_there_ref, level):
    cols = head.shape[0]
    upper = (me >> level) % 2 == 1
    others = by_core(me % 2, part_ref[...], part_there_ref[...])
    whole = held[0].shape == others[0].shape
    need = held[0].shape[1] // 4 + EXTRA
    node = [jnp.where(upper, a[:need], b[:need]) for a, b in zip(held, others)]
    following = [jnp.where(upper, b, a) for a, b in zip(held, others)] if whole else None
    coeffs = by_transpose(halves(mine[:cols] + there[:cols]), unpack_factors(*node))
    low = jnp.where(upper, there[:cols], head) - coeffs
    plane = me >> 3
    below = (1 << (level - 2)) - 1
    second = (plane & below) == (1 << (level - 3))
    high = head - by_transpose(halves(coeffs), unpack_vectors(*held))
    result = jnp.where(second, high, result)
    return low, result, mine[cols:] + there[cols:], following


def line_kernel(me_ref, *refs, level, cut):
    head_ref, result_ref, mine_ref, there_ref, held_ref, part_ref, part_there_ref, head_out, result_out, held_out = refs[:10]
    sends = refs[10:]
    me = me_ref[0]
    held = held_ref[0], held_ref[1]
    low, result, gram, following = line_node(
        me, head_ref[...], result_ref[...], mine_ref[...], there_ref[...], held, part_ref, part_there_ref, level
    )
    cols, quarter = low.shape[0], gram.shape[0]
    ahead = (me >> (level + 1)) % 2 == 1
    head_out[...] = low
    result_out[...] = result
    held_out[0], held_out[1] = following
    value = jnp.where(ahead, plain(halves(low), unpack_vectors(*following)), low)
    if cut:
        sends[0][:quarter] = value[:quarter]
        sends[0][quarter:] = gram
        sends[1][...] = value[quarter:]
    else:
        sends[0][:cols] = value
        sends[0][cols:] = gram


def last_kernel(me_ref, *refs, level, cut):
    head_ref, result_ref, held_ref, part_ref, part_there_ref, done_ref = refs[:6]
    number = 2 if cut else 1
    mines, theres = refs[6 : 6 + number], refs[6 + number : 6 + 2 * number]
    sends, all_ref = refs[6 + 2 * number : 10 + 2 * number], refs[10 + 2 * number]
    me = me_ref[0]
    cols = head_ref.shape[0]
    quarter = sends[0].shape[0] - cols
    quarter = quarter // 2
    values = []
    for parts in (mines, theres):
        if cut:
            values.append(jnp.concatenate([parts[0][:quarter], parts[1][...], parts[0][quarter:]], axis=0))
        else:
            values.append(parts[0][...])
    held = held_ref[0], held_ref[1]
    low, result, gram, _ = line_node(
        me, head_ref[...], result_ref[...], values[0], values[1], held, part_ref, part_there_ref, level
    )
    all_ref[0] = jnp.where((me >> 3) == 0, low, result)
    for j in range(1, 4):
        all_ref[j] = done_ref[j]
    for r in range(4):
        sends[r][:cols] = all_ref[place(me) ^ r]
        sends[r][cols : cols + quarter] = low[:quarter]
        sends[r][cols + quarter :] = gram


def pass_kernel(me_ref, *refs):
    backs, dones, out_ref = refs[:4], refs[4:8], refs[8]
    odd = me_ref[0] % 2 == 1
    cols = dones[0].shape[0]
    for r in range(4):
        out_ref[r, :cols] = jnp.where(odd, backs[r][:cols], dones[r][...])
        out_ref[r, cols:] = backs[r][cols:]


def near_kernel(me_ref, *refs):
    backs, dones, (_, updated_hbm, out_ref, sems) = refs[:4], refs[4:8], refs[8:]
    count, width, half = out_ref.shape
    quarter = half // 4
    me = me_ref[0]
    core = me % 2
    odd = core == 1
    copies = []
    for b in range(count):
        rows = slice(b * quarter, (b + 1) * quarter)
        pieces = [jnp.where(odd, dones[r][rows], backs[r][rows]) for r in range(4)]
        out_ref[b] = jnp.concatenate([by_place(me, pieces, j) for j in range(4)], axis=0).T
        columns = pl.ds(pl.multiple_of(b * width + core * half, half), half)
        copies.append(pltpu.make_async_copy(out_ref.at[b], updated_hbm.at[pl.ds(0, width), columns], sems.at[b]))
        copies[-1].start()
    for copy in copies:
        copy.wait()


def far_kernel(me_ref, *refs, total):
    backs, dones = refs[:4], refs[4:8]
    there_ref, inverse_ref, _, _, updated_hbm, basis_hbm, gram_hbm = refs[8:15]
    panel_ref, sum_ref, out_ref, basis_ref, gram_ref, sems = refs[15:]
    count, width, half = out_ref.shape
    quarter = half // 4
    cols = count * quarter
    me = me_ref[0]
    core = me % 2
    odd = core == 1
    copies = []

    def put(source, target):
        copies.append(pltpu.make_async_copy(source, target, sems.at[len(copies)]))
        copies[-1].start()

    for b in range(count):
        rows = slice(b * quarter, (b + 1) * quarter)
        pieces = [there_ref[r, rows] for r in range(4)]
        far = jnp.concatenate([by_place(me, pieces, j) for j in range(4)], axis=0).T
        out_ref[b] = far
        columns = pl.ds(pl.multiple_of(b * width + (1 - core) * half, half), half)
        put(out_ref.at[b], updated_hbm.at[pl.ds(0, width), columns])
        if b == 0:
            pieces = [jnp.where(odd, dones[r][rows], backs[r][rows]) for r in range(4)]
            near = jnp.concatenate([by_place(me, pieces, j) for j in range(4)], axis=0).T
            head = jnp.concatenate(by_core(core, near, far), axis=1)
            basis = plain(halves(head), halves(inverse_ref[...]))
            basis_ref[...] = jnp.where(me == 0, 0.0, basis)
            put(basis_ref, basis_hbm.at[pl.ds(0, width)])

    def target(part, r):
        return pl.ds(pl.multiple_of(part * half + (place(me) ^ r) * quarter, quarter), quarter)

    for r in range(4):
        panel_ref[target(core, r)] = backs[r][cols : cols + quarter]
        sum_ref[target(core, r)] = backs[r][cols + quarter :]
        panel_ref[target(1 - core, r)] = there_ref[r, cols : cols + quarter]
        sum_ref[target(1 - core, r)] = there_ref[r, cols + quarter :]
    panel = halves(panel_ref[...])
    gram_ref[...] = (sum_ref[...] - by_transpose(panel, panel)) / total
    put(gram_ref, gram_hbm)
    for copy in copies:
        copy.wait()


def body(trailing, leaf_vectors, leaf_factors, tree_vectors, tree_factors, inverse_factor):
    rows, columns = trailing.shape
    width = leaf_vectors.shape[1]
    half = width // 2
    quarter = half // 4
    count = columns // width
    devices = lax.axis_size("rows")
    levels = devices.bit_length() - 1
    me = lax.axis_index("rows").astype(jnp.int32)
    me_array = me.reshape(1)
    part_shape = (half + EXTRA, width)
    latest = []

    def exchange(value, shift):
        return lax.ppermute(value, "rows", [(i, i ^ shift) for i in range(devices)])

    def among(value, shift, member):
        return lax.ppermute(value, "rows", [(i, i ^ shift if member(i) else i) for i in range(devices)])

    def around(values):
        there = [exchange(values[r], 2 * r) for r in (3, 1, 2)]
        return [values[0], there[1], there[2], there[0]]

    def shape(*dims):
        return jax.ShapeDtypeStruct(dims, F32)

    def vmem(*dims):
        return pltpu.VMEM(dims, F32)

    def sems(number):
        return pltpu.SemaphoreType.DMA((number,))

    def call(kernel, operands, outs, scratch=(), away_in=(), away_out=(), aliases=(), before=(), work=1, chained=True):
        number = len(operands)
        operands = [pltpu.with_memory_space_constraint(x, pltpu.HBM) if i in away_in else x for i, x in enumerate(operands)]
        outs = [(pltpu.HBM if i in away_out else pltpu.VMEM)(x.shape, x.dtype) for i, x in enumerate(outs)]
        unused = [*latest, *before] if chained else []

        def kernel_on(*refs):
            kernel(*refs[: number + 1], *refs[number + 1 + len(unused) :])

        values = pl.pallas_call(
            kernel_on,
            out_shape=tuple(outs),
            in_specs=[SCALAR]
            + [AWAY if i in away_in else WHOLE for i in range(number)]
            + [pl.BlockSpec(memory_space=pl.ANY)] * len(unused),
            out_specs=tuple(AWAY if i in away_out else WHOLE for i in range(len(outs))),
            scratch_shapes=list(scratch),
            input_output_aliases=dict(aliases),
            compiler_params=PARAMS,
            cost_estimate=pl.CostEstimate(flops=work, bytes_accessed=1, transcendentals=0),
        )(me_array, *operands, *unused)
        if chained and 0 not in away_out:
            latest[:] = values[:1]
        return values

    raw = [exchange(tree_vectors, 1), exchange(tree_factors, 1)]
    blocks = count // 2
    more = count - blocks
    split = jax.ShapeDtypeStruct((2, width, rows), BF16), jax.ShapeDtypeStruct((2, rows, width), BF16)
    rows_a = blocks * half + half
    own_a, away_one, away_two, rest_a, later, inverse_factor, across, combined = call(
        leaf_first_kernel, (trailing, leaf_vectors, leaf_factors, inverse_factor),
        [shape(rows_a, width), shape(rows_a // 2, width), shape(rows_a // 2, width)]
        + [shape(blocks, width, width), shape(more, rows, width), shape(width, width), *split],
        [
            vmem(blocks, rows, width), vmem(rows, width), vmem(width, width), vmem(width, width), vmem(rows_a, width),
            sems(count * (rows // width) + 3),
        ],
        range(4),
    )
    there_a = [exchange(away_one, 1), exchange(away_two, 1)]

    chip_low, chip_high, chip_part = call(
        pack_kernel, (tree_vectors, tree_factors, *raw),
        (shape(2, *part_shape), shape(2, *part_shape), shape(*part_shape)),
        [vmem(4, width, width), sems(4)], (),
    )
    plane_parts = [exchange(chip_part, 2 * r) for r in (3, 1, 2)]
    plane_parts = [plane_parts[1], plane_parts[2], plane_parts[0]]

    own_b, rest_b, *aways = call(
        leaf_second_kernel, (later, across, combined),
        [shape(more * half, width), shape(more, width, width)] + [shape(half, width)] * more,
        [vmem(width, width)], before=there_a,
    )
    theres = [exchange(away, 1) for away in aways]
    cols = count * quarter
    outs = call(
        core_kernel, (own_a, own_b, *there_a, *theres, chip_high),
        [shape(cols + quarter, width)] * 4 + [shape(cols, width)] * 4,
        [vmem(count * half + half, width), vmem(count * half, width)],
    )
    sends, dones = outs[:4], outs[4:]
    stack, held_part = call(
        gather_kernel, (chip_part, *plane_parts), (shape(3, *part_shape), shape(*part_shape)), work=1,
    )
    gots = around(sends)
    stack_there = exchange(stack, 1)
    parts = [exchange(held_part, 8)]
    for level in range(4, levels):
        short = 3 * quarter if level == levels - 1 else half + EXTRA
        (held_part,) = call(
            functools.partial(hold_kernel, level=level - 1), (held_part, parts[-1]), (shape(short, width),),
        )
        parts.append(exchange(held_part, 1 << level))

    ready, held = call(
        prepare_kernel, (chip_low, stack, stack_there),
        (jax.ShapeDtypeStruct((4, 4, width, width), BF16), shape(2, *part_shape)),
    )
    heads, gram_part = call(
        sort_kernel, gots, (shape(4, cols, width), shape(quarter, width)), work=1,
    )
    head, send, plane_done = call(
        functools.partial(plane_kernel, level=3), (heads, gram_part, ready),
        (shape(cols, width), shape(cols + quarter, width), shape(4, cols, width)),
    )
    result = head
    mines, theres = [send], [exchange(send, 8)]
    for level in range(3, levels):
        part = parts[level - 3]
        part_there = exchange(part, 1)
        if level == levels - 1:
            sends = call(
                functools.partial(last_kernel, level=level, cut=len(mines) == 2),
                (head, result, held, part, part_there, plane_done, *mines, *theres),
                [shape(cols + 2 * quarter, width)] * 4, [vmem(4, cols, width)],
            )
        else:
            cut = False
            outs = [shape(2 * quarter, width), shape(cols - quarter, width)] if cut else [shape(cols + quarter, width)]
            head, result, held, *outs = call(
                functools.partial(line_kernel, level=level, cut=cut),
                (head, result, mines[0], theres[0], held, part, part_there),
                [shape(cols, width), shape(cols, width), shape(*held.shape)] + outs,
            )
            mines, theres = outs, [exchange(outs[0], 2 << level)]
            if cut:
                theres.append(among(outs[1], 2 << level, lambda i: (i >> 3) % (1 << (level - 2)) == 0))

    backs = around(sends)
    _, updated, basis = call(
        store_kernel, (rest_a, rest_b, inverse_factor), (shape(8, width), shape(rows, columns), shape(rows, width)),
        [vmem(width, width), sems(count + 1)], (), (1, 2),
    )
    (back,) = call(pass_kernel, (*backs, *dones), (shape(4, cols + 2 * quarter, width),))
    there = exchange(back, 1)
    (updated,) = call(
        near_kernel, (*backs, *dones, updated), (shape(rows, columns),),
        [vmem(count, width, half), sems(count)], (8,), (0,), {9: 0},
    )
    return call(
        functools.partial(far_kernel, total=float(rows * devices)),
        (*backs, *dones, there, inverse_factor, updated, basis),
        (shape(rows, columns), shape(rows, width), shape(width, width)),
        [vmem(width, width), vmem(width, width), vmem(count, width, half), vmem(width, width), vmem(width, width), sems(count + 2)],
        (10, 11), (0, 1, 2), {11: 0, 12: 1},
    )


def solution(mesh):
    in_specs = (
        P("rows", None),
        P("rows", None),
        P("rows", None),
        P("rows", None),
        P("rows", None),
        P(),
    )
    out_specs = (P("rows", None), P("rows", None), P())
    return jax.shard_map(body, mesh=mesh, in_specs=in_specs, out_specs=out_specs, check_vma=False)
```

```python
import functools
import jax
import jax.numpy as jnp
from jax import lax
from jax.experimental import pallas as pl
from jax.experimental.pallas import tpu as pltpu
from jax.sharding import PartitionSpec as P

F32 = jnp.float32
BF16 = jnp.bfloat16
EXTRA = 8
PARAMS = pltpu.CompilerParams(vmem_limit_bytes=20 * 1024 * 1024)
WHOLE = pl.BlockSpec(memory_space=pltpu.VMEM)
SCALAR = pl.BlockSpec(memory_space=pltpu.SMEM)
AWAY = pl.BlockSpec(memory_space=pltpu.HBM)


def halves(value):
    high = value.astype(BF16)
    return high, (value - high.astype(F32)).astype(BF16)


def times(left, right, sides):
    first = jnp.concatenate([left[0], left[0], left[1]], axis=sides[0])
    second = jnp.concatenate([right[0], right[1], right[0]], axis=sides[1])
    dims = ((sides[:1], sides[1:]), ((), ()))
    return lax.dot_general(first, second, dims, preferred_element_type=F32)


def plain(left, right):
    return times(left, right, (1, 0))


def by_transpose(left, right):
    return times(left, right, (1, 1))


def masks(size):
    row = lax.broadcasted_iota(jnp.int32, (size, size), 0)
    col = lax.broadcasted_iota(jnp.int32, (size, size), 1)
    return row, col


def diagonal_of(square):
    row, col = masks(square.shape[0])
    return jnp.sum(jnp.where(row == col, square, 0.0), axis=0, keepdims=True)


def pack_kernel(me_ref, *refs):
    sources, (low_ref, high_ref, part_ref), (buffer_ref, sems) = refs[:4], refs[4:7], refs[7:]
    copies = [pltpu.make_async_copy(source, buffer_ref.at[i], sems.at[i]) for i, source in enumerate(sources)]
    for copy in copies:
        copy.start()
    for copy in copies:
        copy.wait()
    core = me_ref[0] % 2
    half = buffer_ref.shape[1] // 2
    row, col = masks(half)
    both_vectors = by_core(core, buffer_ref[0], buffer_ref[2])
    both_factors = by_core(core, buffer_ref[1], buffer_ref[3])
    for vectors, factors, out_ref in zip(both_vectors, both_factors, (low_ref, high_ref)):
        first, second = factors[:half, :half], factors[half:, half:]
        square = jnp.where(row > col, first.T, jnp.where(row < col, second, 0.0))
        t_rows = jnp.concatenate([square, factors[:half, half:].T], axis=1)
        t_diagonal = jnp.concatenate([diagonal_of(first), diagonal_of(second)], axis=1)
        first, second = vectors[:half, :half], vectors[half:, half:]
        square = jnp.where(row <= col, first, second.T)
        v_rows = jnp.concatenate([square, vectors[:half, half:]], axis=1)
        v_diagonal = jnp.concatenate([diagonal_of(second)] * 2, axis=1)
        line = lax.broadcasted_iota(jnp.int32, (EXTRA, 2 * half), 0)
        diagonals = jnp.where(line == 0, t_diagonal, v_diagonal)
        for part in range(2):
            rows = slice(part * half // 2, (part + 1) * half // 2)
            out_ref[part, : half // 2] = t_rows[rows]
            out_ref[part, half // 2 : half // 2 + EXTRA] = diagonals
            out_ref[part, half // 2 + EXTRA :] = v_rows[rows]
    part_ref[...] = low_ref[core]


def unpack_factors(first, second):
    half = first.shape[1] // 2
    rows = jnp.concatenate([first[: half // 2], second[: half // 2]], axis=0)
    row, col = masks(half)
    square, corner = rows[:, :half], rows[:, half:]
    diagonal = first[half // 2 : half // 2 + 1]
    upper_left = jnp.where(row > col, square, jnp.where(row == col, diagonal[:, :half], 0.0))
    lower_right = jnp.where(row > col, square.T, jnp.where(row == col, diagonal[:, half:], 0.0))
    above = jnp.concatenate([upper_left, jnp.zeros_like(upper_left)], axis=1)
    return halves(jnp.concatenate([above, jnp.concatenate([corner, lower_right], axis=1)], axis=0))


def unpack_vectors(first, second):
    half = first.shape[1] // 2
    start = half // 2 + EXTRA
    rows = jnp.concatenate([first[start:], second[start:]], axis=0)
    row, col = masks(half)
    square, corner = rows[:, :half], rows[:, half:]
    diagonal = first[half // 2 + 1 : half // 2 + 2, :half]
    upper_left = jnp.where(row <= col, square, 0.0)
    lower_right = jnp.where(row < col, square.T, jnp.where(row == col, diagonal, 0.0))
    above = jnp.concatenate([upper_left, corner], axis=1)
    return halves(jnp.concatenate([above, jnp.concatenate([jnp.zeros_like(corner), lower_right], axis=1)], axis=0))


def unpack(first, second):
    return unpack_vectors(first, second), unpack_factors(first, second)


def by_core(core, mine, there):
    odd = core == 1
    return jnp.where(odd, there, mine), jnp.where(odd, mine, there)


def place(me):
    return (me >> 1) & 3


def by_place(me, parts, wanted):
    source = place(me) ^ wanted
    out = parts[0]
    for r in range(1, 4):
        out = jnp.where(source == r, parts[r], out)
    return out


def tree_node(low, high, reflector):
    vectors, factors = reflector
    node = by_transpose(halves(low + plain(halves(high), vectors)), factors)
    return low - node, high - by_transpose(halves(node), vectors)


def leaf_first_kernel(
    me_ref, trailing_hbm, vectors_hbm, factors_hbm, inverse_hbm,
    own_ref, away_one, away_two, rest_ref, later_ref, inverse_ref, across_ref, combined_ref,
    part_ref, vectors_ref, factors_ref, value_ref, away_ref, sems,
):
    count, rows, width = part_ref.shape
    copies = []

    def fetch(source, target):
        copies.append(pltpu.make_async_copy(source, target, sems.at[len(copies)]))
        copies[-1].start()
        return copies[-1]

    def fetch_part(b, target):
        cuts = [slice(c, c + width) for c in range(0, rows, width)]
        return [fetch(trailing_hbm.at[c, pl.ds(b * width, width)], target.at[c]) for c in cuts]

    first = [fetch(vectors_hbm, vectors_ref), fetch(factors_hbm, factors_ref)]
    parts = [fetch_part(b, part_ref.at[b]) for b in range(count)]
    last = [fetch_part(count + b, later_ref.at[b]) for b in range(later_ref.shape[0])]
    last.append([fetch(inverse_hbm, inverse_ref)])
    for copy in first:
        copy.wait()
    vectors = vectors_ref[...]
    across = halves(vectors.T)
    across_ref[0], across_ref[1] = across
    combined = halves(by_transpose(halves(vectors), halves(factors_ref[...])))
    combined_ref[0], combined_ref[1] = combined
    for b in range(count):
        for copy in parts[b]:
            copy.wait()
        leaf_block(me_ref, part_ref[b], across, combined, value_ref, rest_ref.at[b], own_ref, away_ref, b)
    panel = part_ref[0]
    value_ref[...] = plain(halves(panel.T), halves(panel))
    hand_over(me_ref, value_ref, own_ref, away_ref, count)
    cut = away_one.shape[0]
    away_one[...] = away_ref[:cut]
    away_two[...] = away_ref[cut:]
    for group in last:
        for copy in group:
            copy.wait()


def hand_over(me_ref, value_ref, own_ref, away_ref, slot):
    half = value_ref.shape[0] // 2
    core = me_ref[0] % 2
    target = slice(slot * half, (slot + 1) * half)
    own_ref[target] = value_ref[pl.ds(pl.multiple_of(core * half, half), half)]
    away_ref[target] = value_ref[pl.ds(pl.multiple_of((1 - core) * half, half), half)]


def leaf_block(me_ref, part, across, combined, value_ref, rest_ref, own_ref, away_ref, slot):
    width = value_ref.shape[0]
    out = part - plain(combined, halves(plain(across, halves(part))))
    rest_ref[...] = out[width:]
    value_ref[...] = out[:width].T
    hand_over(me_ref, value_ref, own_ref, away_ref, slot)


def leaf_second_kernel(me_ref, later_ref, across_ref, combined_ref, own_ref, rest_ref, *refs):
    aways, value_ref = refs[:-1], refs[-1]
    half = value_ref.shape[0] // 2
    across = across_ref[0], across_ref[1]
    combined = combined_ref[0], combined_ref[1]
    for b in range(later_ref.shape[0]):
        own_b = own_ref.at[pl.ds(b * half, half)]
        leaf_block(me_ref, later_ref[b], across, combined, value_ref, rest_ref.at[b], own_b, aways[b], 0)


def store_kernel(me_ref, first_ref, second_ref, inverse_ref, mark_ref, updated_hbm, basis_hbm, basis_ref, sems):
    count, width = first_ref.shape[:2]
    copies = []
    for b in range(count + second_ref.shape[0]):
        source = first_ref.at[b] if b < count else second_ref.at[b - count]
        target = updated_hbm.at[pl.ds(width, width), pl.ds(b * width, width)]
        copies.append(pltpu.make_async_copy(source, target, sems.at[b]))
        copies[-1].start()
    basis_ref[...] = plain(halves(first_ref[0]), halves(inverse_ref[...]))
    copies.append(pltpu.make_async_copy(basis_ref, basis_hbm.at[pl.ds(width, width)], sems.at[len(copies)]))
    mark_ref[...] = jnp.zeros_like(mark_ref)
    copies[-1].start()
    for copy in copies:
        copy.wait()


def core_kernel(
    me_ref, own_a_ref, own_b_ref, one_ref, two_ref, *refs
):
    more = len(refs) - 12
    there_bs, packed_ref = refs[:more], refs[more]
    sends, dones, (gram_ref, low_ref, high_ref) = refs[more + 1 : more + 5], refs[more + 5 : more + 9], refs[more + 9 :]
    me = me_ref[0]
    width = own_a_ref.shape[1]
    half = width // 2
    quarter = half // 4
    cut = own_a_ref.shape[0] - half
    count = cut // half + len(there_bs)
    odd = me % 2 == 1
    there_a = jnp.concatenate([one_ref[...], two_ref[...]], axis=0)
    gram_ref[...] = own_a_ref[cut:] + there_a[cut:]
    mine = jnp.concatenate([own_a_ref[:cut], own_b_ref[...]], axis=0)
    there = jnp.concatenate([there_a[:cut]] + [ref[...] for ref in there_bs], axis=0)
    low = jnp.where(odd, there, mine)
    high = jnp.where(odd, mine, there)
    low, high = tree_node(low, high, unpack(packed_ref[0], packed_ref[1]))
    low_ref[...] = low
    high_ref[...] = high
    for r in range(4):
        start = (place(me) ^ r) * quarter
        for b in range(count):
            source = pl.ds(pl.multiple_of(b * half + start, quarter), quarter)
            target = slice(b * quarter, (b + 1) * quarter)
            sends[r][target] = low_ref[source]
            dones[r][target] = high_ref[source]


def gather_kernel(me_ref, *refs):
    parts, (stack_ref, held_ref) = refs[:4], refs[4:]
    for r in range(1, 4):
        stack_ref[r - 1] = parts[r][...]
    held_ref[...] = by_place(me_ref[0], [ref[...] for ref in parts], 0)


def hold_kernel(me_ref, held_ref, part_ref, out_ref, *, level):
    rows = slice(0, out_ref.shape[0])
    out_ref[...] = jnp.where((me_ref[0] >> level) % 2 == 1, part_ref[rows], held_ref[rows])


def sort_kernel(me_ref, *refs):
    parts = [ref[...] for ref in refs[:4]]
    for j in range(4):
        refs[4][j] = by_place(me_ref[0], parts, j)


def add_kernel(me_ref, first_ref, second_ref, out_ref):
    out_ref[...] = first_ref[...] + second_ref[...]


def fill(send_ref, value):
    cols = value.shape[0]
    send_ref[:cols] = value
    send_ref[cols:] = jnp.zeros_like(send_ref[cols:])


def prepare_kernel(me_ref, packed_ref, stack_ref, stack_there_ref, ready_ref, held_ref):
    me = me_ref[0]
    pairs = [(packed_ref[0], packed_ref[1])]
    pairs += [by_core(me % 2, stack_ref[r], stack_there_ref[r]) for r in range(3)]
    firsts, seconds = [pair[0] for pair in pairs], [pair[1] for pair in pairs]
    pairs = [(by_place(me, firsts, j), by_place(me, seconds, j)) for j in range(4)]
    held_ref[0], held_ref[1] = pairs[0]
    for j in range(4):
        (ready_ref[j, 0], ready_ref[j, 1]), (ready_ref[j, 2], ready_ref[j, 3]) = unpack(*pairs[j])


def plane_kernel(me_ref, heads_ref, ready_ref, head_ref, send_ref, done_ref, *, level):
    reflectors = [((ready_ref[j, 0], ready_ref[j, 1]), (ready_ref[j, 2], ready_ref[j, 3])) for j in range(4)]
    heads = [heads_ref[j] for j in range(4)]
    heads[0], heads[1] = tree_node(heads[0], heads[1], reflectors[1])
    heads[2], heads[3] = tree_node(heads[2], heads[3], reflectors[3])
    heads[0], heads[2] = tree_node(heads[0], heads[2], reflectors[2])
    for j in range(4):
        done_ref[j] = heads[j]
    head_ref[...] = heads[0]
    upper = (me_ref[0] >> level) % 2 == 1
    fill(send_ref, jnp.where(upper, plain(halves(heads[0]), reflectors[0][0]), heads[0]))


def line_node(me_ref, head_ref, result_ref, mine_ref, there_ref, held_ref, part_ref, part_there_ref, level):
    me = me_ref[0]
    cols = head_ref.shape[0]
    upper = (me >> level) % 2 == 1
    held = held_ref[0], held_ref[1]
    others = by_core(me % 2, part_ref[...], part_there_ref[...])
    whole = held[0].shape == others[0].shape
    need = held[0].shape[1] // 4 + EXTRA
    node = [jnp.where(upper, a[:need], b[:need]) for a, b in zip(held, others)]
    following = [jnp.where(upper, b, a) for a, b in zip(held, others)] if whole else None
    head, there = head_ref[...], there_ref[:cols]
    coeffs = by_transpose(halves(mine_ref[:cols] + there), unpack_factors(*node))
    low = jnp.where(upper, there, head) - coeffs
    plane = me >> 3
    below = (1 << (level - 2)) - 1
    second = (plane & below) == (1 << (level - 3))
    high = head - by_transpose(halves(coeffs), unpack_vectors(*held))
    return low, jnp.where(second, high, result_ref[...]), following


def line_kernel(me_ref, *refs, level):
    head_out, result_out, held_out, send_ref = refs[7:]
    low, result, following = line_node(me_ref, *refs[:7], level)
    ahead = (me_ref[0] >> (level + 1)) % 2 == 1
    head_out[...] = low
    result_out[...] = result
    held_out[0], held_out[1] = following
    fill(send_ref, jnp.where(ahead, plain(halves(low), unpack_vectors(*following)), low))


def last_kernel(me_ref, *refs, level):
    done_ref, sends, all_ref = refs[7], refs[8:12], refs[12]
    me = me_ref[0]
    low, result, _ = line_node(me_ref, *refs[:7], level)
    cols = low.shape[0]
    all_ref[0] = jnp.where((me >> 3) == 0, low, result)
    for j in range(1, 4):
        all_ref[j] = done_ref[j]
    for r in range(4):
        sends[r][:cols] = all_ref[place(me) ^ r]
        sends[r][cols:] = low[: sends[r].shape[0] - cols]


def pass_kernel(me_ref, *refs):
    backs, dones, (gram_ref, out_ref) = refs[:4], refs[4:8], refs[8:]
    odd = me_ref[0] % 2 == 1
    cols, rows = dones[0].shape[0], backs[0].shape[0]
    quarter = rows - cols
    for r in range(4):
        out_ref[r, :cols] = jnp.where(odd, backs[r][:cols], dones[r][...])
        out_ref[r, cols:rows] = backs[r][cols:]
        out_ref[r, rows:] = gram_ref[r * quarter : (r + 1) * quarter]


def near_kernel(me_ref, *refs):
    backs, dones, (_, updated_hbm, out_ref, sems) = refs[:4], refs[4:8], refs[8:]
    count, width, half = out_ref.shape
    quarter = half // 4
    me = me_ref[0]
    core = me % 2
    odd = core == 1
    copies = []
    for b in range(count):
        rows = slice(b * quarter, (b + 1) * quarter)
        pieces = [jnp.where(odd, dones[r][rows], backs[r][rows]) for r in range(4)]
        out_ref[b] = jnp.concatenate([by_place(me, pieces, j) for j in range(4)], axis=0).T
        columns = pl.ds(pl.multiple_of(b * width + core * half, half), half)
        copies.append(pltpu.make_async_copy(out_ref.at[b], updated_hbm.at[pl.ds(0, width), columns], sems.at[b]))
        copies[-1].start()
    for copy in copies:
        copy.wait()


def far_kernel(me_ref, *refs, total):
    backs, dones = refs[:4], refs[4:8]
    there_ref, half_ref, inverse_ref, _, _, updated_hbm, basis_hbm, gram_hbm = refs[8:16]
    panel_ref, sum_ref, out_ref, basis_ref, gram_ref, sems = refs[16:]
    count, width, half = out_ref.shape
    quarter = half // 4
    cols = count * quarter
    me = me_ref[0]
    core = me % 2
    odd = core == 1
    copies = []

    def put(source, target):
        copies.append(pltpu.make_async_copy(source, target, sems.at[len(copies)]))
        copies[-1].start()

    for b in range(count):
        rows = slice(b * quarter, (b + 1) * quarter)
        pieces = [there_ref[r, rows] for r in range(4)]
        far = jnp.concatenate([by_place(me, pieces, j) for j in range(4)], axis=0).T
        out_ref[b] = far
        columns = pl.ds(pl.multiple_of(b * width + (1 - core) * half, half), half)
        put(out_ref.at[b], updated_hbm.at[pl.ds(0, width), columns])
        if b == 0:
            pieces = [jnp.where(odd, dones[r][rows], backs[r][rows]) for r in range(4)]
            near = jnp.concatenate([by_place(me, pieces, j) for j in range(4)], axis=0).T
            head = jnp.concatenate(by_core(core, near, far), axis=1)
            basis = plain(halves(head), halves(inverse_ref[...]))
            basis_ref[...] = jnp.where(me == 0, 0.0, basis)
            put(basis_ref, basis_hbm.at[pl.ds(0, width)])

    def target(part, r):
        return pl.ds(pl.multiple_of(part * half + (place(me) ^ r) * quarter, quarter), quarter)

    for r in range(4):
        panel_ref[target(core, r)] = backs[r][cols:]
        panel_ref[target(1 - core, r)] = there_ref[r, cols : cols + quarter]
        rows = pl.ds(pl.multiple_of((1 - core) * half + r * quarter, quarter), quarter)
        sum_ref[rows] = there_ref[r, cols + quarter :]
    sum_ref[pl.ds(pl.multiple_of(core * half, half), half)] = half_ref[...]
    panel = halves(panel_ref[...])
    gram_ref[...] = (sum_ref[...] - by_transpose(panel, panel)) / total
    put(gram_ref, gram_hbm)
    for copy in copies:
        copy.wait()


def body(trailing, leaf_vectors, leaf_factors, tree_vectors, tree_factors, inverse_factor):
    rows, columns = trailing.shape
    width = leaf_vectors.shape[1]
    half = width // 2
    quarter = half // 4
    count = columns // width
    devices = lax.axis_size("rows")
    levels = devices.bit_length() - 1
    me = lax.axis_index("rows").astype(jnp.int32)
    me_array = me.reshape(1)
    part_shape = (half + EXTRA, width)
    latest = []

    def exchange(value, shift):
        return lax.ppermute(value, "rows", [(i, i ^ shift) for i in range(devices)])

    def among(value, shift, member):
        return lax.ppermute(value, "rows", [(i, i ^ shift if member(i) else i) for i in range(devices)])

    def around(values):
        there = [exchange(values[r], 2 * r) for r in (3, 1, 2)]
        return [values[0], there[1], there[2], there[0]]

    def shape(*dims):
        return jax.ShapeDtypeStruct(dims, F32)

    def vmem(*dims):
        return pltpu.VMEM(dims, F32)

    def sems(number):
        return pltpu.SemaphoreType.DMA((number,))

    def call(kernel, operands, outs, scratch=(), away_in=(), away_out=(), aliases=(), before=(), work=1, chained=True):
        number = len(operands)
        operands = [pltpu.with_memory_space_constraint(x, pltpu.HBM) if i in away_in else x for i, x in enumerate(operands)]
        outs = [(pltpu.HBM if i in away_out else pltpu.VMEM)(x.shape, x.dtype) for i, x in enumerate(outs)]
        unused = [*latest, *before] if chained else []

        def kernel_on(*refs):
            kernel(*refs[: number + 1], *refs[number + 1 + len(unused) :])

        values = pl.pallas_call(
            kernel_on,
            out_shape=tuple(outs),
            in_specs=[SCALAR]
            + [AWAY if i in away_in else WHOLE for i in range(number)]
            + [pl.BlockSpec(memory_space=pl.ANY)] * len(unused),
            out_specs=tuple(AWAY if i in away_out else WHOLE for i in range(len(outs))),
            scratch_shapes=list(scratch),
            input_output_aliases=dict(aliases),
            compiler_params=PARAMS,
            cost_estimate=pl.CostEstimate(flops=work, bytes_accessed=1, transcendentals=0),
        )(me_array, *operands, *unused)
        if chained and 0 not in away_out:
            latest[:] = values[:1]
        return values

    raw = [exchange(tree_vectors, 1), exchange(tree_factors, 1)]
    blocks = count // 2
    more = count - blocks
    split = jax.ShapeDtypeStruct((2, width, rows), BF16), jax.ShapeDtypeStruct((2, rows, width), BF16)
    rows_a = blocks * half + half
    own_a, away_one, away_two, rest_a, later, inverse_factor, across, combined = call(
        leaf_first_kernel, (trailing, leaf_vectors, leaf_factors, inverse_factor),
        [shape(rows_a, width), shape(rows_a // 2, width), shape(rows_a // 2, width)]
        + [shape(blocks, width, width), shape(more, rows, width), shape(width, width), *split],
        [
            vmem(blocks, rows, width), vmem(rows, width), vmem(width, width), vmem(width, width), vmem(rows_a, width),
            sems(count * (rows // width) + 3),
        ],
        range(4),
    )
    there_a = [exchange(away_one, 1), exchange(away_two, 1)]

    chip_low, chip_high, chip_part = call(
        pack_kernel, (tree_vectors, tree_factors, *raw),
        (shape(2, *part_shape), shape(2, *part_shape), shape(*part_shape)),
        [vmem(4, width, width), sems(4)], (),
    )
    plane_parts = [exchange(chip_part, 2 * r) for r in (3, 1, 2)]
    plane_parts = [plane_parts[1], plane_parts[2], plane_parts[0]]

    own_b, rest_b, *aways = call(
        leaf_second_kernel, (later, across, combined),
        [shape(more * half, width), shape(more, width, width)] + [shape(half, width)] * more,
        [vmem(width, width)], before=there_a,
    )
    theres = [exchange(away, 1) for away in aways]
    cols = count * quarter
    outs = call(
        core_kernel, (own_a, own_b, *there_a, *theres, chip_high),
        [shape(cols, width)] * 8 + [shape(half, width)],
        [vmem(count * half, width), vmem(count * half, width)],
    )
    sends, dones, gram_half = outs[:4], outs[4:8], outs[8]
    for level in (levels - 1, 1, 2, *range(3, levels - 1)):
        (gram_half,) = call(
            add_kernel, (gram_half, exchange(gram_half, 1 << level)), (shape(half, width),), chained=False
        )
    stack, held_part = call(
        gather_kernel, (chip_part, *plane_parts), (shape(3, *part_shape), shape(*part_shape)), work=1,
    )
    gots = around(sends)
    stack_there = exchange(stack, 1)
    parts = [exchange(held_part, 8)]
    for level in range(4, levels):
        short = 3 * quarter if level == levels - 1 else half + EXTRA
        (held_part,) = call(
            functools.partial(hold_kernel, level=level - 1), (held_part, parts[-1]), (shape(short, width),),
            chained=False,
        )
        parts.append(exchange(held_part, 1 << level))

    ready, held = call(
        prepare_kernel, (chip_low, stack, stack_there),
        (jax.ShapeDtypeStruct((4, 4, width, width), BF16), shape(2, *part_shape)),
    )
    (heads,) = call(sort_kernel, gots, (shape(4, cols, width),))
    head, send, plane_done = call(
        functools.partial(plane_kernel, level=3), (heads, ready),
        (shape(cols, width), shape(cols + 24, width), shape(4, cols, width)),
    )
    result = head
    for level in range(3, levels):
        part = parts[level - 3]
        operands = (head, result, send, exchange(send, 1 << level), held, part, exchange(part, 1))
        if level == levels - 1:
            sends = call(
                functools.partial(last_kernel, level=level), (*operands, plane_done),
                [shape(cols + quarter, width)] * 4, [vmem(4, cols, width)],
            )
        else:
            head, result, held, send = call(
                functools.partial(line_kernel, level=level), operands,
                [shape(cols, width), shape(cols, width), shape(*held.shape), shape(cols + 8, width)],
            )

    backs = around(sends)
    _, updated, basis = call(
        store_kernel, (rest_a, rest_b, inverse_factor), (shape(8, width), shape(rows, columns), shape(rows, width)),
        [vmem(width, width), sems(count + 1)], (), (1, 2),
    )
    (back,) = call(pass_kernel, (*backs, *dones, gram_half), (shape(4, cols + 2 * quarter, width),))
    there = exchange(back, 1)
    (updated,) = call(
        near_kernel, (*backs, *dones, updated), (shape(rows, columns),),
        [vmem(count, width, half), sems(count)], (8,), (0,), {9: 0},
    )
    return call(
        functools.partial(far_kernel, total=float(rows * devices)),
        (*backs, *dones, there, gram_half, inverse_factor, updated, basis),
        (shape(rows, columns), shape(rows, width), shape(width, width)),
        [vmem(width, width), vmem(width, width), vmem(count, width, half), vmem(width, width), vmem(width, width), sems(count + 2)],
        (11, 12), (0, 1, 2), {12: 0, 13: 1},
    )


def solution(mesh):
    in_specs = (
        P("rows", None),
        P("rows", None),
        P("rows", None),
        P("rows", None),
        P("rows", None),
        P(),
    )
    out_specs = (P("rows", None), P("rows", None), P())
    return jax.shard_map(body, mesh=mesh, in_specs=in_specs, out_specs=out_specs, check_vma=False)
```

```python
import functools
import jax
import jax.numpy as jnp
from jax import lax
from jax.experimental import pallas as pl
from jax.experimental.pallas import tpu as pltpu
from jax.sharding import PartitionSpec as P

F32 = jnp.float32
BF16 = jnp.bfloat16
EXTRA = 8
PARAMS = pltpu.CompilerParams(vmem_limit_bytes=20 * 1024 * 1024)
WHOLE = pl.BlockSpec(memory_space=pltpu.VMEM)
SCALAR = pl.BlockSpec(memory_space=pltpu.SMEM)
AWAY = pl.BlockSpec(memory_space=pltpu.HBM)


def halves(value):
    high = value.astype(BF16)
    return high, (value - high.astype(F32)).astype(BF16)


def times(left, right, sides):
    first = jnp.concatenate([left[0], left[0], left[1]], axis=sides[0])
    second = jnp.concatenate([right[0], right[1], right[0]], axis=sides[1])
    dims = ((sides[:1], sides[1:]), ((), ()))
    return lax.dot_general(first, second, dims, preferred_element_type=F32)


def plain(left, right):
    return times(left, right, (1, 0))


def by_transpose(left, right):
    return times(left, right, (1, 1))


def masks(size):
    row = lax.broadcasted_iota(jnp.int32, (size, size), 0)
    col = lax.broadcasted_iota(jnp.int32, (size, size), 1)
    return row, col


def diagonal_of(square):
    row, col = masks(square.shape[0])
    return jnp.sum(jnp.where(row == col, square, 0.0), axis=0, keepdims=True)


def pack_kernel(me_ref, *refs):
    sources, (low_ref, high_ref, part_ref), (buffer_ref, sems) = refs[:4], refs[4:7], refs[7:]
    copies = [pltpu.make_async_copy(source, buffer_ref.at[i], sems.at[i]) for i, source in enumerate(sources)]
    for copy in copies:
        copy.start()
    for copy in copies:
        copy.wait()
    core = me_ref[0] % 2
    half = buffer_ref.shape[1] // 2
    row, col = masks(half)
    both_vectors = by_core(core, buffer_ref[0], buffer_ref[2])
    both_factors = by_core(core, buffer_ref[1], buffer_ref[3])
    for vectors, factors, out_ref in zip(both_vectors, both_factors, (low_ref, high_ref)):
        first, second = factors[:half, :half], factors[half:, half:]
        square = jnp.where(row > col, first.T, jnp.where(row < col, second, 0.0))
        t_rows = jnp.concatenate([square, factors[:half, half:].T], axis=1)
        t_diagonal = jnp.concatenate([diagonal_of(first), diagonal_of(second)], axis=1)
        first, second = vectors[:half, :half], vectors[half:, half:]
        square = jnp.where(row <= col, first, second.T)
        v_rows = jnp.concatenate([square, vectors[:half, half:]], axis=1)
        v_diagonal = jnp.concatenate([diagonal_of(second)] * 2, axis=1)
        line = lax.broadcasted_iota(jnp.int32, (EXTRA, 2 * half), 0)
        diagonals = jnp.where(line == 0, t_diagonal, v_diagonal)
        for part in range(2):
            rows = slice(part * half // 2, (part + 1) * half // 2)
            out_ref[part, : half // 2] = t_rows[rows]
            out_ref[part, half // 2 : half // 2 + EXTRA] = diagonals
            out_ref[part, half // 2 + EXTRA :] = v_rows[rows]
    part_ref[...] = low_ref[core]


def unpack_factors(first, second):
    half = first.shape[1] // 2
    rows = jnp.concatenate([first[: half // 2], second[: half // 2]], axis=0)
    row, col = masks(half)
    square, corner = rows[:, :half], rows[:, half:]
    diagonal = first[half // 2 : half // 2 + 1]
    upper_left = jnp.where(row > col, square, jnp.where(row == col, diagonal[:, :half], 0.0))
    lower_right = jnp.where(row > col, square.T, jnp.where(row == col, diagonal[:, half:], 0.0))
    above = jnp.concatenate([upper_left, jnp.zeros_like(upper_left)], axis=1)
    return halves(jnp.concatenate([above, jnp.concatenate([corner, lower_right], axis=1)], axis=0))


def unpack_vectors(first, second):
    half = first.shape[1] // 2
    start = half // 2 + EXTRA
    rows = jnp.concatenate([first[start:], second[start:]], axis=0)
    row, col = masks(half)
    square, corner = rows[:, :half], rows[:, half:]
    diagonal = first[half // 2 + 1 : half // 2 + 2, :half]
    upper_left = jnp.where(row <= col, square, 0.0)
    lower_right = jnp.where(row < col, square.T, jnp.where(row == col, diagonal, 0.0))
    above = jnp.concatenate([upper_left, corner], axis=1)
    return halves(jnp.concatenate([above, jnp.concatenate([jnp.zeros_like(corner), lower_right], axis=1)], axis=0))


def unpack(first, second):
    return unpack_vectors(first, second), unpack_factors(first, second)


def by_core(core, mine, there):
    odd = core == 1
    return jnp.where(odd, there, mine), jnp.where(odd, mine, there)


def place(me):
    return (me >> 1) & 3


def by_place(me, parts, wanted):
    source = place(me) ^ wanted
    out = parts[0]
    for r in range(1, 4):
        out = jnp.where(source == r, parts[r], out)
    return out


def tree_node(low, high, reflector):
    vectors, factors = reflector
    node = by_transpose(halves(low + plain(halves(high), vectors)), factors)
    return low - node, high - by_transpose(halves(node), vectors)


def leaf_first_kernel(
    me_ref, trailing_hbm, vectors_hbm, factors_hbm, inverse_hbm,
    own_ref, away_one, away_two, rest_ref, later_ref, inverse_ref, across_ref, combined_ref,
    part_ref, vectors_ref, factors_ref, value_ref, away_ref, sems,
):
    count, rows, width = part_ref.shape
    copies = []

    def fetch(source, target):
        copies.append(pltpu.make_async_copy(source, target, sems.at[len(copies)]))
        copies[-1].start()
        return copies[-1]

    def fetch_part(b, target):
        cuts = [slice(c, c + width) for c in range(0, rows, width)]
        return [fetch(trailing_hbm.at[c, pl.ds(b * width, width)], target.at[c]) for c in cuts]

    first = [fetch(vectors_hbm, vectors_ref), fetch(factors_hbm, factors_ref)]
    parts = [fetch_part(b, part_ref.at[b]) for b in range(count)]
    last = [fetch_part(count + b, later_ref.at[b]) for b in range(later_ref.shape[0])]
    last.append([fetch(inverse_hbm, inverse_ref)])
    for copy in first:
        copy.wait()
    vectors = vectors_ref[...]
    across = halves(vectors.T)
    across_ref[0], across_ref[1] = across
    combined = halves(by_transpose(halves(vectors), halves(factors_ref[...])))
    combined_ref[0], combined_ref[1] = combined
    for b in range(count):
        for copy in parts[b]:
            copy.wait()
        leaf_block(me_ref, part_ref[b], across, combined, value_ref, rest_ref.at[b], own_ref, away_ref, b)
    panel = part_ref[0]
    value_ref[...] = plain(halves(panel.T), halves(panel))
    hand_over(me_ref, value_ref, own_ref, away_ref, count)
    cut = away_one.shape[0]
    away_one[...] = away_ref[:cut]
    away_two[...] = away_ref[cut:]
    for group in last:
        for copy in group:
            copy.wait()


def hand_over(me_ref, value_ref, own_ref, away_ref, slot):
    half = value_ref.shape[0] // 2
    core = me_ref[0] % 2
    target = slice(slot * half, (slot + 1) * half)
    own_ref[target] = value_ref[pl.ds(pl.multiple_of(core * half, half), half)]
    away_ref[target] = value_ref[pl.ds(pl.multiple_of((1 - core) * half, half), half)]


def leaf_block(me_ref, part, across, combined, value_ref, rest_ref, own_ref, away_ref, slot):
    width = value_ref.shape[0]
    out = part - plain(combined, halves(plain(across, halves(part))))
    rest_ref[...] = out[width:]
    value_ref[...] = out[:width].T
    hand_over(me_ref, value_ref, own_ref, away_ref, slot)


def leaf_second_kernel(me_ref, later_ref, across_ref, combined_ref, own_ref, rest_ref, *refs):
    aways, value_ref = refs[:-1], refs[-1]
    half = value_ref.shape[0] // 2
    across = across_ref[0], across_ref[1]
    combined = combined_ref[0], combined_ref[1]
    for b in range(later_ref.shape[0]):
        own_b = own_ref.at[pl.ds(b * half, half)]
        leaf_block(me_ref, later_ref[b], across, combined, value_ref, rest_ref.at[b], own_b, aways[b], 0)


def store_kernel(me_ref, first_ref, second_ref, inverse_ref, mark_ref, updated_hbm, basis_hbm, basis_ref, sems):
    count, width = first_ref.shape[:2]
    copies = []
    for b in range(count + second_ref.shape[0]):
        source = first_ref.at[b] if b < count else second_ref.at[b - count]
        target = updated_hbm.at[pl.ds(width, width), pl.ds(b * width, width)]
        copies.append(pltpu.make_async_copy(source, target, sems.at[b]))
        copies[-1].start()
    basis_ref[...] = plain(halves(first_ref[0]), halves(inverse_ref[...]))
    copies.append(pltpu.make_async_copy(basis_ref, basis_hbm.at[pl.ds(width, width)], sems.at[len(copies)]))
    mark_ref[...] = jnp.zeros_like(mark_ref)
    copies[-1].start()
    for copy in copies:
        copy.wait()


def core_kernel(
    me_ref, own_a_ref, own_b_ref, one_ref, two_ref, *refs
):
    more = len(refs) - 12
    there_bs, packed_ref = refs[:more], refs[more]
    sends, dones, (gram_ref, low_ref, high_ref) = refs[more + 1 : more + 5], refs[more + 5 : more + 9], refs[more + 9 :]
    me = me_ref[0]
    width = own_a_ref.shape[1]
    half = width // 2
    quarter = half // 4
    cut = own_a_ref.shape[0] - half
    count = cut // half + len(there_bs)
    odd = me % 2 == 1
    there_a = jnp.concatenate([one_ref[...], two_ref[...]], axis=0)
    gram_ref[...] = own_a_ref[cut:] + there_a[cut:]
    mine = jnp.concatenate([own_a_ref[:cut], own_b_ref[...]], axis=0)
    there = jnp.concatenate([there_a[:cut]] + [ref[...] for ref in there_bs], axis=0)
    low = jnp.where(odd, there, mine)
    high = jnp.where(odd, mine, there)
    low, high = tree_node(low, high, unpack(packed_ref[0], packed_ref[1]))
    low_ref[...] = low
    high_ref[...] = high
    for r in range(4):
        start = (place(me) ^ r) * quarter
        for b in range(count):
            source = pl.ds(pl.multiple_of(b * half + start, quarter), quarter)
            target = slice(b * quarter, (b + 1) * quarter)
            sends[r][target] = low_ref[source]
            dones[r][target] = high_ref[source]
        if sends[r].shape[0] > count * quarter:
            sends[r][count * quarter :] = jnp.zeros_like(sends[r][count * quarter :])


def gather_kernel(me_ref, *refs):
    parts, (stack_ref, held_ref) = refs[:4], refs[4:]
    for r in range(1, 4):
        stack_ref[r - 1] = parts[r][...]
    held_ref[...] = by_place(me_ref[0], [ref[...] for ref in parts], 0)


def hold_kernel(me_ref, held_ref, part_ref, out_ref, *, level):
    rows = slice(0, out_ref.shape[0])
    out_ref[...] = jnp.where((me_ref[0] >> level) % 2 == 1, part_ref[rows], held_ref[rows])


def sort_kernel(me_ref, *refs):
    parts = [ref[: refs[4].shape[1]] for ref in refs[:4]]
    for j in range(4):
        refs[4][j] = by_place(me_ref[0], parts, j)


def add_kernel(me_ref, first_ref, second_ref, out_ref):
    out_ref[...] = first_ref[...] + second_ref[...]


def fill(send_ref, value):
    cols = value.shape[0]
    send_ref[:cols] = value
    if send_ref.shape[0] > cols:
        send_ref[cols:] = jnp.zeros_like(send_ref[cols:])


def prepare_kernel(me_ref, packed_ref, stack_ref, stack_there_ref, ready_ref, held_ref):
    me = me_ref[0]
    pairs = [(packed_ref[0], packed_ref[1])]
    pairs += [by_core(me % 2, stack_ref[r], stack_there_ref[r]) for r in range(3)]
    firsts, seconds = [pair[0] for pair in pairs], [pair[1] for pair in pairs]
    pairs = [(by_place(me, firsts, j), by_place(me, seconds, j)) for j in range(4)]
    held_ref[0], held_ref[1] = pairs[0]
    for j in range(4):
        (ready_ref[j, 0], ready_ref[j, 1]), (ready_ref[j, 2], ready_ref[j, 3]) = unpack(*pairs[j])


def plane_kernel(me_ref, heads_ref, ready_ref, head_ref, send_ref, done_ref, *, level):
    reflectors = [((ready_ref[j, 0], ready_ref[j, 1]), (ready_ref[j, 2], ready_ref[j, 3])) for j in range(4)]
    heads = [heads_ref[j] for j in range(4)]
    heads[0], heads[1] = tree_node(heads[0], heads[1], reflectors[1])
    heads[2], heads[3] = tree_node(heads[2], heads[3], reflectors[3])
    heads[0], heads[2] = tree_node(heads[0], heads[2], reflectors[2])
    for j in range(4):
        done_ref[j] = heads[j]
    head_ref[...] = heads[0]
    upper = (me_ref[0] >> level) % 2 == 1
    fill(send_ref, jnp.where(upper, plain(halves(heads[0]), reflectors[0][0]), heads[0]))


def line_node(me_ref, head_ref, result_ref, mine_ref, there_ref, held_ref, part_ref, part_there_ref, level):
    me = me_ref[0]
    cols = head_ref.shape[0]
    upper = (me >> level) % 2 == 1
    held = held_ref[0], held_ref[1]
    others = by_core(me % 2, part_ref[...], part_there_ref[...])
    whole = held[0].shape == others[0].shape
    need = held[0].shape[1] // 4 + EXTRA
    node = [jnp.where(upper, a[:need], b[:need]) for a, b in zip(held, others)]
    following = [jnp.where(upper, b, a) for a, b in zip(held, others)] if whole else None
    head, there = head_ref[...], there_ref[:cols]
    coeffs = by_transpose(halves(mine_ref[:cols] + there), unpack_factors(*node))
    low = jnp.where(upper, there, head) - coeffs
    plane = me >> 3
    below = (1 << (level - 2)) - 1
    second = (plane & below) == (1 << (level - 3))
    high = head - by_transpose(halves(coeffs), unpack_vectors(*held))
    return low, jnp.where(second, high, result_ref[...]), following


def line_kernel(me_ref, *refs, level):
    head_out, result_out, held_out, send_ref = refs[7:]
    low, result, following = line_node(me_ref, *refs[:7], level)
    ahead = (me_ref[0] >> (level + 1)) % 2 == 1
    head_out[...] = low
    result_out[...] = result
    held_out[0], held_out[1] = following
    fill(send_ref, jnp.where(ahead, plain(halves(low), unpack_vectors(*following)), low))


def last_kernel(me_ref, *refs, level):
    done_ref, sends, all_ref = refs[7], refs[8:12], refs[12]
    me = me_ref[0]
    low, result, _ = line_node(me_ref, *refs[:7], level)
    cols = low.shape[0]
    all_ref[0] = jnp.where((me >> 3) == 0, low, result)
    for j in range(1, 4):
        all_ref[j] = done_ref[j]
    for r in range(4):
        sends[r][:cols] = all_ref[place(me) ^ r]
        sends[r][cols:] = low[: sends[r].shape[0] - cols]


def pass_kernel(me_ref, *refs):
    backs, dones, (gram_ref, out_ref) = refs[:4], refs[4:8], refs[8:]
    odd = me_ref[0] % 2 == 1
    cols, rows = dones[0].shape[0], backs[0].shape[0]
    quarter = rows - cols
    for r in range(4):
        out_ref[r, :cols] = jnp.where(odd, backs[r][:cols], dones[r][...])
        out_ref[r, cols:rows] = backs[r][cols:rows]
        out_ref[r, rows:] = gram_ref[r * quarter : (r + 1) * quarter]


def near_kernel(me_ref, *refs):
    backs, dones, (_, updated_hbm, out_ref, sems) = refs[:4], refs[4:8], refs[8:]
    count, width, half = out_ref.shape
    quarter = half // 4
    me = me_ref[0]
    core = me % 2
    odd = core == 1
    copies = []
    for b in range(count):
        rows = slice(b * quarter, (b + 1) * quarter)
        pieces = [jnp.where(odd, dones[r][rows], backs[r][rows]) for r in range(4)]
        out_ref[b] = jnp.concatenate([by_place(me, pieces, j) for j in range(4)], axis=0).T
        columns = pl.ds(pl.multiple_of(b * width + core * half, half), half)
        copies.append(pltpu.make_async_copy(out_ref.at[b], updated_hbm.at[pl.ds(0, width), columns], sems.at[b]))
        copies[-1].start()
    for copy in copies:
        copy.wait()


def far_kernel(me_ref, *refs, total):
    backs, dones = refs[:4], refs[4:8]
    there_ref, half_ref, inverse_ref, _, _, updated_hbm, basis_hbm, gram_hbm = refs[8:16]
    panel_ref, sum_ref, out_ref, basis_ref, gram_ref, sems = refs[16:]
    count, width, half = out_ref.shape
    quarter = half // 4
    cols = count * quarter
    me = me_ref[0]
    core = me % 2
    odd = core == 1
    copies = []

    def put(source, target):
        copies.append(pltpu.make_async_copy(source, target, sems.at[len(copies)]))
        copies[-1].start()

    for b in range(count):
        rows = slice(b * quarter, (b + 1) * quarter)
        pieces = [there_ref[r, rows] for r in range(4)]
        far = jnp.concatenate([by_place(me, pieces, j) for j in range(4)], axis=0).T
        out_ref[b] = far
        columns = pl.ds(pl.multiple_of(b * width + (1 - core) * half, half), half)
        put(out_ref.at[b], updated_hbm.at[pl.ds(0, width), columns])
        if b == 0:
            pieces = [jnp.where(odd, dones[r][rows], backs[r][rows]) for r in range(4)]
            near = jnp.concatenate([by_place(me, pieces, j) for j in range(4)], axis=0).T
            head = jnp.concatenate(by_core(core, near, far), axis=1)
            basis = plain(halves(head), halves(inverse_ref[...]))
            basis_ref[...] = jnp.where(me == 0, 0.0, basis)
            put(basis_ref, basis_hbm.at[pl.ds(0, width)])

    def target(part, r):
        return pl.ds(pl.multiple_of(part * half + (place(me) ^ r) * quarter, quarter), quarter)

    for r in range(4):
        panel_ref[target(core, r)] = backs[r][cols : cols + quarter]
        panel_ref[target(1 - core, r)] = there_ref[r, cols : cols + quarter]
        rows = pl.ds(pl.multiple_of((1 - core) * half + r * quarter, quarter), quarter)
        sum_ref[rows] = there_ref[r, cols + quarter :]
    sum_ref[pl.ds(pl.multiple_of(core * half, half), half)] = half_ref[...]
    panel = halves(panel_ref[...])
    gram_ref[...] = (sum_ref[...] - by_transpose(panel, panel)) / total
    put(gram_ref, gram_hbm)
    for copy in copies:
        copy.wait()


def body(trailing, leaf_vectors, leaf_factors, tree_vectors, tree_factors, inverse_factor):
    rows, columns = trailing.shape
    width = leaf_vectors.shape[1]
    half = width // 2
    quarter = half // 4
    count = columns // width
    devices = lax.axis_size("rows")
    levels = devices.bit_length() - 1
    me = lax.axis_index("rows").astype(jnp.int32)
    me_array = me.reshape(1)
    part_shape = (half + EXTRA, width)
    latest = []

    def exchange(value, shift):
        return lax.ppermute(value, "rows", [(i, i ^ shift) for i in range(devices)])

    def among(value, shift, member):
        return lax.ppermute(value, "rows", [(i, i ^ shift if member(i) else i) for i in range(devices)])

    def around(values):
        there = [exchange(values[r], 2 * r) for r in (3, 1, 2)]
        return [values[0], there[1], there[2], there[0]]

    def shape(*dims):
        return jax.ShapeDtypeStruct(dims, F32)

    def vmem(*dims):
        return pltpu.VMEM(dims, F32)

    def sems(number):
        return pltpu.SemaphoreType.DMA((number,))

    def call(kernel, operands, outs, scratch=(), away_in=(), away_out=(), aliases=(), before=(), work=1, chained=True):
        number = len(operands)
        operands = [pltpu.with_memory_space_constraint(x, pltpu.HBM) if i in away_in else x for i, x in enumerate(operands)]
        outs = [(pltpu.HBM if i in away_out else pltpu.VMEM)(x.shape, x.dtype) for i, x in enumerate(outs)]
        unused = [*latest, *before] if chained else []

        def kernel_on(*refs):
            kernel(*refs[: number + 1], *refs[number + 1 + len(unused) :])

        values = pl.pallas_call(
            kernel_on,
            out_shape=tuple(outs),
            in_specs=[SCALAR]
            + [AWAY if i in away_in else WHOLE for i in range(number)]
            + [pl.BlockSpec(memory_space=pl.ANY)] * len(unused),
            out_specs=tuple(AWAY if i in away_out else WHOLE for i in range(len(outs))),
            scratch_shapes=list(scratch),
            input_output_aliases=dict(aliases),
            compiler_params=PARAMS,
            cost_estimate=pl.CostEstimate(flops=work, bytes_accessed=1, transcendentals=0),
        )(me_array, *operands, *unused)
        if chained and 0 not in away_out:
            latest[:] = values[:1]
        return values

    raw = [exchange(tree_vectors, 1), exchange(tree_factors, 1)]
    blocks = count // 2
    more = count - blocks
    split = jax.ShapeDtypeStruct((2, width, rows), BF16), jax.ShapeDtypeStruct((2, rows, width), BF16)
    rows_a = blocks * half + half
    own_a, away_one, away_two, rest_a, later, inverse_factor, across, combined = call(
        leaf_first_kernel, (trailing, leaf_vectors, leaf_factors, inverse_factor),
        [shape(rows_a, width), shape(rows_a // 2, width), shape(rows_a // 2, width)]
        + [shape(blocks, width, width), shape(more, rows, width), shape(width, width), *split],
        [
            vmem(blocks, rows, width), vmem(rows, width), vmem(width, width), vmem(width, width), vmem(rows_a, width),
            sems(count * (rows // width) + 3),
        ],
        range(4),
    )
    there_a = [exchange(away_one, 1), exchange(away_two, 1)]

    chip_low, chip_high, chip_part = call(
        pack_kernel, (tree_vectors, tree_factors, *raw),
        (shape(2, *part_shape), shape(2, *part_shape), shape(*part_shape)),
        [vmem(4, width, width), sems(4)], (),
    )
    plane_parts = [exchange(chip_part, 2 * r) for r in (3, 1, 2)]
    plane_parts = [plane_parts[1], plane_parts[2], plane_parts[0]]

    own_b, rest_b, *aways = call(
        leaf_second_kernel, (later, across, combined),
        [shape(more * half, width), shape(more, width, width)] + [shape(half, width)] * more,
        [vmem(width, width)], before=there_a,
    )
    theres = [exchange(away, 1) for away in aways]
    cols = count * quarter
    outs = call(
        core_kernel, (own_a, own_b, *there_a, *theres, chip_high),
        [shape(cols, width)] * 3 + [shape(cols + 8, width)] + [shape(cols, width)] * 4 + [shape(half, width)],
        [vmem(count * half, width), vmem(count * half, width)],
    )
    sends, dones, gram_half = outs[:4], outs[4:8], outs[8]
    for level in (levels - 1, 1, 2, *range(3, levels - 1)):
        (gram_half,) = call(
            add_kernel, (gram_half, exchange(gram_half, 1 << level)), (shape(half, width),), chained=False
        )
    stack, held_part = call(
        gather_kernel, (chip_part, *plane_parts), (shape(3, *part_shape), shape(*part_shape)), work=1,
    )
    gots = around(sends)
    stack_there = exchange(stack, 1)
    parts = [exchange(held_part, 8)]
    for level in range(4, levels):
        short = half // 2 + EXTRA if level == levels - 1 else half + EXTRA
        (held_part,) = call(
            functools.partial(hold_kernel, level=level - 1), (held_part, parts[-1]), (shape(short, width),),
            chained=False,
        )
        parts.append(exchange(held_part, 1 << level))

    ready, held = call(
        prepare_kernel, (chip_low, stack, stack_there),
        (jax.ShapeDtypeStruct((4, 4, width, width), BF16), shape(2, *part_shape)),
    )
    (heads,) = call(sort_kernel, gots, (shape(4, cols, width),))
    head, send, plane_done = call(
        functools.partial(plane_kernel, level=3), (heads, ready),
        (shape(cols, width), shape(cols + 24, width), shape(4, cols, width)),
    )
    result = head
    for level in range(3, levels):
        part = parts[level - 3]
        operands = (head, result, send, exchange(send, 1 << level), held, part, exchange(part, 1))
        if level == levels - 1:
            sends = call(
                functools.partial(last_kernel, level=level), (*operands, plane_done),
                [shape(cols + quarter, width)] * 3 + [shape(cols + quarter + 8, width)], [vmem(4, cols, width)],
            )
        else:
            head, result, held, send = call(
                functools.partial(line_kernel, level=level), operands,
                [shape(cols, width), shape(cols, width), shape(*held.shape), shape(cols + 0, width)],
            )

    backs = around(sends)
    _, updated, basis = call(
        store_kernel, (rest_a, rest_b, inverse_factor), (shape(8, width), shape(rows, columns), shape(rows, width)),
        [vmem(width, width), sems(count + 1)], (), (1, 2),
    )
    (back,) = call(pass_kernel, (*backs, *dones, gram_half), (shape(4, cols + 2 * quarter, width),))
    there = exchange(back, 1)
    (updated,) = call(
        near_kernel, (*backs, *dones, updated), (shape(rows, columns),),
        [vmem(count, width, half), sems(count)], (8,), (0,), {9: 0},
    )
    return call(
        functools.partial(far_kernel, total=float(rows * devices)),
        (*backs, *dones, there, gram_half, inverse_factor, updated, basis),
        (shape(rows, columns), shape(rows, width), shape(width, width)),
        [vmem(width, width), vmem(width, width), vmem(count, width, half), vmem(width, width), vmem(width, width), sems(count + 2)],
        (11, 12), (0, 1, 2), {12: 0, 13: 1},
    )


def solution(mesh):
    in_specs = (
        P("rows", None),
        P("rows", None),
        P("rows", None),
        P("rows", None),
        P("rows", None),
        P(),
    )
    out_specs = (P("rows", None), P("rows", None), P())
    return jax.shard_map(body, mesh=mesh, in_specs=in_specs, out_specs=out_specs, check_vma=False)
```

```python
import functools
import jax
import jax.numpy as jnp
from jax import lax
from jax.experimental import pallas as pl
from jax.experimental.pallas import tpu as pltpu
from jax.sharding import PartitionSpec as P

F32 = jnp.float32
BF16 = jnp.bfloat16
EXTRA = 8
PARAMS = pltpu.CompilerParams(vmem_limit_bytes=20 * 1024 * 1024)
WHOLE = pl.BlockSpec(memory_space=pltpu.VMEM)
SCALAR = pl.BlockSpec(memory_space=pltpu.SMEM)
AWAY = pl.BlockSpec(memory_space=pltpu.HBM)


def halves(value):
    high = value.astype(BF16)
    return high, (value - high.astype(F32)).astype(BF16)


def times(left, right, sides):
    first = jnp.concatenate([left[0], left[0], left[1]], axis=sides[0])
    second = jnp.concatenate([right[0], right[1], right[0]], axis=sides[1])
    dims = ((sides[:1], sides[1:]), ((), ()))
    return lax.dot_general(first, second, dims, preferred_element_type=F32)


def plain(left, right):
    return times(left, right, (1, 0))


def by_transpose(left, right):
    return times(left, right, (1, 1))


def masks(size):
    row = lax.broadcasted_iota(jnp.int32, (size, size), 0)
    col = lax.broadcasted_iota(jnp.int32, (size, size), 1)
    return row, col


def diagonal_of(square):
    row, col = masks(square.shape[0])
    return jnp.sum(jnp.where(row == col, square, 0.0), axis=0, keepdims=True)


def pack_kernel(me_ref, *refs):
    sources, (low_ref, high_ref, part_ref), (buffer_ref, sems) = refs[:4], refs[4:7], refs[7:]
    copies = [pltpu.make_async_copy(source, buffer_ref.at[i], sems.at[i]) for i, source in enumerate(sources)]
    for copy in copies:
        copy.start()
    for copy in copies:
        copy.wait()
    core = me_ref[0] % 2
    half = buffer_ref.shape[1] // 2
    row, col = masks(half)
    both_vectors = by_core(core, buffer_ref[0], buffer_ref[2])
    both_factors = by_core(core, buffer_ref[1], buffer_ref[3])
    for vectors, factors, out_ref in zip(both_vectors, both_factors, (low_ref, high_ref)):
        first, second = factors[:half, :half], factors[half:, half:]
        square = jnp.where(row > col, first.T, jnp.where(row < col, second, 0.0))
        t_rows = jnp.concatenate([square, factors[:half, half:].T], axis=1)
        t_diagonal = jnp.concatenate([diagonal_of(first), diagonal_of(second)], axis=1)
        first, second = vectors[:half, :half], vectors[half:, half:]
        square = jnp.where(row <= col, first, second.T)
        v_rows = jnp.concatenate([square, vectors[:half, half:]], axis=1)
        v_diagonal = jnp.concatenate([diagonal_of(second)] * 2, axis=1)
        line = lax.broadcasted_iota(jnp.int32, (EXTRA, 2 * half), 0)
        diagonals = jnp.where(line == 0, t_diagonal, v_diagonal)
        for part in range(2):
            rows = slice(part * half // 2, (part + 1) * half // 2)
            out_ref[part, : half // 2] = t_rows[rows]
            out_ref[part, half // 2 : half // 2 + EXTRA] = diagonals
            out_ref[part, half // 2 + EXTRA :] = v_rows[rows]
    part_ref[...] = low_ref[core]


def unpack_factors(first, second):
    half = first.shape[1] // 2
    rows = jnp.concatenate([first[: half // 2], second[: half // 2]], axis=0)
    row, col = masks(half)
    square, corner = rows[:, :half], rows[:, half:]
    diagonal = first[half // 2 : half // 2 + 1]
    upper_left = jnp.where(row > col, square, jnp.where(row == col, diagonal[:, :half], 0.0))
    lower_right = jnp.where(row > col, square.T, jnp.where(row == col, diagonal[:, half:], 0.0))
    above = jnp.concatenate([upper_left, jnp.zeros_like(upper_left)], axis=1)
    return halves(jnp.concatenate([above, jnp.concatenate([corner, lower_right], axis=1)], axis=0))


def unpack_vectors(first, second):
    half = first.shape[1] // 2
    start = half // 2 + EXTRA
    rows = jnp.concatenate([first[start:], second[start:]], axis=0)
    row, col = masks(half)
    square, corner = rows[:, :half], rows[:, half:]
    diagonal = first[half // 2 + 1 : half // 2 + 2, :half]
    upper_left = jnp.where(row <= col, square, 0.0)
    lower_right = jnp.where(row < col, square.T, jnp.where(row == col, diagonal, 0.0))
    above = jnp.concatenate([upper_left, corner], axis=1)
    return halves(jnp.concatenate([above, jnp.concatenate([jnp.zeros_like(corner), lower_right], axis=1)], axis=0))


def unpack(first, second):
    return unpack_vectors(first, second), unpack_factors(first, second)


def by_core(core, mine, there):
    odd = core == 1
    return jnp.where(odd, there, mine), jnp.where(odd, mine, there)


def place(me):
    return (me >> 1) & 3


def by_place(me, parts, wanted):
    source = place(me) ^ wanted
    out = parts[0]
    for r in range(1, 4):
        out = jnp.where(source == r, parts[r], out)
    return out


def tree_node(low, high, reflector):
    vectors, factors = reflector
    node = by_transpose(halves(low + plain(halves(high), vectors)), factors)
    return low - node, high - by_transpose(halves(node), vectors)


def leaf_first_kernel(
    me_ref, trailing_hbm, vectors_hbm, factors_hbm, inverse_hbm,
    own_ref, away_one, away_two, rest_ref, later_ref, inverse_ref, across_ref, combined_ref,
    part_ref, vectors_ref, factors_ref, value_ref, away_ref, sems,
):
    count, rows, width = part_ref.shape
    copies = []

    def fetch(source, target):
        copies.append(pltpu.make_async_copy(source, target, sems.at[len(copies)]))
        copies[-1].start()
        return copies[-1]

    def fetch_part(b, target):
        cuts = [slice(c, c + width) for c in range(0, rows, width)]
        return [fetch(trailing_hbm.at[c, pl.ds(b * width, width)], target.at[c]) for c in cuts]

    first = [fetch(vectors_hbm, vectors_ref), fetch(factors_hbm, factors_ref)]
    parts = [fetch_part(b, part_ref.at[b]) for b in range(count)]
    for copy in first:
        copy.wait()
    last = [fetch_part(count + b, later_ref.at[b]) for b in range(later_ref.shape[0])]
    last.append([fetch(inverse_hbm, inverse_ref)])
    vectors = vectors_ref[...]
    across = halves(vectors.T)
    across_ref[0], across_ref[1] = across
    combined = halves(by_transpose(halves(vectors), halves(factors_ref[...])))
    combined_ref[0], combined_ref[1] = combined
    for b in range(count):
        for copy in parts[b]:
            copy.wait()
        leaf_block(me_ref, part_ref[b], across, combined, value_ref, rest_ref.at[b], own_ref, away_ref, b)
    panel = part_ref[0]
    value_ref[...] = plain(halves(panel.T), halves(panel))
    hand_over(me_ref, value_ref, own_ref, away_ref, count)
    cut = away_one.shape[0]
    away_one[...] = away_ref[:cut]
    away_two[...] = away_ref[cut:]
    for group in last:
        for copy in group:
            copy.wait()


def hand_over(me_ref, value_ref, own_ref, away_ref, slot):
    half = value_ref.shape[0] // 2
    core = me_ref[0] % 2
    target = slice(slot * half, (slot + 1) * half)
    own_ref[target] = value_ref[pl.ds(pl.multiple_of(core * half, half), half)]
    away_ref[target] = value_ref[pl.ds(pl.multiple_of((1 - core) * half, half), half)]


def leaf_block(me_ref, part, across, combined, value_ref, rest_ref, own_ref, away_ref, slot):
    width = value_ref.shape[0]
    out = part - plain(combined, halves(plain(across, halves(part))))
    rest_ref[...] = out[width:]
    value_ref[...] = out[:width].T
    hand_over(me_ref, value_ref, own_ref, away_ref, slot)


def leaf_second_kernel(me_ref, later_ref, across_ref, combined_ref, own_ref, rest_ref, *refs):
    aways, value_ref = refs[:-1], refs[-1]
    half = value_ref.shape[0] // 2
    across = across_ref[0], across_ref[1]
    combined = combined_ref[0], combined_ref[1]
    for b in range(later_ref.shape[0]):
        own_b = own_ref.at[pl.ds(b * half, half)]
        leaf_block(me_ref, later_ref[b], across, combined, value_ref, rest_ref.at[b], own_b, aways[b], 0)


def store_kernel(me_ref, first_ref, second_ref, inverse_ref, mark_ref, updated_hbm, basis_hbm, basis_ref, sems):
    count, width = first_ref.shape[:2]
    copies = []
    for b in range(count + second_ref.shape[0]):
        source = first_ref.at[b] if b < count else second_ref.at[b - count]
        target = updated_hbm.at[pl.ds(width, width), pl.ds(b * width, width)]
        copies.append(pltpu.make_async_copy(source, target, sems.at[b]))
        copies[-1].start()
    basis_ref[...] = plain(halves(first_ref[0]), halves(inverse_ref[...]))
    copies.append(pltpu.make_async_copy(basis_ref, basis_hbm.at[pl.ds(width, width)], sems.at[len(copies)]))
    mark_ref[...] = jnp.zeros_like(mark_ref)
    copies[-1].start()
    for copy in copies:
        copy.wait()


def core_kernel(
    me_ref, own_a_ref, own_b_ref, one_ref, two_ref, *refs
):
    more = len(refs) - 12
    there_bs, packed_ref = refs[:more], refs[more]
    sends, dones, (gram_ref, low_ref, high_ref) = refs[more + 1 : more + 5], refs[more + 5 : more + 9], refs[more + 9 :]
    me = me_ref[0]
    width = own_a_ref.shape[1]
    half = width // 2
    quarter = half // 4
    cut = own_a_ref.shape[0] - half
    count = cut // half + len(there_bs)
    odd = me % 2 == 1
    there_a = jnp.concatenate([one_ref[...], two_ref[...]], axis=0)
    gram_ref[...] = own_a_ref[cut:] + there_a[cut:]
    mine = jnp.concatenate([own_a_ref[:cut], own_b_ref[...]], axis=0)
    there = jnp.concatenate([there_a[:cut]] + [ref[...] for ref in there_bs], axis=0)
    low = jnp.where(odd, there, mine)
    high = jnp.where(odd, mine, there)
    low, high = tree_node(low, high, unpack(packed_ref[0], packed_ref[1]))
    low_ref[...] = low
    high_ref[...] = high
    for r in range(4):
        start = (place(me) ^ r) * quarter
        for b in range(count):
            source = pl.ds(pl.multiple_of(b * half + start, quarter), quarter)
            target = slice(b * quarter, (b + 1) * quarter)
            sends[r][target] = low_ref[source]
            dones[r][target] = high_ref[source]
        if sends[r].shape[0] > count * quarter:
            sends[r][count * quarter :] = jnp.zeros_like(sends[r][count * quarter :])


def gather_kernel(me_ref, *refs):
    parts, (stack_ref, held_ref) = refs[:4], refs[4:]
    for r in range(1, 4):
        stack_ref[r - 1] = parts[r][...]
    held_ref[...] = by_place(me_ref[0], [ref[...] for ref in parts], 0)


def hold_kernel(me_ref, held_ref, part_ref, out_ref, *, level):
    rows = slice(0, out_ref.shape[0])
    out_ref[...] = jnp.where((me_ref[0] >> level) % 2 == 1, part_ref[rows], held_ref[rows])


def sort_kernel(me_ref, *refs):
    parts = [ref[: refs[4].shape[1]] for ref in refs[:4]]
    for j in range(4):
        refs[4][j] = by_place(me_ref[0], parts, j)


def add_kernel(me_ref, first_ref, second_ref, out_ref):
    out_ref[...] = first_ref[...] + second_ref[...]


def fill(send_ref, value):
    cols = value.shape[0]
    send_ref[:cols] = value
    if send_ref.shape[0] > cols:
        send_ref[cols:] = jnp.zeros_like(send_ref[cols:])


def prepare_kernel(me_ref, packed_ref, stack_ref, stack_there_ref, ready_ref, held_ref):
    me = me_ref[0]
    pairs = [(packed_ref[0], packed_ref[1])]
    pairs += [by_core(me % 2, stack_ref[r], stack_there_ref[r]) for r in range(3)]
    firsts, seconds = [pair[0] for pair in pairs], [pair[1] for pair in pairs]
    pairs = [(by_place(me, firsts, j), by_place(me, seconds, j)) for j in range(4)]
    held_ref[0], held_ref[1] = pairs[0]
    for j in range(4):
        (ready_ref[j, 0], ready_ref[j, 1]), (ready_ref[j, 2], ready_ref[j, 3]) = unpack(*pairs[j])


def plane_kernel(me_ref, heads_ref, ready_ref, head_ref, send_ref, done_ref, *, level):
    reflectors = [((ready_ref[j, 0], ready_ref[j, 1]), (ready_ref[j, 2], ready_ref[j, 3])) for j in range(4)]
    heads = [heads_ref[j] for j in range(4)]
    heads[0], heads[1] = tree_node(heads[0], heads[1], reflectors[1])
    heads[2], heads[3] = tree_node(heads[2], heads[3], reflectors[3])
    heads[0], heads[2] = tree_node(heads[0], heads[2], reflectors[2])
    for j in range(4):
        done_ref[j] = heads[j]
    head_ref[...] = heads[0]
    upper = (me_ref[0] >> level) % 2 == 1
    fill(send_ref, jnp.where(upper, plain(halves(heads[0]), reflectors[0][0]), heads[0]))


def line_node(me_ref, head_ref, result_ref, mine_ref, there_ref, held_ref, part_ref, part_there_ref, level):
    me = me_ref[0]
    cols = head_ref.shape[0]
    upper = (me >> level) % 2 == 1
    held = held_ref[0], held_ref[1]
    others = by_core(me % 2, part_ref[...], part_there_ref[...])
    whole = held[0].shape == others[0].shape
    need = held[0].shape[1] // 4 + EXTRA
    node = [jnp.where(upper, a[:need], b[:need]) for a, b in zip(held, others)]
    following = [jnp.where(upper, b, a) for a, b in zip(held, others)] if whole else None
    head, there = head_ref[...], there_ref[:cols]
    coeffs = by_transpose(halves(mine_ref[:cols] + there), unpack_factors(*node))
    low = jnp.where(upper, there, head) - coeffs
    plane = me >> 3
    below = (1 << (level - 2)) - 1
    second = (plane & below) == (1 << (level - 3))
    high = head - by_transpose(halves(coeffs), unpack_vectors(*held))
    return low, jnp.where(second, high, result_ref[...]), following


def line_kernel(me_ref, *refs, level):
    head_out, result_out, held_out, send_ref = refs[7:]
    low, result, following = line_node(me_ref, *refs[:7], level)
    ahead = (me_ref[0] >> (level + 1)) % 2 == 1
    head_out[...] = low
    result_out[...] = result
    held_out[0], held_out[1] = following
    fill(send_ref, jnp.where(ahead, plain(halves(low), unpack_vectors(*following)), low))


def last_kernel(me_ref, *refs, level):
    done_ref, sends, all_ref = refs[7], refs[8:12], refs[12]
    me = me_ref[0]
    low, result, _ = line_node(me_ref, *refs[:7], level)
    cols = low.shape[0]
    all_ref[0] = jnp.where((me >> 3) == 0, low, result)
    for j in range(1, 4):
        all_ref[j] = done_ref[j]
    for r in range(4):
        sends[r][:cols] = all_ref[place(me) ^ r]
        sends[r][cols:] = low[: sends[r].shape[0] - cols]


def pass_kernel(me_ref, *refs):
    backs, dones, out_ref = refs[:4], refs[4:8], refs[8]
    odd = me_ref[0] % 2 == 1
    cols, rows = dones[0].shape[0], out_ref.shape[1]
    for r in range(4):
        out_ref[r, :cols] = jnp.where(odd, backs[r][:cols], dones[r][...])
        out_ref[r, cols:] = backs[r][cols:rows]


def near_kernel(me_ref, *refs):
    backs, dones, (_, updated_hbm, out_ref, sems) = refs[:4], refs[4:8], refs[8:]
    count, width, half = out_ref.shape
    quarter = half // 4
    me = me_ref[0]
    core = me % 2
    odd = core == 1
    copies = []
    for b in range(count):
        rows = slice(b * quarter, (b + 1) * quarter)
        pieces = [jnp.where(odd, dones[r][rows], backs[r][rows]) for r in range(4)]
        out_ref[b] = jnp.concatenate([by_place(me, pieces, j) for j in range(4)], axis=0).T
        columns = pl.ds(pl.multiple_of(b * width + core * half, half), half)
        copies.append(pltpu.make_async_copy(out_ref.at[b], updated_hbm.at[pl.ds(0, width), columns], sems.at[b]))
        copies[-1].start()
    for copy in copies:
        copy.wait()


def far_kernel(me_ref, *refs, total):
    backs, dones = refs[:4], refs[4:8]
    there_ref, half_ref, half_there, inverse_ref, _, _, updated_hbm, basis_hbm, gram_hbm = refs[8:17]
    panel_ref, sum_ref, out_ref, basis_ref, gram_ref, sems = refs[17:]
    count, width, half = out_ref.shape
    quarter = half // 4
    cols = count * quarter
    me = me_ref[0]
    core = me % 2
    odd = core == 1
    copies = []

    def put(source, target):
        copies.append(pltpu.make_async_copy(source, target, sems.at[len(copies)]))
        copies[-1].start()

    def target(part, r):
        return pl.ds(pl.multiple_of(part * half + (place(me) ^ r) * quarter, quarter), quarter)

    for r in range(4):
        panel_ref[target(core, r)] = backs[r][cols : cols + quarter]
        panel_ref[target(1 - core, r)] = there_ref[r, cols:]
    sum_ref[pl.ds(pl.multiple_of(core * half, half), half)] = half_ref[...]
    sum_ref[pl.ds(pl.multiple_of((1 - core) * half, half), half)] = half_there[...]
    panel = halves(panel_ref[...])
    gram_ref[...] = (sum_ref[...] - by_transpose(panel, panel)) / total
    put(gram_ref, gram_hbm)
    for b in range(count):
        rows = slice(b * quarter, (b + 1) * quarter)
        pieces = [there_ref[r, rows] for r in range(4)]
        far = jnp.concatenate([by_place(me, pieces, j) for j in range(4)], axis=0).T
        out_ref[b] = far
        columns = pl.ds(pl.multiple_of(b * width + (1 - core) * half, half), half)
        put(out_ref.at[b], updated_hbm.at[pl.ds(0, width), columns])
        if b == 0:
            pieces = [jnp.where(odd, dones[r][rows], backs[r][rows]) for r in range(4)]
            near = jnp.concatenate([by_place(me, pieces, j) for j in range(4)], axis=0).T
            head = jnp.concatenate(by_core(core, near, far), axis=1)
            basis = plain(halves(head), halves(inverse_ref[...]))
            basis_ref[...] = jnp.where(me == 0, 0.0, basis)
            put(basis_ref, basis_hbm.at[pl.ds(0, width)])
    for copy in copies:
        copy.wait()


def body(trailing, leaf_vectors, leaf_factors, tree_vectors, tree_factors, inverse_factor):
    rows, columns = trailing.shape
    width = leaf_vectors.shape[1]
    half = width // 2
    quarter = half // 4
    count = columns // width
    devices = lax.axis_size("rows")
    levels = devices.bit_length() - 1
    me = lax.axis_index("rows").astype(jnp.int32)
    me_array = me.reshape(1)
    part_shape = (half + EXTRA, width)
    latest = []

    def exchange(value, shift):
        return lax.ppermute(value, "rows", [(i, i ^ shift) for i in range(devices)])

    def among(value, shift, member):
        return lax.ppermute(value, "rows", [(i, i ^ shift if member(i) else i) for i in range(devices)])

    def around(values):
        there = [exchange(values[r], 2 * r) for r in (3, 1, 2)]
        return [values[0], there[1], there[2], there[0]]

    def shape(*dims):
        return jax.ShapeDtypeStruct(dims, F32)

    def vmem(*dims):
        return pltpu.VMEM(dims, F32)

    def sems(number):
        return pltpu.SemaphoreType.DMA((number,))

    def call(kernel, operands, outs, scratch=(), away_in=(), away_out=(), aliases=(), before=(), work=1, chained=True):
        number = len(operands)
        operands = [pltpu.with_memory_space_constraint(x, pltpu.HBM) if i in away_in else x for i, x in enumerate(operands)]
        outs = [(pltpu.HBM if i in away_out else pltpu.VMEM)(x.shape, x.dtype) for i, x in enumerate(outs)]
        unused = [*latest, *before] if chained else []

        def kernel_on(*refs):
            kernel(*refs[: number + 1], *refs[number + 1 + len(unused) :])

        values = pl.pallas_call(
            kernel_on,
            out_shape=tuple(outs),
            in_specs=[SCALAR]
            + [AWAY if i in away_in else WHOLE for i in range(number)]
            + [pl.BlockSpec(memory_space=pl.ANY)] * len(unused),
            out_specs=tuple(AWAY if i in away_out else WHOLE for i in range(len(outs))),
            scratch_shapes=list(scratch),
            input_output_aliases=dict(aliases),
            compiler_params=PARAMS,
            cost_estimate=pl.CostEstimate(flops=work, bytes_accessed=1, transcendentals=0),
        )(me_array, *operands, *unused)
        if chained and 0 not in away_out:
            latest[:] = values[:1]
        return values

    raw = [exchange(tree_vectors, 1), exchange(tree_factors, 1)]
    blocks = count // 2
    more = count - blocks
    split = jax.ShapeDtypeStruct((2, width, rows), BF16), jax.ShapeDtypeStruct((2, rows, width), BF16)
    rows_a = blocks * half + half
    own_a, away_one, away_two, rest_a, later, inverse_factor, across, combined = call(
        leaf_first_kernel, (trailing, leaf_vectors, leaf_factors, inverse_factor),
        [shape(rows_a, width), shape(rows_a // 2, width), shape(rows_a // 2, width)]
        + [shape(blocks, width, width), shape(more, rows, width), shape(width, width), *split],
        [
            vmem(blocks, rows, width), vmem(rows, width), vmem(width, width), vmem(width, width), vmem(rows_a, width),
            sems(count * (rows // width) + 3),
        ],
        range(4),
    )
    there_a = [exchange(away_one, 1), exchange(away_two, 1)]

    chip_low, chip_high, chip_part = call(
        pack_kernel, (tree_vectors, tree_factors, *raw),
        (shape(2, *part_shape), shape(2, *part_shape), shape(*part_shape)),
        [vmem(4, width, width), sems(4)], (),
    )
    plane_parts = [exchange(chip_part, 2 * r) for r in (3, 1, 2)]
    plane_parts = [plane_parts[1], plane_parts[2], plane_parts[0]]

    own_b, rest_b, *aways = call(
        leaf_second_kernel, (later, across, combined),
        [shape(more * half, width), shape(more, width, width)] + [shape(half, width)] * more,
        [vmem(width, width)], before=there_a,
    )
    theres = [exchange(away, 1) for away in aways]
    cols = count * quarter
    outs = call(
        core_kernel, (own_a, own_b, *there_a, *theres, chip_high),
        [shape(cols, width)] * 3 + [shape(cols + 8, width)] + [shape(cols, width)] * 4 + [shape(half, width)],
        [vmem(count * half, width), vmem(count * half, width)],
    )
    sends, dones, gram_half = outs[:4], outs[4:8], outs[8]
    for level in (levels - 1, 1, 2, *range(3, levels - 1)):
        (gram_half,) = call(
            add_kernel, (gram_half, exchange(gram_half, 1 << level)), (shape(half, width),), chained=False
        )
    stack, held_part = call(
        gather_kernel, (chip_part, *plane_parts), (shape(3, *part_shape), shape(*part_shape)), work=1,
    )
    gots = around(sends)
    stack_there = exchange(stack, 1)
    parts = [exchange(held_part, 8)]
    for level in range(4, levels):
        short = half // 2 + EXTRA if level == levels - 1 else half + EXTRA
        (held_part,) = call(
            functools.partial(hold_kernel, level=level - 1), (held_part, parts[-1]), (shape(short, width),),
            chained=False,
        )
        parts.append(exchange(held_part, 1 << level))

    ready, held = call(
        prepare_kernel, (chip_low, stack, stack_there),
        (jax.ShapeDtypeStruct((4, 4, width, width), BF16), shape(2, *part_shape)),
    )
    (heads,) = call(sort_kernel, gots, (shape(4, cols, width),))
    head, send, plane_done = call(
        functools.partial(plane_kernel, level=3), (heads, ready),
        (shape(cols, width), shape(cols + 24, width), shape(4, cols, width)),
    )
    result = head
    for level in range(3, levels):
        part = parts[level - 3]
        operands = (head, result, send, exchange(send, 1 << level), held, part, exchange(part, 1))
        if level == levels - 1:
            sends = call(
                functools.partial(last_kernel, level=level), (*operands, plane_done),
                [shape(cols + quarter, width)] * 3 + [shape(cols + quarter + 8, width)], [vmem(4, cols, width)],
            )
        else:
            head, result, held, send = call(
                functools.partial(line_kernel, level=level), operands,
                [shape(cols, width), shape(cols, width), shape(*held.shape), shape(cols + 0, width)],
            )

    backs = around(sends)
    _, updated, basis = call(
        store_kernel, (rest_a, rest_b, inverse_factor), (shape(8, width), shape(rows, columns), shape(rows, width)),
        [vmem(width, width), sems(count + 1)], (), (1, 2),
    )
    gram_there = exchange(gram_half, 1)
    (back,) = call(pass_kernel, (*backs, *dones), (shape(4, cols + quarter, width),), before=(gram_half,))
    there = exchange(back, 1)
    (updated,) = call(
        near_kernel, (*backs, *dones, updated), (shape(rows, columns),),
        [vmem(count, width, half), sems(count)], (8,), (0,), {9: 0},
    )
    return call(
        functools.partial(far_kernel, total=float(rows * devices)),
        (*backs, *dones, there, gram_half, gram_there, inverse_factor, updated, basis),
        (shape(rows, columns), shape(rows, width), shape(width, width)),
        [vmem(width, width), vmem(width, width), vmem(count, width, half), vmem(width, width), vmem(width, width), sems(count + 2)],
        (12, 13), (0, 1, 2), {13: 0, 14: 1},
    )


def solution(mesh):
    in_specs = (
        P("rows", None),
        P("rows", None),
        P("rows", None),
        P("rows", None),
        P("rows", None),
        P(),
    )
    out_specs = (P("rows", None), P("rows", None), P())
    return jax.shard_map(body, mesh=mesh, in_specs=in_specs, out_specs=out_specs, check_vma=False)
```

```python
import functools
import jax
import jax.numpy as jnp
from jax import lax
from jax.experimental import pallas as pl
from jax.experimental.pallas import tpu as pltpu
from jax.sharding import PartitionSpec as P

F32 = jnp.float32
BF16 = jnp.bfloat16
EXTRA = 8
PARAMS = pltpu.CompilerParams(vmem_limit_bytes=20 * 1024 * 1024)
WHOLE = pl.BlockSpec(memory_space=pltpu.VMEM)
SCALAR = pl.BlockSpec(memory_space=pltpu.SMEM)
AWAY = pl.BlockSpec(memory_space=pltpu.HBM)


def halves(value):
    high = value.astype(BF16)
    return high, (value - high.astype(F32)).astype(BF16)


def times(left, right, sides):
    first = jnp.concatenate([left[0], left[0], left[1]], axis=sides[0])
    second = jnp.concatenate([right[0], right[1], right[0]], axis=sides[1])
    dims = ((sides[:1], sides[1:]), ((), ()))
    return lax.dot_general(first, second, dims, preferred_element_type=F32)


def plain(left, right):
    return times(left, right, (1, 0))


def by_transpose(left, right):
    return times(left, right, (1, 1))


def masks(size):
    row = lax.broadcasted_iota(jnp.int32, (size, size), 0)
    col = lax.broadcasted_iota(jnp.int32, (size, size), 1)
    return row, col


def diagonal_of(square):
    row, col = masks(square.shape[0])
    return jnp.sum(jnp.where(row == col, square, 0.0), axis=0, keepdims=True)


def pack_kernel(me_ref, *refs):
    sources, (low_ref, high_ref, part_ref), (buffer_ref, sems) = refs[:4], refs[4:7], refs[7:]
    copies = [pltpu.make_async_copy(source, buffer_ref.at[i], sems.at[i]) for i, source in enumerate(sources)]
    for copy in copies:
        copy.start()
    for copy in copies:
        copy.wait()
    core = me_ref[0] % 2
    half = buffer_ref.shape[1] // 2
    row, col = masks(half)
    both_vectors = by_core(core, buffer_ref[0], buffer_ref[2])
    both_factors = by_core(core, buffer_ref[1], buffer_ref[3])
    for vectors, factors, out_ref in zip(both_vectors, both_factors, (low_ref, high_ref)):
        first, second = factors[:half, :half], factors[half:, half:]
        square = jnp.where(row > col, first.T, jnp.where(row < col, second, 0.0))
        t_rows = jnp.concatenate([square, factors[:half, half:].T], axis=1)
        t_diagonal = jnp.concatenate([diagonal_of(first), diagonal_of(second)], axis=1)
        first, second = vectors[:half, :half], vectors[half:, half:]
        square = jnp.where(row <= col, first, second.T)
        v_rows = jnp.concatenate([square, vectors[:half, half:]], axis=1)
        v_diagonal = jnp.concatenate([diagonal_of(second)] * 2, axis=1)
        line = lax.broadcasted_iota(jnp.int32, (EXTRA, 2 * half), 0)
        diagonals = jnp.where(line == 0, t_diagonal, v_diagonal)
        for part in range(2):
            rows = slice(part * half // 2, (part + 1) * half // 2)
            out_ref[part, : half // 2] = t_rows[rows]
            out_ref[part, half // 2 : half // 2 + EXTRA] = diagonals
            out_ref[part, half // 2 + EXTRA :] = v_rows[rows]
    part_ref[...] = low_ref[core]


def unpack_factors(first, second):
    half = first.shape[1] // 2
    rows = jnp.concatenate([first[: half // 2], second[: half // 2]], axis=0)
    row, col = masks(half)
    square, corner = rows[:, :half], rows[:, half:]
    diagonal = first[half // 2 : half // 2 + 1]
    upper_left = jnp.where(row > col, square, jnp.where(row == col, diagonal[:, :half], 0.0))
    lower_right = jnp.where(row > col, square.T, jnp.where(row == col, diagonal[:, half:], 0.0))
    above = jnp.concatenate([upper_left, jnp.zeros_like(upper_left)], axis=1)
    return halves(jnp.concatenate([above, jnp.concatenate([corner, lower_right], axis=1)], axis=0))


def unpack_vectors(first, second):
    half = first.shape[1] // 2
    start = half // 2 + EXTRA
    rows = jnp.concatenate([first[start:], second[start:]], axis=0)
    row, col = masks(half)
    square, corner = rows[:, :half], rows[:, half:]
    diagonal = first[half // 2 + 1 : half // 2 + 2, :half]
    upper_left = jnp.where(row <= col, square, 0.0)
    lower_right = jnp.where(row < col, square.T, jnp.where(row == col, diagonal, 0.0))
    above = jnp.concatenate([upper_left, corner], axis=1)
    return halves(jnp.concatenate([above, jnp.concatenate([jnp.zeros_like(corner), lower_right], axis=1)], axis=0))


def unpack(first, second):
    return unpack_vectors(first, second), unpack_factors(first, second)


def by_core(core, mine, there):
    odd = core == 1
    return jnp.where(odd, there, mine), jnp.where(odd, mine, there)


def place(me):
    return (me >> 1) & 3


def by_place(me, parts, wanted):
    source = place(me) ^ wanted
    out = parts[0]
    for r in range(1, 4):
        out = jnp.where(source == r, parts[r], out)
    return out


def tree_node(low, high, reflector):
    vectors, factors = reflector
    node = by_transpose(halves(low + plain(halves(high), vectors)), factors)
    return low - node, high - by_transpose(halves(node), vectors)


def leaf_first_kernel(
    me_ref, trailing_hbm, vectors_hbm, factors_hbm, inverse_hbm,
    own_ref, away_one, away_two, rest_ref, later_ref, inverse_ref, across_ref, combined_ref,
    part_ref, vectors_ref, factors_ref, value_ref, away_ref, sems,
):
    count, rows, width = part_ref.shape
    copies = []

    def fetch(source, target):
        copies.append(pltpu.make_async_copy(source, target, sems.at[len(copies)]))
        copies[-1].start()
        return copies[-1]

    def fetch_part(b, target):
        cuts = [slice(c, c + width) for c in range(0, rows, width)]
        return [fetch(trailing_hbm.at[c, pl.ds(b * width, width)], target.at[c]) for c in cuts]

    first = [fetch(vectors_hbm, vectors_ref), fetch(factors_hbm, factors_ref)]
    parts = [fetch_part(b, part_ref.at[b]) for b in range(count)]
    for copy in first:
        copy.wait()
    last = [fetch_part(count + b, later_ref.at[b]) for b in range(later_ref.shape[0])]
    last.append([fetch(inverse_hbm, inverse_ref)])
    vectors = vectors_ref[...]
    across = halves(vectors.T)
    across_ref[0], across_ref[1] = across
    combined = halves(by_transpose(halves(vectors), halves(factors_ref[...])))
    combined_ref[0], combined_ref[1] = combined
    for b in range(count):
        for copy in parts[b]:
            copy.wait()
        leaf_block(me_ref, part_ref[b], across, combined, value_ref, rest_ref.at[b], own_ref, away_ref, b)
    panel = part_ref[0]
    value_ref[...] = plain(halves(panel.T), halves(panel))
    hand_over(me_ref, value_ref, own_ref, away_ref, count)
    cut = away_one.shape[0]
    away_one[...] = away_ref[:cut]
    away_two[...] = away_ref[cut:]
    for group in last:
        for copy in group:
            copy.wait()


def hand_over(me_ref, value_ref, own_ref, away_ref, slot):
    half = value_ref.shape[0] // 2
    core = me_ref[0] % 2
    target = slice(slot * half, (slot + 1) * half)
    own_ref[target] = value_ref[pl.ds(pl.multiple_of(core * half, half), half)]
    away_ref[target] = value_ref[pl.ds(pl.multiple_of((1 - core) * half, half), half)]


def leaf_block(me_ref, part, across, combined, value_ref, rest_ref, own_ref, away_ref, slot):
    width = value_ref.shape[0]
    out = part - plain(combined, halves(plain(across, halves(part))))
    rest_ref[...] = out[width:]
    value_ref[...] = out[:width].T
    hand_over(me_ref, value_ref, own_ref, away_ref, slot)


def leaf_second_kernel(me_ref, later_ref, across_ref, combined_ref, own_ref, rest_ref, *refs):
    aways, value_ref = refs[:-1], refs[-1]
    half = value_ref.shape[0] // 2
    across = across_ref[0], across_ref[1]
    combined = combined_ref[0], combined_ref[1]
    for b in range(later_ref.shape[0]):
        own_b = own_ref.at[pl.ds(b * half, half)]
        leaf_block(me_ref, later_ref[b], across, combined, value_ref, rest_ref.at[b], own_b, aways[b], 0)


def store_kernel(me_ref, first_ref, second_ref, inverse_ref, mark_ref, updated_hbm, basis_hbm, basis_ref, sems):
    count, width = first_ref.shape[:2]
    copies = []
    for b in range(count + second_ref.shape[0]):
        source = first_ref.at[b] if b < count else second_ref.at[b - count]
        target = updated_hbm.at[pl.ds(width, width), pl.ds(b * width, width)]
        copies.append(pltpu.make_async_copy(source, target, sems.at[b]))
        copies[-1].start()
    basis_ref[...] = plain(halves(first_ref[0]), halves(inverse_ref[...]))
    copies.append(pltpu.make_async_copy(basis_ref, basis_hbm.at[pl.ds(width, width)], sems.at[len(copies)]))
    mark_ref[...] = jnp.zeros_like(mark_ref)
    copies[-1].start()
    for copy in copies:
        copy.wait()


def core_kernel(
    me_ref, own_a_ref, own_b_ref, one_ref, two_ref, *refs
):
    more = len(refs) - 12
    there_bs, packed_ref = refs[:more], refs[more]
    sends, dones, (gram_ref, low_ref, high_ref) = refs[more + 1 : more + 5], refs[more + 5 : more + 9], refs[more + 9 :]
    me = me_ref[0]
    width = own_a_ref.shape[1]
    half = width // 2
    quarter = half // 4
    cut = own_a_ref.shape[0] - half
    count = cut // half + len(there_bs)
    odd = me % 2 == 1
    there_a = jnp.concatenate([one_ref[...], two_ref[...]], axis=0)
    gram_ref[...] = own_a_ref[cut:] + there_a[cut:]
    mine = jnp.concatenate([own_a_ref[:cut], own_b_ref[...]], axis=0)
    there = jnp.concatenate([there_a[:cut]] + [ref[...] for ref in there_bs], axis=0)
    low = jnp.where(odd, there, mine)
    high = jnp.where(odd, mine, there)
    low, high = tree_node(low, high, unpack(packed_ref[0], packed_ref[1]))
    low_ref[...] = low
    high_ref[...] = high
    for r in range(4):
        start = (place(me) ^ r) * quarter
        for b in range(count):
            source = pl.ds(pl.multiple_of(b * half + start, quarter), quarter)
            target = slice(b * quarter, (b + 1) * quarter)
            sends[r][target] = low_ref[source]
            dones[r][target] = high_ref[source]
        if sends[r].shape[0] > count * quarter:
            sends[r][count * quarter :] = jnp.zeros_like(sends[r][count * quarter :])


def gather_kernel(me_ref, *refs):
    parts, (stack_ref, held_ref) = refs[:4], refs[4:]
    for r in range(1, 4):
        stack_ref[r - 1] = parts[r][...]
    held_ref[...] = by_place(me_ref[0], [ref[...] for ref in parts], 0)


def hold_kernel(me_ref, held_ref, part_ref, out_ref, *, level):
    rows = slice(0, out_ref.shape[0])
    out_ref[...] = jnp.where((me_ref[0] >> level) % 2 == 1, part_ref[rows], held_ref[rows])


def add_kernel(me_ref, first_ref, second_ref, out_ref):
    out_ref[...] = first_ref[...] + second_ref[...]


def fill(send_ref, value):
    cols = value.shape[0]
    send_ref[:cols] = value
    if send_ref.shape[0] > cols:
        send_ref[cols:] = jnp.zeros_like(send_ref[cols:])


def prepare_kernel(me_ref, packed_ref, stack_ref, stack_there_ref, joint_ref, vectors_ref, held_ref):
    me = me_ref[0]
    pairs = [(packed_ref[0], packed_ref[1])]
    pairs += [by_core(me % 2, stack_ref[r], stack_there_ref[r]) for r in range(3)]
    firsts, seconds = [pair[0] for pair in pairs], [pair[1] for pair in pairs]
    pairs = [(by_place(me, firsts, j), by_place(me, seconds, j)) for j in range(4)]
    held_ref[0], held_ref[1] = pairs[0]
    for j in range(4):
        vectors = unpack_vectors(*pairs[j])
        vectors_ref[j, 0], vectors_ref[j, 1] = vectors
        if j > 0:
            factors = unpack_factors(*pairs[j])
            natural = (factors[0].astype(F32) + factors[1].astype(F32)).T
            joint = jnp.concatenate([natural, by_transpose(vectors, factors)], axis=0)
            joint_ref[j - 1, 0], joint_ref[j - 1, 1] = halves(joint)


def plane_kernel(me_ref, *refs, level):
    gots, (joint_ref, vectors_ref, head_ref, send_ref, done_ref) = refs[:4], refs[4:]
    cols = head_ref.shape[0]
    parts = [ref[:cols] for ref in gots]
    heads = [by_place(me_ref[0], parts, j) for j in range(4)]
    for low, high, j in ((0, 1, 1), (2, 3, 3), (0, 2, 2)):
        both = jnp.concatenate([heads[low], heads[high]], axis=1)
        coeffs = plain(halves(both), (joint_ref[j - 1, 0], joint_ref[j - 1, 1]))
        heads[low] = heads[low] - coeffs
        heads[high] = heads[high] - by_transpose(halves(coeffs), (vectors_ref[j, 0], vectors_ref[j, 1]))
    for j in range(4):
        done_ref[j] = heads[j]
    head_ref[...] = heads[0]
    upper = (me_ref[0] >> level) % 2 == 1
    ahead = plain(halves(heads[0]), (vectors_ref[0, 0], vectors_ref[0, 1]))
    fill(send_ref, jnp.where(upper, ahead, heads[0]))


def ready_kernel(me_ref, held_ref, part_ref, part_there_ref, ready_ref, *outs, level):
    me = me_ref[0]
    upper = (me >> level) % 2 == 1
    held = held_ref[0], held_ref[1]
    others = by_core(me % 2, part_ref[...], part_there_ref[...])
    need = held[0].shape[1] // 4 + EXTRA
    node = [jnp.where(upper, a[:need], b[:need]) for a, b in zip(held, others)]
    ready_ref[0], ready_ref[1] = unpack_factors(*node)
    ready_ref[2], ready_ref[3] = unpack_vectors(*held)
    if outs:
        following = [jnp.where(upper, b, a) for a, b in zip(held, others)]
        ready_ref[4], ready_ref[5] = unpack_vectors(*following)
        outs[0][0], outs[0][1] = following


def line_node(me_ref, head_ref, result_ref, mine_ref, there_ref, ready_ref, level):
    me = me_ref[0]
    cols = head_ref.shape[0]
    upper = (me >> level) % 2 == 1
    head, there = head_ref[...], there_ref[:cols]
    coeffs = by_transpose(halves(mine_ref[:cols] + there), (ready_ref[0], ready_ref[1]))
    low = jnp.where(upper, there, head) - coeffs
    plane = me >> 3
    below = (1 << (level - 2)) - 1
    second = (plane & below) == (1 << (level - 3))
    high = head - by_transpose(halves(coeffs), (ready_ref[2], ready_ref[3]))
    return low, jnp.where(second, high, result_ref[...])


def line_kernel(me_ref, *refs, level):
    ready_ref, (head_out, result_out, send_ref) = refs[4], refs[5:]
    low, result = line_node(me_ref, *refs[:5], level)
    ahead = (me_ref[0] >> (level + 1)) % 2 == 1
    head_out[...] = low
    result_out[...] = result
    fill(send_ref, jnp.where(ahead, plain(halves(low), (ready_ref[4], ready_ref[5])), low))


def last_kernel(me_ref, *refs, level):
    done_ref, sends, all_ref = refs[5], refs[6:10], refs[10]
    me = me_ref[0]
    low, result = line_node(me_ref, *refs[:5], level)
    cols = low.shape[0]
    all_ref[0] = jnp.where((me >> 3) == 0, low, result)
    for j in range(1, 4):
        all_ref[j] = done_ref[j]
    for r in range(4):
        sends[r][:cols] = all_ref[place(me) ^ r]
        sends[r][cols:] = low[: sends[r].shape[0] - cols]


def pass_kernel(me_ref, *refs):
    backs, dones, out_ref = refs[:4], refs[4:8], refs[8]
    odd = me_ref[0] % 2 == 1
    cols, rows = dones[0].shape[0], out_ref.shape[1]
    for r in range(4):
        out_ref[r, :cols] = jnp.where(odd, backs[r][:cols], dones[r][...])
        out_ref[r, cols:] = backs[r][cols:rows]


def near_kernel(me_ref, *refs):
    backs, dones, (_, updated_hbm, out_ref, sems) = refs[:4], refs[4:8], refs[8:]
    count, width, half = out_ref.shape
    quarter = half // 4
    me = me_ref[0]
    core = me % 2
    odd = core == 1
    copies = []
    for b in range(count):
        rows = slice(b * quarter, (b + 1) * quarter)
        pieces = [jnp.where(odd, dones[r][rows], backs[r][rows]) for r in range(4)]
        out_ref[b] = jnp.concatenate([by_place(me, pieces, j) for j in range(4)], axis=0).T
        columns = pl.ds(pl.multiple_of(b * width + core * half, half), half)
        copies.append(pltpu.make_async_copy(out_ref.at[b], updated_hbm.at[pl.ds(0, width), columns], sems.at[b]))
        copies[-1].start()
    for copy in copies:
        copy.wait()


def far_kernel(me_ref, *refs, total):
    backs, dones = refs[:4], refs[4:8]
    there_ref, half_ref, half_there, inverse_ref, _, _, updated_hbm, basis_hbm, gram_hbm = refs[8:17]
    panel_ref, sum_ref, out_ref, basis_ref, gram_ref, sems = refs[17:]
    count, width, half = out_ref.shape
    quarter = half // 4
    cols = count * quarter
    me = me_ref[0]
    core = me % 2
    odd = core == 1
    copies = []

    def put(source, target):
        copies.append(pltpu.make_async_copy(source, target, sems.at[len(copies)]))
        copies[-1].start()

    def target(part, r):
        return pl.ds(pl.multiple_of(part * half + (place(me) ^ r) * quarter, quarter), quarter)

    for r in range(4):
        panel_ref[target(core, r)] = backs[r][cols : cols + quarter]
        panel_ref[target(1 - core, r)] = there_ref[r, cols:]
    sum_ref[pl.ds(pl.multiple_of(core * half, half), half)] = half_ref[...]
    sum_ref[pl.ds(pl.multiple_of((1 - core) * half, half), half)] = half_there[...]
    panel = halves(panel_ref[...])
    gram_ref[...] = (sum_ref[...] - by_transpose(panel, panel)) / total
    put(gram_ref, gram_hbm)
    for b in range(count):
        rows = slice(b * quarter, (b + 1) * quarter)
        pieces = [there_ref[r, rows] for r in range(4)]
        far = jnp.concatenate([by_place(me, pieces, j) for j in range(4)], axis=0).T
        out_ref[b] = far
        columns = pl.ds(pl.multiple_of(b * width + (1 - core) * half, half), half)
        put(out_ref.at[b], updated_hbm.at[pl.ds(0, width), columns])
        if b == 0:
            pieces = [jnp.where(odd, dones[r][rows], backs[r][rows]) for r in range(4)]
            near = jnp.concatenate([by_place(me, pieces, j) for j in range(4)], axis=0).T
            head = jnp.concatenate(by_core(core, near, far), axis=1)
            basis = plain(halves(head), halves(inverse_ref[...]))
            basis_ref[...] = jnp.where(me == 0, 0.0, basis)
            put(basis_ref, basis_hbm.at[pl.ds(0, width)])
    for copy in copies:
        copy.wait()


def body(trailing, leaf_vectors, leaf_factors, tree_vectors, tree_factors, inverse_factor):
    rows, columns = trailing.shape
    width = leaf_vectors.shape[1]
    half = width // 2
    quarter = half // 4
    count = columns // width
    devices = lax.axis_size("rows")
    levels = devices.bit_length() - 1
    me = lax.axis_index("rows").astype(jnp.int32)
    me_array = me.reshape(1)
    part_shape = (half + EXTRA, width)
    latest = []

    def exchange(value, shift):
        return lax.ppermute(value, "rows", [(i, i ^ shift) for i in range(devices)])

    def among(value, shift, member):
        return lax.ppermute(value, "rows", [(i, i ^ shift if member(i) else i) for i in range(devices)])

    def around(values):
        there = [exchange(values[r], 2 * r) for r in (3, 1, 2)]
        return [values[0], there[1], there[2], there[0]]

    def shape(*dims):
        return jax.ShapeDtypeStruct(dims, F32)

    def vmem(*dims):
        return pltpu.VMEM(dims, F32)

    def sems(number):
        return pltpu.SemaphoreType.DMA((number,))

    def call(kernel, operands, outs, scratch=(), away_in=(), away_out=(), aliases=(), before=(), work=1, chained=True):
        number = len(operands)
        operands = [pltpu.with_memory_space_constraint(x, pltpu.HBM) if i in away_in else x for i, x in enumerate(operands)]
        outs = [(pltpu.HBM if i in away_out else pltpu.VMEM)(x.shape, x.dtype) for i, x in enumerate(outs)]
        unused = [*latest, *before] if chained else []

        def kernel_on(*refs):
            kernel(*refs[: number + 1], *refs[number + 1 + len(unused) :])

        values = pl.pallas_call(
            kernel_on,
            out_shape=tuple(outs),
            in_specs=[SCALAR]
            + [AWAY if i in away_in else WHOLE for i in range(number)]
            + [pl.BlockSpec(memory_space=pl.ANY)] * len(unused),
            out_specs=tuple(AWAY if i in away_out else WHOLE for i in range(len(outs))),
            scratch_shapes=list(scratch),
            input_output_aliases=dict(aliases),
            compiler_params=PARAMS,
            cost_estimate=pl.CostEstimate(flops=work, bytes_accessed=1, transcendentals=0),
        )(me_array, *operands, *unused)
        if chained and 0 not in away_out:
            latest[:] = values[:1]
        return values

    raw = [exchange(tree_vectors, 1), exchange(tree_factors, 1)]
    blocks = count // 2
    more = count - blocks
    both = jax.ShapeDtypeStruct((2, width, rows), BF16), jax.ShapeDtypeStruct((2, rows, width), BF16)
    rows_a = blocks * half + half
    own_a, away_one, away_two, rest_a, later, inverse_factor, across, combined = call(
        leaf_first_kernel, (trailing, leaf_vectors, leaf_factors, inverse_factor),
        [shape(rows_a, width), shape(rows_a // 2, width), shape(rows_a // 2, width)]
        + [shape(blocks, width, width), shape(more, rows, width), shape(width, width), *both],
        [
            vmem(blocks, rows, width), vmem(rows, width), vmem(width, width), vmem(width, width), vmem(rows_a, width),
            sems(count * (rows // width) + 3),
        ],
        range(4),
    )
    there_a = [exchange(away_one, 1), exchange(away_two, 1)]

    chip_low, chip_high, chip_part = call(
        pack_kernel, (tree_vectors, tree_factors, *raw),
        (shape(2, *part_shape), shape(2, *part_shape), shape(*part_shape)),
        [vmem(4, width, width), sems(4)], (),
    )
    plane_parts = [exchange(chip_part, 2 * r) for r in (3, 1, 2)]
    plane_parts = [plane_parts[1], plane_parts[2], plane_parts[0]]

    own_b, rest_b, *aways = call(
        leaf_second_kernel, (later, across, combined),
        [shape(more * half, width), shape(more, width, width)] + [shape(half, width)] * more,
        [vmem(width, width)], before=there_a,
    )
    theres = [exchange(away, 1) for away in aways]
    cols = count * quarter
    outs = call(
        core_kernel, (own_a, own_b, *there_a, *theres, chip_high),
        [shape(cols, width)] * 3 + [shape(cols + 8, width)] + [shape(cols, width)] * 4 + [shape(half, width)],
        [vmem(count * half, width), vmem(count * half, width)],
    )
    sends, dones, gram_half = outs[:4], outs[4:8], outs[8]
    for level in (levels - 1, 1, 2, *range(3, levels - 1)):
        (gram_half,) = call(
            add_kernel, (gram_half, exchange(gram_half, 1 << level)), (shape(half, width),), chained=False
        )
    stack, held_part = call(
        gather_kernel, (chip_part, *plane_parts), (shape(3, *part_shape), shape(*part_shape)), work=1,
    )
    gots = around(sends)
    stack_there = exchange(stack, 1)
    parts = [exchange(held_part, 8)]
    for level in range(4, levels):
        short = half // 2 + EXTRA if level == levels - 1 else half + EXTRA
        (held_part,) = call(
            functools.partial(hold_kernel, level=level - 1), (held_part, parts[-1]), (shape(short, width),),
            chained=False,
        )
        parts.append(exchange(held_part, 1 << level))

    def split(*dims):
        return jax.ShapeDtypeStruct(dims, BF16)

    joint, vectors, held = call(
        prepare_kernel, (chip_low, stack, stack_there),
        (split(3, 2, 2 * width, width), split(4, 2, width, width), shape(2, *part_shape)),
    )
    head, send, plane_done = call(
        functools.partial(plane_kernel, level=3), (*gots, joint, vectors),
        (shape(cols, width), shape(cols + 24, width), shape(4, cols, width)),
    )
    result = head
    for level in range(3, levels):
        part = parts[level - 3]
        last = level == levels - 1
        ready, *helds = call(
            functools.partial(ready_kernel, level=level), (held, part, exchange(part, 1)),
            [split(4 if last else 6, width, width)] + ([] if last else [shape(2, *part_shape)]),
        )
        operands = (head, result, send, exchange(send, 1 << level), ready)
        if last:
            sends = call(
                functools.partial(last_kernel, level=level), (*operands, plane_done),
                [shape(cols + quarter, width)] * 3 + [shape(cols + quarter + 8, width)], [vmem(4, cols, width)],
            )
        else:
            (held,) = helds
            head, result, send = call(
                functools.partial(line_kernel, level=level), operands,
                [shape(cols, width), shape(cols, width), shape(cols, width)],
            )

    backs = around(sends)
    _, updated, basis = call(
        store_kernel, (rest_a, rest_b, inverse_factor), (shape(8, width), shape(rows, columns), shape(rows, width)),
        [vmem(width, width), sems(count + 1)], (), (1, 2),
    )
    gram_there = exchange(gram_half, 1)
    (back,) = call(pass_kernel, (*backs, *dones), (shape(4, cols + quarter, width),), before=(gram_half,))
    there = exchange(back, 1)
    (updated,) = call(
        near_kernel, (*backs, *dones, updated), (shape(rows, columns),),
        [vmem(count, width, half), sems(count)], (8,), (0,), {9: 0},
    )
    return call(
        functools.partial(far_kernel, total=float(rows * devices)),
        (*backs, *dones, there, gram_half, gram_there, inverse_factor, updated, basis),
        (shape(rows, columns), shape(rows, width), shape(width, width)),
        [vmem(width, width), vmem(width, width), vmem(count, width, half), vmem(width, width), vmem(width, width), sems(count + 2)],
        (12, 13), (0, 1, 2), {13: 0, 14: 1},
    )


def solution(mesh):
    in_specs = (
        P("rows", None),
        P("rows", None),
        P("rows", None),
        P("rows", None),
        P("rows", None),
        P(),
    )
    out_specs = (P("rows", None), P("rows", None), P())
    return jax.shard_map(body, mesh=mesh, in_specs=in_specs, out_specs=out_specs, check_vma=False)
```

```python
import functools
import jax
import jax.numpy as jnp
from jax import lax
from jax.experimental import pallas as pl
from jax.experimental.pallas import tpu as pltpu
from jax.sharding import PartitionSpec as P

F32 = jnp.float32
BF16 = jnp.bfloat16
EXTRA = 8
PARAMS = pltpu.CompilerParams(vmem_limit_bytes=20 * 1024 * 1024)
WHOLE = pl.BlockSpec(memory_space=pltpu.VMEM)
SCALAR = pl.BlockSpec(memory_space=pltpu.SMEM)
AWAY = pl.BlockSpec(memory_space=pltpu.HBM)


def halves(value):
    high = value.astype(BF16)
    return high, (value - high.astype(F32)).astype(BF16)


def times(left, right, sides):
    first = jnp.concatenate([left[0], left[0], left[1]], axis=sides[0])
    second = jnp.concatenate([right[0], right[1], right[0]], axis=sides[1])
    dims = ((sides[:1], sides[1:]), ((), ()))
    return lax.dot_general(first, second, dims, preferred_element_type=F32)


def plain(left, right):
    return times(left, right, (1, 0))


def by_transpose(left, right):
    return times(left, right, (1, 1))


def masks(size):
    row = lax.broadcasted_iota(jnp.int32, (size, size), 0)
    col = lax.broadcasted_iota(jnp.int32, (size, size), 1)
    return row, col


def diagonal_of(square):
    row, col = masks(square.shape[0])
    return jnp.sum(jnp.where(row == col, square, 0.0), axis=0, keepdims=True)


def pack_kernel(me_ref, *refs):
    sources, (low_ref, high_ref, part_ref), (buffer_ref, sems) = refs[:4], refs[4:7], refs[7:]
    copies = [pltpu.make_async_copy(source, buffer_ref.at[i], sems.at[i]) for i, source in enumerate(sources)]
    for copy in copies:
        copy.start()
    for copy in copies:
        copy.wait()
    core = me_ref[0] % 2
    half = buffer_ref.shape[1] // 2
    row, col = masks(half)
    both_vectors = by_core(core, buffer_ref[0], buffer_ref[2])
    both_factors = by_core(core, buffer_ref[1], buffer_ref[3])
    for vectors, factors, out_ref in zip(both_vectors, both_factors, (low_ref, high_ref)):
        first, second = factors[:half, :half], factors[half:, half:]
        square = jnp.where(row > col, first.T, jnp.where(row < col, second, 0.0))
        t_rows = jnp.concatenate([square, factors[:half, half:].T], axis=1)
        t_diagonal = jnp.concatenate([diagonal_of(first), diagonal_of(second)], axis=1)
        first, second = vectors[:half, :half], vectors[half:, half:]
        square = jnp.where(row <= col, first, second.T)
        v_rows = jnp.concatenate([square, vectors[:half, half:]], axis=1)
        v_diagonal = jnp.concatenate([diagonal_of(second)] * 2, axis=1)
        line = lax.broadcasted_iota(jnp.int32, (EXTRA, 2 * half), 0)
        diagonals = jnp.where(line == 0, t_diagonal, v_diagonal)
        for part in range(2):
            rows = slice(part * half // 2, (part + 1) * half // 2)
            out_ref[part, : half // 2] = t_rows[rows]
            out_ref[part, half // 2 : half // 2 + EXTRA] = diagonals
            out_ref[part, half // 2 + EXTRA :] = v_rows[rows]
    part_ref[...] = low_ref[core]


def unpack_factors(first, second):
    half = first.shape[1] // 2
    rows = jnp.concatenate([first[: half // 2], second[: half // 2]], axis=0)
    row, col = masks(half)
    square, corner = rows[:, :half], rows[:, half:]
    diagonal = first[half // 2 : half // 2 + 1]
    upper_left = jnp.where(row > col, square, jnp.where(row == col, diagonal[:, :half], 0.0))
    lower_right = jnp.where(row > col, square.T, jnp.where(row == col, diagonal[:, half:], 0.0))
    above = jnp.concatenate([upper_left, jnp.zeros_like(upper_left)], axis=1)
    return halves(jnp.concatenate([above, jnp.concatenate([corner, lower_right], axis=1)], axis=0))


def unpack_vectors(first, second):
    half = first.shape[1] // 2
    start = half // 2 + EXTRA
    rows = jnp.concatenate([first[start:], second[start:]], axis=0)
    row, col = masks(half)
    square, corner = rows[:, :half], rows[:, half:]
    diagonal = first[half // 2 + 1 : half // 2 + 2, :half]
    upper_left = jnp.where(row <= col, square, 0.0)
    lower_right = jnp.where(row < col, square.T, jnp.where(row == col, diagonal, 0.0))
    above = jnp.concatenate([upper_left, corner], axis=1)
    return halves(jnp.concatenate([above, jnp.concatenate([jnp.zeros_like(corner), lower_right], axis=1)], axis=0))


def unpack(first, second):
    return unpack_vectors(first, second), unpack_factors(first, second)


def by_core(core, mine, there):
    odd = core == 1
    return jnp.where(odd, there, mine), jnp.where(odd, mine, there)


def place(me):
    return (me >> 1) & 3


def by_place(me, parts, wanted):
    source = place(me) ^ wanted
    out = parts[0]
    for r in range(1, 4):
        out = jnp.where(source == r, parts[r], out)
    return out


def tree_node(low, high, reflector):
    vectors, factors = reflector
    node = by_transpose(halves(low + plain(halves(high), vectors)), factors)
    return low - node, high - by_transpose(halves(node), vectors)


def leaf_first_kernel(
    me_ref, trailing_hbm, vectors_hbm, factors_hbm, inverse_hbm,
    own_ref, away_one, away_two, rest_ref, later_ref, inverse_ref, across_ref, combined_ref,
    part_ref, vectors_ref, factors_ref, value_ref, away_ref, sems,
):
    count, rows, width = part_ref.shape
    copies = []

    def fetch(source, target):
        copies.append(pltpu.make_async_copy(source, target, sems.at[len(copies)]))
        copies[-1].start()
        return copies[-1]

    def fetch_part(b, target):
        cuts = [slice(c, c + width) for c in range(0, rows, width)]
        return [fetch(trailing_hbm.at[c, pl.ds(b * width, width)], target.at[c]) for c in cuts]

    first = [fetch(vectors_hbm, vectors_ref), fetch(factors_hbm, factors_ref)]
    parts = [fetch_part(b, part_ref.at[b]) for b in range(count)]
    for copy in first:
        copy.wait()
    last = [fetch_part(count + b, later_ref.at[b]) for b in range(later_ref.shape[0])]
    last.append([fetch(inverse_hbm, inverse_ref)])
    vectors = vectors_ref[...]
    across = halves(vectors.T)
    across_ref[0], across_ref[1] = across
    combined = halves(by_transpose(halves(vectors), halves(factors_ref[...])))
    combined_ref[0], combined_ref[1] = combined
    for b in range(count):
        for copy in parts[b]:
            copy.wait()
        leaf_block(me_ref, part_ref[b], across, combined, value_ref, rest_ref.at[b], own_ref, away_ref, b)
    panel = part_ref[0]
    value_ref[...] = plain(halves(panel.T), halves(panel))
    hand_over(me_ref, value_ref, own_ref, away_ref, count)
    cut = away_one.shape[0]
    away_one[...] = away_ref[:cut]
    away_two[...] = away_ref[cut:]
    for group in last:
        for copy in group:
            copy.wait()


def hand_over(me_ref, value_ref, own_ref, away_ref, slot):
    half = value_ref.shape[0] // 2
    core = me_ref[0] % 2
    target = slice(slot * half, (slot + 1) * half)
    own_ref[target] = value_ref[pl.ds(pl.multiple_of(core * half, half), half)]
    away_ref[target] = value_ref[pl.ds(pl.multiple_of((1 - core) * half, half), half)]


def leaf_block(me_ref, part, across, combined, value_ref, rest_ref, own_ref, away_ref, slot):
    width = value_ref.shape[0]
    out = part - plain(combined, halves(plain(across, halves(part))))
    rest_ref[...] = out[width:]
    value_ref[...] = out[:width].T
    hand_over(me_ref, value_ref, own_ref, away_ref, slot)


def leaf_second_kernel(me_ref, later_ref, across_ref, combined_ref, own_ref, rest_ref, *refs):
    aways, value_ref = refs[:-1], refs[-1]
    half = value_ref.shape[0] // 2
    across = across_ref[0], across_ref[1]
    combined = combined_ref[0], combined_ref[1]
    for b in range(later_ref.shape[0]):
        own_b = own_ref.at[pl.ds(b * half, half)]
        leaf_block(me_ref, later_ref[b], across, combined, value_ref, rest_ref.at[b], own_b, aways[b], 0)


def store_kernel(me_ref, first_ref, second_ref, inverse_ref, mark_ref, updated_hbm, basis_hbm, basis_ref, sems):
    count, width = first_ref.shape[:2]
    copies = []
    for b in range(count + second_ref.shape[0]):
        source = first_ref.at[b] if b < count else second_ref.at[b - count]
        target = updated_hbm.at[pl.ds(width, width), pl.ds(b * width, width)]
        copies.append(pltpu.make_async_copy(source, target, sems.at[b]))
        copies[-1].start()
    basis_ref[...] = plain(halves(first_ref[0]), halves(inverse_ref[...]))
    copies.append(pltpu.make_async_copy(basis_ref, basis_hbm.at[pl.ds(width, width)], sems.at[len(copies)]))
    mark_ref[...] = jnp.zeros_like(mark_ref)
    copies[-1].start()
    for copy in copies:
        copy.wait()


def core_kernel(
    me_ref, own_a_ref, own_b_ref, one_ref, two_ref, *refs
):
    more = len(refs) - 12
    there_bs, packed_ref = refs[:more], refs[more]
    sends, dones, (gram_ref, low_ref, high_ref) = refs[more + 1 : more + 5], refs[more + 5 : more + 9], refs[more + 9 :]
    me = me_ref[0]
    width = own_a_ref.shape[1]
    half = width // 2
    quarter = half // 4
    cut = own_a_ref.shape[0] - half
    count = cut // half + len(there_bs)
    odd = me % 2 == 1
    there_a = jnp.concatenate([one_ref[...], two_ref[...]], axis=0)
    gram_ref[...] = own_a_ref[cut:] + there_a[cut:]
    mine = jnp.concatenate([own_a_ref[:cut], own_b_ref[...]], axis=0)
    there = jnp.concatenate([there_a[:cut]] + [ref[...] for ref in there_bs], axis=0)
    low = jnp.where(odd, there, mine)
    high = jnp.where(odd, mine, there)
    low, high = tree_node(low, high, unpack(packed_ref[0], packed_ref[1]))
    low_ref[...] = low
    high_ref[...] = high
    for r in range(4):
        start = (place(me) ^ r) * quarter
        for b in range(count):
            source = pl.ds(pl.multiple_of(b * half + start, quarter), quarter)
            target = slice(b * quarter, (b + 1) * quarter)
            sends[r][target] = low_ref[source]
            dones[r][target] = high_ref[source]
        if sends[r].shape[0] > count * quarter:
            sends[r][count * quarter :] = jnp.zeros_like(sends[r][count * quarter :])


def gather_kernel(me_ref, *refs):
    parts, (stack_ref, held_ref) = refs[:4], refs[4:]
    for r in range(1, 4):
        stack_ref[r - 1] = parts[r][...]
    held_ref[...] = by_place(me_ref[0], [ref[...] for ref in parts], 0)


def hold_kernel(me_ref, held_ref, part_ref, out_ref, *, level):
    rows = slice(0, out_ref.shape[0])
    out_ref[...] = jnp.where((me_ref[0] >> level) % 2 == 1, part_ref[rows], held_ref[rows])


def add_kernel(me_ref, first_ref, second_ref, out_ref):
    out_ref[...] = first_ref[...] + second_ref[...]


def fill(send_ref, value):
    cols = value.shape[0]
    send_ref[:cols] = value
    if send_ref.shape[0] > cols:
        send_ref[cols:] = jnp.zeros_like(send_ref[cols:])


def prepare_kernel(me_ref, packed_ref, stack_ref, stack_there_ref, joint_ref, vectors_ref, held_ref):
    me = me_ref[0]
    pairs = [(packed_ref[0], packed_ref[1])]
    pairs += [by_core(me % 2, stack_ref[r], stack_there_ref[r]) for r in range(3)]
    firsts, seconds = [pair[0] for pair in pairs], [pair[1] for pair in pairs]
    pairs = [(by_place(me, firsts, j), by_place(me, seconds, j)) for j in range(4)]
    held_ref[0], held_ref[1] = pairs[0]
    for j in range(4):
        vectors = unpack_vectors(*pairs[j])
        vectors_ref[j, 0], vectors_ref[j, 1] = vectors
        if j > 0:
            factors = unpack_factors(*pairs[j])
            natural = (factors[0].astype(F32) + factors[1].astype(F32)).T
            joint = jnp.concatenate([natural, by_transpose(vectors, factors)], axis=0)
            joint_ref[j - 1, 0], joint_ref[j - 1, 1] = halves(joint)


def plane_kernel(me_ref, *refs, level):
    gots, (joint_ref, vectors_ref, head_ref, send_ref, done_ref) = refs[:4], refs[4:]
    cols = head_ref.shape[0]
    parts = [ref[:cols] for ref in gots]
    heads = [by_place(me_ref[0], parts, j) for j in range(4)]
    for low, high, j in ((0, 1, 1), (2, 3, 3), (0, 2, 2)):
        both = jnp.concatenate([heads[low], heads[high]], axis=1)
        coeffs = plain(halves(both), (joint_ref[j - 1, 0], joint_ref[j - 1, 1]))
        heads[low] = heads[low] - coeffs
        heads[high] = heads[high] - by_transpose(halves(coeffs), (vectors_ref[j, 0], vectors_ref[j, 1]))
    for j in range(4):
        done_ref[j] = heads[j]
    head_ref[...] = heads[0]
    upper = (me_ref[0] >> level) % 2 == 1
    ahead = plain(halves(heads[0]), (vectors_ref[0, 0], vectors_ref[0, 1]))
    fill(send_ref, jnp.where(upper, ahead, heads[0]))


def ready_kernel(me_ref, held_ref, part_ref, part_there_ref, ready_ref, *outs, level):
    me = me_ref[0]
    upper = (me >> level) % 2 == 1
    held = held_ref[0], held_ref[1]
    others = by_core(me % 2, part_ref[...], part_there_ref[...])
    need = held[0].shape[1] // 4 + EXTRA
    node = [jnp.where(upper, a[:need], b[:need]) for a, b in zip(held, others)]
    ready_ref[0], ready_ref[1] = unpack_factors(*node)
    ready_ref[2], ready_ref[3] = unpack_vectors(*held)
    if outs:
        following = [jnp.where(upper, b, a) for a, b in zip(held, others)]
        ready_ref[4], ready_ref[5] = unpack_vectors(*following)
        outs[0][0], outs[0][1] = following


def line_node(me_ref, head_ref, result_ref, mine_ref, there_ref, ready_ref, level):
    me = me_ref[0]
    cols = head_ref.shape[0]
    upper = (me >> level) % 2 == 1
    head, there = head_ref[...], there_ref[:cols]
    coeffs = by_transpose(halves(mine_ref[:cols] + there), (ready_ref[0], ready_ref[1]))
    low = jnp.where(upper, there, head) - coeffs
    plane = me >> 3
    below = (1 << (level - 2)) - 1
    second = (plane & below) == (1 << (level - 3))
    high = head - by_transpose(halves(coeffs), (ready_ref[2], ready_ref[3]))
    return low, jnp.where(second, high, result_ref[...])


def line_kernel(me_ref, *refs, level):
    ready_ref, (head_out, result_out, send_ref) = refs[4], refs[5:]
    low, result = line_node(me_ref, *refs[:5], level)
    ahead = (me_ref[0] >> (level + 1)) % 2 == 1
    head_out[...] = low
    result_out[...] = result
    fill(send_ref, jnp.where(ahead, plain(halves(low), (ready_ref[4], ready_ref[5])), low))


def last_kernel(me_ref, *refs, level):
    done_ref, sends, all_ref = refs[5], refs[6:10], refs[10]
    me = me_ref[0]
    low, result = line_node(me_ref, *refs[:5], level)
    cols = low.shape[0]
    all_ref[0] = jnp.where((me >> 3) == 0, low, result)
    for j in range(1, 4):
        all_ref[j] = done_ref[j]
    for r in range(4):
        sends[r][:cols] = all_ref[place(me) ^ r]
        sends[r][cols:] = low[: sends[r].shape[0] - cols]


def pass_kernel(me_ref, *refs):
    backs, dones, out_ref = refs[:2], refs[2:4], refs[4]
    odd = me_ref[0] % 2 == 1
    cols, rows = dones[0].shape[0], out_ref.shape[1]
    for r in range(2):
        out_ref[r, :cols] = jnp.where(odd, backs[r][:cols], dones[r][...])
        out_ref[r, cols:] = backs[r][cols:rows]


def near_kernel(me_ref, *refs):
    backs, dones, (_, updated_hbm, out_ref, sems) = refs[:4], refs[4:8], refs[8:]
    count, width, half = out_ref.shape
    quarter = half // 4
    me = me_ref[0]
    core = me % 2
    odd = core == 1
    copies = []
    for b in range(count):
        rows = slice(b * quarter, (b + 1) * quarter)
        pieces = [jnp.where(odd, dones[r][rows], backs[r][rows]) for r in range(4)]
        out_ref[b] = jnp.concatenate([by_place(me, pieces, j) for j in range(4)], axis=0).T
        columns = pl.ds(pl.multiple_of(b * width + core * half, half), half)
        copies.append(pltpu.make_async_copy(out_ref.at[b], updated_hbm.at[pl.ds(0, width), columns], sems.at[b]))
        copies[-1].start()
    for copy in copies:
        copy.wait()


def far_kernel(me_ref, *refs, total):
    backs, dones = refs[:4], refs[4:8]
    theres, half_ref, half_there, inverse_ref, _, _, updated_hbm, basis_hbm, gram_hbm = refs[8:10], *refs[10:18]
    panel_ref, sum_ref, out_ref, basis_ref, gram_ref, sems = refs[18:]
    count, width, half = out_ref.shape
    quarter = half // 4
    cols = count * quarter
    me = me_ref[0]
    core = me % 2
    odd = core == 1
    copies = []

    def put(source, target):
        copies.append(pltpu.make_async_copy(source, target, sems.at[len(copies)]))
        copies[-1].start()

    def target(part, r):
        return pl.ds(pl.multiple_of(part * half + (place(me) ^ r) * quarter, quarter), quarter)

    for r in range(4):
        panel_ref[target(core, r)] = backs[r][cols : cols + quarter]
        panel_ref[target(1 - core, r)] = theres[r // 2][r % 2, cols:]
    sum_ref[pl.ds(pl.multiple_of(core * half, half), half)] = half_ref[...]
    sum_ref[pl.ds(pl.multiple_of((1 - core) * half, half), half)] = half_there[...]
    panel = halves(panel_ref[...])
    gram_ref[...] = (sum_ref[...] - by_transpose(panel, panel)) / total
    put(gram_ref, gram_hbm)
    for b in range(count):
        rows = slice(b * quarter, (b + 1) * quarter)
        pieces = [theres[r // 2][r % 2, rows] for r in range(4)]
        far = jnp.concatenate([by_place(me, pieces, j) for j in range(4)], axis=0).T
        out_ref[b] = far
        columns = pl.ds(pl.multiple_of(b * width + (1 - core) * half, half), half)
        put(out_ref.at[b], updated_hbm.at[pl.ds(0, width), columns])
        if b == 0:
            pieces = [jnp.where(odd, dones[r][rows], backs[r][rows]) for r in range(4)]
            near = jnp.concatenate([by_place(me, pieces, j) for j in range(4)], axis=0).T
            head = jnp.concatenate(by_core(core, near, far), axis=1)
            basis = plain(halves(head), halves(inverse_ref[...]))
            basis_ref[...] = jnp.where(me == 0, 0.0, basis)
            put(basis_ref, basis_hbm.at[pl.ds(0, width)])
    for copy in copies:
        copy.wait()


def body(trailing, leaf_vectors, leaf_factors, tree_vectors, tree_factors, inverse_factor):
    rows, columns = trailing.shape
    width = leaf_vectors.shape[1]
    half = width // 2
    quarter = half // 4
    count = columns // width
    devices = lax.axis_size("rows")
    levels = devices.bit_length() - 1
    me = lax.axis_index("rows").astype(jnp.int32)
    me_array = me.reshape(1)
    part_shape = (half + EXTRA, width)
    latest = []

    def exchange(value, shift):
        return lax.ppermute(value, "rows", [(i, i ^ shift) for i in range(devices)])

    def among(value, shift, member):
        return lax.ppermute(value, "rows", [(i, i ^ shift if member(i) else i) for i in range(devices)])

    def around(values):
        there = [exchange(values[r], 2 * r) for r in (3, 1, 2)]
        return [values[0], there[1], there[2], there[0]]

    def shape(*dims):
        return jax.ShapeDtypeStruct(dims, F32)

    def vmem(*dims):
        return pltpu.VMEM(dims, F32)

    def sems(number):
        return pltpu.SemaphoreType.DMA((number,))

    def call(kernel, operands, outs, scratch=(), away_in=(), away_out=(), aliases=(), before=(), work=1, chained=True):
        number = len(operands)
        operands = [pltpu.with_memory_space_constraint(x, pltpu.HBM) if i in away_in else x for i, x in enumerate(operands)]
        outs = [(pltpu.HBM if i in away_out else pltpu.VMEM)(x.shape, x.dtype) for i, x in enumerate(outs)]
        unused = [*latest, *before] if chained else []

        def kernel_on(*refs):
            kernel(*refs[: number + 1], *refs[number + 1 + len(unused) :])

        values = pl.pallas_call(
            kernel_on,
            out_shape=tuple(outs),
            in_specs=[SCALAR]
            + [AWAY if i in away_in else WHOLE for i in range(number)]
            + [pl.BlockSpec(memory_space=pl.ANY)] * len(unused),
            out_specs=tuple(AWAY if i in away_out else WHOLE for i in range(len(outs))),
            scratch_shapes=list(scratch),
            input_output_aliases=dict(aliases),
            compiler_params=PARAMS,
            cost_estimate=pl.CostEstimate(flops=work, bytes_accessed=1, transcendentals=0),
        )(me_array, *operands, *unused)
        if chained and 0 not in away_out:
            latest[:] = values[:1]
        return values

    raw = [exchange(tree_vectors, 1), exchange(tree_factors, 1)]
    blocks = count // 2
    more = count - blocks
    both = jax.ShapeDtypeStruct((2, width, rows), BF16), jax.ShapeDtypeStruct((2, rows, width), BF16)
    rows_a = blocks * half + half
    own_a, away_one, away_two, rest_a, later, inverse_factor, across, combined = call(
        leaf_first_kernel, (trailing, leaf_vectors, leaf_factors, inverse_factor),
        [shape(rows_a, width), shape(rows_a // 2, width), shape(rows_a // 2, width)]
        + [shape(blocks, width, width), shape(more, rows, width), shape(width, width), *both],
        [
            vmem(blocks, rows, width), vmem(rows, width), vmem(width, width), vmem(width, width), vmem(rows_a, width),
            sems(count * (rows // width) + 3),
        ],
        range(4),
    )
    there_a = [exchange(away_one, 1), exchange(away_two, 1)]

    chip_low, chip_high, chip_part = call(
        pack_kernel, (tree_vectors, tree_factors, *raw),
        (shape(2, *part_shape), shape(2, *part_shape), shape(*part_shape)),
        [vmem(4, width, width), sems(4)], (),
    )
    plane_parts = [exchange(chip_part, 2 * r) for r in (3, 1, 2)]
    plane_parts = [plane_parts[1], plane_parts[2], plane_parts[0]]

    own_b, rest_b, *aways = call(
        leaf_second_kernel, (later, across, combined),
        [shape(more * half, width), shape(more, width, width)] + [shape(half, width)] * more,
        [vmem(width, width)], before=there_a,
    )
    theres = [exchange(away, 1) for away in aways]
    cols = count * quarter
    outs = call(
        core_kernel, (own_a, own_b, *there_a, *theres, chip_high),
        [shape(cols, width)] * 3 + [shape(cols + 8, width)] + [shape(cols, width)] * 4 + [shape(half, width)],
        [vmem(count * half, width), vmem(count * half, width)],
    )
    sends, dones, gram_half = outs[:4], outs[4:8], outs[8]
    for level in (levels - 1, 1, 2, *range(3, levels - 1)):
        (gram_half,) = call(
            add_kernel, (gram_half, exchange(gram_half, 1 << level)), (shape(half, width),), chained=False
        )
    stack, held_part = call(
        gather_kernel, (chip_part, *plane_parts), (shape(3, *part_shape), shape(*part_shape)), work=1,
    )
    gots = around(sends)
    stack_there = exchange(stack, 1)
    parts = [exchange(held_part, 8)]
    for level in range(4, levels):
        short = half // 2 + EXTRA if level == levels - 1 else half + EXTRA
        (held_part,) = call(
            functools.partial(hold_kernel, level=level - 1), (held_part, parts[-1]), (shape(short, width),),
            chained=False,
        )
        parts.append(exchange(held_part, 1 << level))

    def split(*dims):
        return jax.ShapeDtypeStruct(dims, BF16)

    joint, vectors, held = call(
        prepare_kernel, (chip_low, stack, stack_there),
        (split(3, 2, 2 * width, width), split(4, 2, width, width), shape(2, *part_shape)),
    )
    head, send, plane_done = call(
        functools.partial(plane_kernel, level=3), (*gots, joint, vectors),
        (shape(cols, width), shape(cols + 24, width), shape(4, cols, width)),
    )
    result = head
    for level in range(3, levels):
        part = parts[level - 3]
        last = level == levels - 1
        ready, *helds = call(
            functools.partial(ready_kernel, level=level), (held, part, exchange(part, 1)),
            [split(4 if last else 6, width, width)] + ([] if last else [shape(2, *part_shape)]),
        )
        operands = (head, result, send, exchange(send, 1 << level), ready)
        if last:
            _, updated, basis = call(
                store_kernel, (rest_a, rest_b, inverse_factor), (shape(8, width), shape(rows, columns), shape(rows, width)),
                [vmem(width, width), sems(count + 1)], (), (1, 2),
            )
            sends = call(
                functools.partial(last_kernel, level=level), (*operands, plane_done),
                [shape(cols + quarter, width)] * 3 + [shape(cols + quarter + 8, width)], [vmem(4, cols, width)],
            )
        else:
            (held,) = helds
            head, result, send = call(
                functools.partial(line_kernel, level=level), operands,
                [shape(cols, width), shape(cols, width), shape(cols, width)],
            )

    backs = around(sends)
    gram_there = exchange(gram_half, 1)
    theres = []
    for r in (0, 2):
        (passed,) = call(
            pass_kernel, (*backs[r : r + 2], *dones[r : r + 2]), (shape(2, cols + quarter, width),),
            before=(gram_half,) if r == 2 else (),
        )
        theres.append(exchange(passed, 1))
    (updated,) = call(
        near_kernel, (*backs, *dones, updated), (shape(rows, columns),),
        [vmem(count, width, half), sems(count)], (8,), (0,), {9: 0},
    )
    return call(
        functools.partial(far_kernel, total=float(rows * devices)),
        (*backs, *dones, *theres, gram_half, gram_there, inverse_factor, updated, basis),
        (shape(rows, columns), shape(rows, width), shape(width, width)),
        [vmem(width, width), vmem(width, width), vmem(count, width, half), vmem(width, width), vmem(width, width), sems(count + 2)],
        (13, 14), (0, 1, 2), {14: 0, 15: 1},
    )


def solution(mesh):
    in_specs = (
        P("rows", None),
        P("rows", None),
        P("rows", None),
        P("rows", None),
        P("rows", None),
        P(),
    )
    out_specs = (P("rows", None), P("rows", None), P())
    return jax.shard_map(body, mesh=mesh, in_specs=in_specs, out_specs=out_specs, check_vma=False)
```

```python
import functools
import jax
import jax.numpy as jnp
from jax import lax
from jax.experimental import pallas as pl
from jax.experimental.pallas import tpu as pltpu
from jax.sharding import PartitionSpec as P

F32 = jnp.float32
BF16 = jnp.bfloat16
EXTRA = 8
PARAMS = pltpu.CompilerParams(vmem_limit_bytes=20 * 1024 * 1024)
WHOLE = pl.BlockSpec(memory_space=pltpu.VMEM)
SCALAR = pl.BlockSpec(memory_space=pltpu.SMEM)
AWAY = pl.BlockSpec(memory_space=pltpu.HBM)


def halves(value):
    high = value.astype(BF16)
    return high, (value - high.astype(F32)).astype(BF16)


def times(left, right, sides):
    first = jnp.concatenate([left[0], left[0], left[1]], axis=sides[0])
    second = jnp.concatenate([right[0], right[1], right[0]], axis=sides[1])
    dims = ((sides[:1], sides[1:]), ((), ()))
    return lax.dot_general(first, second, dims, preferred_element_type=F32)


def plain(left, right):
    return times(left, right, (1, 0))


def by_transpose(left, right):
    return times(left, right, (1, 1))


def masks(size):
    row = lax.broadcasted_iota(jnp.int32, (size, size), 0)
    col = lax.broadcasted_iota(jnp.int32, (size, size), 1)
    return row, col


def diagonal_of(square):
    row, col = masks(square.shape[0])
    return jnp.sum(jnp.where(row == col, square, 0.0), axis=0, keepdims=True)


def load_kernel(me_ref, vectors_hbm, factors_hbm, vectors_ref, factors_ref, sems):
    copies = [
        pltpu.make_async_copy(vectors_hbm, vectors_ref, sems.at[0]),
        pltpu.make_async_copy(factors_hbm, factors_ref, sems.at[1]),
    ]
    for copy in copies:
        copy.start()
    for copy in copies:
        copy.wait()


def pack_kernel(me_ref, *refs):
    sources, (low_ref, high_ref, part_ref), (buffer_ref, sems) = refs[:4], refs[4:7], refs[7:]
    copies = [pltpu.make_async_copy(source, buffer_ref.at[i], sems.at[i]) for i, source in enumerate(sources)]
    for copy in copies:
        copy.start()
    for copy in copies:
        copy.wait()
    core = me_ref[0] % 2
    half = buffer_ref.shape[1] // 2
    row, col = masks(half)
    both_vectors = by_core(core, buffer_ref[0], buffer_ref[2])
    both_factors = by_core(core, buffer_ref[1], buffer_ref[3])
    for vectors, factors, out_ref in zip(both_vectors, both_factors, (low_ref, high_ref)):
        first, second = factors[:half, :half], factors[half:, half:]
        square = jnp.where(row > col, first.T, jnp.where(row < col, second, 0.0))
        t_rows = jnp.concatenate([square, factors[:half, half:].T], axis=1)
        t_diagonal = jnp.concatenate([diagonal_of(first), diagonal_of(second)], axis=1)
        first, second = vectors[:half, :half], vectors[half:, half:]
        square = jnp.where(row <= col, first, second.T)
        v_rows = jnp.concatenate([square, vectors[:half, half:]], axis=1)
        v_diagonal = jnp.concatenate([diagonal_of(second)] * 2, axis=1)
        line = lax.broadcasted_iota(jnp.int32, (EXTRA, 2 * half), 0)
        diagonals = jnp.where(line == 0, t_diagonal, v_diagonal)
        for part in range(2):
            rows = slice(part * half // 2, (part + 1) * half // 2)
            out_ref[part, : half // 2] = t_rows[rows]
            out_ref[part, half // 2 : half // 2 + EXTRA] = diagonals
            out_ref[part, half // 2 + EXTRA :] = v_rows[rows]
    part_ref[...] = low_ref[core]


def unpack_factors(first, second):
    half = first.shape[1] // 2
    rows = jnp.concatenate([first[: half // 2], second[: half // 2]], axis=0)
    row, col = masks(half)
    square, corner = rows[:, :half], rows[:, half:]
    diagonal = first[half // 2 : half // 2 + 1]
    upper_left = jnp.where(row > col, square, jnp.where(row == col, diagonal[:, :half], 0.0))
    lower_right = jnp.where(row > col, square.T, jnp.where(row == col, diagonal[:, half:], 0.0))
    above = jnp.concatenate([upper_left, jnp.zeros_like(upper_left)], axis=1)
    return halves(jnp.concatenate([above, jnp.concatenate([corner, lower_right], axis=1)], axis=0))


def unpack_vectors(first, second):
    half = first.shape[1] // 2
    start = half // 2 + EXTRA
    rows = jnp.concatenate([first[start:], second[start:]], axis=0)
    row, col = masks(half)
    square, corner = rows[:, :half], rows[:, half:]
    diagonal = first[half // 2 + 1 : half // 2 + 2, :half]
    upper_left = jnp.where(row <= col, square, 0.0)
    lower_right = jnp.where(row < col, square.T, jnp.where(row == col, diagonal, 0.0))
    above = jnp.concatenate([upper_left, corner], axis=1)
    return halves(jnp.concatenate([above, jnp.concatenate([jnp.zeros_like(corner), lower_right], axis=1)], axis=0))


def unpack(first, second):
    return unpack_vectors(first, second), unpack_factors(first, second)


def by_core(core, mine, there):
    odd = core == 1
    return jnp.where(odd, there, mine), jnp.where(odd, mine, there)


def place(me):
    return (me >> 1) & 3


def by_place(me, parts, wanted):
    source = place(me) ^ wanted
    out = parts[0]
    for r in range(1, 4):
        out = jnp.where(source == r, parts[r], out)
    return out


def tree_node(low, high, reflector):
    vectors, factors = reflector
    node = by_transpose(halves(low + plain(halves(high), vectors)), factors)
    return low - node, high - by_transpose(halves(node), vectors)


def leaf_kernel(
    me_ref, trailing_hbm, vectors_hbm, factors_hbm, inverse_hbm,
    own_ref, rest_ref, inverse_ref, *refs,
):
    aways, (part_ref, vectors_ref, factors_ref, value_ref, away_ref, sems) = refs[:-6], refs[-6:]
    count, rows, width = part_ref.shape
    copies = []

    def fetch(source, target):
        copies.append(pltpu.make_async_copy(source, target, sems.at[len(copies)]))
        copies[-1].start()
        return copies[-1]

    def fetch_part(b, target):
        cuts = [slice(c, c + width) for c in range(0, rows, width)]
        return [fetch(trailing_hbm.at[c, pl.ds(b * width, width)], target.at[c]) for c in cuts]

    first = [fetch(vectors_hbm, vectors_ref), fetch(factors_hbm, factors_ref)]
    parts = [fetch_part(b, part_ref.at[b]) for b in range(count)]
    inverse_copy = fetch(inverse_hbm, inverse_ref)
    for copy in first:
        copy.wait()
    vectors = vectors_ref[...]
    across = halves(vectors.T)
    combined = halves(by_transpose(halves(vectors), halves(factors_ref[...])))
    for b in range(count):
        for copy in parts[b]:
            copy.wait()
        leaf_block(me_ref, part_ref[b], across, combined, value_ref, rest_ref.at[b], own_ref, away_ref, b)
    panel = part_ref[0]
    value_ref[...] = plain(halves(panel.T), halves(panel))
    hand_over(me_ref, value_ref, own_ref, away_ref, count)
    start = 0
    for out_ref in aways:
        out_ref[...] = away_ref[start : start + out_ref.shape[0]]
        start += out_ref.shape[0]
    inverse_copy.wait()


def hand_over(me_ref, value_ref, own_ref, away_ref, slot):
    half = value_ref.shape[0] // 2
    core = me_ref[0] % 2
    target = slice(slot * half, (slot + 1) * half)
    own_ref[target] = value_ref[pl.ds(pl.multiple_of(core * half, half), half)]
    away_ref[target] = value_ref[pl.ds(pl.multiple_of((1 - core) * half, half), half)]


def leaf_block(me_ref, part, across, combined, value_ref, rest_ref, own_ref, away_ref, slot):
    width = value_ref.shape[0]
    out = part - plain(combined, halves(plain(across, halves(part))))
    rest_ref[...] = out[width:]
    value_ref[...] = out[:width].T
    hand_over(me_ref, value_ref, own_ref, away_ref, slot)


def store_kernel(me_ref, first_ref, inverse_ref, mark_ref, updated_hbm, basis_hbm, basis_ref, sems):
    count, width = first_ref.shape[:2]
    copies = []
    for b in range(count):
        source = first_ref.at[b]
        target = updated_hbm.at[pl.ds(width, width), pl.ds(b * width, width)]
        copies.append(pltpu.make_async_copy(source, target, sems.at[b]))
        copies[-1].start()
    basis_ref[...] = plain(halves(first_ref[0]), halves(inverse_ref[...]))
    copies.append(pltpu.make_async_copy(basis_ref, basis_hbm.at[pl.ds(width, width)], sems.at[len(copies)]))
    mark_ref[...] = jnp.zeros_like(mark_ref)
    copies[-1].start()
    for copy in copies:
        copy.wait()


def core_kernel(me_ref, own_ref, *refs):
    theres, packed_ref, refs = refs[:-12], refs[-12], refs[-11:]
    sends, dones, (gram_ref, low_ref, high_ref) = refs[:4], refs[4:8], refs[8:]
    me = me_ref[0]
    half = own_ref.shape[1] // 2
    quarter = half // 4
    cut = own_ref.shape[0] - half
    count = cut // half
    odd = me % 2 == 1
    there = jnp.concatenate([ref[...] for ref in theres], axis=0)
    gram_ref[...] = own_ref[cut:] + there[cut:]
    mine, there = own_ref[:cut], there[:cut]
    low = jnp.where(odd, there, mine)
    high = jnp.where(odd, mine, there)
    low, high = tree_node(low, high, unpack(packed_ref[0], packed_ref[1]))
    low_ref[...] = low
    high_ref[...] = high
    for r in range(4):
        start = (place(me) ^ r) * quarter
        for b in range(count):
            source = pl.ds(pl.multiple_of(b * half + start, quarter), quarter)
            target = slice(b * quarter, (b + 1) * quarter)
            sends[r][target] = low_ref[source]
            dones[r][target] = high_ref[source]
        if sends[r].shape[0] > count * quarter:
            sends[r][count * quarter :] = jnp.zeros_like(sends[r][count * quarter :])


def gather_kernel(me_ref, *refs):
    parts, (stack_ref, held_ref) = refs[:4], refs[4:]
    for r in range(1, 4):
        stack_ref[r - 1] = parts[r][...]
    held_ref[...] = by_place(me_ref[0], [ref[...] for ref in parts], 0)


def hold_kernel(me_ref, held_ref, part_ref, out_ref, *, level):
    rows = slice(0, out_ref.shape[0])
    out_ref[...] = jnp.where((me_ref[0] >> level) % 2 == 1, part_ref[rows], held_ref[rows])


def add_kernel(me_ref, first_ref, second_ref, out_ref):
    out_ref[...] = first_ref[...] + second_ref[...]


def fill(send_ref, value):
    cols = value.shape[0]
    send_ref[:cols] = value
    if send_ref.shape[0] > cols:
        send_ref[cols:] = jnp.zeros_like(send_ref[cols:])


def prepare_kernel(me_ref, packed_ref, stack_ref, stack_there_ref, joint_ref, vectors_ref, held_ref):
    me = me_ref[0]
    pairs = [(packed_ref[0], packed_ref[1])]
    pairs += [by_core(me % 2, stack_ref[r], stack_there_ref[r]) for r in range(3)]
    firsts, seconds = [pair[0] for pair in pairs], [pair[1] for pair in pairs]
    pairs = [(by_place(me, firsts, j), by_place(me, seconds, j)) for j in range(4)]
    held_ref[0], held_ref[1] = pairs[0]
    for j in range(4):
        vectors = unpack_vectors(*pairs[j])
        vectors_ref[j, 0], vectors_ref[j, 1] = vectors
        if j > 0:
            factors = unpack_factors(*pairs[j])
            natural = (factors[0].astype(F32) + factors[1].astype(F32)).T
            joint = jnp.concatenate([natural, by_transpose(vectors, factors)], axis=0)
            joint_ref[j - 1, 0], joint_ref[j - 1, 1] = halves(joint)


def plane_kernel(me_ref, *refs, level):
    gots, (joint_ref, vectors_ref, head_ref, send_ref, done_ref) = refs[:4], refs[4:]
    cols = head_ref.shape[0]
    parts = [ref[:cols] for ref in gots]
    heads = [by_place(me_ref[0], parts, j) for j in range(4)]
    for low, high, j in ((0, 1, 1), (2, 3, 3), (0, 2, 2)):
        both = jnp.concatenate([heads[low], heads[high]], axis=1)
        coeffs = plain(halves(both), (joint_ref[j - 1, 0], joint_ref[j - 1, 1]))
        heads[low] = heads[low] - coeffs
        heads[high] = heads[high] - by_transpose(halves(coeffs), (vectors_ref[j, 0], vectors_ref[j, 1]))
    for j in range(4):
        done_ref[j] = heads[j]
    head_ref[...] = heads[0]
    upper = (me_ref[0] >> level) % 2 == 1
    ahead = plain(halves(heads[0]), (vectors_ref[0, 0], vectors_ref[0, 1]))
    fill(send_ref, jnp.where(upper, ahead, heads[0]))


def ready_kernel(me_ref, held_ref, part_ref, part_there_ref, ready_ref, *outs, level):
    me = me_ref[0]
    upper = (me >> level) % 2 == 1
    held = held_ref[0], held_ref[1]
    others = by_core(me % 2, part_ref[...], part_there_ref[...])
    need = held[0].shape[1] // 4 + EXTRA
    node = [jnp.where(upper, a[:need], b[:need]) for a, b in zip(held, others)]
    ready_ref[0], ready_ref[1] = unpack_factors(*node)
    ready_ref[2], ready_ref[3] = unpack_vectors(*held)
    if outs:
        following = [jnp.where(upper, b, a) for a, b in zip(held, others)]
        ready_ref[4], ready_ref[5] = unpack_vectors(*following)
        outs[0][0], outs[0][1] = following


def line_node(me_ref, head_ref, result_ref, mine_ref, there_ref, ready_ref, level):
    me = me_ref[0]
    cols = head_ref.shape[0]
    upper = (me >> level) % 2 == 1
    head, there = head_ref[...], there_ref[:cols]
    coeffs = by_transpose(halves(mine_ref[:cols] + there), (ready_ref[0], ready_ref[1]))
    low = jnp.where(upper, there, head) - coeffs
    plane = me >> 3
    below = (1 << (level - 2)) - 1
    second = (plane & below) == (1 << (level - 3))
    high = head - by_transpose(halves(coeffs), (ready_ref[2], ready_ref[3]))
    return low, jnp.where(second, high, result_ref[...])


def line_kernel(me_ref, *refs, level):
    ready_ref, (head_out, result_out, send_ref) = refs[4], refs[5:]
    low, result = line_node(me_ref, *refs[:5], level)
    ahead = (me_ref[0] >> (level + 1)) % 2 == 1
    head_out[...] = low
    result_out[...] = result
    fill(send_ref, jnp.where(ahead, plain(halves(low), (ready_ref[4], ready_ref[5])), low))


def last_kernel(me_ref, *refs, level):
    done_ref, sends, all_ref = refs[5], refs[6:10], refs[10]
    me = me_ref[0]
    low, result = line_node(me_ref, *refs[:5], level)
    cols = low.shape[0]
    all_ref[0] = jnp.where((me >> 3) == 0, low, result)
    for j in range(1, 4):
        all_ref[j] = done_ref[j]
    for r in range(4):
        sends[r][:cols] = all_ref[place(me) ^ r]
        sends[r][cols:] = low[: sends[r].shape[0] - cols]


def pass_kernel(me_ref, *refs):
    backs, dones, out_ref = refs[:2], refs[2:4], refs[4]
    odd = me_ref[0] % 2 == 1
    cols, rows = dones[0].shape[0], out_ref.shape[1]
    for r in range(2):
        out_ref[r, :cols] = jnp.where(odd, backs[r][:cols], dones[r][...])
        out_ref[r, cols:] = backs[r][cols:rows]


def near_kernel(me_ref, *refs):
    backs, dones, (_, updated_hbm, out_ref, sems) = refs[:4], refs[4:8], refs[8:]
    count, width, half = out_ref.shape
    quarter = half // 4
    me = me_ref[0]
    core = me % 2
    odd = core == 1
    copies = []
    for b in range(count):
        rows = slice(b * quarter, (b + 1) * quarter)
        pieces = [jnp.where(odd, dones[r][rows], backs[r][rows]) for r in range(4)]
        out_ref[b] = jnp.concatenate([by_place(me, pieces, j) for j in range(4)], axis=0).T
        columns = pl.ds(pl.multiple_of(b * width + core * half, half), half)
        copies.append(pltpu.make_async_copy(out_ref.at[b], updated_hbm.at[pl.ds(0, width), columns], sems.at[b]))
        copies[-1].start()
    for copy in copies:
        copy.wait()


def far_kernel(me_ref, *refs, total):
    backs, dones = refs[:4], refs[4:8]
    theres, half_ref, half_there, inverse_ref, _, _, updated_hbm, basis_hbm, gram_hbm = refs[8:10], *refs[10:18]
    panel_ref, sum_ref, out_ref, basis_ref, gram_ref, sems = refs[18:]
    count, width, half = out_ref.shape
    quarter = half // 4
    cols = count * quarter
    me = me_ref[0]
    core = me % 2
    odd = core == 1
    copies = []

    def put(source, target):
        copies.append(pltpu.make_async_copy(source, target, sems.at[len(copies)]))
        copies[-1].start()

    def target(part, r):
        return pl.ds(pl.multiple_of(part * half + (place(me) ^ r) * quarter, quarter), quarter)

    for r in range(4):
        panel_ref[target(core, r)] = backs[r][cols : cols + quarter]
        panel_ref[target(1 - core, r)] = theres[r // 2][r % 2, cols:]
    sum_ref[pl.ds(pl.multiple_of(core * half, half), half)] = half_ref[...]
    sum_ref[pl.ds(pl.multiple_of((1 - core) * half, half), half)] = half_there[...]
    panel = halves(panel_ref[...])
    gram_ref[...] = (sum_ref[...] - by_transpose(panel, panel)) / total
    put(gram_ref, gram_hbm)
    for b in range(count):
        rows = slice(b * quarter, (b + 1) * quarter)
        pieces = [theres[r // 2][r % 2, rows] for r in range(4)]
        far = jnp.concatenate([by_place(me, pieces, j) for j in range(4)], axis=0).T
        out_ref[b] = far
        columns = pl.ds(pl.multiple_of(b * width + (1 - core) * half, half), half)
        put(out_ref.at[b], updated_hbm.at[pl.ds(0, width), columns])
        if b == 0:
            pieces = [jnp.where(odd, dones[r][rows], backs[r][rows]) for r in range(4)]
            near = jnp.concatenate([by_place(me, pieces, j) for j in range(4)], axis=0).T
            head = jnp.concatenate(by_core(core, near, far), axis=1)
            basis = plain(halves(head), halves(inverse_ref[...]))
            basis_ref[...] = jnp.where(me == 0, 0.0, basis)
            put(basis_ref, basis_hbm.at[pl.ds(0, width)])
    for copy in copies:
        copy.wait()


def body(trailing, leaf_vectors, leaf_factors, tree_vectors, tree_factors, inverse_factor):
    rows, columns = trailing.shape
    width = leaf_vectors.shape[1]
    half = width // 2
    quarter = half // 4
    count = columns // width
    devices = lax.axis_size("rows")
    levels = devices.bit_length() - 1
    me = lax.axis_index("rows").astype(jnp.int32)
    me_array = me.reshape(1)
    part_shape = (half + EXTRA, width)
    latest = []

    def exchange(value, shift):
        return lax.ppermute(value, "rows", [(i, i ^ shift) for i in range(devices)])

    def among(value, shift, member):
        return lax.ppermute(value, "rows", [(i, i ^ shift if member(i) else i) for i in range(devices)])

    def around(values):
        there = [exchange(values[r], 2 * r) for r in (3, 1, 2)]
        return [values[0], there[1], there[2], there[0]]

    def shape(*dims):
        return jax.ShapeDtypeStruct(dims, F32)

    def vmem(*dims):
        return pltpu.VMEM(dims, F32)

    def sems(number):
        return pltpu.SemaphoreType.DMA((number,))

    def call(kernel, operands, outs, scratch=(), away_in=(), away_out=(), aliases=(), before=(), work=1, chained=True):
        number = len(operands)
        operands = [pltpu.with_memory_space_constraint(x, pltpu.HBM) if i in away_in else x for i, x in enumerate(operands)]
        outs = [(pltpu.HBM if i in away_out else pltpu.VMEM)(x.shape, x.dtype) for i, x in enumerate(outs)]
        unused = [*latest, *before] if chained else []

        def kernel_on(*refs):
            kernel(*refs[: number + 1], *refs[number + 1 + len(unused) :])

        values = pl.pallas_call(
            kernel_on,
            out_shape=tuple(outs),
            in_specs=[SCALAR]
            + [AWAY if i in away_in else WHOLE for i in range(number)]
            + [pl.BlockSpec(memory_space=pl.ANY)] * len(unused),
            out_specs=tuple(AWAY if i in away_out else WHOLE for i in range(len(outs))),
            scratch_shapes=list(scratch),
            input_output_aliases=dict(aliases),
            compiler_params=PARAMS,
            cost_estimate=pl.CostEstimate(flops=work, bytes_accessed=1, transcendentals=0),
        )(me_array, *operands, *unused)
        if chained and 0 not in away_out:
            latest[:] = values[:1]
        return values

    raw = [exchange(tree_vectors, 1), exchange(tree_factors, 1)]
    tree_vectors, tree_factors = call(
        load_kernel, (tree_vectors, tree_factors), [shape(width, width)] * 2, [sems(2)], range(2)
    )

    chip_low, chip_high, chip_part = call(
        pack_kernel, (tree_vectors, tree_factors, *raw),
        (shape(2, *part_shape), shape(2, *part_shape), shape(*part_shape)),
        [vmem(4, width, width), sems(4)], (),
    )
    plane_parts = [exchange(chip_part, 2 * r) for r in (3, 1, 2)]
    plane_parts = [plane_parts[1], plane_parts[2], plane_parts[0]]

    leaf_rows = count * half + half
    piece = leaf_rows // 3 // 8 * 8 + 8
    pieces = [min(piece, leaf_rows - start) for start in range(0, leaf_rows, piece)]
    own, rest, inverse_factor, *aways = call(
        leaf_kernel, (trailing, leaf_vectors, leaf_factors, inverse_factor),
        [shape(leaf_rows, width), shape(count, width, width), shape(width, width)]
        + [shape(piece, width) for piece in pieces],
        [
            vmem(count, rows, width), vmem(rows, width), vmem(width, width), vmem(width, width), vmem(leaf_rows, width),
            sems(count * (rows // width) + 3),
        ],
        range(4),
    )
    theres = [exchange(away, 1) for away in aways]
    stack, held_part = call(
        gather_kernel, (chip_part, *plane_parts), (shape(3, *part_shape), shape(*part_shape)), work=1,
    )
    stack_there = exchange(stack, 1)
    cols = count * quarter
    outs = call(
        core_kernel, (own, *theres, chip_high),
        [shape(cols, width)] * 3 + [shape(cols + 8, width)] + [shape(cols, width)] * 4 + [shape(half, width)],
        [vmem(count * half, width), vmem(count * half, width)],
    )
    sends, dones, gram_half = outs[:4], outs[4:8], outs[8]
    for level in (levels - 1, 1, 2, *range(3, levels - 1)):
        (gram_half,) = call(
            add_kernel, (gram_half, exchange(gram_half, 1 << level)), (shape(half, width),), chained=False
        )
    gots = around(sends)

    parts = [exchange(held_part, 8)]
    for level in range(4, levels):
        short = half // 2 + EXTRA if level == levels - 1 else half + EXTRA
        (held_part,) = call(
            functools.partial(hold_kernel, level=level - 1), (held_part, parts[-1]), (shape(short, width),),
            chained=False,
        )
        parts.append(exchange(held_part, 1 << level))

    def split(*dims):
        return jax.ShapeDtypeStruct(dims, BF16)

    joint, vectors, held = call(
        prepare_kernel, (chip_low, stack, stack_there),
        (split(3, 2, 2 * width, width), split(4, 2, width, width), shape(2, *part_shape)),
    )
    head, send, plane_done = call(
        functools.partial(plane_kernel, level=3), (*gots, joint, vectors),
        (shape(cols, width), shape(cols + 24, width), shape(4, cols, width)),
    )
    result = head
    for level in range(3, levels):
        part = parts[level - 3]
        last = level == levels - 1
        ready, *helds = call(
            functools.partial(ready_kernel, level=level), (held, part, exchange(part, 1)),
            [split(4 if last else 6, width, width)] + ([] if last else [shape(2, *part_shape)]),
        )
        operands = (head, result, send, exchange(send, 1 << level), ready)
        if last:
            _, updated, basis = call(
                store_kernel, (rest, inverse_factor), (shape(8, width), shape(rows, columns), shape(rows, width)),
                [vmem(width, width), sems(count + 1)], (), (1, 2),
            )
            sends = call(
                functools.partial(last_kernel, level=level), (*operands, plane_done),
                [shape(cols + quarter, width)] * 3 + [shape(cols + quarter + 8, width)], [vmem(4, cols, width)],
            )
        else:
            (held,) = helds
            head, result, send = call(
                functools.partial(line_kernel, level=level), operands,
                [shape(cols, width), shape(cols, width), shape(cols, width)],
            )

    backs = around(sends)
    gram_there = exchange(gram_half, 1)
    theres = []
    for r in (0, 2):
        (passed,) = call(
            pass_kernel, (*backs[r : r + 2], *dones[r : r + 2]), (shape(2, cols + quarter, width),),
            before=(gram_half,) if r == 2 else (),
        )
        theres.append(exchange(passed, 1))
    (updated,) = call(
        near_kernel, (*backs, *dones, updated), (shape(rows, columns),),
        [vmem(count, width, half), sems(count)], (8,), (0,), {9: 0},
    )
    return call(
        functools.partial(far_kernel, total=float(rows * devices)),
        (*backs, *dones, *theres, gram_half, gram_there, inverse_factor, updated, basis),
        (shape(rows, columns), shape(rows, width), shape(width, width)),
        [vmem(width, width), vmem(width, width), vmem(count, width, half), vmem(width, width), vmem(width, width), sems(count + 2)],
        (13, 14), (0, 1, 2), {14: 0, 15: 1},
    )


def solution(mesh):
    in_specs = (
        P("rows", None),
        P("rows", None),
        P("rows", None),
        P("rows", None),
        P("rows", None),
        P(),
    )
    out_specs = (P("rows", None), P("rows", None), P())
    return jax.shard_map(body, mesh=mesh, in_specs=in_specs, out_specs=out_specs, check_vma=False)
```

```python
import functools
import jax
import jax.numpy as jnp
from jax import lax
from jax.experimental import pallas as pl
from jax.experimental.pallas import tpu as pltpu
from jax.sharding import PartitionSpec as P

F32 = jnp.float32
BF16 = jnp.bfloat16
EXTRA = 8
PARAMS = pltpu.CompilerParams(vmem_limit_bytes=20 * 1024 * 1024)
WHOLE = pl.BlockSpec(memory_space=pltpu.VMEM)
SCALAR = pl.BlockSpec(memory_space=pltpu.SMEM)
AWAY = pl.BlockSpec(memory_space=pltpu.HBM)


def halves(value):
    high = value.astype(BF16)
    return high, (value - high.astype(F32)).astype(BF16)


def times(left, right, sides):
    first = jnp.concatenate([left[0], left[0], left[1]], axis=sides[0])
    second = jnp.concatenate([right[0], right[1], right[0]], axis=sides[1])
    dims = ((sides[:1], sides[1:]), ((), ()))
    return lax.dot_general(first, second, dims, preferred_element_type=F32)


def plain(left, right):
    return times(left, right, (1, 0))


def by_transpose(left, right):
    return times(left, right, (1, 1))


def masks(size):
    row = lax.broadcasted_iota(jnp.int32, (size, size), 0)
    col = lax.broadcasted_iota(jnp.int32, (size, size), 1)
    return row, col


def diagonal_of(square):
    row, col = masks(square.shape[0])
    return jnp.sum(jnp.where(row == col, square, 0.0), axis=0, keepdims=True)


def pack_kernel(me_ref, *refs):
    sources, (low_ref, high_ref, part_ref), (buffer_ref, sems) = refs[:4], refs[4:7], refs[7:]
    copies = [pltpu.make_async_copy(source, buffer_ref.at[i], sems.at[i]) for i, source in enumerate(sources)]
    for copy in copies:
        copy.start()
    for copy in copies:
        copy.wait()
    core = me_ref[0] % 2
    half = buffer_ref.shape[1] // 2
    row, col = masks(half)
    both_vectors = by_core(core, buffer_ref[0], buffer_ref[2])
    both_factors = by_core(core, buffer_ref[1], buffer_ref[3])
    for vectors, factors, out_ref in zip(both_vectors, both_factors, (low_ref, high_ref)):
        first, second = factors[:half, :half], factors[half:, half:]
        square = jnp.where(row > col, first.T, jnp.where(row < col, second, 0.0))
        t_rows = jnp.concatenate([square, factors[:half, half:].T], axis=1)
        t_diagonal = jnp.concatenate([diagonal_of(first), diagonal_of(second)], axis=1)
        first, second = vectors[:half, :half], vectors[half:, half:]
        square = jnp.where(row <= col, first, second.T)
        v_rows = jnp.concatenate([square, vectors[:half, half:]], axis=1)
        v_diagonal = jnp.concatenate([diagonal_of(second)] * 2, axis=1)
        line = lax.broadcasted_iota(jnp.int32, (EXTRA, 2 * half), 0)
        diagonals = jnp.where(line == 0, t_diagonal, v_diagonal)
        for part in range(2):
            rows = slice(part * half // 2, (part + 1) * half // 2)
            out_ref[part, : half // 2] = t_rows[rows]
            out_ref[part, half // 2 : half // 2 + EXTRA] = diagonals
            out_ref[part, half // 2 + EXTRA :] = v_rows[rows]
    part_ref[...] = low_ref[core]


def unpack_factors(first, second):
    half = first.shape[1] // 2
    rows = jnp.concatenate([first[: half // 2], second[: half // 2]], axis=0)
    row, col = masks(half)
    square, corner = rows[:, :half], rows[:, half:]
    diagonal = first[half // 2 : half // 2 + 1]
    upper_left = jnp.where(row > col, square, jnp.where(row == col, diagonal[:, :half], 0.0))
    lower_right = jnp.where(row > col, square.T, jnp.where(row == col, diagonal[:, half:], 0.0))
    above = jnp.concatenate([upper_left, jnp.zeros_like(upper_left)], axis=1)
    return halves(jnp.concatenate([above, jnp.concatenate([corner, lower_right], axis=1)], axis=0))


def unpack_vectors(first, second):
    half = first.shape[1] // 2
    start = half // 2 + EXTRA
    rows = jnp.concatenate([first[start:], second[start:]], axis=0)
    row, col = masks(half)
    square, corner = rows[:, :half], rows[:, half:]
    diagonal = first[half // 2 + 1 : half // 2 + 2, :half]
    upper_left = jnp.where(row <= col, square, 0.0)
    lower_right = jnp.where(row < col, square.T, jnp.where(row == col, diagonal, 0.0))
    above = jnp.concatenate([upper_left, corner], axis=1)
    return halves(jnp.concatenate([above, jnp.concatenate([jnp.zeros_like(corner), lower_right], axis=1)], axis=0))


def unpack(first, second):
    return unpack_vectors(first, second), unpack_factors(first, second)


def by_core(core, mine, there):
    odd = core == 1
    return jnp.where(odd, there, mine), jnp.where(odd, mine, there)


def place(me):
    return (me >> 1) & 3


def by_place(me, parts, wanted):
    source = place(me) ^ wanted
    out = parts[0]
    for r in range(1, 4):
        out = jnp.where(source == r, parts[r], out)
    return out


def tree_node(low, high, reflector):
    vectors, factors = reflector
    node = by_transpose(halves(low + plain(halves(high), vectors)), factors)
    return low - node, high - by_transpose(halves(node), vectors)


def leaf_first_kernel(
    me_ref, trailing_hbm, vectors_hbm, factors_hbm, inverse_hbm,
    own_ref, away_one, away_two, rest_ref, later_ref, inverse_ref, across_ref, combined_ref,
    part_ref, vectors_ref, factors_ref, value_ref, away_ref, sems,
):
    count, rows, width = part_ref.shape
    copies = []

    def fetch(source, target):
        copies.append(pltpu.make_async_copy(source, target, sems.at[len(copies)]))
        copies[-1].start()
        return copies[-1]

    def fetch_part(b, target):
        cuts = [slice(c, c + width) for c in range(0, rows, width)]
        return [fetch(trailing_hbm.at[c, pl.ds(b * width, width)], target.at[c]) for c in cuts]

    first = [fetch(vectors_hbm, vectors_ref), fetch(factors_hbm, factors_ref)]
    parts = [fetch_part(b, part_ref.at[b]) for b in range(count)]
    for copy in first:
        copy.wait()
    last = [fetch_part(count + b, later_ref.at[b]) for b in range(later_ref.shape[0])]
    last.append([fetch(inverse_hbm, inverse_ref)])
    vectors = vectors_ref[...]
    across = halves(vectors.T)
    across_ref[0], across_ref[1] = across
    combined = halves(by_transpose(halves(vectors), halves(factors_ref[...])))
    combined_ref[0], combined_ref[1] = combined
    for b in range(count):
        for copy in parts[b]:
            copy.wait()
        leaf_block(me_ref, part_ref[b], across, combined, value_ref, rest_ref.at[b], own_ref, away_ref, b)
    panel = part_ref[0]
    value_ref[...] = plain(halves(panel.T), halves(panel))
    hand_over(me_ref, value_ref, own_ref, away_ref, count)
    cut = away_one.shape[0]
    away_one[...] = away_ref[:cut]
    away_two[...] = away_ref[cut:]
    for group in last:
        for copy in group:
            copy.wait()


def hand_over(me_ref, value_ref, own_ref, away_ref, slot):
    half = value_ref.shape[0] // 2
    core = me_ref[0] % 2
    target = slice(slot * half, (slot + 1) * half)
    own_ref[target] = value_ref[pl.ds(pl.multiple_of(core * half, half), half)]
    away_ref[target] = value_ref[pl.ds(pl.multiple_of((1 - core) * half, half), half)]


def leaf_block(me_ref, part, across, combined, value_ref, rest_ref, own_ref, away_ref, slot):
    width = value_ref.shape[0]
    out = part - plain(combined, halves(plain(across, halves(part))))
    rest_ref[...] = out[width:]
    value_ref[...] = out[:width].T
    hand_over(me_ref, value_ref, own_ref, away_ref, slot)


def leaf_second_kernel(me_ref, later_ref, across_ref, combined_ref, own_ref, rest_ref, *refs):
    aways, value_ref = refs[:-1], refs[-1]
    half = value_ref.shape[0] // 2
    across = across_ref[0], across_ref[1]
    combined = combined_ref[0], combined_ref[1]
    for b in range(later_ref.shape[0]):
        own_b = own_ref.at[pl.ds(b * half, half)]
        leaf_block(me_ref, later_ref[b], across, combined, value_ref, rest_ref.at[b], own_b, aways[b], 0)


def store_kernel(me_ref, first_ref, second_ref, inverse_ref, mark_ref, updated_hbm, basis_hbm, basis_ref, sems):
    count, width = first_ref.shape[:2]
    copies = []
    for b in range(count + second_ref.shape[0]):
        source = first_ref.at[b] if b < count else second_ref.at[b - count]
        target = updated_hbm.at[pl.ds(width, width), pl.ds(b * width, width)]
        copies.append(pltpu.make_async_copy(source, target, sems.at[b]))
        copies[-1].start()
    basis_ref[...] = plain(halves(first_ref[0]), halves(inverse_ref[...]))
    copies.append(pltpu.make_async_copy(basis_ref, basis_hbm.at[pl.ds(width, width)], sems.at[len(copies)]))
    mark_ref[...] = jnp.zeros_like(mark_ref)
    copies[-1].start()
    for copy in copies:
        copy.wait()


def core_first_kernel(me_ref, own_ref, one_ref, two_ref, packed_ref, low_ref, high_ref, gram_ref):
    cut = low_ref.shape[0]
    there = jnp.concatenate([one_ref[...], two_ref[...]], axis=0)
    gram_ref[...] = own_ref[cut:] + there[cut:]
    core_node(me_ref, own_ref[:cut], there[:cut], packed_ref, low_ref, high_ref)


def core_node(me_ref, mine, there, packed_ref, low_ref, high_ref):
    odd = me_ref[0] % 2 == 1
    low, high = jnp.where(odd, there, mine), jnp.where(odd, mine, there)
    low_ref[...], high_ref[...] = tree_node(low, high, unpack(packed_ref[0], packed_ref[1]))


def core_kernel(me_ref, low_a_ref, high_a_ref, own_ref, *refs):
    theres, packed_ref, refs = refs[:-11], refs[-11], refs[-10:]
    sends, dones, (low_ref, high_ref) = refs[:4], refs[4:8], refs[8:]
    me = me_ref[0]
    half = own_ref.shape[1] // 2
    quarter = half // 4
    there = jnp.concatenate([ref[...] for ref in theres], axis=0)
    core_node(me_ref, own_ref[...], there, packed_ref, low_ref, high_ref)
    first = low_a_ref.shape[0] // half
    count = first + own_ref.shape[0] // half
    for r in range(4):
        start = (place(me) ^ r) * quarter
        for b in range(count):
            lows, highs, block = (low_a_ref, high_a_ref, b) if b < first else (low_ref, high_ref, b - first)
            source = pl.ds(pl.multiple_of(block * half + start, quarter), quarter)
            target = slice(b * quarter, (b + 1) * quarter)
            sends[r][target] = lows[source]
            dones[r][target] = highs[source]
        if sends[r].shape[0] > count * quarter:
            sends[r][count * quarter :] = jnp.zeros_like(sends[r][count * quarter :])


def gather_kernel(me_ref, *refs):
    parts, (stack_ref, held_ref) = refs[:4], refs[4:]
    for r in range(1, 4):
        stack_ref[r - 1] = parts[r][...]
    held_ref[...] = by_place(me_ref[0], [ref[...] for ref in parts], 0)


def hold_kernel(me_ref, held_ref, part_ref, out_ref, *, level):
    rows = slice(0, out_ref.shape[0])
    out_ref[...] = jnp.where((me_ref[0] >> level) % 2 == 1, part_ref[rows], held_ref[rows])


def add_kernel(me_ref, first_ref, second_ref, out_ref):
    out_ref[...] = first_ref[...] + second_ref[...]


def fill(send_ref, value):
    cols = value.shape[0]
    send_ref[:cols] = value
    if send_ref.shape[0] > cols:
        send_ref[cols:] = jnp.zeros_like(send_ref[cols:])


def prepare_kernel(me_ref, packed_ref, stack_ref, stack_there_ref, joint_ref, vectors_ref, held_ref):
    me = me_ref[0]
    pairs = [(packed_ref[0], packed_ref[1])]
    pairs += [by_core(me % 2, stack_ref[r], stack_there_ref[r]) for r in range(3)]
    firsts, seconds = [pair[0] for pair in pairs], [pair[1] for pair in pairs]
    pairs = [(by_place(me, firsts, j), by_place(me, seconds, j)) for j in range(4)]
    held_ref[0], held_ref[1] = pairs[0]
    for j in range(4):
        vectors = unpack_vectors(*pairs[j])
        vectors_ref[j, 0], vectors_ref[j, 1] = vectors
        if j > 0:
            factors = unpack_factors(*pairs[j])
            natural = (factors[0].astype(F32) + factors[1].astype(F32)).T
            joint = jnp.concatenate([natural, by_transpose(vectors, factors)], axis=0)
            joint_ref[j - 1, 0], joint_ref[j - 1, 1] = halves(joint)


def plane_kernel(me_ref, *refs, level):
    gots, (joint_ref, vectors_ref, head_ref, send_ref, done_ref) = refs[:4], refs[4:]
    cols = head_ref.shape[0]
    parts = [ref[:cols] for ref in gots]
    heads = [by_place(me_ref[0], parts, j) for j in range(4)]
    for low, high, j in ((0, 1, 1), (2, 3, 3), (0, 2, 2)):
        both = jnp.concatenate([heads[low], heads[high]], axis=1)
        coeffs = plain(halves(both), (joint_ref[j - 1, 0], joint_ref[j - 1, 1]))
        heads[low] = heads[low] - coeffs
        heads[high] = heads[high] - by_transpose(halves(coeffs), (vectors_ref[j, 0], vectors_ref[j, 1]))
    for j in range(4):
        done_ref[j] = heads[j]
    head_ref[...] = heads[0]
    upper = (me_ref[0] >> level) % 2 == 1
    ahead = plain(halves(heads[0]), (vectors_ref[0, 0], vectors_ref[0, 1]))
    fill(send_ref, jnp.where(upper, ahead, heads[0]))


def ready_kernel(me_ref, held_ref, part_ref, part_there_ref, ready_ref, *outs, level):
    me = me_ref[0]
    upper = (me >> level) % 2 == 1
    held = held_ref[0], held_ref[1]
    others = by_core(me % 2, part_ref[...], part_there_ref[...])
    need = held[0].shape[1] // 4 + EXTRA
    node = [jnp.where(upper, a[:need], b[:need]) for a, b in zip(held, others)]
    ready_ref[0], ready_ref[1] = unpack_factors(*node)
    ready_ref[2], ready_ref[3] = unpack_vectors(*held)
    if outs:
        following = [jnp.where(upper, b, a) for a, b in zip(held, others)]
        ready_ref[4], ready_ref[5] = unpack_vectors(*following)
        outs[0][0], outs[0][1] = following


def line_node(me_ref, head_ref, result_ref, mine_ref, there_ref, ready_ref, level):
    me = me_ref[0]
    cols = head_ref.shape[0]
    upper = (me >> level) % 2 == 1
    head, there = head_ref[...], there_ref[:cols]
    coeffs = by_transpose(halves(mine_ref[:cols] + there), (ready_ref[0], ready_ref[1]))
    low = jnp.where(upper, there, head) - coeffs
    plane = me >> 3
    below = (1 << (level - 2)) - 1
    second = (plane & below) == (1 << (level - 3))
    high = head - by_transpose(halves(coeffs), (ready_ref[2], ready_ref[3]))
    return low, jnp.where(second, high, result_ref[...])


def line_kernel(me_ref, *refs, level):
    ready_ref, (head_out, result_out, send_ref) = refs[4], refs[5:]
    low, result = line_node(me_ref, *refs[:5], level)
    ahead = (me_ref[0] >> (level + 1)) % 2 == 1
    head_out[...] = low
    result_out[...] = result
    fill(send_ref, jnp.where(ahead, plain(halves(low), (ready_ref[4], ready_ref[5])), low))


def last_kernel(me_ref, *refs, level):
    done_ref, sends, all_ref = refs[5], refs[6:10], refs[10]
    me = me_ref[0]
    low, result = line_node(me_ref, *refs[:5], level)
    cols = low.shape[0]
    all_ref[0] = jnp.where((me >> 3) == 0, low, result)
    for j in range(1, 4):
        all_ref[j] = done_ref[j]
    for r in range(4):
        sends[r][:cols] = all_ref[place(me) ^ r]
        sends[r][cols:] = low[: sends[r].shape[0] - cols]


def pass_kernel(me_ref, *refs):
    backs, dones, out_ref = refs[:2], refs[2:4], refs[4]
    odd = me_ref[0] % 2 == 1
    cols, rows = dones[0].shape[0], out_ref.shape[1]
    for r in range(2):
        out_ref[r, :cols] = jnp.where(odd, backs[r][:cols], dones[r][...])
        out_ref[r, cols:] = backs[r][cols:rows]


def near_kernel(me_ref, *refs):
    backs, dones, (_, updated_hbm, out_ref, sems) = refs[:4], refs[4:8], refs[8:]
    count, width, half = out_ref.shape
    quarter = half // 4
    me = me_ref[0]
    core = me % 2
    odd = core == 1
    copies = []
    for b in range(count):
        rows = slice(b * quarter, (b + 1) * quarter)
        pieces = [jnp.where(odd, dones[r][rows], backs[r][rows]) for r in range(4)]
        out_ref[b] = jnp.concatenate([by_place(me, pieces, j) for j in range(4)], axis=0).T
        columns = pl.ds(pl.multiple_of(b * width + core * half, half), half)
        copies.append(pltpu.make_async_copy(out_ref.at[b], updated_hbm.at[pl.ds(0, width), columns], sems.at[b]))
        copies[-1].start()
    for copy in copies:
        copy.wait()


def far_kernel(me_ref, *refs, total):
    backs, dones = refs[:4], refs[4:8]
    theres, half_ref, half_there, inverse_ref, _, _, updated_hbm, basis_hbm, gram_hbm = refs[8:10], *refs[10:18]
    panel_ref, sum_ref, out_ref, basis_ref, gram_ref, sems = refs[18:]
    count, width, half = out_ref.shape
    quarter = half // 4
    cols = count * quarter
    me = me_ref[0]
    core = me % 2
    odd = core == 1
    copies = []

    def put(source, target):
        copies.append(pltpu.make_async_copy(source, target, sems.at[len(copies)]))
        copies[-1].start()

    def target(part, r):
        return pl.ds(pl.multiple_of(part * half + (place(me) ^ r) * quarter, quarter), quarter)

    for r in range(4):
        panel_ref[target(core, r)] = backs[r][cols : cols + quarter]
        panel_ref[target(1 - core, r)] = theres[r // 2][r % 2, cols:]
    sum_ref[pl.ds(pl.multiple_of(core * half, half), half)] = half_ref[...]
    sum_ref[pl.ds(pl.multiple_of((1 - core) * half, half), half)] = half_there[...]
    panel = halves(panel_ref[...])
    gram_ref[...] = (sum_ref[...] - by_transpose(panel, panel)) / total
    put(gram_ref, gram_hbm)
    for b in range(count):
        rows = slice(b * quarter, (b + 1) * quarter)
        pieces = [theres[r // 2][r % 2, rows] for r in range(4)]
        far = jnp.concatenate([by_place(me, pieces, j) for j in range(4)], axis=0).T
        out_ref[b] = far
        columns = pl.ds(pl.multiple_of(b * width + (1 - core) * half, half), half)
        put(out_ref.at[b], updated_hbm.at[pl.ds(0, width), columns])
        if b == 0:
            pieces = [jnp.where(odd, dones[r][rows], backs[r][rows]) for r in range(4)]
            near = jnp.concatenate([by_place(me, pieces, j) for j in range(4)], axis=0).T
            head = jnp.concatenate(by_core(core, near, far), axis=1)
            basis = plain(halves(head), halves(inverse_ref[...]))
            basis_ref[...] = jnp.where(me == 0, 0.0, basis)
            put(basis_ref, basis_hbm.at[pl.ds(0, width)])
    for copy in copies:
        copy.wait()


def body(trailing, leaf_vectors, leaf_factors, tree_vectors, tree_factors, inverse_factor):
    rows, columns = trailing.shape
    width = leaf_vectors.shape[1]
    half = width // 2
    quarter = half // 4
    count = columns // width
    devices = lax.axis_size("rows")
    levels = devices.bit_length() - 1
    me = lax.axis_index("rows").astype(jnp.int32)
    me_array = me.reshape(1)
    part_shape = (half + EXTRA, width)
    latest = []

    def exchange(value, shift):
        return lax.ppermute(value, "rows", [(i, i ^ shift) for i in range(devices)])

    def among(value, shift, member):
        return lax.ppermute(value, "rows", [(i, i ^ shift if member(i) else i) for i in range(devices)])

    def around(values):
        there = [exchange(values[r], 2 * r) for r in (3, 1, 2)]
        return [values[0], there[1], there[2], there[0]]

    def shape(*dims):
        return jax.ShapeDtypeStruct(dims, F32)

    def vmem(*dims):
        return pltpu.VMEM(dims, F32)

    def sems(number):
        return pltpu.SemaphoreType.DMA((number,))

    def call(kernel, operands, outs, scratch=(), away_in=(), away_out=(), aliases=(), before=(), work=1, chained=True):
        number = len(operands)
        operands = [pltpu.with_memory_space_constraint(x, pltpu.HBM) if i in away_in else x for i, x in enumerate(operands)]
        outs = [(pltpu.HBM if i in away_out else pltpu.VMEM)(x.shape, x.dtype) for i, x in enumerate(outs)]
        unused = [*latest, *before] if chained else []

        def kernel_on(*refs):
            kernel(*refs[: number + 1], *refs[number + 1 + len(unused) :])

        values = pl.pallas_call(
            kernel_on,
            out_shape=tuple(outs),
            in_specs=[SCALAR]
            + [AWAY if i in away_in else WHOLE for i in range(number)]
            + [pl.BlockSpec(memory_space=pl.ANY)] * len(unused),
            out_specs=tuple(AWAY if i in away_out else WHOLE for i in range(len(outs))),
            scratch_shapes=list(scratch),
            input_output_aliases=dict(aliases),
            compiler_params=PARAMS,
            cost_estimate=pl.CostEstimate(flops=work, bytes_accessed=1, transcendentals=0),
        )(me_array, *operands, *unused)
        if chained and 0 not in away_out:
            latest[:] = values[:1]
        return values

    raw = [exchange(tree_vectors, 1), exchange(tree_factors, 1)]
    blocks = count // 2
    more = count - blocks
    both = jax.ShapeDtypeStruct((2, width, rows), BF16), jax.ShapeDtypeStruct((2, rows, width), BF16)
    rows_a = blocks * half + half
    own_a, away_one, away_two, rest_a, later, inverse_factor, across, combined = call(
        leaf_first_kernel, (trailing, leaf_vectors, leaf_factors, inverse_factor),
        [shape(rows_a, width), shape(rows_a // 2, width), shape(rows_a // 2, width)]
        + [shape(blocks, width, width), shape(more, rows, width), shape(width, width), *both],
        [
            vmem(blocks, rows, width), vmem(rows, width), vmem(width, width), vmem(width, width), vmem(rows_a, width),
            sems(count * (rows // width) + 3),
        ],
        range(4),
    )
    there_a = [exchange(away_one, 1), exchange(away_two, 1)]

    chip_low, chip_high, chip_part = call(
        pack_kernel, (tree_vectors, tree_factors, *raw),
        (shape(2, *part_shape), shape(2, *part_shape), shape(*part_shape)),
        [vmem(4, width, width), sems(4)], (),
    )
    plane_parts = [exchange(chip_part, 2 * r) for r in (3, 1, 2)]
    plane_parts = [plane_parts[1], plane_parts[2], plane_parts[0]]

    own_b, rest_b, *aways = call(
        leaf_second_kernel, (later, across, combined),
        [shape(more * half, width), shape(more, width, width)] + [shape(half, width)] * more,
        [vmem(width, width)], before=there_a,
    )
    theres = [exchange(away, 1) for away in aways]
    cols = count * quarter
    low_a, high_a, gram_half = call(
        core_first_kernel, (own_a, *there_a, chip_high),
        [shape(blocks * half, width)] * 2 + [shape(half, width)],
    )
    outs = call(
        core_kernel, (low_a, high_a, own_b, *theres, chip_high),
        [shape(cols, width)] * 3 + [shape(cols + 8, width)] + [shape(cols, width)] * 4,
        [vmem(more * half, width), vmem(more * half, width)],
    )
    sends, dones = outs[:4], outs[4:8]
    for level in (levels - 1, 1, 2, *range(3, levels - 1)):
        (gram_half,) = call(
            add_kernel, (gram_half, exchange(gram_half, 1 << level)), (shape(half, width),), chained=False
        )
    stack, held_part = call(
        gather_kernel, (chip_part, *plane_parts), (shape(3, *part_shape), shape(*part_shape)), work=1,
    )
    gots = around(sends)
    stack_there = exchange(stack, 1)
    parts = [exchange(held_part, 8)]
    for level in range(4, levels):
        short = half // 2 + EXTRA if level == levels - 1 else half + EXTRA
        (held_part,) = call(
            functools.partial(hold_kernel, level=level - 1), (held_part, parts[-1]), (shape(short, width),),
            chained=False,
        )
        parts.append(exchange(held_part, 1 << level))

    def split(*dims):
        return jax.ShapeDtypeStruct(dims, BF16)

    joint, vectors, held = call(
        prepare_kernel, (chip_low, stack, stack_there),
        (split(3, 2, 2 * width, width), split(4, 2, width, width), shape(2, *part_shape)),
    )
    head, send, plane_done = call(
        functools.partial(plane_kernel, level=3), (*gots, joint, vectors),
        (shape(cols, width), shape(cols + 24, width), shape(4, cols, width)),
    )
    result = head
    for level in range(3, levels):
        part = parts[level - 3]
        last = level == levels - 1
        ready, *helds = call(
            functools.partial(ready_kernel, level=level), (held, part, exchange(part, 1)),
            [split(4 if last else 6, width, width)] + ([] if last else [shape(2, *part_shape)]),
        )
        operands = (head, result, send, exchange(send, 1 << level), ready)
        if last:
            _, updated, basis = call(
                store_kernel, (rest_a, rest_b, inverse_factor), (shape(8, width), shape(rows, columns), shape(rows, width)),
                [vmem(width, width), sems(count + 1)], (), (1, 2),
            )
            sends = call(
                functools.partial(last_kernel, level=level), (*operands, plane_done),
                [shape(cols + quarter, width)] * 3 + [shape(cols + quarter + 8, width)], [vmem(4, cols, width)],
            )
        else:
            (held,) = helds
            head, result, send = call(
                functools.partial(line_kernel, level=level), operands,
                [shape(cols, width), shape(cols, width), shape(cols, width)],
            )

    backs = around(sends)
    gram_there = exchange(gram_half, 1)
    theres = []
    for r in (0, 2):
        (passed,) = call(
            pass_kernel, (*backs[r : r + 2], *dones[r : r + 2]), (shape(2, cols + quarter, width),),
            before=(gram_half,) if r == 2 else (),
        )
        theres.append(exchange(passed, 1))
    (updated,) = call(
        near_kernel, (*backs, *dones, updated), (shape(rows, columns),),
        [vmem(count, width, half), sems(count)], (8,), (0,), {9: 0},
    )
    return call(
        functools.partial(far_kernel, total=float(rows * devices)),
        (*backs, *dones, *theres, gram_half, gram_there, inverse_factor, updated, basis),
        (shape(rows, columns), shape(rows, width), shape(width, width)),
        [vmem(width, width), vmem(width, width), vmem(count, width, half), vmem(width, width), vmem(width, width), sems(count + 2)],
        (13, 14), (0, 1, 2), {14: 0, 15: 1},
    )


def solution(mesh):
    in_specs = (
        P("rows", None),
        P("rows", None),
        P("rows", None),
        P("rows", None),
        P("rows", None),
        P(),
    )
    out_specs = (P("rows", None), P("rows", None), P())
    return jax.shard_map(body, mesh=mesh, in_specs=in_specs, out_specs=out_specs, check_vma=False)
```

```python
import functools
import jax
import jax.numpy as jnp
from jax import lax
from jax.experimental import pallas as pl
from jax.experimental.pallas import tpu as pltpu
from jax.sharding import PartitionSpec as P

F32 = jnp.float32
BF16 = jnp.bfloat16
EXTRA = 8
PARAMS = pltpu.CompilerParams(vmem_limit_bytes=20 * 1024 * 1024)
WHOLE = pl.BlockSpec(memory_space=pltpu.VMEM)
SCALAR = pl.BlockSpec(memory_space=pltpu.SMEM)
AWAY = pl.BlockSpec(memory_space=pltpu.HBM)


def halves(value):
    high = value.astype(BF16)
    return high, (value - high.astype(F32)).astype(BF16)


def times(left, right, sides):
    first = jnp.concatenate([left[0], left[0], left[1]], axis=sides[0])
    second = jnp.concatenate([right[0], right[1], right[0]], axis=sides[1])
    dims = ((sides[:1], sides[1:]), ((), ()))
    return lax.dot_general(first, second, dims, preferred_element_type=F32)


def plain(left, right):
    return times(left, right, (1, 0))


def by_transpose(left, right):
    return times(left, right, (1, 1))


def masks(size):
    row = lax.broadcasted_iota(jnp.int32, (size, size), 0)
    col = lax.broadcasted_iota(jnp.int32, (size, size), 1)
    return row, col


def diagonal_of(square):
    row, col = masks(square.shape[0])
    return jnp.sum(jnp.where(row == col, square, 0.0), axis=0, keepdims=True)


def pack_kernel(me_ref, *refs):
    sources, (low_ref, high_ref, part_ref), (buffer_ref, sems) = refs[:4], refs[4:7], refs[7:]
    copies = [pltpu.make_async_copy(source, buffer_ref.at[i], sems.at[i]) for i, source in enumerate(sources)]
    for copy in copies:
        copy.start()
    for copy in copies:
        copy.wait()
    core = me_ref[0] % 2
    half = buffer_ref.shape[1] // 2
    row, col = masks(half)
    both_vectors = by_core(core, buffer_ref[0], buffer_ref[2])
    both_factors = by_core(core, buffer_ref[1], buffer_ref[3])
    for vectors, factors, out_ref in zip(both_vectors, both_factors, (low_ref, high_ref)):
        first, second = factors[:half, :half], factors[half:, half:]
        square = jnp.where(row > col, first.T, jnp.where(row < col, second, 0.0))
        t_rows = jnp.concatenate([square, factors[:half, half:].T], axis=1)
        t_diagonal = jnp.concatenate([diagonal_of(first), diagonal_of(second)], axis=1)
        first, second = vectors[:half, :half], vectors[half:, half:]
        square = jnp.where(row <= col, first, second.T)
        v_rows = jnp.concatenate([square, vectors[:half, half:]], axis=1)
        v_diagonal = jnp.concatenate([diagonal_of(second)] * 2, axis=1)
        line = lax.broadcasted_iota(jnp.int32, (EXTRA, 2 * half), 0)
        diagonals = jnp.where(line == 0, t_diagonal, v_diagonal)
        for part in range(2):
            rows = slice(part * half // 2, (part + 1) * half // 2)
            out_ref[part, : half // 2] = t_rows[rows]
            out_ref[part, half // 2 : half // 2 + EXTRA] = diagonals
            out_ref[part, half // 2 + EXTRA :] = v_rows[rows]
    part_ref[...] = low_ref[core]


def unpack_factors(first, second):
    half = first.shape[1] // 2
    rows = jnp.concatenate([first[: half // 2], second[: half // 2]], axis=0)
    row, col = masks(half)
    square, corner = rows[:, :half], rows[:, half:]
    diagonal = first[half // 2 : half // 2 + 1]
    upper_left = jnp.where(row > col, square, jnp.where(row == col, diagonal[:, :half], 0.0))
    lower_right = jnp.where(row > col, square.T, jnp.where(row == col, diagonal[:, half:], 0.0))
    above = jnp.concatenate([upper_left, jnp.zeros_like(upper_left)], axis=1)
    return halves(jnp.concatenate([above, jnp.concatenate([corner, lower_right], axis=1)], axis=0))


def unpack_vectors(first, second):
    half = first.shape[1] // 2
    start = half // 2 + EXTRA
    rows = jnp.concatenate([first[start:], second[start:]], axis=0)
    row, col = masks(half)
    square, corner = rows[:, :half], rows[:, half:]
    diagonal = first[half // 2 + 1 : half // 2 + 2, :half]
    upper_left = jnp.where(row <= col, square, 0.0)
    lower_right = jnp.where(row < col, square.T, jnp.where(row == col, diagonal, 0.0))
    above = jnp.concatenate([upper_left, corner], axis=1)
    return halves(jnp.concatenate([above, jnp.concatenate([jnp.zeros_like(corner), lower_right], axis=1)], axis=0))


def unpack(first, second):
    return unpack_vectors(first, second), unpack_factors(first, second)


def by_core(core, mine, there):
    odd = core == 1
    return jnp.where(odd, there, mine), jnp.where(odd, mine, there)


def place(me):
    return (me >> 1) & 3


def by_place(me, parts, wanted):
    source = place(me) ^ wanted
    out = parts[0]
    for r in range(1, 4):
        out = jnp.where(source == r, parts[r], out)
    return out


def tree_node(low, high, reflector):
    vectors, factors = reflector
    node = by_transpose(halves(low + plain(halves(high), vectors)), factors)
    return low - node, high - by_transpose(halves(node), vectors)


def leaf_first_kernel(
    me_ref, trailing_hbm, vectors_hbm, factors_hbm, inverse_hbm,
    own_ref, away_one, away_two, rest_ref, later_ref, inverse_ref, across_ref, combined_ref,
    part_ref, vectors_ref, factors_ref, value_ref, away_ref, sems,
):
    count, rows, width = part_ref.shape
    copies = []

    def fetch(source, target):
        copies.append(pltpu.make_async_copy(source, target, sems.at[len(copies)]))
        copies[-1].start()
        return copies[-1]

    def fetch_part(b, target):
        cuts = [slice(c, c + width) for c in range(0, rows, width)]
        return [fetch(trailing_hbm.at[c, pl.ds(b * width, width)], target.at[c]) for c in cuts]

    first = [fetch(vectors_hbm, vectors_ref), fetch(factors_hbm, factors_ref)]
    parts = [fetch_part(b, part_ref.at[b]) for b in range(count)]
    for copy in first:
        copy.wait()
    last = [fetch_part(count + b, later_ref.at[b]) for b in range(later_ref.shape[0])]
    last.append([fetch(inverse_hbm, inverse_ref)])
    vectors = vectors_ref[...]
    across = halves(vectors.T)
    across_ref[0], across_ref[1] = across
    combined = halves(by_transpose(halves(vectors), halves(factors_ref[...])))
    combined_ref[0], combined_ref[1] = combined
    for b in range(count):
        for copy in parts[b]:
            copy.wait()
        leaf_block(me_ref, part_ref[b], across, combined, value_ref, rest_ref.at[b], own_ref, away_ref, b)
    panel = part_ref[0]
    value_ref[...] = plain(halves(panel.T), halves(panel))
    hand_over(me_ref, value_ref, own_ref, away_ref, count)
    cut = away_one.shape[0]
    away_one[...] = away_ref[:cut]
    away_two[...] = away_ref[cut:]
    for group in last:
        for copy in group:
            copy.wait()


def hand_over(me_ref, value_ref, own_ref, away_ref, slot):
    half = value_ref.shape[0] // 2
    core = me_ref[0] % 2
    target = slice(slot * half, (slot + 1) * half)
    own_ref[target] = value_ref[pl.ds(pl.multiple_of(core * half, half), half)]
    away_ref[target] = value_ref[pl.ds(pl.multiple_of((1 - core) * half, half), half)]


def leaf_block(me_ref, part, across, combined, value_ref, rest_ref, own_ref, away_ref, slot):
    width = value_ref.shape[0]
    out = part - plain(combined, halves(plain(across, halves(part))))
    rest_ref[...] = out[width:]
    value_ref[...] = out[:width].T
    hand_over(me_ref, value_ref, own_ref, away_ref, slot)


def leaf_second_kernel(me_ref, later_ref, across_ref, combined_ref, own_ref, rest_ref, *refs):
    aways, value_ref = refs[:-1], refs[-1]
    half = value_ref.shape[0] // 2
    across = across_ref[0], across_ref[1]
    combined = combined_ref[0], combined_ref[1]
    for b in range(later_ref.shape[0]):
        own_b = own_ref.at[pl.ds(b * half, half)]
        leaf_block(me_ref, later_ref[b], across, combined, value_ref, rest_ref.at[b], own_b, aways[b], 0)


def store_kernel(me_ref, first_ref, second_ref, inverse_ref, mark_ref, updated_hbm, basis_hbm, basis_ref, sems):
    count, width = first_ref.shape[:2]
    copies = []
    for b in range(count + second_ref.shape[0]):
        source = first_ref.at[b] if b < count else second_ref.at[b - count]
        target = updated_hbm.at[pl.ds(width, width), pl.ds(b * width, width)]
        copies.append(pltpu.make_async_copy(source, target, sems.at[b]))
        copies[-1].start()
    basis_ref[...] = plain(halves(first_ref[0]), halves(inverse_ref[...]))
    copies.append(pltpu.make_async_copy(basis_ref, basis_hbm.at[pl.ds(width, width)], sems.at[len(copies)]))
    mark_ref[...] = jnp.zeros_like(mark_ref)
    copies[-1].start()
    for copy in copies:
        copy.wait()


def core_kernel(
    me_ref, own_a_ref, own_b_ref, one_ref, two_ref, *refs
):
    more = len(refs) - 12
    there_bs, packed_ref = refs[:more], refs[more]
    sends, dones, (gram_ref, low_ref, high_ref) = refs[more + 1 : more + 5], refs[more + 5 : more + 9], refs[more + 9 :]
    me = me_ref[0]
    width = own_a_ref.shape[1]
    half = width // 2
    quarter = half // 4
    cut = own_a_ref.shape[0] - half
    count = cut // half + len(there_bs)
    odd = me % 2 == 1
    there_a = jnp.concatenate([one_ref[...], two_ref[...]], axis=0)
    gram_ref[...] = own_a_ref[cut:] + there_a[cut:]
    mine = jnp.concatenate([own_a_ref[:cut], own_b_ref[...]], axis=0)
    there = jnp.concatenate([there_a[:cut]] + [ref[...] for ref in there_bs], axis=0)
    low = jnp.where(odd, there, mine)
    high = jnp.where(odd, mine, there)
    low, high = tree_node(low, high, unpack(packed_ref[0], packed_ref[1]))
    low_ref[...] = low
    high_ref[...] = high
    for r in range(4):
        start = (place(me) ^ r) * quarter
        for b in range(count):
            source = pl.ds(pl.multiple_of(b * half + start, quarter), quarter)
            target = slice(b * quarter, (b + 1) * quarter)
            sends[r][target] = low_ref[source]
            dones[r][target] = high_ref[source]
        if sends[r].shape[0] > count * quarter:
            sends[r][count * quarter :] = jnp.zeros_like(sends[r][count * quarter :])


def gather_kernel(me_ref, *refs):
    parts, (stack_ref, held_ref) = refs[:4], refs[4:]
    for r in range(1, 4):
        stack_ref[r - 1] = parts[r][...]
    held_ref[...] = by_place(me_ref[0], [ref[...] for ref in parts], 0)


def hold_kernel(me_ref, held_ref, part_ref, out_ref, *, level):
    rows = slice(0, out_ref.shape[0])
    out_ref[...] = jnp.where((me_ref[0] >> level) % 2 == 1, part_ref[rows], held_ref[rows])


def add_kernel(me_ref, first_ref, second_ref, out_ref):
    out_ref[...] = first_ref[...] + second_ref[...]


def fill(send_ref, value):
    cols = value.shape[0]
    send_ref[:cols] = value
    if send_ref.shape[0] > cols:
        send_ref[cols:] = jnp.zeros_like(send_ref[cols:])


def prepare_kernel(me_ref, packed_ref, stack_ref, stack_there_ref, joint_ref, vectors_ref, held_ref):
    me = me_ref[0]
    pairs = [(packed_ref[0], packed_ref[1])]
    pairs += [by_core(me % 2, stack_ref[r], stack_there_ref[r]) for r in range(3)]
    firsts, seconds = [pair[0] for pair in pairs], [pair[1] for pair in pairs]
    pairs = [(by_place(me, firsts, j), by_place(me, seconds, j)) for j in range(4)]
    held_ref[0], held_ref[1] = pairs[0]
    for j in range(4):
        vectors = unpack_vectors(*pairs[j])
        vectors_ref[j, 0], vectors_ref[j, 1] = vectors
        if j > 0:
            factors = unpack_factors(*pairs[j])
            natural = (factors[0].astype(F32) + factors[1].astype(F32)).T
            joint = jnp.concatenate([natural, by_transpose(vectors, factors)], axis=0)
            joint_ref[j - 1, 0], joint_ref[j - 1, 1] = halves(joint)


def plane_kernel(me_ref, *refs, level):
    gots, (joint_ref, vectors_ref, head_ref, send_ref, done_ref) = refs[:4], refs[4:]
    cols = head_ref.shape[0]
    parts = [ref[:cols] for ref in gots]
    heads = [by_place(me_ref[0], parts, j) for j in range(4)]
    for low, high, j in ((0, 1, 1), (2, 3, 3), (0, 2, 2)):
        both = jnp.concatenate([heads[low], heads[high]], axis=1)
        coeffs = plain(halves(both), (joint_ref[j - 1, 0], joint_ref[j - 1, 1]))
        heads[low] = heads[low] - coeffs
        heads[high] = heads[high] - by_transpose(halves(coeffs), (vectors_ref[j, 0], vectors_ref[j, 1]))
    for j in range(4):
        done_ref[j] = heads[j]
    head_ref[...] = heads[0]
    upper = (me_ref[0] >> level) % 2 == 1
    ahead = plain(halves(heads[0]), (vectors_ref[0, 0], vectors_ref[0, 1]))
    fill(send_ref, jnp.where(upper, ahead, heads[0]))


def ready_kernel(me_ref, held_ref, part_ref, part_there_ref, ready_ref, *outs, level):
    me = me_ref[0]
    upper = (me >> level) % 2 == 1
    held = held_ref[0], held_ref[1]
    others = by_core(me % 2, part_ref[...], part_there_ref[...])
    need = held[0].shape[1] // 4 + EXTRA
    node = [jnp.where(upper, a[:need], b[:need]) for a, b in zip(held, others)]
    ready_ref[0], ready_ref[1] = unpack_factors(*node)
    ready_ref[2], ready_ref[3] = unpack_vectors(*held)
    if outs:
        following = [jnp.where(upper, b, a) for a, b in zip(held, others)]
        ready_ref[4], ready_ref[5] = unpack_vectors(*following)
        outs[0][0], outs[0][1] = following


def line_node(me_ref, head_ref, result_ref, mine_ref, there_ref, ready_ref, level):
    me = me_ref[0]
    cols = head_ref.shape[0]
    upper = (me >> level) % 2 == 1
    head, there = head_ref[...], there_ref[:cols]
    coeffs = by_transpose(halves(mine_ref[:cols] + there), (ready_ref[0], ready_ref[1]))
    low = jnp.where(upper, there, head) - coeffs
    plane = me >> 3
    below = (1 << (level - 2)) - 1
    second = (plane & below) == (1 << (level - 3))
    high = head - by_transpose(halves(coeffs), (ready_ref[2], ready_ref[3]))
    return low, jnp.where(second, high, result_ref[...])


def line_kernel(me_ref, *refs, level):
    ready_ref, (head_out, result_out, send_ref) = refs[4], refs[5:]
    low, result = line_node(me_ref, *refs[:5], level)
    ahead = (me_ref[0] >> (level + 1)) % 2 == 1
    head_out[...] = low
    result_out[...] = result
    fill(send_ref, jnp.where(ahead, plain(halves(low), (ready_ref[4], ready_ref[5])), low))


def last_kernel(me_ref, *refs, level):
    done_ref, sends, all_ref = refs[5], refs[6:10], refs[10]
    me = me_ref[0]
    low, result = line_node(me_ref, *refs[:5], level)
    cols = low.shape[0]
    all_ref[0] = jnp.where((me >> 3) == 0, low, result)
    for j in range(1, 4):
        all_ref[j] = done_ref[j]
    for r in range(4):
        sends[r][:cols] = all_ref[place(me) ^ r]
        sends[r][cols:] = low[: sends[r].shape[0] - cols]


def pass_kernel(me_ref, *refs):
    backs, dones, out_ref = refs[:2], refs[2:4], refs[4]
    odd = me_ref[0] % 2 == 1
    cols, rows = dones[0].shape[0], backs[0].shape[0]
    for r in range(2):
        out_ref[r, :cols] = jnp.where(odd, backs[r][:cols], dones[r][...])
        out_ref[r, cols:rows] = backs[r][cols:]
        if out_ref.shape[1] > rows:
            out_ref[r, rows:] = jnp.zeros_like(out_ref[r, rows:])


def near_kernel(me_ref, *refs):
    backs, dones, (_, updated_hbm, out_ref, sems) = refs[:4], refs[4:8], refs[8:]
    count, width, half = out_ref.shape
    quarter = half // 4
    me = me_ref[0]
    core = me % 2
    odd = core == 1
    copies = []
    for b in range(count):
        rows = slice(b * quarter, (b + 1) * quarter)
        pieces = [jnp.where(odd, dones[r][rows], backs[r][rows]) for r in range(4)]
        out_ref[b] = jnp.concatenate([by_place(me, pieces, j) for j in range(4)], axis=0).T
        columns = pl.ds(pl.multiple_of(b * width + core * half, half), half)
        copies.append(pltpu.make_async_copy(out_ref.at[b], updated_hbm.at[pl.ds(0, width), columns], sems.at[b]))
        copies[-1].start()
    for copy in copies:
        copy.wait()


def far_kernel(me_ref, *refs, total):
    backs, dones = refs[:4], refs[4:8]
    theres, half_ref, half_there, inverse_ref, _, _, updated_hbm, basis_hbm, gram_hbm = refs[8:10], *refs[10:18]
    panel_ref, sum_ref, out_ref, basis_ref, gram_ref, sems = refs[18:]
    count, width, half = out_ref.shape
    quarter = half // 4
    cols = count * quarter
    me = me_ref[0]
    core = me % 2
    odd = core == 1
    copies = []

    def put(source, target):
        copies.append(pltpu.make_async_copy(source, target, sems.at[len(copies)]))
        copies[-1].start()

    def target(part, r):
        return pl.ds(pl.multiple_of(part * half + (place(me) ^ r) * quarter, quarter), quarter)

    for r in range(4):
        panel_ref[target(core, r)] = backs[r][cols : cols + quarter]
        panel_ref[target(1 - core, r)] = theres[r // 2][r % 2, cols : cols + quarter]
    sum_ref[pl.ds(pl.multiple_of(core * half, half), half)] = half_ref[...]
    sum_ref[pl.ds(pl.multiple_of((1 - core) * half, half), half)] = half_there[...]
    panel = halves(panel_ref[...])
    gram_ref[...] = (sum_ref[...] - by_transpose(panel, panel)) / total
    put(gram_ref, gram_hbm)
    for b in range(count):
        rows = slice(b * quarter, (b + 1) * quarter)
        pieces = [theres[r // 2][r % 2, rows] for r in range(4)]
        far = jnp.concatenate([by_place(me, pieces, j) for j in range(4)], axis=0).T
        out_ref[b] = far
        columns = pl.ds(pl.multiple_of(b * width + (1 - core) * half, half), half)
        put(out_ref.at[b], updated_hbm.at[pl.ds(0, width), columns])
        if b == 0:
            pieces = [jnp.where(odd, dones[r][rows], backs[r][rows]) for r in range(4)]
            near = jnp.concatenate([by_place(me, pieces, j) for j in range(4)], axis=0).T
            head = jnp.concatenate(by_core(core, near, far), axis=1)
            basis = plain(halves(head), halves(inverse_ref[...]))
            basis_ref[...] = jnp.where(me == 0, 0.0, basis)
            put(basis_ref, basis_hbm.at[pl.ds(0, width)])
    for copy in copies:
        copy.wait()


def body(trailing, leaf_vectors, leaf_factors, tree_vectors, tree_factors, inverse_factor):
    rows, columns = trailing.shape
    width = leaf_vectors.shape[1]
    half = width // 2
    quarter = half // 4
    count = columns // width
    devices = lax.axis_size("rows")
    levels = devices.bit_length() - 1
    me = lax.axis_index("rows").astype(jnp.int32)
    me_array = me.reshape(1)
    part_shape = (half + EXTRA, width)
    latest = []

    def exchange(value, shift):
        return lax.ppermute(value, "rows", [(i, i ^ shift) for i in range(devices)])

    def among(value, shift, member):
        return lax.ppermute(value, "rows", [(i, i ^ shift if member(i) else i) for i in range(devices)])

    def around(values):
        there = [exchange(values[r], 2 * r) for r in (3, 1, 2)]
        return [values[0], there[1], there[2], there[0]]

    def shape(*dims):
        return jax.ShapeDtypeStruct(dims, F32)

    def vmem(*dims):
        return pltpu.VMEM(dims, F32)

    def sems(number):
        return pltpu.SemaphoreType.DMA((number,))

    def call(kernel, operands, outs, scratch=(), away_in=(), away_out=(), aliases=(), before=(), work=1, chained=True):
        number = len(operands)
        operands = [pltpu.with_memory_space_constraint(x, pltpu.HBM) if i in away_in else x for i, x in enumerate(operands)]
        outs = [(pltpu.HBM if i in away_out else pltpu.VMEM)(x.shape, x.dtype) for i, x in enumerate(outs)]
        unused = [*latest, *before] if chained else []

        def kernel_on(*refs):
            kernel(*refs[: number + 1], *refs[number + 1 + len(unused) :])

        values = pl.pallas_call(
            kernel_on,
            out_shape=tuple(outs),
            in_specs=[SCALAR]
            + [AWAY if i in away_in else WHOLE for i in range(number)]
            + [pl.BlockSpec(memory_space=pl.ANY)] * len(unused),
            out_specs=tuple(AWAY if i in away_out else WHOLE for i in range(len(outs))),
            scratch_shapes=list(scratch),
            input_output_aliases=dict(aliases),
            compiler_params=PARAMS,
            cost_estimate=pl.CostEstimate(flops=work, bytes_accessed=1, transcendentals=0),
        )(me_array, *operands, *unused)
        if chained and 0 not in away_out:
            latest[:] = values[:1]
        return values

    raw = [exchange(tree_vectors, 1), exchange(tree_factors, 1)]
    blocks = count // 2
    more = count - blocks
    both = jax.ShapeDtypeStruct((2, width, rows), BF16), jax.ShapeDtypeStruct((2, rows, width), BF16)
    rows_a = blocks * half + half
    own_a, away_one, away_two, rest_a, later, inverse_factor, across, combined = call(
        leaf_first_kernel, (trailing, leaf_vectors, leaf_factors, inverse_factor),
        [shape(rows_a, width), shape(rows_a // 2, width), shape(rows_a // 2, width)]
        + [shape(blocks, width, width), shape(more, rows, width), shape(width, width), *both],
        [
            vmem(blocks, rows, width), vmem(rows, width), vmem(width, width), vmem(width, width), vmem(rows_a, width),
            sems(count * (rows // width) + 3),
        ],
        range(4),
    )
    there_a = [exchange(away_one, 1), exchange(away_two, 1)]

    chip_low, chip_high, chip_part = call(
        pack_kernel, (tree_vectors, tree_factors, *raw),
        (shape(2, *part_shape), shape(2, *part_shape), shape(*part_shape)),
        [vmem(4, width, width), sems(4)], (),
    )
    plane_parts = [exchange(chip_part, 2 * r) for r in (3, 1, 2)]
    plane_parts = [plane_parts[1], plane_parts[2], plane_parts[0]]

    own_b, rest_b, *aways = call(
        leaf_second_kernel, (later, across, combined),
        [shape(more * half, width), shape(more, width, width)] + [shape(half, width)] * more,
        [vmem(width, width)], before=there_a,
    )
    theres = [exchange(away, 1) for away in aways]
    cols = count * quarter
    outs = call(
        core_kernel, (own_a, own_b, *there_a, *theres, chip_high),
        [shape(cols, width)] * 8 + [shape(half, width)],
        [vmem(count * half, width), vmem(count * half, width)],
    )
    sends, dones, gram_half = outs[:4], outs[4:8], outs[8]
    for level in (levels - 1, 1, 2, *range(3, levels - 1)):
        (gram_half,) = call(
            add_kernel, (gram_half, exchange(gram_half, 1 << level)), (shape(half, width),), chained=False
        )
    stack, held_part = call(
        gather_kernel, (chip_part, *plane_parts), (shape(3, *part_shape), shape(*part_shape)), work=1,
    )
    gots = around(sends)
    stack_there = exchange(stack, 1)
    parts = [exchange(held_part, 8)]
    for level in range(4, levels):
        short = half // 2 + EXTRA if level == levels - 1 else half + EXTRA
        (held_part,) = call(
            functools.partial(hold_kernel, level=level - 1), (held_part, parts[-1]), (shape(short, width),),
            chained=False,
        )
        parts.append(exchange(held_part, 1 << level))

    def split(*dims):
        return jax.ShapeDtypeStruct(dims, BF16)

    joint, vectors, held = call(
        prepare_kernel, (chip_low, stack, stack_there),
        (split(3, 2, 2 * width, width), split(4, 2, width, width), shape(2, *part_shape)),
    )
    head, send, plane_done = call(
        functools.partial(plane_kernel, level=3), (*gots, joint, vectors),
        (shape(cols, width), shape(cols + 24, width), shape(4, cols, width)),
    )
    result = head
    for level in range(3, levels):
        part = parts[level - 3]
        last = level == levels - 1
        ready, *helds = call(
            functools.partial(ready_kernel, level=level), (held, part, exchange(part, 1)),
            [split(4 if last else 6, width, width)] + ([] if last else [shape(2, *part_shape)]),
        )
        operands = (head, result, send, exchange(send, 1 << level), ready)
        if last:
            _, updated, basis = call(
                store_kernel, (rest_a, rest_b, inverse_factor), (shape(8, width), shape(rows, columns), shape(rows, width)),
                [vmem(width, width), sems(count + 1)], (), (1, 2),
            )
            sends = call(
                functools.partial(last_kernel, level=level), (*operands, plane_done),
                [shape(cols + quarter, width)] * 4, [vmem(4, cols, width)],
            )
        else:
            (held,) = helds
            head, result, send = call(
                functools.partial(line_kernel, level=level), operands,
                [shape(cols, width), shape(cols, width), shape(cols, width)],
            )

    backs = around(sends)
    gram_there = exchange(gram_half, 1)
    theres = []
    for r in (0, 2):
        (passed,) = call(
            pass_kernel, (*backs[r : r + 2], *dones[r : r + 2]), (shape(2, cols + quarter + (8 if r == 0 else 0), width),),
            before=(gram_half,) if r == 2 else (),
        )
        theres.append(exchange(passed, 1))
    (updated,) = call(
        near_kernel, (*backs, *dones, updated), (shape(rows, columns),),
        [vmem(count, width, half), sems(count)], (8,), (0,), {9: 0},
    )
    return call(
        functools.partial(far_kernel, total=float(rows * devices)),
        (*backs, *dones, *theres, gram_half, gram_there, inverse_factor, updated, basis),
        (shape(rows, columns), shape(rows, width), shape(width, width)),
        [vmem(width, width), vmem(width, width), vmem(count, width, half), vmem(width, width), vmem(width, width), sems(count + 2)],
        (13, 14), (0, 1, 2), {14: 0, 15: 1},
    )


def solution(mesh):
    in_specs = (
        P("rows", None),
        P("rows", None),
        P("rows", None),
        P("rows", None),
        P("rows", None),
        P(),
    )
    out_specs = (P("rows", None), P("rows", None), P())
    return jax.shard_map(body, mesh=mesh, in_specs=in_specs, out_specs=out_specs, check_vma=False)
```

```python
import functools
import jax
import jax.numpy as jnp
from jax import lax
from jax.experimental import pallas as pl
from jax.experimental.pallas import tpu as pltpu
from jax.sharding import PartitionSpec as P

F32 = jnp.float32
BF16 = jnp.bfloat16
EXTRA = 8
PARAMS = pltpu.CompilerParams(vmem_limit_bytes=20 * 1024 * 1024)
WHOLE = pl.BlockSpec(memory_space=pltpu.VMEM)
SCALAR = pl.BlockSpec(memory_space=pltpu.SMEM)
AWAY = pl.BlockSpec(memory_space=pltpu.HBM)


def halves(value):
    high = value.astype(BF16)
    return high, (value - high.astype(F32)).astype(BF16)


def times(left, right, sides):
    first = jnp.concatenate([left[0], left[0], left[1]], axis=sides[0])
    second = jnp.concatenate([right[0], right[1], right[0]], axis=sides[1])
    dims = ((sides[:1], sides[1:]), ((), ()))
    return lax.dot_general(first, second, dims, preferred_element_type=F32)


def plain(left, right):
    return times(left, right, (1, 0))


def by_transpose(left, right):
    return times(left, right, (1, 1))


def masks(size):
    row = lax.broadcasted_iota(jnp.int32, (size, size), 0)
    col = lax.broadcasted_iota(jnp.int32, (size, size), 1)
    return row, col


def diagonal_of(square):
    row, col = masks(square.shape[0])
    return jnp.sum(jnp.where(row == col, square, 0.0), axis=0, keepdims=True)


def pack_kernel(me_ref, *refs):
    sources, (low_ref, high_ref, part_ref), (buffer_ref, sems) = refs[:4], refs[4:7], refs[7:]
    copies = [pltpu.make_async_copy(source, buffer_ref.at[i], sems.at[i]) for i, source in enumerate(sources)]
    for copy in copies:
        copy.start()
    for copy in copies:
        copy.wait()
    core = me_ref[0] % 2
    half = buffer_ref.shape[1] // 2
    row, col = masks(half)
    both_vectors = by_core(core, buffer_ref[0], buffer_ref[2])
    both_factors = by_core(core, buffer_ref[1], buffer_ref[3])
    for vectors, factors, out_ref in zip(both_vectors, both_factors, (low_ref, high_ref)):
        first, second = factors[:half, :half], factors[half:, half:]
        square = jnp.where(row > col, first.T, jnp.where(row < col, second, 0.0))
        t_rows = jnp.concatenate([square, factors[:half, half:].T], axis=1)
        t_diagonal = jnp.concatenate([diagonal_of(first), diagonal_of(second)], axis=1)
        first, second = vectors[:half, :half], vectors[half:, half:]
        square = jnp.where(row <= col, first, second.T)
        v_rows = jnp.concatenate([square, vectors[:half, half:]], axis=1)
        v_diagonal = jnp.concatenate([diagonal_of(second)] * 2, axis=1)
        line = lax.broadcasted_iota(jnp.int32, (EXTRA, 2 * half), 0)
        diagonals = jnp.where(line == 0, t_diagonal, v_diagonal)
        for part in range(2):
            rows = slice(part * half // 2, (part + 1) * half // 2)
            out_ref[part, : half // 2] = t_rows[rows]
            out_ref[part, half // 2 : half // 2 + EXTRA] = diagonals
            out_ref[part, half // 2 + EXTRA :] = v_rows[rows]
    part_ref[...] = low_ref[core]


def unpack_factors(first, second):
    half = first.shape[1] // 2
    rows = jnp.concatenate([first[: half // 2], second[: half // 2]], axis=0)
    row, col = masks(half)
    square, corner = rows[:, :half], rows[:, half:]
    diagonal = first[half // 2 : half // 2 + 1]
    upper_left = jnp.where(row > col, square, jnp.where(row == col, diagonal[:, :half], 0.0))
    lower_right = jnp.where(row > col, square.T, jnp.where(row == col, diagonal[:, half:], 0.0))
    above = jnp.concatenate([upper_left, jnp.zeros_like(upper_left)], axis=1)
    return halves(jnp.concatenate([above, jnp.concatenate([corner, lower_right], axis=1)], axis=0))


def unpack_vectors(first, second):
    half = first.shape[1] // 2
    start = half // 2 + EXTRA
    rows = jnp.concatenate([first[start:], second[start:]], axis=0)
    row, col = masks(half)
    square, corner = rows[:, :half], rows[:, half:]
    diagonal = first[half // 2 + 1 : half // 2 + 2, :half]
    upper_left = jnp.where(row <= col, square, 0.0)
    lower_right = jnp.where(row < col, square.T, jnp.where(row == col, diagonal, 0.0))
    above = jnp.concatenate([upper_left, corner], axis=1)
    return halves(jnp.concatenate([above, jnp.concatenate([jnp.zeros_like(corner), lower_right], axis=1)], axis=0))


def unpack(first, second):
    return unpack_vectors(first, second), unpack_factors(first, second)


def by_core(core, mine, there):
    odd = core == 1
    return jnp.where(odd, there, mine), jnp.where(odd, mine, there)


def place(me):
    return (me >> 1) & 3


def by_place(me, parts, wanted):
    source = place(me) ^ wanted
    out = parts[0]
    for r in range(1, 4):
        out = jnp.where(source == r, parts[r], out)
    return out


def tree_node(low, high, reflector):
    vectors, factors = reflector
    node = by_transpose(halves(low + plain(halves(high), vectors)), factors)
    return low - node, high - by_transpose(halves(node), vectors)


def leaf_first_kernel(
    me_ref, trailing_hbm, vectors_hbm, factors_hbm, inverse_hbm,
    own_ref, away_one, away_two, rest_ref, later_ref, inverse_ref, across_ref, combined_ref,
    part_ref, vectors_ref, factors_ref, value_ref, away_ref, sems,
):
    count, rows, width = part_ref.shape
    copies = []

    def fetch(source, target):
        copies.append(pltpu.make_async_copy(source, target, sems.at[len(copies)]))
        copies[-1].start()
        return copies[-1]

    def fetch_part(b, target):
        cuts = [slice(c, c + width) for c in range(0, rows, width)]
        return [fetch(trailing_hbm.at[c, pl.ds(b * width, width)], target.at[c]) for c in cuts]

    first = [fetch(vectors_hbm, vectors_ref), fetch(factors_hbm, factors_ref)]
    parts = [fetch_part(b, part_ref.at[b]) for b in range(count)]
    for copy in first:
        copy.wait()
    last = [fetch_part(count + b, later_ref.at[b]) for b in range(later_ref.shape[0])]
    last.append([fetch(inverse_hbm, inverse_ref)])
    vectors = vectors_ref[...]
    across = halves(vectors.T)
    across_ref[0], across_ref[1] = across
    combined = halves(by_transpose(halves(vectors), halves(factors_ref[...])))
    combined_ref[0], combined_ref[1] = combined
    for b in range(count):
        for copy in parts[b]:
            copy.wait()
        leaf_block(me_ref, part_ref[b], across, combined, value_ref, rest_ref.at[b], own_ref, away_ref, b)
    panel = part_ref[0]
    value_ref[...] = plain(halves(panel.T), halves(panel))
    hand_over(me_ref, value_ref, own_ref, away_ref, count)
    cut = away_one.shape[0]
    away_one[...] = away_ref[:cut]
    away_two[...] = away_ref[cut:]
    for group in last:
        for copy in group:
            copy.wait()


def hand_over(me_ref, value_ref, own_ref, away_ref, slot):
    half = value_ref.shape[0] // 2
    core = me_ref[0] % 2
    target = slice(slot * half, (slot + 1) * half)
    own_ref[target] = value_ref[pl.ds(pl.multiple_of(core * half, half), half)]
    away_ref[target] = value_ref[pl.ds(pl.multiple_of((1 - core) * half, half), half)]


def leaf_block(me_ref, part, across, combined, value_ref, rest_ref, own_ref, away_ref, slot):
    width = value_ref.shape[0]
    out = part - plain(combined, halves(plain(across, halves(part))))
    rest_ref[...] = out[width:]
    value_ref[...] = out[:width].T
    hand_over(me_ref, value_ref, own_ref, away_ref, slot)


def leaf_second_kernel(me_ref, later_ref, across_ref, combined_ref, own_ref, rest_ref, *refs):
    aways, value_ref = refs[:-1], refs[-1]
    half = value_ref.shape[0] // 2
    across = across_ref[0], across_ref[1]
    combined = combined_ref[0], combined_ref[1]
    for b in range(later_ref.shape[0]):
        own_b = own_ref.at[pl.ds(b * half, half)]
        leaf_block(me_ref, later_ref[b], across, combined, value_ref, rest_ref.at[b], own_b, aways[b], 0)


def store_kernel(me_ref, first_ref, second_ref, inverse_ref, mark_ref, updated_hbm, basis_hbm, basis_ref, sems):
    count, width = first_ref.shape[:2]
    copies = []
    for b in range(count + second_ref.shape[0]):
        source = first_ref.at[b] if b < count else second_ref.at[b - count]
        target = updated_hbm.at[pl.ds(width, width), pl.ds(b * width, width)]
        copies.append(pltpu.make_async_copy(source, target, sems.at[b]))
        copies[-1].start()
    basis_ref[...] = plain(halves(first_ref[0]), halves(inverse_ref[...]))
    copies.append(pltpu.make_async_copy(basis_ref, basis_hbm.at[pl.ds(width, width)], sems.at[len(copies)]))
    mark_ref[...] = jnp.zeros_like(mark_ref)
    copies[-1].start()
    for copy in copies:
        copy.wait()


def core_kernel(
    me_ref, own_a_ref, own_b_ref, one_ref, two_ref, *refs
):
    more = len(refs) - 12
    there_bs, packed_ref = refs[:more], refs[more]
    sends, dones, (gram_ref, low_ref, high_ref) = refs[more + 1 : more + 5], refs[more + 5 : more + 9], refs[more + 9 :]
    me = me_ref[0]
    width = own_a_ref.shape[1]
    half = width // 2
    quarter = half // 4
    cut = own_a_ref.shape[0] - half
    count = cut // half + len(there_bs)
    odd = me % 2 == 1
    there_a = jnp.concatenate([one_ref[...], two_ref[...]], axis=0)
    gram_ref[...] = own_a_ref[cut:] + there_a[cut:]
    mine = jnp.concatenate([own_a_ref[:cut], own_b_ref[...]], axis=0)
    there = jnp.concatenate([there_a[:cut]] + [ref[...] for ref in there_bs], axis=0)
    low = jnp.where(odd, there, mine)
    high = jnp.where(odd, mine, there)
    low, high = tree_node(low, high, unpack(packed_ref[0], packed_ref[1]))
    low_ref[...] = low
    high_ref[...] = high
    for r in range(4):
        start = (place(me) ^ r) * quarter
        for b in range(count):
            source = pl.ds(pl.multiple_of(b * half + start, quarter), quarter)
            target = slice(b * quarter, (b + 1) * quarter)
            sends[r][target] = low_ref[source]
            dones[r][target] = high_ref[source]
        if sends[r].shape[0] > count * quarter:
            sends[r][count * quarter :] = jnp.zeros_like(sends[r][count * quarter :])


def gather_kernel(me_ref, *refs):
    parts, (stack_ref, held_ref) = refs[:4], refs[4:]
    for r in range(1, 4):
        stack_ref[r - 1] = parts[r][...]
    held_ref[...] = by_place(me_ref[0], [ref[...] for ref in parts], 0)


def hold_kernel(me_ref, held_ref, part_ref, out_ref, *, level):
    rows = slice(0, out_ref.shape[0])
    out_ref[...] = jnp.where((me_ref[0] >> level) % 2 == 1, part_ref[rows], held_ref[rows])


def add_kernel(me_ref, first_ref, second_ref, out_ref):
    out_ref[...] = first_ref[...] + second_ref[...]


def fill(send_ref, value):
    cols = value.shape[0]
    send_ref[:cols] = value
    if send_ref.shape[0] > cols:
        send_ref[cols:] = jnp.zeros_like(send_ref[cols:])


def prepare_kernel(me_ref, packed_ref, stack_ref, stack_there_ref, joint_ref, vectors_ref, held_ref):
    me = me_ref[0]
    pairs = [(packed_ref[0], packed_ref[1])]
    pairs += [by_core(me % 2, stack_ref[r], stack_there_ref[r]) for r in range(3)]
    firsts, seconds = [pair[0] for pair in pairs], [pair[1] for pair in pairs]
    pairs = [(by_place(me, firsts, j), by_place(me, seconds, j)) for j in range(4)]
    held_ref[0], held_ref[1] = pairs[0]
    for j in range(4):
        vectors = unpack_vectors(*pairs[j])
        vectors_ref[j, 0], vectors_ref[j, 1] = vectors
        if j > 0:
            factors = unpack_factors(*pairs[j])
            natural = (factors[0].astype(F32) + factors[1].astype(F32)).T
            joint = jnp.concatenate([natural, by_transpose(vectors, factors)], axis=0)
            joint_ref[j - 1, 0], joint_ref[j - 1, 1] = halves(joint)


def plane_kernel(me_ref, *refs, level):
    gots, (joint_ref, vectors_ref, head_ref, send_ref, done_ref) = refs[:4], refs[4:]
    cols = head_ref.shape[0]
    parts = [ref[:cols] for ref in gots]
    heads = [by_place(me_ref[0], parts, j) for j in range(4)]
    for low, high, j in ((0, 1, 1), (2, 3, 3), (0, 2, 2)):
        both = jnp.concatenate([heads[low], heads[high]], axis=1)
        coeffs = plain(halves(both), (joint_ref[j - 1, 0], joint_ref[j - 1, 1]))
        heads[low] = heads[low] - coeffs
        heads[high] = heads[high] - by_transpose(halves(coeffs), (vectors_ref[j, 0], vectors_ref[j, 1]))
    for j in range(4):
        done_ref[j] = heads[j]
    head_ref[...] = heads[0]
    upper = (me_ref[0] >> level) % 2 == 1
    ahead = plain(halves(heads[0]), (vectors_ref[0, 0], vectors_ref[0, 1]))
    fill(send_ref, jnp.where(upper, ahead, heads[0]))


def ready_kernel(me_ref, held_ref, part_ref, part_there_ref, ready_ref, *outs, level):
    me = me_ref[0]
    upper = (me >> level) % 2 == 1
    held = held_ref[0], held_ref[1]
    others = by_core(me % 2, part_ref[...], part_there_ref[...])
    need = held[0].shape[1] // 4 + EXTRA
    node = [jnp.where(upper, a[:need], b[:need]) for a, b in zip(held, others)]
    ready_ref[0], ready_ref[1] = unpack_factors(*node)
    ready_ref[2], ready_ref[3] = unpack_vectors(*held)
    if outs:
        following = [jnp.where(upper, b, a) for a, b in zip(held, others)]
        ready_ref[4], ready_ref[5] = unpack_vectors(*following)
        outs[0][0], outs[0][1] = following


def line_node(me_ref, head_ref, result_ref, mine_ref, there_ref, ready_ref, level):
    me = me_ref[0]
    cols = head_ref.shape[0]
    upper = (me >> level) % 2 == 1
    head, there = head_ref[...], there_ref[:cols]
    coeffs = by_transpose(halves(mine_ref[:cols] + there), (ready_ref[0], ready_ref[1]))
    low = jnp.where(upper, there, head) - coeffs
    plane = me >> 3
    below = (1 << (level - 2)) - 1
    second = (plane & below) == (1 << (level - 3))
    high = head - by_transpose(halves(coeffs), (ready_ref[2], ready_ref[3]))
    return low, jnp.where(second, high, result_ref[...])


def line_kernel(me_ref, *refs, level):
    ready_ref, (head_out, result_out, send_ref) = refs[4], refs[5:]
    low, result = line_node(me_ref, *refs[:5], level)
    ahead = (me_ref[0] >> (level + 1)) % 2 == 1
    head_out[...] = low
    result_out[...] = result
    fill(send_ref, jnp.where(ahead, plain(halves(low), (ready_ref[4], ready_ref[5])), low))


def last_kernel(me_ref, *refs, level):
    done_ref, sends, all_ref = refs[5], refs[6:10], refs[10]
    me = me_ref[0]
    low, result = line_node(me_ref, *refs[:5], level)
    cols = low.shape[0]
    all_ref[0] = jnp.where((me >> 3) == 0, low, result)
    for j in range(1, 4):
        all_ref[j] = done_ref[j]
    for r in range(4):
        sends[r][:cols] = all_ref[place(me) ^ r]
        sends[r][cols:] = low[: sends[r].shape[0] - cols]


def pass_kernel(me_ref, *refs):
    backs, dones, out_ref = refs[:2], refs[2:4], refs[4]
    odd = me_ref[0] % 2 == 1
    cols, rows = dones[0].shape[0], backs[0].shape[0]
    for r in range(2):
        out_ref[r, :cols] = jnp.where(odd, backs[r][:cols], dones[r][...])
        out_ref[r, cols:rows] = backs[r][cols:]
        if out_ref.shape[1] > rows:
            out_ref[r, rows:] = jnp.zeros_like(out_ref[r, rows:])


def near_kernel(me_ref, *refs):
    backs, dones, (_, updated_hbm, out_ref, sems) = refs[:4], refs[4:8], refs[8:]
    count, width, half = out_ref.shape
    quarter = half // 4
    me = me_ref[0]
    core = me % 2
    odd = core == 1
    copies = []
    for b in range(count):
        rows = slice(b * quarter, (b + 1) * quarter)
        pieces = [jnp.where(odd, dones[r][rows], backs[r][rows]) for r in range(4)]
        out_ref[b] = jnp.concatenate([by_place(me, pieces, j) for j in range(4)], axis=0).T
        columns = pl.ds(pl.multiple_of(b * width + core * half, half), half)
        copies.append(pltpu.make_async_copy(out_ref.at[b], updated_hbm.at[pl.ds(0, width), columns], sems.at[b]))
        copies[-1].start()
    for copy in copies:
        copy.wait()


def far_kernel(me_ref, *refs, total):
    backs, dones = refs[:4], refs[4:8]
    theres, half_ref, half_there, inverse_ref, _, _, updated_hbm, basis_hbm, gram_hbm = refs[8:10], *refs[10:18]
    panel_ref, sum_ref, out_ref, basis_ref, gram_ref, sems = refs[18:]
    count, width, half = out_ref.shape
    quarter = half // 4
    cols = count * quarter
    me = me_ref[0]
    core = me % 2
    odd = core == 1
    copies = []

    def put(source, target):
        copies.append(pltpu.make_async_copy(source, target, sems.at[len(copies)]))
        copies[-1].start()

    def target(part, r):
        return pl.ds(pl.multiple_of(part * half + (place(me) ^ r) * quarter, quarter), quarter)

    for r in range(4):
        panel_ref[target(core, r)] = backs[r][cols : cols + quarter]
        panel_ref[target(1 - core, r)] = theres[r // 2][r % 2, cols : cols + quarter]
    sum_ref[pl.ds(pl.multiple_of(core * half, half), half)] = half_ref[...]
    sum_ref[pl.ds(pl.multiple_of((1 - core) * half, half), half)] = half_there[...]
    panel = halves(panel_ref[...])
    gram_ref[...] = (sum_ref[...] - by_transpose(panel, panel)) / total
    put(gram_ref, gram_hbm)
    for b in range(count):
        rows = slice(b * quarter, (b + 1) * quarter)
        pieces = [theres[r // 2][r % 2, rows] for r in range(4)]
        far = jnp.concatenate([by_place(me, pieces, j) for j in range(4)], axis=0).T
        out_ref[b] = far
        columns = pl.ds(pl.multiple_of(b * width + (1 - core) * half, half), half)
        put(out_ref.at[b], updated_hbm.at[pl.ds(0, width), columns])
        if b == 0:
            pieces = [jnp.where(odd, dones[r][rows], backs[r][rows]) for r in range(4)]
            near = jnp.concatenate([by_place(me, pieces, j) for j in range(4)], axis=0).T
            head = jnp.concatenate(by_core(core, near, far), axis=1)
            basis = plain(halves(head), halves(inverse_ref[...]))
            basis_ref[...] = jnp.where(me == 0, 0.0, basis)
            put(basis_ref, basis_hbm.at[pl.ds(0, width)])
    for copy in copies:
        copy.wait()


def body(trailing, leaf_vectors, leaf_factors, tree_vectors, tree_factors, inverse_factor):
    rows, columns = trailing.shape
    width = leaf_vectors.shape[1]
    half = width // 2
    quarter = half // 4
    count = columns // width
    devices = lax.axis_size("rows")
    levels = devices.bit_length() - 1
    me = lax.axis_index("rows").astype(jnp.int32)
    me_array = me.reshape(1)
    part_shape = (half + EXTRA, width)
    latest = []

    def exchange(value, shift):
        return lax.ppermute(value, "rows", [(i, i ^ shift) for i in range(devices)])

    def among(value, shift, member):
        return lax.ppermute(value, "rows", [(i, i ^ shift if member(i) else i) for i in range(devices)])

    def around(values):
        there = [exchange(values[r], 2 * r) for r in (3, 1, 2)]
        return [values[0], there[1], there[2], there[0]]

    def shape(*dims):
        return jax.ShapeDtypeStruct(dims, F32)

    def vmem(*dims):
        return pltpu.VMEM(dims, F32)

    def sems(number):
        return pltpu.SemaphoreType.DMA((number,))

    def call(kernel, operands, outs, scratch=(), away_in=(), away_out=(), aliases=(), before=(), work=1, chained=True):
        number = len(operands)
        operands = [pltpu.with_memory_space_constraint(x, pltpu.HBM) if i in away_in else x for i, x in enumerate(operands)]
        outs = [(pltpu.HBM if i in away_out else pltpu.VMEM)(x.shape, x.dtype) for i, x in enumerate(outs)]
        unused = [*latest, *before] if chained else []

        def kernel_on(*refs):
            kernel(*refs[: number + 1], *refs[number + 1 + len(unused) :])

        values = pl.pallas_call(
            kernel_on,
            out_shape=tuple(outs),
            in_specs=[SCALAR]
            + [AWAY if i in away_in else WHOLE for i in range(number)]
            + [pl.BlockSpec(memory_space=pl.ANY)] * len(unused),
            out_specs=tuple(AWAY if i in away_out else WHOLE for i in range(len(outs))),
            scratch_shapes=list(scratch),
            input_output_aliases=dict(aliases),
            compiler_params=PARAMS,
            cost_estimate=pl.CostEstimate(flops=work, bytes_accessed=1, transcendentals=0),
        )(me_array, *operands, *unused)
        if chained and 0 not in away_out:
            latest[:] = values[:1]
        return values

    raw = [exchange(tree_vectors, 1), exchange(tree_factors, 1)]
    blocks = count // 2
    more = count - blocks
    both = jax.ShapeDtypeStruct((2, width, rows), BF16), jax.ShapeDtypeStruct((2, rows, width), BF16)
    rows_a = blocks * half + half
    own_a, away_one, away_two, rest_a, later, inverse_factor, across, combined = call(
        leaf_first_kernel, (trailing, leaf_vectors, leaf_factors, inverse_factor),
        [shape(rows_a, width), shape(rows_a // 2, width), shape(rows_a // 2, width)]
        + [shape(blocks, width, width), shape(more, rows, width), shape(width, width), *both],
        [
            vmem(blocks, rows, width), vmem(rows, width), vmem(width, width), vmem(width, width), vmem(rows_a, width),
            sems(count * (rows // width) + 3),
        ],
        range(4),
    )
    there_a = [exchange(away_one, 1), exchange(away_two, 1)]

    chip_low, chip_high, chip_part = call(
        pack_kernel, (tree_vectors, tree_factors, *raw),
        (shape(2, *part_shape), shape(2, *part_shape), shape(*part_shape)),
        [vmem(4, width, width), sems(4)], (),
    )
    plane_parts = [exchange(chip_part, 2 * r) for r in (3, 1, 2)]
    plane_parts = [plane_parts[1], plane_parts[2], plane_parts[0]]

    own_b, rest_b, *aways = call(
        leaf_second_kernel, (later, across, combined),
        [shape(more * half, width), shape(more, width, width)] + [shape(half, width)] * more,
        [vmem(width, width)], before=there_a,
    )
    theres = [exchange(away, 1) for away in aways]
    cols = count * quarter
    outs = call(
        core_kernel, (own_a, own_b, *there_a, *theres, chip_high),
        [shape(cols, width)] * 8 + [shape(half, width)],
        [vmem(count * half, width), vmem(count * half, width)],
    )
    sends, dones, gram_half = outs[:4], outs[4:8], outs[8]
    for level in (levels - 1, 1, 2, *range(3, levels - 1)):
        (gram_half,) = call(
            add_kernel, (gram_half, exchange(gram_half, 1 << level)), (shape(half, width),), chained=False
        )
    stack, held_part = call(
        gather_kernel, (chip_part, *plane_parts), (shape(3, *part_shape), shape(*part_shape)), work=1,
    )
    gots = around(sends)
    stack_there = exchange(stack, 1)
    parts = [exchange(held_part, 8)]
    for level in range(4, levels):
        short = half // 2 + EXTRA if level == levels - 1 else half + EXTRA
        (held_part,) = call(
            functools.partial(hold_kernel, level=level - 1), (held_part, parts[-1]), (shape(short, width),),
            chained=False,
        )
        parts.append(exchange(held_part, 1 << level))

    def split(*dims):
        return jax.ShapeDtypeStruct(dims, BF16)

    joint, vectors, held = call(
        prepare_kernel, (chip_low, stack, stack_there),
        (split(3, 2, 2 * width, width), split(4, 2, width, width), shape(2, *part_shape)),
    )
    head, send, plane_done = call(
        functools.partial(plane_kernel, level=3), (*gots, joint, vectors),
        (shape(cols, width), shape(cols + 16, width), shape(4, cols, width)),
    )
    result = head
    for level in range(3, levels):
        part = parts[level - 3]
        last = level == levels - 1
        ready, *helds = call(
            functools.partial(ready_kernel, level=level), (held, part, exchange(part, 1)),
            [split(4 if last else 6, width, width)] + ([] if last else [shape(2, *part_shape)]),
        )
        operands = (head, result, send, exchange(send, 1 << level), ready)
        if last:
            _, updated, basis = call(
                store_kernel, (rest_a, rest_b, inverse_factor), (shape(8, width), shape(rows, columns), shape(rows, width)),
                [vmem(width, width), sems(count + 1)], (), (1, 2),
            )
            sends = call(
                functools.partial(last_kernel, level=level), (*operands, plane_done),
                [shape(cols + quarter, width)] * 4, [vmem(4, cols, width)],
            )
        else:
            (held,) = helds
            head, result, send = call(
                functools.partial(line_kernel, level=level), operands,
                [shape(cols, width), shape(cols, width), shape(cols, width)],
            )

    backs = around(sends)
    gram_there = exchange(gram_half, 1)
    theres = []
    for r in (0, 2):
        (passed,) = call(
            pass_kernel, (*backs[r : r + 2], *dones[r : r + 2]), (shape(2, cols + quarter + (8 if r == 0 else 0), width),),
            before=(gram_half,) if r == 2 else (),
        )
        theres.append(exchange(passed, 1))
    (updated,) = call(
        near_kernel, (*backs, *dones, updated), (shape(rows, columns),),
        [vmem(count, width, half), sems(count)], (8,), (0,), {9: 0},
    )
    return call(
        functools.partial(far_kernel, total=float(rows * devices)),
        (*backs, *dones, *theres, gram_half, gram_there, inverse_factor, updated, basis),
        (shape(rows, columns), shape(rows, width), shape(width, width)),
        [vmem(width, width), vmem(width, width), vmem(count, width, half), vmem(width, width), vmem(width, width), sems(count + 2)],
        (13, 14), (0, 1, 2), {14: 0, 15: 1},
    )


def solution(mesh):
    in_specs = (
        P("rows", None),
        P("rows", None),
        P("rows", None),
        P("rows", None),
        P("rows", None),
        P(),
    )
    out_specs = (P("rows", None), P("rows", None), P())
    return jax.shard_map(body, mesh=mesh, in_specs=in_specs, out_specs=out_specs, check_vma=False)
```
